32 devices in a mesh: items: 2 (over core), height: 4 (over y, x), tensor: 4 (over z).
Axes of the slice: x: 2, y: 2, z: 4, core: 2. Of those that a mesh axis runs over, the one named last changes fastest.
Arguments:
- hidden: float32 [2, 1024, 1280], P('items', 'height'), may hold values from -48 to 48
- text_states: float32 [2, 77, 2048], P('items'), may hold values from -6 to 6
- bucket: int32 [2], P('items'), may hold values from 0 to 2
- timestep: int32 [2], P('items'), may hold values from 0 to 999
- gain_in: float32 [1280], P(('items', 'height')), may hold values from 0.5 to 1.5
- conv_first: float32 [3, 3, 1280, 1280], P(None, None, ('items', 'height'), 'tensor'), may hold values from -0.0546875 to 0.0546875
- time_weight: float32 [1280, 1280], P(('items', 'height'), 'tensor'), may hold values from -0.15625 to 0.15625
- gain_mid: float32 [1280], P('tensor'), may hold values from 0.5 to 1.5
- conv_second: float32 [3, 3, 1280, 1280], P(None, None, 'tensor', ('items', 'height')), may hold values from -0.0546875 to 0.0546875
- gain_attn_norm: float32 [1280], P('tensor'), may hold values from 0.5 to 1.5
- proj_in: float32 [1280, 1280], P('tensor', ('items', 'height')), may hold values from -0.15625 to 0.15625
- gain_self: float32 [1280], P(('items', 'height')), may hold values from 0.5 to 1.5
- query_self: float32 [1280, 1280], P(('items', 'height'), 'tensor'), may hold values from -0.15625 to 0.15625
- key_self: float32 [1280, 1280], P(('items', 'height'), 'tensor'), may hold values from -0.25 to 0.25
- value_self: float32 [1280, 1280], P(('items', 'height'), 'tensor'), may hold values from -0.15625 to 0.15625
- out_self: float32 [1280, 1280], P('tensor', ('items', 'height')), may hold values from -2 to 2
- gain_cross: float32 [1280], P(('items', 'height')), may hold values from 0.5 to 1.5
- query_cross: float32 [1280, 1280], P(('items', 'height'), 'tensor'), may hold values from -0.25 to 0.25
- key_cross: float32 [2048, 1280], P(('items', 'height'), 'tensor'), may hold values from -0.125 to 0.125
- value_cross: float32 [2048, 1280], P(('items', 'height'), 'tensor'), may hold values from -0.125 to 0.125
- out_cross: float32 [1280, 1280], P('tensor', ('items', 'height')), may hold values from -0.5 to 0.5
- gain_ff: float32 [1280], P(('items', 'height')), may hold values from 0.5 to 1.5
- ff_in: float32 [1280, 2, 5120], P(('items', 'height'), None, 'tensor'), may hold values from -0.15625 to 0.15625
- ff_out: float32 [5120, 1280], P('tensor', ('items', 'height')), may hold values from -0.078125 to 0.078125
- proj_out: float32 [1280, 1280], P(('items', 'height'), 'tensor'), may hold values from -0.15625 to 0.15625
- cotangent: float32 [2, 1024, 1280], P('items', 'height', 'tensor'), may hold values from -6 to 6
Outputs:
- output: float32 [2, 1024, 1280], P('items', 'height', 'tensor')
- grad_hidden: float32 [2, 1024, 1280], P('items', 'height')
- grad_gain_in: float32 [1280], P(('items', 'height'))
- grad_conv_first: float32 [3, 3, 1280, 1280], P(None, None, ('items', 'height'), 'tensor')
- grad_time_weight: float32 [1280, 1280], P(('items', 'height'), 'tensor')
- grad_gain_mid: float32 [1280], P('tensor')
- grad_conv_second: float32 [3, 3, 1280, 1280], P(None, None, 'tensor', ('items', 'height'))
- grad_gain_attn_norm: float32 [1280], P('tensor')
- grad_proj_in: float32 [1280, 1280], P('tensor', ('items', 'height'))
- grad_gain_self: float32 [1280], P(('items', 'height'))
- grad_query_self: float32 [1280, 1280], P(('items', 'height'), 'tensor')
- grad_key_self: float32 [1280, 1280], P(('items', 'height'), 'tensor')
- grad_value_self: float32 [1280, 1280], P(('items', 'height'), 'tensor')
- grad_out_self: float32 [1280, 1280], P('tensor', ('items', 'height'))
- grad_gain_cross: float32 [1280], P(('items', 'height'))
- grad_query_cross: float32 [1280, 1280], P(('items', 'height'), 'tensor')
- grad_key_cross: float32 [2048, 1280], P(('items', 'height'), 'tensor')
- grad_value_cross: float32 [2048, 1280], P(('items', 'height'), 'tensor')
- grad_out_cross: float32 [1280, 1280], P('tensor', ('items', 'height'))
- grad_gain_ff: float32 [1280], P(('items', 'height'))
- grad_ff_in: float32 [1280, 2, 5120], P(('items', 'height'), None, 'tensor')
- grad_ff_out: float32 [5120, 1280], P('tensor', ('items', 'height'))
- grad_proj_out: float32 [1280, 1280], P(('items', 'height'), 'tensor')
The draws below stay inside these ranges and needn't reach their ends.
Inputs may be any that keep to these rules, and one draw needn't show every extreme that they name: bucket 0 is a 32 by 32 image, 1 is 24 by 40, 2 is 20 by 48.
All inputs are finite; a program needn't handle non-finite values.
Results may differ from the reference program's by a relative error of at most 0.0003.
Values sent between devices are 32-bit elements; how exact they have to be, the bound alone decides.
No kernel may reach another device: no remote copies, remote signals or barrier semaphores. Data moves between devices by JAX's collectives and lax.ppermute only.
A program may use at most 384 MiB of HBM per device.

```python
import math
import jax
import jax.numpy as jnp
from jax import lax

C = 1280
HEADS = 20
HEAD_DIM = 64
GROUPS = 32
FF = 5120
TEXT_DIM = 2048
TEXT_LEN = 77
SLOTS = 256
ITEMS = 2
ROWS_ALL = 1024
N_HEIGHT = 4


def draw_hidden(key, part):
    key = jax.random.fold_in(key, 11)
    base_key, chan_key, row_key = jax.random.split(key, 3)
    strip_count = ROWS_ALL // SLOTS
    strip_index = (jnp.arange(ROWS_ALL) // SLOTS).astype(jnp.float32)
    rising = jnp.exp(jnp.log(3.0) * strip_index / (strip_count - 1)) / 1.7
    channel_scale = jnp.exp(jax.random.uniform(chan_key, (C,), jnp.float32, -1.15, 1.15))
    jitter = jnp.exp(jax.random.uniform(row_key, (ITEMS, ROWS_ALL, 1), jnp.float32, -0.5, 0.5))
    base = jnp.clip(jax.random.normal(base_key, (ITEMS, ROWS_ALL, C), jnp.float32), -5.0, 5.0)
    return base * rising[None, :, None] * channel_scale * jitter


def levels(own_key, extent, cuts, low, top_value):
    def one(axis_at, parts):
        draws = jax.random.uniform(jax.random.fold_in(jax.random.fold_in(own_key, 6), axis_at), (parts,), jnp.float32, low / len(cuts), top_value / len(cuts))
        return jnp.repeat(jnp.exp(draws), extent[axis_at] // parts).reshape((-1,) + (1,) * (len(extent) - axis_at - 1))

    loudness = one(*cuts[0])
    for cut in cuts[1:]:
        loudness = loudness * one(*cut)
    return loudness


def scatter_about(key, extent, spread, bound, cuts=(), held_as=jnp.bfloat16):
    factor_of = levels(key, extent, cuts, -0.22, 0.18) if cuts else 1.0
    entries = jax.random.normal(key, extent, jnp.float32) * spread * factor_of
    return jnp.minimum(jnp.maximum(entries, -bound), bound).astype(held_as)


def setup_inputs(seed: int = 0) -> dict:
    streams_of = jax.random.split(jax.random.key(seed), 27)
    hidden = draw_hidden(jax.random.fold_in(streams_of[26], 71), 0)
    text_states = scatter_about(streams_of[1], (ITEMS, TEXT_LEN, TEXT_DIM), 1.0, 6.0, ((0, 2),), jnp.float32)
    bucket = jax.random.randint(streams_of[2], (ITEMS,), 0, 3).astype(jnp.int32)
    timestep = jax.random.randint(streams_of[3], (ITEMS,), 0, 1000).astype(jnp.int32)
    gain_in = jnp.clip(1.0 + 0.1 * jax.random.normal(streams_of[4], (C,), jnp.float32), 0.5, 1.5)
    conv_first = scatter_about(streams_of[5], (3, 3, C, C), (9 * C) ** -0.5, 0.0546875, ((2, 8), (3, 4)), jnp.float32)
    time_weight = scatter_about(streams_of[6], (C, C), C ** -0.5, 0.15625, ((0, 8), (1, 4)), jnp.float32)
    gain_mid = jnp.clip(1.0 + 0.1 * jax.random.normal(streams_of[7], (C,), jnp.float32), 0.5, 1.5)
    conv_second = scatter_about(streams_of[8], (3, 3, C, C), (9 * C) ** -0.5, 0.0546875, ((2, 4), (3, 8)), jnp.float32)
    gain_attn_norm = jnp.clip(1.0 + 0.1 * jax.random.normal(streams_of[9], (C,), jnp.float32), 0.5, 1.5)
    proj_in = scatter_about(streams_of[10], (C, C), C ** -0.5, 0.15625, ((0, 4), (1, 8)), jnp.float32)
    gain_self = jnp.clip(1.0 + 0.1 * jax.random.normal(streams_of[11], (C,), jnp.float32), 0.5, 1.5)
    query_self = scatter_about(streams_of[12], (C, C), C ** -0.5, 0.15625, ((0, 8), (1, 4)), jnp.float32)
    key_self = scatter_about(streams_of[13], (C, C), (C // 2) ** -0.5, 0.25, ((0, 8), (1, 4)), jnp.float32)
    value_self = scatter_about(streams_of[14], (C, C), C ** -0.5, 0.15625, ((0, 8), (1, 4)), jnp.float32)
    out_self = scatter_about(streams_of[15], (C, C), 10 ** -0.5, 2.0, ((0, 4), (1, 8)), jnp.float32)
    gain_cross = jnp.clip(1.0 + 0.1 * jax.random.normal(streams_of[16], (C,), jnp.float32), 0.5, 1.5)
    query_cross = scatter_about(streams_of[17], (C, C), (C // 2) ** -0.5, 0.25, ((0, 8), (1, 4)), jnp.float32)
    key_cross = scatter_about(streams_of[18], (TEXT_DIM, C), TEXT_DIM ** -0.5, 0.125, ((0, 8), (1, 4)), jnp.float32)
    value_cross = scatter_about(streams_of[19], (TEXT_DIM, C), TEXT_DIM ** -0.5, 0.125, ((0, 8), (1, 4)), jnp.float32)
    out_cross = scatter_about(streams_of[20], (C, C), 120 ** -0.5, 0.5, ((0, 4), (1, 8)), jnp.float32)
    gain_ff = jnp.clip(1.0 + 0.1 * jax.random.normal(streams_of[21], (C,), jnp.float32), 0.5, 1.5)
    ff_in = scatter_about(streams_of[22], (C, 2, FF), C ** -0.5, 0.15625, ((0, 8), (2, 4)), jnp.float32)
    ff_out = scatter_about(streams_of[23], (FF, C), FF ** -0.5, 0.078125, ((0, 4), (1, 8)), jnp.float32)
    proj_out = scatter_about(streams_of[24], (C, C), C ** -0.5, 0.15625, ((0, 8), (1, 4)), jnp.float32)
    cotangent = scatter_about(streams_of[25], (ITEMS, ROWS_ALL, C), 1.0, 6.0, ((0, 2), (1, 4), (2, 4)), jnp.float32)
    return dict(hidden=hidden, text_states=text_states, bucket=bucket, timestep=timestep, gain_in=gain_in, conv_first=conv_first, time_weight=time_weight, gain_mid=gain_mid, conv_second=conv_second, gain_attn_norm=gain_attn_norm, proj_in=proj_in, gain_self=gain_self, query_self=query_self, key_self=key_self, value_self=value_self, out_self=out_self, gain_cross=gain_cross, query_cross=query_cross, key_cross=key_cross, value_cross=value_cross, out_cross=out_cross, gain_ff=gain_ff, ff_in=ff_in, ff_out=ff_out, proj_out=proj_out, cotangent=cotangent)


highest = lax.Precision.HIGHEST
norm_eps = 1e-05
masked_score = -1e+30
margin_rows = 64

def grid_shape(bucket):
    strip_rows = jnp.where(bucket == 0, 8, jnp.where(bucket == 1, 6, 5)).astype(jnp.int32)
    strip_width = jnp.where(bucket == 0, 32, jnp.where(bucket == 1, 40, 48)).astype(jnp.int32)
    return (strip_rows, strip_width)

def matmul(left, right):
    return jnp.dot(left, right, precision=highest, preferred_element_type=jnp.float32)

def to_image(rows_flat, strip_rows, strip_width):
    cell_span = strip_rows * strip_width
    place_index = jnp.arange(N_HEIGHT * SLOTS, dtype=jnp.int32)
    strip_index = jnp.minimum(place_index // cell_span, N_HEIGHT - 1)
    source = (strip_index * SLOTS + place_index % cell_span).astype(jnp.int32)
    valid_mask = place_index < N_HEIGHT * cell_span
    return (rows_flat[source] * valid_mask[:, None].astype(jnp.float32), valid_mask)

def to_strips(image_cells, strip_rows, strip_width):
    cell_span = strip_rows * strip_width
    place_index = jnp.arange(N_HEIGHT * SLOTS, dtype=jnp.int32)
    within = place_index % SLOTS
    source = jnp.minimum(place_index // SLOTS * cell_span + within, N_HEIGHT * SLOTS - 1).astype(jnp.int32)
    return image_cells[source] * (within < cell_span)[:, None].astype(jnp.float32)

def conv_image(image_cells, weight, strip_width, valid_mask):
    length = image_cells.shape[0]
    padded = jnp.pad(image_cells, ((margin_rows, margin_rows), (0, 0)))
    column = jnp.arange(length, dtype=jnp.int32) % strip_width
    accum = jnp.zeros((length, weight.shape[3]), jnp.float32)
    for row_step in (-1, 0, 1):
        for col_step in (-1, 0, 1):
            shifted = lax.dynamic_slice_in_dim(padded, margin_rows + row_step * strip_width + col_step, length, 0)
            keep_mask = valid_mask & (column + col_step >= 0) & (column + col_step < strip_width)
            accum = accum + matmul(shifted * keep_mask[:, None].astype(jnp.float32), weight[row_step + 1, col_step + 1])
    return accum * valid_mask[:, None].astype(jnp.float32)

def group_norm(image_cells, gain_vector, valid_col, group_count):
    length, channels = image_cells.shape
    size_group = channels // GROUPS
    grouped = (image_cells * valid_col).reshape(length, GROUPS, size_group)
    mean_val = lax.optimization_barrier(jnp.sum(grouped, axis=(0, 2))) / group_count
    var_val = lax.optimization_barrier(jnp.sum(grouped * grouped, axis=(0, 2))) / group_count - mean_val * mean_val
    mean_chan = jnp.repeat(mean_val, size_group)
    inv_chan = jnp.repeat(lax.rsqrt(var_val + norm_eps), size_group)
    return (image_cells - mean_chan) * inv_chan * valid_col * gain_vector

def layer_norm(values, gain_vector):
    mean_val = lax.optimization_barrier(jnp.mean(values, axis=-1, keepdims=True))
    var_val = lax.optimization_barrier(jnp.mean(values * values, axis=-1, keepdims=True)) - mean_val * mean_val
    return (values - mean_val) * lax.rsqrt(var_val + norm_eps) * gain_vector

def attend(queries, keys_all, values_all, key_valid):
    row_count = queries.shape[0]
    query_heads = queries.reshape(row_count, HEADS, HEAD_DIM)
    key_heads = keys_all.reshape(keys_all.shape[0], HEADS, HEAD_DIM)
    value_heads = values_all.reshape(values_all.shape[0], HEADS, HEAD_DIM)
    scores = jnp.einsum('qhd,khd->hqk', query_heads, key_heads, precision=highest) * (1.0 / math.sqrt(HEAD_DIM))
    scores = jnp.where(key_valid[None, None, :], scores, masked_score)
    row_peak = lax.optimization_barrier(jnp.max(scores, axis=-1, keepdims=True))
    exponent = jnp.exp(scores - row_peak)
    soft_weights = exponent / lax.optimization_barrier(jnp.sum(exponent, axis=-1, keepdims=True))
    attended = jnp.einsum('hqk,khd->qhd', soft_weights, value_heads, precision=highest)
    return attended.reshape(row_count, HEADS * HEAD_DIM)

def time_features(time_item):
    half_width = C // 2
    frequency = jnp.exp(-math.log(10000.0) * jnp.arange(half_width, dtype=jnp.float32) / half_width)
    angles = time_item.astype(jnp.float32) * frequency
    return jnp.concatenate([jnp.cos(angles), jnp.sin(angles)], axis=0)

def item_forward(params, rows_flat, text_item, bucket_item, time_item):
    gain_in, conv_first, time_weight, gain_mid, conv_second, gain_attn_norm, proj_in, gain_self, query_self, key_self, value_self, out_self, gain_cross, query_cross, key_cross, value_cross, out_cross, gain_ff, ff_in, ff_out, proj_out = params
    strip_rows, strip_width = grid_shape(bucket_item)
    image_cells, valid_mask = to_image(rows_flat, strip_rows, strip_width)
    valid_col = valid_mask[:, None].astype(jnp.float32)
    group_count = (N_HEIGHT * strip_rows * strip_width * (C // GROUPS)).astype(jnp.float32)
    act_first = jax.nn.silu(group_norm(image_cells, gain_in, valid_col, group_count))
    time_term = matmul(jax.nn.silu(time_features(time_item))[None, :], time_weight)
    conv_one = (conv_image(act_first, conv_first, strip_width, valid_mask) + time_term) * valid_col
    act_second = jax.nn.silu(group_norm(conv_one, gain_mid, valid_col, group_count))
    residual = image_cells + conv_image(act_second, conv_second, strip_width, valid_mask)
    projected = matmul(group_norm(residual, gain_attn_norm, valid_col, group_count), proj_in)
    normed_self = layer_norm(projected, gain_self)
    attended_self = attend(matmul(normed_self, query_self), matmul(normed_self, key_self), matmul(normed_self, value_self), valid_mask)
    after_self = projected + matmul(attended_self, out_self)
    normed_cross = layer_norm(after_self, gain_cross)
    text_valid = jnp.ones((text_item.shape[0],), dtype=bool)
    attended_cross = attend(matmul(normed_cross, query_cross), matmul(text_item, key_cross), matmul(text_item, value_cross), text_valid)
    after_cross = after_self + matmul(attended_cross, out_cross)
    normed_ff = layer_norm(after_cross, gain_ff)
    hidden_ff = jnp.einsum('lc,cjf->ljf', normed_ff, ff_in, precision=highest)
    ff_act = hidden_ff[:, 0] * jax.nn.gelu(hidden_ff[:, 1], approximate=False)
    after_ff = after_cross + matmul(ff_act, ff_out)
    image_out = (residual + matmul(after_ff, proj_out)) * valid_col
    return to_strips(image_out, strip_rows, strip_width)

def reference(hidden, text_states, bucket, timestep, gain_in, conv_first, time_weight, gain_mid, conv_second, gain_attn_norm, proj_in, gain_self, query_self, key_self, value_self, out_self, gain_cross, query_cross, key_cross, value_cross, out_cross, gain_ff, ff_in, ff_out, proj_out, cotangent):
    params = (gain_in, conv_first, time_weight, gain_mid, conv_second, gain_attn_norm, proj_in, gain_self, query_self, key_self, value_self, out_self, gain_cross, query_cross, key_cross, value_cross, out_cross, gain_ff, ff_in, ff_out, proj_out)

    def forward_all(hidden_in, param_list):

        def item_step(operands):
            return item_forward(param_list, operands[0], operands[1], operands[2], operands[3])
        return lax.map(jax.checkpoint(item_step), (hidden_in, text_states, bucket, timestep))
    output, pullback = jax.vjp(forward_all, hidden, params)
    grad_hidden, grad_params = pullback(cotangent)
    return (output, grad_hidden, grad_params[0], grad_params[1], grad_params[2], grad_params[3], grad_params[4], grad_params[5], grad_params[6], grad_params[7], grad_params[8], grad_params[9], grad_params[10], grad_params[11], grad_params[12], grad_params[13], grad_params[14], grad_params[15], grad_params[16], grad_params[17], grad_params[18], grad_params[19], grad_params[20])
```

```python
import functools
import math

import jax
import jax.numpy as jnp
from jax import lax
from jax.experimental import pallas as pl
from jax.experimental.pallas import tpu as pltpu
from jax.sharding import PartitionSpec as P

HEAD_DIM = 64
GROUPS = 32
EDGE = 48


highest = lax.Precision.HIGHEST
norm_eps = 1e-05
masked_score = -1e30
edge_margin = 56
high = lax.Precision.HIGH
margin = 64
I, H, T = "items", "height", "tensor"
IH = (I, H)
E0 = "bc,bn->cn"
E1 = "bhqk,bkhd->bqhd"
E2 = "bhqk,bqhd->bkhd"
E3 = "bqhd,bkhd->bhqk"
E4 = "bqhd,bqhd->bhq"
E5 = "bsc,bsjf->cjf"
E6 = "bsc,cjf->bsjf"
E7 = "bsjf,cjf->bsc"
E8 = "bsk,bsn->kn"
E9 = "bsk,kn->bsn"
E10 = "bsn,kn->bsk"
QK, PV, PQ = "qhd,khd->hqk", "hqk,khd->qhd", "hqk,qhd->khd"


def padded_2(block, sides, width):
    for axis, dim in sides:
        count = lax.axis_size(axis)
        forward = [(i, i + 1) for i in range(count - 1)]
        backward = [(target, source) for source, target in forward]
        low = lax.ppermute(
            lax.slice_in_dim(block, block.shape[dim] - width, None, axis=dim), axis, forward
        )
        high = lax.ppermute(lax.slice_in_dim(block, 0, width, axis=dim), axis, backward)
        block = jnp.concatenate([low, block, high], axis=dim)
    return block


def grid_shape(bucket):
    strip_rows = jnp.where(bucket == 0, 8, jnp.where(bucket == 1, 6, 5)).astype(jnp.int32)
    strip_width = jnp.where(bucket == 0, 32, jnp.where(bucket == 1, 40, 48)).astype(jnp.int32)
    return (strip_rows, strip_width)


def tokens_dot(values, weight):
    return jnp.einsum(E9, values, weight, precision=highest)


def tokens_back(grad_values, weight):
    return jnp.einsum(E10, grad_values, weight, precision=highest)


def tokens_grad(values, grad_values):
    return jnp.einsum(E8, values, grad_values, precision=highest)


def tensor_sum(values):
    return lax.psum(values, T)


def expand_groups(stat, size_group):
    return jnp.repeat(stat, size_group, axis=1)[:, None, :]


def group_stats(values, valid_col, group_count, counts):
    item_count, slot_count, channels = values.shape
    size_group = channels // group_count
    grouped = (values * valid_col).reshape(item_count, slot_count, group_count, size_group)
    sum_values = jnp.sum(grouped, axis=(1, 3))
    sum_squares = jnp.sum(grouped * grouped, axis=(1, 3))
    sum_values, sum_squares = lax.psum((sum_values, sum_squares), H)
    mean_val = sum_values / counts[:, None]
    var_val = sum_squares / counts[:, None] - mean_val * mean_val
    return (
        expand_groups(mean_val, size_group),
        expand_groups(lax.rsqrt(var_val + norm_eps), size_group),
    )


def group_back(grad_out, centred, inv_std, gain_vector, valid_col, group_count, counts):
    item_count, slot_count, channels = grad_out.shape
    size_group = channels // group_count
    scaled = grad_out * gain_vector * valid_col
    sum_first = jnp.sum(
        scaled.reshape(item_count, slot_count, group_count, size_group), axis=(1, 3)
    )
    sum_second = jnp.sum(
        (scaled * centred).reshape(item_count, slot_count, group_count, size_group), axis=(1, 3)
    )
    sum_first, sum_second = lax.psum((sum_first, sum_second), H)
    mean_first = expand_groups(sum_first / counts[:, None], size_group)
    mean_second = expand_groups(sum_second / counts[:, None], size_group)
    grad_in = inv_std * (scaled - mean_first - centred * mean_second) * valid_col
    return (grad_in, jnp.sum(grad_out * centred, axis=(0, 1)))


def layer_norm(values, gain_vector):
    mean_val = jnp.mean(values, axis=-1, keepdims=True)
    var_val = jnp.mean(values * values, axis=-1, keepdims=True) - mean_val * mean_val
    inv_std = lax.rsqrt(var_val + norm_eps)
    centred = (values - mean_val) * inv_std
    return (centred * gain_vector, centred, inv_std)


def layer_back(grad_out, centred, inv_std, gain_vector):
    scaled = grad_out * gain_vector
    grad_in = inv_std * (
        scaled
        - jnp.mean(scaled, axis=-1, keepdims=True)
        - centred * jnp.mean(scaled * centred, axis=-1, keepdims=True)
    )
    return (grad_in, jnp.sum(grad_out * centred, axis=(0, 1)))


def edge_rows(values, strip_rows, strip_width):
    item_count, slot_count, channels = values.shape
    position = jnp.arange(EDGE, dtype=jnp.int32)

    def edge_one_item(item_vals, rows_here, width_here):
        keep_mask = (position < width_here)[:, None].astype(jnp.float32)
        padded = jnp.concatenate([item_vals, jnp.zeros((EDGE, channels), jnp.float32)], axis=0)
        top_row = item_vals[:EDGE] * keep_mask
        bottom_row = (
            lax.dynamic_slice_in_dim(padded, (rows_here - 1) * width_here, EDGE, 0) * keep_mask
        )
        return jnp.stack([top_row, bottom_row])

    return jax.vmap(edge_one_item)(values, strip_rows, strip_width)


def neighbour_stack(values, strip_rows, strip_width):
    edge_pair = edge_rows(values, strip_rows, strip_width)
    beside_all = padded_2(edge_pair, ((H, 1),), 1)
    item_count, slot_count, channels = values.shape
    position = jnp.arange(slot_count, dtype=jnp.int32)

    def neighbour_one_item(item_vals, item_around, rows_here, width_here):
        cell_span = rows_here * width_here
        extended = jnp.zeros((2 * edge_margin + slot_count, channels), jnp.float32)
        extended = lax.dynamic_update_slice_in_dim(
            extended, item_around[0], edge_margin - width_here, 0
        )
        extended = lax.dynamic_update_slice_in_dim(extended, item_vals, edge_margin, 0)
        extended = lax.dynamic_update_slice_in_dim(
            extended, item_around[3], edge_margin + cell_span, 0
        )
        column = position % width_here
        shifted_list = []
        for row_step in (-1, 0, 1):
            for col_step in (-1, 0, 1):
                shifted = lax.dynamic_slice_in_dim(
                    extended, edge_margin + row_step * width_here + col_step, slot_count, 0
                )
                keep_mask = (
                    (column + col_step >= 0)
                    & (column + col_step < width_here)
                    & (position < cell_span)
                )
                shifted_list.append(shifted * keep_mask[:, None].astype(jnp.float32))
        return jnp.stack(shifted_list, axis=1)

    return jax.vmap(neighbour_one_item)(values, beside_all, strip_rows, strip_width)


def conv_apply(neighbours, weight):
    item_count, slot_count = (neighbours.shape[0], neighbours.shape[1])
    flattened = neighbours.reshape(item_count, slot_count, -1)
    return tokens_dot(flattened, weight.reshape(-1, weight.shape[3]))


def conv_input_grad(neighbours_grad, weight):
    flipped = jnp.transpose(weight[::-1, ::-1], (0, 1, 3, 2))
    return conv_apply(neighbours_grad, flipped)


def conv_weight_grad(neighbours, grad_out, weight_shape):
    flattened = neighbours.reshape(neighbours.shape[0], neighbours.shape[1], -1)
    return tokens_grad(flattened, grad_out).reshape(weight_shape)


def time_features(timestep, channels):
    half_width = channels // 2
    frequency = jnp.exp(-math.log(10000.0) * jnp.arange(half_width, dtype=jnp.float32) / half_width)
    angles = timestep.astype(jnp.float32)[:, None] * frequency[None, :]
    return jnp.concatenate([jnp.cos(angles), jnp.sin(angles)], axis=1)


def exact_gelu(values):
    return jax.nn.gelu(values, approximate=False)


def head_split(values, heads_here):
    return values.reshape(
        values.shape[0], values.shape[1], heads_here, values.shape[2] // heads_here
    )


def score_block(queries, keys_all, key_valid, heads_here):
    head_size = queries.shape[2] // heads_here
    scores = jnp.einsum(
        E3,
        head_split(queries, heads_here),
        head_split(keys_all, heads_here),
        precision=highest,
    ) * (1.0 / math.sqrt(head_size))
    return jnp.where(key_valid[:, None, None, :], scores, masked_score)


def attend(queries, keys_all, values_all, key_valid, heads_here):
    scores = score_block(queries, keys_all, key_valid, heads_here)
    row_peak = jnp.max(scores, axis=-1, keepdims=True)
    exponent = jnp.exp(scores - row_peak)
    row_total = jnp.sum(exponent, axis=-1, keepdims=True)
    soft_weights = exponent / row_total
    attended = jnp.einsum(
        E1, soft_weights, head_split(values_all, heads_here), precision=highest
    )
    return (attended.reshape(queries.shape), row_peak + jnp.log(row_total))


def attend_back(
    queries, keys_all, values_all, key_valid, heads_here, attended, log_total, grad_attended
):
    head_size = queries.shape[2] // heads_here
    scaling = 1.0 / math.sqrt(head_size)
    soft_weights = jnp.exp(score_block(queries, keys_all, key_valid, heads_here) - log_total)
    grad_heads = head_split(grad_attended, heads_here)
    grad_soft = jnp.einsum(
        E3, grad_heads, head_split(values_all, heads_here), precision=highest
    )
    row_delta = jnp.einsum(
        E4, grad_heads, head_split(attended, heads_here), precision=highest
    )
    grad_scores = soft_weights * (grad_soft - row_delta[..., None])
    grad_query = (
        jnp.einsum(
            E1, grad_scores, head_split(keys_all, heads_here), precision=highest
        )
        * scaling
    )
    grad_key = (
        jnp.einsum(
            E2, grad_scores, head_split(queries, heads_here), precision=highest
        )
        * scaling
    )
    grad_value = jnp.einsum(E2, soft_weights, grad_heads, precision=highest)
    return (
        grad_query.reshape(queries.shape),
        grad_key.reshape(keys_all.shape),
        grad_value.reshape(values_all.shape),
    )


def shards(
    hidden,
    text_states,
    bucket,
    timestep,
    gain_in,
    conv_first,
    time_weight,
    gain_mid,
    conv_second,
    gain_attn_norm,
    proj_in,
    gain_self,
    query_self,
    key_self,
    value_self,
    out_self,
    gain_cross,
    query_cross,
    key_cross,
    value_cross,
    out_cross,
    gain_ff,
    ff_in,
    ff_out,
    proj_out,
    cotangent,
):
    item_count, slot_count, channels = hidden.shape
    local_width = gain_mid.shape[0]
    local_groups = GROUPS * local_width // channels
    heads_here = local_width // HEAD_DIM
    height_count = lax.axis_size(H)
    width_ih = lax.axis_size(I) * lax.axis_size(H)
    offset = lax.axis_index(T) * local_width
    strip_rows, strip_width = grid_shape(bucket)
    cell_span = strip_rows * strip_width
    position = jnp.arange(slot_count, dtype=jnp.int32)
    valid_mask = position[None, :] < cell_span[:, None]
    valid_col = valid_mask[:, :, None].astype(jnp.float32)
    full_counts = (height_count * cell_span * (channels // GROUPS)).astype(jnp.float32)
    key_valid = jnp.tile(valid_mask, (1, height_count))
    text_valid = jnp.ones((item_count, text_states.shape[1]), dtype=bool)
    resnet_full = (
        lax.all_gather(gain_in, IH, axis=0, tiled=True),
        lax.all_gather(conv_first, IH, axis=2, tiled=True),
        lax.all_gather(time_weight, IH, axis=0, tiled=True),
        lax.all_gather(conv_second, IH, axis=3, tiled=True),
    )
    block_full = (
        lax.all_gather(proj_in, IH, axis=1, tiled=True),
        lax.all_gather(gain_self, IH, axis=0, tiled=True),
        lax.all_gather(query_self, IH, axis=0, tiled=True),
        lax.all_gather(key_self, IH, axis=0, tiled=True),
        lax.all_gather(value_self, IH, axis=0, tiled=True),
        lax.all_gather(out_self, IH, axis=1, tiled=True),
        lax.all_gather(gain_cross, IH, axis=0, tiled=True),
        lax.all_gather(query_cross, IH, axis=0, tiled=True),
        lax.all_gather(key_cross, IH, axis=0, tiled=True),
        lax.all_gather(value_cross, IH, axis=0, tiled=True),
        lax.all_gather(out_cross, IH, axis=1, tiled=True),
        lax.all_gather(gain_ff, IH, axis=0, tiled=True),
        lax.all_gather(ff_in, IH, axis=0, tiled=True),
        lax.all_gather(ff_out, IH, axis=1, tiled=True),
        lax.all_gather(proj_out, IH, axis=0, tiled=True),
    )
    gain_in_full, conv_first_full, time_full, conv_second_full = resnet_full
    (
        proj_in_full,
        gain_self_full,
        query_self_full,
        key_self_full,
        value_self_full,
        out_self_full,
        gain_cross_full,
        query_cross_full,
        key_cross_full,
        value_cross_full,
        out_cross_full,
        gain_ff_full,
        ff_in_full,
        ff_out_full,
        proj_out_full,
    ) = block_full
    source = hidden * valid_col
    mean_one, inv_one = group_stats(source, valid_col, GROUPS, full_counts)
    centred_one = (source - mean_one) * inv_one * valid_col
    norm_one = centred_one * gain_in_full
    act_one, silu_pull_one = jax.vjp(jax.nn.silu, norm_one)
    stack_one = neighbour_stack(act_one, strip_rows, strip_width)
    silu_features = jax.nn.silu(time_features(timestep, channels))
    time_term = jnp.dot(
        silu_features, time_full, precision=highest, preferred_element_type=jnp.float32
    )
    conv_one = (conv_apply(stack_one, conv_first_full) + time_term[:, None, :]) * valid_col
    mean_two, inv_two = group_stats(conv_one, valid_col, local_groups, full_counts)
    centred_two = (conv_one - mean_two) * inv_two * valid_col
    norm_two = centred_two * gain_mid
    act_two, silu_pull_two = jax.vjp(jax.nn.silu, norm_two)
    stack_two = neighbour_stack(act_two, strip_rows, strip_width)
    conv_two = tensor_sum(conv_apply(stack_two, conv_second_full)) * valid_col
    residual = source + conv_two
    residual_local = lax.dynamic_slice_in_dim(residual, offset, local_width, 2)
    mean_three, inv_three = group_stats(residual_local, valid_col, local_groups, full_counts)
    centred_three = (residual_local - mean_three) * inv_three * valid_col
    norm_three = centred_three * gain_attn_norm
    projected = tensor_sum(tokens_dot(norm_three, proj_in_full))
    normed_self, centred_self, inv_self = layer_norm(projected, gain_self_full)
    queries = tokens_dot(normed_self, query_self_full)
    keys_here = tokens_dot(normed_self, key_self_full)
    values_here = tokens_dot(normed_self, value_self_full)
    keys_all, values_all = (
        lax.all_gather(keys_here, H, axis=1, tiled=True),
        lax.all_gather(values_here, H, axis=1, tiled=True),
    )
    attn_self, total_self = attend(queries, keys_all, values_all, key_valid, heads_here)
    after_self = projected + tensor_sum(tokens_dot(attn_self, out_self_full))
    normed_cross, centred_cross, inv_cross = layer_norm(after_self, gain_cross_full)
    queries_cross = tokens_dot(normed_cross, query_cross_full)
    keys_text = tokens_dot(text_states, key_cross_full)
    values_text = tokens_dot(text_states, value_cross_full)
    attn_cross, total_cross = attend(queries_cross, keys_text, values_text, text_valid, heads_here)
    after_cross = after_self + tensor_sum(tokens_dot(attn_cross, out_cross_full))
    normed_ff, centred_ff, inv_ff = layer_norm(after_cross, gain_ff_full)
    hidden_ff = jnp.einsum(E6, normed_ff, ff_in_full, precision=highest)
    value_half = hidden_ff[:, :, 0]
    gate_act, gelu_pull = jax.vjp(exact_gelu, hidden_ff[:, :, 1])
    ff_act = value_half * gate_act
    after_ff = after_cross + tensor_sum(tokens_dot(ff_act, ff_out_full))
    output = (residual_local + tokens_dot(after_ff, proj_out_full)) * valid_col
    (
        proj_in_back,
        gain_self_back,
        query_self_back,
        key_self_back,
        value_self_back,
        out_self_back,
        gain_cross_back,
        query_cross_back,
        key_cross_back,
        value_cross_back,
        out_cross_back,
        gain_ff_back,
        ff_in_back,
        ff_out_back,
        proj_out_back,
    ) = block_full
    grad_local = cotangent * valid_col
    grad_proj_out = tokens_grad(after_ff, grad_local)
    grad_after_ff = tensor_sum(tokens_back(grad_local, proj_out_back))
    grad_ff_out = tokens_grad(ff_act, grad_after_ff)
    grad_ff_act = tokens_back(grad_after_ff, ff_out_back)
    grad_value_half = grad_ff_act * gate_act
    grad_gate_half = gelu_pull(grad_ff_act * value_half)[0]
    grad_hidden_ff = jnp.stack([grad_value_half, grad_gate_half], axis=2)
    grad_ff_in = jnp.einsum(E5, normed_ff, grad_hidden_ff, precision=highest)
    grad_normed_ff = tensor_sum(
        jnp.einsum(E7, grad_hidden_ff, ff_in_back, precision=highest)
    )
    back_ff, grad_gain_ff = layer_back(grad_normed_ff, centred_ff, inv_ff, gain_ff_back)
    grad_after_cross = grad_after_ff + back_ff
    grad_out_cross = tokens_grad(attn_cross, grad_after_cross)
    grad_attn_cross = tokens_back(grad_after_cross, out_cross_back)
    grad_queries_cross, grad_keys_text, grad_values_text = attend_back(
        queries_cross,
        keys_text,
        values_text,
        text_valid,
        heads_here,
        attn_cross,
        total_cross,
        grad_attn_cross,
    )
    grad_query_cross = tokens_grad(normed_cross, grad_queries_cross)
    grad_key_cross = tokens_grad(text_states, grad_keys_text)
    grad_value_cross = tokens_grad(text_states, grad_values_text)
    grad_normed_cross = tensor_sum(tokens_back(grad_queries_cross, query_cross_back))
    back_cross, grad_gain_cross = layer_back(
        grad_normed_cross, centred_cross, inv_cross, gain_cross_back
    )
    grad_after_self = grad_after_cross + back_cross
    grad_out_self = tokens_grad(attn_self, grad_after_self)
    grad_attn_self = tokens_back(grad_after_self, out_self_back)
    grad_queries, grad_keys_all, grad_values_all = attend_back(
        queries, keys_all, values_all, key_valid, heads_here, attn_self, total_self, grad_attn_self
    )
    grad_keys_here, grad_values_here = (
        lax.psum_scatter(grad_keys_all, H, scatter_dimension=1, tiled=True),
        lax.psum_scatter(grad_values_all, H, scatter_dimension=1, tiled=True),
    )
    grad_query_self = tokens_grad(normed_self, grad_queries)
    grad_key_self = tokens_grad(normed_self, grad_keys_here)
    grad_value_self = tokens_grad(normed_self, grad_values_here)
    grad_normed_self = tensor_sum(
        tokens_back(grad_queries, query_self_back)
        + tokens_back(grad_keys_here, key_self_back)
        + tokens_back(grad_values_here, value_self_back)
    )
    back_self, grad_gain_self = layer_back(grad_normed_self, centred_self, inv_self, gain_self_back)
    grad_projected = grad_after_self + back_self
    grad_proj_in = tokens_grad(norm_three, grad_projected)
    grad_norm_three = tokens_back(grad_projected, proj_in_back)
    back_three, grad_gain_attn = group_back(
        grad_norm_three,
        centred_three,
        inv_three,
        gain_attn_norm,
        valid_col,
        local_groups,
        full_counts,
    )
    grad_residual_local = grad_local + back_three
    block_grads = (
        lax.psum_scatter(grad_proj_in, IH, scatter_dimension=1, tiled=True),
        lax.psum_scatter(
            jnp.tile(grad_gain_attn, width_ih), IH, scatter_dimension=0, tiled=True
        ),
        lax.psum_scatter(grad_gain_self, IH, scatter_dimension=0, tiled=True),
        lax.psum_scatter(grad_query_self, IH, scatter_dimension=0, tiled=True),
        lax.psum_scatter(grad_key_self, IH, scatter_dimension=0, tiled=True),
        lax.psum_scatter(grad_value_self, IH, scatter_dimension=0, tiled=True),
        lax.psum_scatter(grad_out_self, IH, scatter_dimension=1, tiled=True),
        lax.psum_scatter(grad_gain_cross, IH, scatter_dimension=0, tiled=True),
        lax.psum_scatter(grad_query_cross, IH, scatter_dimension=0, tiled=True),
        lax.psum_scatter(grad_key_cross, IH, scatter_dimension=0, tiled=True),
        lax.psum_scatter(grad_value_cross, IH, scatter_dimension=0, tiled=True),
        lax.psum_scatter(grad_out_cross, IH, scatter_dimension=1, tiled=True),
        lax.psum_scatter(grad_gain_ff, IH, scatter_dimension=0, tiled=True),
        lax.psum_scatter(grad_ff_in, IH, scatter_dimension=0, tiled=True),
        lax.psum_scatter(grad_ff_out, IH, scatter_dimension=1, tiled=True),
        lax.psum_scatter(grad_proj_out, IH, scatter_dimension=0, tiled=True),
    )
    gain_in_back, conv_first_back, time_back, conv_second_back = resnet_full
    grad_residual = lax.all_gather(grad_residual_local, T, axis=2, tiled=True)
    grad_conv_second = conv_weight_grad(stack_two, grad_residual, conv_second_back.shape)
    stack_grad_two = neighbour_stack(grad_residual, strip_rows, strip_width)
    grad_act_two = conv_input_grad(stack_grad_two, conv_second_back)
    grad_norm_two = silu_pull_two(grad_act_two)[0]
    grad_conv_one, grad_gain_mid = group_back(
        grad_norm_two, centred_two, inv_two, gain_mid, valid_col, local_groups, full_counts
    )
    grad_time_term = jnp.sum(grad_conv_one, axis=1)
    grad_time_weight = jnp.einsum(E0, silu_features, grad_time_term, precision=highest)
    grad_conv_first = conv_weight_grad(stack_one, grad_conv_one, conv_first_back.shape)
    stack_grad_one = neighbour_stack(grad_conv_one, strip_rows, strip_width)
    grad_act_one = tensor_sum(conv_input_grad(stack_grad_one, conv_first_back))
    grad_norm_one = silu_pull_one(grad_act_one)[0]
    back_one, grad_gain_in = group_back(
        grad_norm_one, centred_one, inv_one, gain_in_back, valid_col, GROUPS, full_counts
    )
    grad_hidden = (grad_residual + back_one) * valid_col
    resnet_grads = (
        lax.psum_scatter(grad_gain_in, IH, scatter_dimension=0, tiled=True),
        lax.psum_scatter(grad_conv_first, IH, scatter_dimension=2, tiled=True),
        lax.psum_scatter(grad_time_weight, IH, scatter_dimension=0, tiled=True),
        lax.psum_scatter(
            jnp.tile(grad_gain_mid, width_ih), IH, scatter_dimension=0, tiled=True
        ),
        lax.psum_scatter(grad_conv_second, IH, scatter_dimension=3, tiled=True),
    )
    return (
        output,
        grad_hidden,
        resnet_grads[0],
        resnet_grads[1],
        resnet_grads[2],
        resnet_grads[3],
        resnet_grads[4],
        block_grads[1],
        block_grads[0],
        block_grads[2],
        block_grads[3],
        block_grads[4],
        block_grads[5],
        block_grads[6],
        block_grads[7],
        block_grads[8],
        block_grads[9],
        block_grads[10],
        block_grads[11],
        block_grads[12],
        block_grads[13],
        block_grads[14],
        block_grads[15],
    )


def mm(left, right, left_dim, right_dim):
    return lax.dot_general(
        left,
        right,
        (((left_dim,), (right_dim,)), ((), ())),
        precision=high,
        preferred_element_type=jnp.float32,
    )


def swap(values):
    return lax.ppermute(values, I, [(0, 1), (1, 0)])


def flip(values, step):
    return lax.ppermute(values, H, [(s, s ^ step) for s in range(4)])


def turn(values, step):
    return lax.ppermute(values, T, [(s, (s + step) % 4) for s in range(4)])


def z_pieces(values):
    return [values] + [turn(values, 4 - j) for j in (1, 2, 3)]


def z_collect(pieces):
    total = pieces[0]
    for j in (1, 2, 3):
        total = total + turn(pieces[j], j)
    return total


def z_exchange(pieces):
    return [pieces[0]] + [turn(pieces[4 - j], 4 - j) for j in (1, 2, 3)]


def z_order(pieces, axis):
    t = lax.axis_index(T)
    shape = list(pieces[0].shape)
    shape.insert(axis, 4)
    whole = jnp.zeros(shape, pieces[0].dtype)
    for j in range(4):
        whole = lax.dynamic_update_index_in_dim(whole, pieces[j], lax.rem(t + j, 4), axis)
    return whole


def z_sum(values):
    return jnp.sum(z_order(z_pieces(values), 0), axis=0)


def h_collect(pieces):
    total = pieces[0]
    for j in (1, 2, 3):
        total = total + flip(pieces[j], j)
    return total


def h_sum(values):
    h = lax.axis_index(H)
    pieces = [values] + [flip(values, j) for j in (1, 2, 3)]
    whole = jnp.zeros((4,) + values.shape, values.dtype)
    for j in range(4):
        whole = lax.dynamic_update_index_in_dim(whole, pieces[j], h ^ j, 0)
    return jnp.sum(whole, axis=0)


def pick(values, index, axis=0):
    return lax.dynamic_index_in_dim(values, index, axis, keepdims=False)


def plane_sum(own, other):
    own = own + swap(other)
    part = h_collect([own[j] for j in range(4)])
    pieces = [part] + [flip(part, j) for j in (1, 2, 3)]
    return pieces + [swap(piece) for piece in pieces]


def q_to_s(values):
    moved = lax.all_to_all(values.reshape((8,) + values.shape[2:]), IH, 0, 0)
    return jnp.moveaxis(moved, 0, 1).reshape(values.shape[2], -1)


def s_to_q(values):
    cut = jnp.moveaxis(values.reshape(values.shape[0], 8, -1), 1, 0)
    moved = lax.all_to_all(cut, IH, 0, 0)
    return moved.reshape((2, 4) + moved.shape[1:])


def group_sum(channel_sums):
    shape = channel_sums.shape
    groups = jnp.sum(channel_sums.reshape(shape[:-1] + (shape[-1] // 40, 40)), axis=-1)
    return jnp.repeat(groups, 40, axis=-1)


IMAGE_ROWS = 1152
TAP_ROWS = range(16, 1136, 160)


def halves(values):
    top = values.astype(jnp.bfloat16)
    return top, (values - top.astype(jnp.float32)).astype(jnp.bfloat16)


def dot_halves(left, right, left_dim, right_dim):
    def one(a, b):
        return lax.dot_general(
            a, b, (((left_dim,), (right_dim,)), ((), ())), preferred_element_type=jnp.float32
        )

    return one(left[0], right[0]) + (one(left[0], right[1]) + one(left[1], right[0]))


def marks_of(marks, b):
    return marks[2 * b], marks[2 * b + 1]


def row_mask(span, rows, columns):
    return (lax.broadcasted_iota(jnp.int32, (rows, columns), 0) < span).astype(jnp.float32)


def put_strip(image, b, strip, span, values):
    at = pl.multiple_of(margin + strip * span, 8)
    image[b, pl.ds(at, 240)] = values[:240]

    @pl.when(span == 256)
    def _():
        image[b, pl.ds(pl.multiple_of(at + 240, 8), 16)] = values[240:]


def widen(wide, image, b, width, sign):
    channels = image.shape[2]
    width_f = width.astype(jnp.float32)
    for base in TAP_ROWS:
        row = lax.broadcasted_iota(jnp.int32, (160, channels), 0).astype(jnp.float32)
        cell = row + float(base - margin)
        column = cell - width_f * jnp.floor((cell + 0.5) / width_f)
        for j in range(3):
            step = sign * (j - 1)
            values = image[b, base + step : base + step + 160, :]
            if step < 0:
                values = jnp.where(column > 0.5, values, 0.0)
            if step > 0:
                values = jnp.where(column < width_f - 1.5, values, 0.0)
            wide[base : base + 160, j * channels : (j + 1) * channels] = values


def split_weight(weight, top, low):
    for k in range(3):
        rows = weight.shape[0] // 3
        first, second = halves(weight[k * rows : (k + 1) * rows, :])
        top[k * rows : (k + 1) * rows, :] = first
        low[k * rows : (k + 1) * rows, :] = second


def conv_strip(wide, top, low, strip, span, width, sign):
    rows = top.shape[0] // 3
    total = None
    for i in range(3):
        at = pl.multiple_of(margin + strip * span + sign * (i - 1) * width, 8)
        taps = halves(wide[pl.ds(at, 256), :])
        part = dot_halves(
            taps, (top[i * rows : (i + 1) * rows, :], low[i * rows : (i + 1) * rows, :]), 1, 0
        )
        total = part if total is None else total + part
    return total * row_mask(span, 256, total.shape[1])


def group_rows(sums):
    channels = sums.shape[1]
    lane = lax.broadcasted_iota(jnp.int32, (1, channels), 1)
    result = jnp.zeros((1, channels), jnp.float32)
    for g in range(channels // 40):
        inside = (lane >= 40 * g) & (lane < 40 * g + 40)
        result = jnp.where(inside, jnp.sum(jnp.where(inside, sums, 0.0)), result)
    return result


def group_row_stats(total, squares, span):
    count = (span * 160).astype(jnp.float32)
    mean = group_rows(total) / count
    var = group_rows(squares) / count - mean * mean
    return mean, lax.rsqrt(var + norm_eps)


def column_sum(values):
    return jnp.sum(values, axis=0, keepdims=True)


def first_kernel(marks, source, gain, tau, weight, own, other, image, stats, wide, top, low):
    item, h = marks[4], marks[5]
    split_weight(weight, top, low)
    image[...] = jnp.zeros_like(image)
    for b, out in ((0, own), (1, other)):
        span, width = marks_of(marks, b)
        base = (item ^ b) * 4
        total = jnp.zeros((1, 160), jnp.float32)
        squares = jnp.zeros((1, 160), jnp.float32)
        for k in range(4):
            values = source[base + k]
            total = total + column_sum(values)
            squares = squares + column_sum(values * values)
        mean, inv = group_row_stats(total, squares, span)
        stats[b, 0:1, :] = mean
        stats[b, 1:2, :] = inv
        for k in range(4):
            norm = (source[base + k] - mean) * inv * row_mask(span, 256, 160) * gain[...]
            put_strip(image, b, k, span, norm * jax.nn.sigmoid(norm))
        widen(wide, image, b, width, 1)
        added = tau[b : b + 1, :]

        def step(k, _):
            conv = conv_strip(wide, top, low, k, span, width, 1)
            out[k ^ h] = conv + added * row_mask(span, 256, 320)
            return 0

        lax.fori_loop(0, 4, step, 0)


def put_quarters(outs, tile, place, t):
    for j in range(4):
        at = pl.multiple_of(lax.rem(t + j, 4) * 64, 8)
        outs[j][place] = tile[pl.ds(at, 64), :]


def second_kernel(marks, *refs):
    strips, gain, weight = refs[:8], refs[8], refs[9]
    outs, image, stats = refs[10:14], refs[14], refs[15]
    wide, top, low, tile = refs[16:]
    item, h, t = marks[4], marks[5], marks[6]
    split_weight(weight, top, low)
    image[...] = jnp.zeros_like(image)
    for b in range(2):
        span, width = marks_of(marks, b)
        total = jnp.zeros((1, 320), jnp.float32)
        squares = jnp.zeros((1, 320), jnp.float32)
        for j in range(4):
            values = strips[4 * b + j][...]
            total = total + column_sum(values)
            squares = squares + column_sum(values * values)
        mean, inv = group_row_stats(total, squares, span)
        stats[b, 0:1, :] = mean
        stats[b, 1:2, :] = inv
        for j in range(4):
            values = strips[4 * b + j][...]
            norm = (values - mean) * inv * row_mask(span, 256, 320) * gain[...]
            put_strip(image, b, h ^ j, span, norm * jax.nn.sigmoid(norm))
        widen(wide, image, b, width, 1)

        def step(k, _):
            tile[...] = conv_strip(wide, top, low, k, span, width, 1)
            put_quarters(outs, tile, (item ^ b) * 4 + k, t)
            return 0

        lax.fori_loop(0, 4, step, 0)


def second_back_kernel(marks, *refs):
    quarters, weight = refs[:4], refs[4]
    own, other, image = refs[5:8]
    wide, top, low = refs[8:]
    item, h, t = marks[4], marks[5], marks[6]
    split_weight(weight, top, low)
    image[...] = jnp.zeros_like(image)
    for b, out in ((0, own), (1, other)):
        span, width = marks_of(marks, b)

        def fill(k, _):
            for j in range(4):
                q = lax.rem(t + j, 4)
                values = quarters[j][(item ^ b) * 4 + k]
                at = pl.multiple_of(margin + k * span + q * 64, 8)
                image[b, pl.ds(at, 48)] = values[:48]

                @pl.when((q < 3) | (span == 256))
                def _():
                    image[b, pl.ds(pl.multiple_of(at + 48, 8), 16)] = values[48:]

            return 0

        lax.fori_loop(0, 4, fill, 0)
        widen(wide, image, b, width, -1)

        def step(k, _):
            out[k ^ h] = conv_strip(wide, top, low, k, span, width, -1)
            return 0

        lax.fori_loop(0, 4, step, 0)


def first_back_kernel(marks, *refs):
    grads, strips, gain, stats, weight = refs[:8], refs[8:16], refs[16], refs[17], refs[18]
    outs, image, sums, grad_gain = refs[19:23], refs[23], refs[24], refs[25]
    wide, top, low, tile, scaled_at, centred_at = refs[26:]
    item, h, t = marks[4], marks[5], marks[6]
    split_weight(weight, top, low)
    image[...] = jnp.zeros_like(image)
    gain_total = jnp.zeros((1, 320), jnp.float32)
    for b in range(2):
        span, width = marks_of(marks, b)
        mean, inv = stats[b, 0:1, :], stats[b, 1:2, :]
        first = jnp.zeros((1, 320), jnp.float32)
        second = jnp.zeros((1, 320), jnp.float32)
        for j in range(4):
            centred = (strips[4 * b + j][...] - mean) * inv * row_mask(span, 256, 320)
            norm = centred * gain[...]
            gate = jax.nn.sigmoid(norm)
            grad_norm = grads[4 * b + j][...] * gate * (1.0 + norm * (1.0 - gate))
            scaled = grad_norm * gain[...]
            first = first + column_sum(scaled)
            second = second + column_sum(scaled * centred)
            gain_total = gain_total + column_sum(grad_norm * centred)
            scaled_at[j] = scaled
            centred_at[j] = centred
        count = (span * 160).astype(jnp.float32)
        first = group_rows(first) / count
        second = group_rows(second) / count
        tau_total = jnp.zeros((1, 320), jnp.float32)
        for j in range(4):
            grad = inv * row_mask(span, 256, 320) * (
                scaled_at[j] - first - centred_at[j] * second
            )
            tau_total = tau_total + column_sum(grad)
            put_strip(image, b, h ^ j, span, grad)
        sums[b : b + 1, :] = tau_total
        widen(wide, image, b, width, -1)

        def step(k, _):
            tile[...] = conv_strip(wide, top, low, k, span, width, -1)
            put_quarters(outs, tile, (item ^ b) * 4 + k, t)
            return 0

        lax.fori_loop(0, 4, step, 0)
    grad_gain[...] = gain_total


def first_weight_kernel(marks, image, grad, out, wide):
    out[...] = jnp.zeros_like(out)
    for b in range(2):
        _, width = marks_of(marks, b)
        widen(wide, image, b, width, 1)
        for i in range(3):

            def step(c, _):
                at = pl.multiple_of(margin + c * 256 + (i - 1) * width, 8)
                taps = halves(wide[pl.ds(at, 256), :].T)
                cells = halves(grad[b, pl.ds(pl.multiple_of(margin + c * 256, 8), 256), :])
                part = dot_halves(taps, cells, 1, 0)
                for j in range(3):
                    out[3 * i + j] += part[160 * j : 160 * j + 160]
                return 0

            lax.fori_loop(0, 4, step, 0)


def second_weight_kernel(marks, image, grad, out, wide, total):
    for i in range(3):
        total[...] = jnp.zeros_like(total)
        for b in range(2):
            _, width = marks_of(marks, b)
            widen(wide, grad, b, width, -1)

            def step(c, _):
                at = pl.multiple_of(margin + c * 256 - (i - 1) * width, 8)
                cells = halves(image[b, pl.ds(pl.multiple_of(margin + c * 256, 8), 256), :].T)
                total[...] += dot_halves(cells, halves(wide[pl.ds(at, 256), :]), 1, 0)
                return 0

            lax.fori_loop(0, 4, step, 0)
        for j in range(3):
            out[3 * i + j] = total[:, 160 * j : 160 * j + 160]


def run_kernel(body, marks, inputs, outs, scratch, flops):
    in_smem = pl.BlockSpec(memory_space=pltpu.SMEM)
    in_vmem = pl.BlockSpec(memory_space=pltpu.VMEM)
    return pl.pallas_call(
        body,
        out_shape=[jax.ShapeDtypeStruct(shape, jnp.float32) for shape in outs],
        in_specs=[in_smem] + [in_vmem] * len(inputs),
        out_specs=[in_vmem] * len(outs),
        scratch_shapes=[pltpu.VMEM(shape, kind) for shape, kind in scratch],
        compiler_params=pltpu.CompilerParams(vmem_limit_bytes=56 * 1024 * 1024),
        cost_estimate=pl.CostEstimate(
            flops=flops, bytes_accessed=10 * 1024 * 1024, transcendentals=0
        ),
    )(marks, *inputs)


def weight_kernel(plan, *refs):
    count = 1 + max(which for block in plan for _, _, which in block)
    lefts, right, out = refs[:count], refs[count], refs[count + 1]
    tokens = right.shape[0]
    for number, block in enumerate(plan):

        @pl.when(pl.program_id(0) == number)
        def _():
            for begin, columns, which in block:
                top, low = halves(right[:, begin : begin + columns])
                if tokens <= 64:
                    stacked = jnp.concatenate([top, low, top], axis=0)
                for m in range(0, 1280, 256):
                    cells = lefts[which][:, m : m + 256].T
                    if tokens <= 64:
                        first, second = halves(cells)
                        first = jnp.concatenate([first, first, second], axis=1)
                        part = jnp.dot(first, stacked, preferred_element_type=jnp.float32)
                    else:
                        part = dot_halves(halves(cells), (top, low), 1, 0)
                    out[m : m + 256, begin : begin + columns] = part


def weight_grads(plan, lefts, right):
    tokens = right.shape[0]
    blocks = len(plan)
    return pl.pallas_call(
        functools.partial(weight_kernel, plan),
        out_shape=jax.ShapeDtypeStruct((1280, 1280 * blocks), jnp.float32),
        grid=(blocks,),
        in_specs=[pl.BlockSpec((tokens, 1280), lambda i: (0, 0))] * len(lefts)
        + [pl.BlockSpec((tokens, 1280), lambda i: (0, i))],
        out_specs=pl.BlockSpec((1280, 1280), lambda i: (0, i)),
        compiler_params=pltpu.CompilerParams(vmem_limit_bytes=48 * 1024 * 1024),
        cost_estimate=pl.CostEstimate(
            flops=6 * tokens * 1280 * 1280 * blocks,
            bytes_accessed=7 * 1024 * 1024 * blocks,
            transcendentals=0,
        ),
    )(*lefts, right)


def after(values, *events):
    return lax.optimization_barrier((values,) + events)[0]


def together(*values):
    return lax.optimization_barrier(values)


CONV_FLOPS = 6 * 2048 * 1440 * 320


def first_conv(marks, source, gain, tau, weight):
    f32, b16 = jnp.float32, jnp.bfloat16
    return run_kernel(
        first_kernel,
        marks,
        (source, gain, tau, weight),
        [(4, 256, 320), (4, 256, 320), (2, IMAGE_ROWS, 160), (2, 8, 160)],
        [((IMAGE_ROWS, 480), f32), ((1440, 320), b16), ((1440, 320), b16)],
        CONV_FLOPS,
    )


def second_conv(marks, strips, gain, weight):
    f32, b16 = jnp.float32, jnp.bfloat16
    return run_kernel(
        second_kernel,
        marks,
        (*strips, gain, weight),
        [(8, 64, 160)] * 4 + [(2, IMAGE_ROWS, 320), (2, 8, 320)],
        [
            ((IMAGE_ROWS, 960), f32),
            ((2880, 160), b16),
            ((2880, 160), b16),
            ((256, 160), f32),
        ],
        CONV_FLOPS,
    )


def second_conv_back(marks, quarters, weight):
    f32, b16 = jnp.float32, jnp.bfloat16
    return run_kernel(
        second_back_kernel,
        marks,
        (*quarters, weight),
        [(4, 256, 320), (4, 256, 320), (2, IMAGE_ROWS, 160)],
        [((IMAGE_ROWS, 480), f32), ((1440, 320), b16), ((1440, 320), b16)],
        CONV_FLOPS,
    )


def first_conv_back(marks, grads, strips, gain, stats, weight):
    f32, b16 = jnp.float32, jnp.bfloat16
    return run_kernel(
        first_back_kernel,
        marks,
        (*grads, *strips, gain, stats, weight),
        [(8, 64, 160)] * 4 + [(2, IMAGE_ROWS, 320), (2, 320), (1, 320)],
        [
            ((IMAGE_ROWS, 960), f32),
            ((2880, 160), b16),
            ((2880, 160), b16),
            ((256, 160), f32),
            ((4, 256, 320), f32),
            ((4, 256, 320), f32),
        ],
        CONV_FLOPS,
    )


def first_conv_weight(marks, image, grad):
    return run_kernel(
        first_weight_kernel,
        marks,
        (image, grad),
        [(9, 160, 320)],
        [((IMAGE_ROWS, 480), jnp.float32)],
        CONV_FLOPS,
    )[0]


def second_conv_weight(marks, image, grad):
    return run_kernel(
        second_weight_kernel,
        marks,
        (image, grad),
        [(9, 320, 160)],
        [((IMAGE_ROWS, 480), jnp.float32), ((320, 480), jnp.float32)],
        CONV_FLOPS,
    )[0]


def heads_of(values, count):
    return values.reshape(values.shape[0], count, HEAD_DIM)


def ein(form, left, right):
    return jnp.einsum(form, left, right, precision=high, preferred_element_type=jnp.float32)


def soft_attend(queries, keys, values, key_valid, count):
    scores = ein(QK, heads_of(queries, count), heads_of(keys, count)) * (1.0 / math.sqrt(HEAD_DIM))
    if key_valid is not None:
        scores = jnp.where(key_valid[None, None, :], scores, masked_score)
    exponent = jnp.exp(scores - jnp.max(scores, axis=-1, keepdims=True))
    weights = exponent / jnp.sum(exponent, axis=-1, keepdims=True)
    attended = ein(PV, weights, heads_of(values, count))
    return attended.reshape(queries.shape), weights


def soft_back(queries, keys, values, count, weights, attended, grad_out):
    scaling = 1.0 / math.sqrt(HEAD_DIM)
    grad_heads = heads_of(grad_out, count)
    grad_soft = ein(QK, grad_heads, heads_of(values, count))
    delta = jnp.sum(grad_heads * heads_of(attended, count), axis=-1).T
    grad_scores = weights * (grad_soft - delta[..., None])
    grad_query = ein(PV, grad_scores, heads_of(keys, count)) * scaling
    grad_key = ein(PQ, grad_scores, heads_of(queries, count)) * scaling
    grad_value = ein(PQ, weights, grad_heads)
    return (
        grad_query.reshape(queries.shape),
        grad_key.reshape(keys.shape),
        grad_value.reshape(values.shape),
    )


def layer_grad(grad_out, centred, inv_std, gain_vector):
    scaled = grad_out * gain_vector
    grad_in = inv_std * (
        scaled
        - jnp.mean(scaled, axis=-1, keepdims=True)
        - centred * jnp.mean(scaled * centred, axis=-1, keepdims=True)
    )
    return grad_in, jnp.sum(grad_out * centred, axis=0)


def layer_forward(values, gain_vector):
    mean_val = jnp.mean(values, axis=-1, keepdims=True)
    var_val = jnp.mean(values * values, axis=-1, keepdims=True) - mean_val * mean_val
    inv_std = lax.rsqrt(var_val + norm_eps)
    centred = (values - mean_val) * inv_std
    return centred * gain_vector, centred, inv_std


def gather_plane(block):
    return lax.all_gather(block, IH, axis=0, tiled=True)


def scatter_plane(block):
    return lax.psum_scatter(block, IH, scatter_dimension=0, tiled=True)


def strip_sums(values):
    return jnp.sum(values, axis=(1, 2))


def grid_cells(bucket):
    strip_rows, strip_width = grid_shape(bucket)
    return strip_rows * strip_width


def fast_shards(
    hidden,
    text_states,
    bucket,
    timestep,
    gain_in,
    conv_first,
    time_weight,
    gain_mid,
    conv_second,
    gain_attn_norm,
    proj_in,
    gain_self,
    query_self,
    key_self,
    value_self,
    out_self,
    gain_cross,
    query_cross,
    key_cross,
    value_cross,
    out_cross,
    gain_ff,
    ff_in,
    ff_out,
    proj_out,
    cotangent,
):
    item, h, t = lax.axis_index(I), lax.axis_index(H), lax.axis_index(T)
    block = item * 4 + h
    width, wide = 160, 320
    channels = 1280

    def rows_of(values):
        return [values[64 * j : 64 * j + 64] for j in range(4)]

    own_span = grid_cells(bucket[0])
    slot = jnp.arange(256, dtype=jnp.int32)
    own_valid = (slot < own_span).astype(jnp.float32)[:, None]
    source = s_to_q(hidden[0] * own_valid).reshape(8, 256, width)
    both = jnp.stack([bucket[0], timestep[0]]).astype(jnp.float32)
    both_other = swap(both)
    pair = jnp.where(item == 0, jnp.stack([both, both_other]), jnp.stack([both_other, both]))
    times = jnp.stack([both[1], both_other[1]])
    strip_rows, strip_width = grid_shape(pair[:, 0].astype(jnp.int32))
    spans = strip_rows * strip_width
    marks = jnp.stack(
        [
            own_span,
            pick(strip_width, item),
            pick(spans, 1 - item),
            pick(strip_width, 1 - item),
            item,
            h,
            t,
        ]
    ).astype(jnp.int32)
    counts = (4 * spans * 40).astype(jnp.float32)[:, None]
    quarter_slot = t * 64 + jnp.arange(64, dtype=jnp.int32)
    q_valid = (quarter_slot[None, :] < spans[:, None]).astype(jnp.float32)[:, None, :, None]
    relative_slot = jnp.mod(t * 64 + slot, 256)
    key_valid = jnp.tile(relative_slot < own_span, 4)

    def spread(stat):
        return stat[:, None, None, :]

    def quarter(values):
        return lax.dynamic_slice_in_dim(values, t * 64, 64, 2)

    gains = jnp.stack([gain_self, gain_cross, gain_ff], axis=1)
    attn_full = gather_plane(
        jnp.concatenate(
            [
                query_self,
                key_self,
                value_self,
                proj_out,
                out_self.T,
                jnp.pad(gains, ((0, 0), (0, 125))),
            ],
            axis=1,
        )
    )
    qkv_full = attn_full[:, :960]
    proj_out_full = attn_full[:, 960:1280]
    out_self_full = attn_full[:, 1280:1600]
    gain_rows = attn_full[:, 1600:1603].T
    gain_self_full, gain_cross_full, gain_ff_full = (gain_rows[k : k + 1] for k in range(3))

    own_third = jnp.concatenate([proj_in.T, query_cross, out_cross.T], axis=1)
    own_third = jnp.concatenate(
        [own_third, jnp.pad(gain_attn_norm[None, :], ((0, 7), (0, 640)))], axis=0
    )
    third_pieces = z_pieces(own_third)

    features = jax.nn.silu(time_features(times, channels))
    own_features = lax.dynamic_slice_in_dim(features, block * width, width, 1)
    tau = mm(own_features, time_weight, 1, 0)
    own_one, other_one, image_one, stats_one = first_conv(
        marks, source, gain_in[None, :], tau, conv_first.reshape(9 * width, wide)
    )
    strips_one = plane_sum(own_one, other_one)

    third = z_order(after(third_pieces, own_one), 1)
    gain_attn_full = third[160, :, :320].reshape(1, channels)
    third = third[:160].reshape(160, 4, 3, 320).transpose(0, 2, 1, 3).reshape(160, 3840)
    third_full = gather_plane(third)
    proj_in_full = third_full[:, :1280]
    query_cross_full = third_full[:, 1280:2560]
    out_cross_full = third_full[:, 2560:]

    ff_full = gather_plane(jnp.concatenate([ff_in.reshape(160, 2560), ff_out.T], axis=1))
    ff_in_full = ff_full[:, :2560]
    ff_out_full = ff_full[:, 2560:]

    cot = after(cotangent[0] * own_valid, own_one)
    cot_relative = lax.dynamic_slice_in_dim(jnp.concatenate([cot, cot], axis=0), t * 64, 256, 0)
    cot_pieces = z_exchange(rows_of(cot_relative))
    grad_ff_part = mm(cot_relative, proj_out_full, 1, 1)
    grad_after_ff = z_collect(rows_of(grad_ff_part))

    *strips_one, grad_after_ff = together(*strips_one, grad_after_ff)
    *conv_two, image_two, stats_two = second_conv(
        marks, strips_one, gain_mid[None, :], conv_second.reshape(9 * wide, width)
    )
    conv_two_sum = z_collect(conv_two)

    text_here = after(text_states[0], conv_two[0])
    text_own = lax.dynamic_slice_in_dim(text_here, block * 256, 256, 1)
    text_other = swap(lax.dynamic_slice_in_dim(text_here, ((1 - item) * 4 + h) * 256, 256, 1))
    text_weight = jnp.concatenate([key_cross, value_cross], axis=1)
    text_part = mm(text_own, text_weight, 1, 0) + swap(mm(text_other, text_weight, 1, 0))
    text_sum = h_sum(text_part)
    cot_s = z_order(after(cot_pieces, conv_two[0]), 1)
    cot_q = s_to_q(cot_s.reshape(64, channels))
    residual_q = quarter(source.reshape(2, 4, 256, width)) + conv_two_sum.reshape(2, 4, 64, width)

    sums = z_sum(jnp.stack([strip_sums(residual_q), strip_sums(residual_q * residual_q)]))
    mean_three = group_sum(sums[0]) / counts
    var_three = group_sum(sums[1]) / counts - mean_three * mean_three
    inv_three = lax.rsqrt(var_three + norm_eps)
    centred_three = (residual_q - spread(mean_three)) * spread(inv_three) * q_valid
    norm_three = q_to_s(centred_three) * gain_attn_full
    projected = mm(norm_three, proj_in_full, 1, 1)

    normed_self, centred_self, inv_self = layer_forward(projected, gain_self_full)
    normed_self_all = jnp.concatenate(z_pieces(normed_self), axis=0)
    qkv = mm(normed_self_all, qkv_full, 1, 0)
    queries = qkv[:, :wide]
    kv_pieces = [qkv[:, wide:]] + [flip(qkv[:, wide:], j) for j in (1, 2, 3)]
    text_kv = z_order(z_pieces(after(text_sum, qkv)), 1)
    keys_text = text_kv[:, :, :320].reshape(-1, channels)
    values_text = text_kv[:, :, 320:].reshape(-1, channels)
    grad_after_ff_all = jnp.concatenate(z_pieces(after(grad_after_ff, qkv)), axis=0)

    kv_all = jnp.concatenate(kv_pieces, axis=0)
    keys_all, values_all = kv_all[:, :wide], kv_all[:, wide:]
    attn_self, weights_self = soft_attend(queries, keys_all, values_all, key_valid, 5)
    self_part = mm(attn_self, out_self_full, 1, 1)
    self_sum = z_collect(rows_of(self_part))
    grad_ff_act = mm(after(grad_after_ff_all, self_part), ff_out_full, 1, 0)
    residual_s = q_to_s(after(residual_q, self_part))
    self_sum, grad_ff_act = together(self_sum, grad_ff_act)
    after_self = projected + self_sum

    normed_cross, centred_cross, inv_cross = layer_forward(after_self, gain_cross_full)
    queries_cross = mm(normed_cross, query_cross_full, 1, 0)
    attn_cross, weights_cross = soft_attend(queries_cross, keys_text, values_text, None, 20)
    after_cross = after_self + mm(attn_cross, out_cross_full, 1, 1)

    normed_ff, centred_ff, inv_ff = layer_forward(after_cross, gain_ff_full)
    normed_ff_all = jnp.concatenate(z_pieces(normed_ff), axis=0)
    hidden_ff = mm(normed_ff_all, ff_in_full, 1, 0)
    value_half, gate_half = hidden_ff[:, :channels], hidden_ff[:, channels:]
    phi = 0.5 * (1.0 + lax.erf(gate_half * math.sqrt(0.5)))
    slope = phi + gate_half * jnp.exp(-0.5 * gate_half * gate_half) * (1.0 / math.sqrt(2 * math.pi))
    gate_act = gate_half * phi
    ff_act = value_half * gate_act
    grad_value = grad_ff_act * gate_act
    grad_gate = grad_ff_act * value_half * slope
    grad_hidden_ff = jnp.concatenate([grad_value, grad_gate], axis=1)
    grad_normed_part = mm(grad_hidden_ff, ff_in_full, 1, 1)
    grad_normed_ff = z_collect(rows_of(grad_normed_part))
    ff_right = after(jnp.concatenate([grad_hidden_ff, ff_act], axis=1), grad_normed_part)
    ff_grads = weight_grads(
        (((0, 1280, 0),), ((0, 1280, 0),), ((0, 1280, 1),)),
        (normed_ff_all, grad_after_ff_all),
        ff_right,
    )
    grad_normed_ff, ff_grads = together(grad_normed_ff, ff_grads)
    ff_grads = scatter_plane(ff_grads)

    back_ff, grad_gain_ff = layer_grad(grad_normed_ff, centred_ff, inv_ff, gain_ff_full)
    grad_after_cross = grad_after_ff + back_ff
    grad_attn_cross = mm(grad_after_cross, out_cross_full, 1, 0)
    grad_queries_cross, grad_keys_text, grad_values_text = soft_back(
        queries_cross, keys_text, values_text, 20, weights_cross, attn_cross, grad_attn_cross
    )
    grad_normed_cross = mm(grad_queries_cross, query_cross_full, 1, 1)
    back_cross, grad_gain_cross = layer_grad(
        grad_normed_cross, centred_cross, inv_cross, gain_cross_full
    )
    grad_after_self = grad_after_cross + back_cross
    grad_pieces = z_pieces(grad_after_self)
    cross_right = after(
        jnp.concatenate([grad_queries_cross, attn_cross], axis=1), grad_after_self
    )
    cross_grads = weight_grads(
        (((0, 1280, 0),), ((0, 1280, 1),)), (normed_cross, grad_after_cross), cross_right
    )
    *grad_pieces, cross_grads = together(*grad_pieces, cross_grads)
    cross_grads = scatter_plane(cross_grads)
    text_grads = jnp.concatenate(
        [grad_keys_text.reshape(-1, 4, wide), grad_values_text.reshape(-1, 4, wide)], axis=2
    )

    grad_after_self_all = jnp.concatenate(grad_pieces, axis=0)
    grad_attn_self = mm(grad_after_self_all, out_self_full, 1, 0)
    grad_queries, grad_keys_all, grad_values_all = soft_back(
        queries, keys_all, values_all, 5, weights_self, attn_self, grad_attn_self
    )
    grad_kv_all = jnp.concatenate([grad_keys_all, grad_values_all], axis=1)
    grad_kv = h_collect([grad_kv_all[256 * j : 256 * j + 256] for j in range(4)])
    text_grads = after(text_grads, grad_kv_all)
    text_grads = z_collect([pick(text_grads, lax.rem(t + j, 4), 1) for j in range(4)])
    out_part = mm(after(ff_act, grad_kv_all), ff_out_full, 1, 1)
    grad_kv, out_part = together(grad_kv, out_part)

    grad_qkv = jnp.concatenate([grad_queries, grad_kv], axis=1)
    grad_normed_part = mm(grad_qkv, qkv_full, 1, 1)
    grad_normed_self = z_collect(rows_of(grad_normed_part))
    text_grads = h_sum(after(text_grads, grad_normed_part))

    back_self, grad_gain_self = layer_grad(grad_normed_self, centred_self, inv_self, gain_self_full)
    grad_projected = grad_after_self + back_self
    grad_norm_three = mm(grad_projected, proj_in_full, 1, 0)

    both_grads = s_to_q(
        jnp.concatenate([grad_norm_three * gain_attn_full, grad_norm_three], axis=0)
    )
    attn_right = jnp.concatenate(
        [
            jnp.concatenate([grad_qkv, attn_self], axis=1),
            jnp.pad(norm_three, ((0, 192), (0, 0))),
        ],
        axis=1,
    )
    attn_grads = weight_grads(
        (((0, 960, 0), (960, 320, 1)), ((0, 1280, 2),)),
        (
            normed_self_all,
            grad_after_self_all,
            jnp.pad(grad_projected, ((0, 192), (0, 0))),
        ),
        after(attn_right, grad_norm_three),
    )
    both_grads, attn_grads = together(both_grads, attn_grads)
    attn_grads = scatter_plane(attn_grads)

    scaled_three, grad_three = both_grads[:, :, :64] * q_valid, both_grads[:, :, 64:]
    sums = z_sum(
        jnp.stack(
            [
                strip_sums(scaled_three),
                strip_sums(scaled_three * centred_three),
                strip_sums(grad_three * centred_three),
            ]
        )
    )
    grad_gain_three = jnp.sum(sums[2], axis=0)
    grad_residual_q = cot_q + spread(inv_three) * q_valid * (
        scaled_three
        - spread(group_sum(sums[0]) / counts)
        - centred_three * spread(group_sum(sums[1]) / counts)
    )

    own_two, other_two, image_back = second_conv_back(
        marks,
        z_pieces(grad_residual_q.reshape(8, 64, width)),
        conv_second.transpose(0, 1, 3, 2).reshape(9 * width, wide),
    )
    grad_act_two = plane_sum(own_two, other_two)
    grad_conv_second = second_conv_weight(marks, image_two, after(image_back, own_two)).reshape(
        3, 3, wide, width
    )
    after_ff = after_cross + z_collect(rows_of(after(out_part, own_two)))
    after_ff_all = jnp.concatenate(z_pieces(after_ff), axis=0)
    residual_cut = jnp.moveaxis(after(residual_s, own_two).reshape(64, 4, wide), 1, 0)
    residual_all = jnp.concatenate(
        z_exchange([pick(residual_cut, lax.rem(t + j, 4)) for j in range(4)]), axis=0
    )
    output = residual_all + mm(after_ff_all, proj_out_full, 1, 0)
    output = jnp.concatenate([output, output], axis=0)
    output = lax.dynamic_slice_in_dim(output, lax.rem(4 - t, 4) * 64, 256, 0) * own_valid
    grad_proj_out = scatter_plane(mm(after_ff_all, cot_relative, 0, 0))
    grad_text_weight = mm(text_own, text_grads, 0, 0) + mm(text_other, swap(text_grads), 0, 0)
    gain_sums = z_sum(after(jnp.stack([grad_gain_self, grad_gain_cross, grad_gain_ff]), own_two))
    *grad_act_two, grad_conv_second, output = together(*grad_act_two, grad_conv_second, output)

    *grad_act_one, image_grad, grad_tau, grad_gain_mid = first_conv_back(
        marks,
        grad_act_two,
        strips_one,
        gain_mid[None, :],
        stats_two,
        conv_first.transpose(0, 1, 3, 2).reshape(9 * wide, width),
    )
    grad_act_one_sum = z_collect(grad_act_one)
    grad_conv_first = first_conv_weight(marks, image_one, after(image_grad, grad_act_one[0]))
    grad_act_one_sum, grad_conv_first = together(grad_act_one_sum, grad_conv_first)
    grad_conv_first = grad_conv_first.reshape(3, 3, width, wide)
    grad_time_weight = mm(own_features, grad_tau, 0, 0)

    grad_act_one_sum = grad_act_one_sum.reshape(2, 4, 64, width)
    stats_one = jnp.where(item == 0, stats_one, stats_one[::-1])
    mean_one, inv_one = stats_one[:, 0], stats_one[:, 1]
    centred_one_q = (quarter(source.reshape(2, 4, 256, width)) - spread(mean_one)) * (
        spread(inv_one) * q_valid
    )
    norm_one_q = centred_one_q * gain_in
    gate_one = jax.nn.sigmoid(norm_one_q)
    grad_norm_one = grad_act_one_sum * gate_one * (1.0 + norm_one_q * (1.0 - gate_one))
    scaled_one = grad_norm_one * gain_in
    sums = z_sum(
        jnp.stack(
            [
                strip_sums(scaled_one),
                strip_sums(scaled_one * centred_one_q),
                strip_sums(grad_norm_one * centred_one_q),
            ]
        )
    )
    grad_gain_in = jnp.sum(sums[2], axis=0)
    grad_hidden = grad_residual_q + spread(inv_one) * q_valid * (
        scaled_one
        - spread(group_sum(sums[0]) / counts)
        - centred_one_q * spread(group_sum(sums[1]) / counts)
    )
    extra = jnp.concatenate(
        [
            jnp.broadcast_to(grad_gain_three, (8, 1, width)),
            jnp.moveaxis(gain_sums.reshape(3, 8, width), 1, 0),
            jnp.zeros((8, 4, width), jnp.float32),
        ],
        axis=1,
    )
    moved = jnp.concatenate([grad_hidden.reshape(8, 64, width), extra], axis=1)
    moved = lax.all_to_all(moved, IH, 0, 0)
    grad_hidden = jnp.moveaxis(moved[:, :64], 0, 1).reshape(64, channels)
    grad_hidden = z_order(z_pieces(grad_hidden), 0).reshape(256, channels)
    grad_gain_attn = lax.dynamic_slice_in_dim(
        moved[:, 64].reshape(channels), t * wide, wide, 0
    )
    gain_sums = jnp.sum(moved[:, 65:68], axis=0)

    grad_query_cross, grad_out_cross = z_shares(cross_grads, 2)
    (grad_proj_in,) = z_shares(attn_grads[:, 1280:], 1)

    return (
        output[None],
        grad_hidden[None],
        grad_gain_in,
        grad_conv_first,
        grad_time_weight,
        grad_gain_mid[0],
        grad_conv_second,
        grad_gain_attn,
        grad_proj_in.T,
        gain_sums[0],
        attn_grads[:, :320],
        attn_grads[:, 320:640],
        attn_grads[:, 640:960],
        attn_grads[:, 960:1280].T,
        gain_sums[1],
        grad_query_cross,
        grad_text_weight[:, :wide],
        grad_text_weight[:, wide:],
        grad_out_cross.T,
        gain_sums[2],
        ff_grads[:, :2560].reshape(width, 2, channels),
        ff_grads[:, 2560:].T,
        grad_proj_out,
    )


def z_shares(columns, count):
    t = lax.axis_index(T)
    cut = columns.reshape(columns.shape[0], count, 4, 320)
    own = z_collect([pick(cut, lax.rem(t + j, 4), 2) for j in range(4)])
    return [own[:, k] for k in range(count)]


def solution(mesh):
    placed = (
        P(I, H, None),
        P(I, None, None),
        P(I),
        P(I),
        P(IH),
        P(None, None, IH, T),
        P(IH, T),
        P(T),
        P(None, None, T, IH),
        P(T),
        P(T, IH),
        P(IH),
        P(IH, T),
        P(IH, T),
        P(IH, T),
        P(T, IH),
        P(IH),
        P(IH, T),
        P(IH, T),
        P(IH, T),
        P(T, IH),
        P(IH),
        P(IH, None, T),
        P(T, IH),
        P(IH, T),
        P(I, H, T),
    )
    sizes = (mesh.shape[I], mesh.shape[H], mesh.shape[T])
    body = fast_shards if sizes == (2, 4, 4) else shards
    return jax.shard_map(
        body,
        mesh=mesh,
        in_specs=placed,
        out_specs=(
            P(I, H, T),
            P(I, H, None),
            P(IH),
            P(None, None, IH, T),
            P(IH, T),
            P(T),
            P(None, None, T, IH),
            P(T),
            P(T, IH),
            P(IH),
            P(IH, T),
            P(IH, T),
            P(IH, T),
            P(T, IH),
            P(IH),
            P(IH, T),
            P(IH, T),
            P(IH, T),
            P(T, IH),
            P(IH),
            P(IH, None, T),
            P(T, IH),
            P(IH, T),
        ),
        check_vma=False,
    )
```

```python
import functools
import math

import jax
import jax.numpy as jnp
from jax import lax
from jax.experimental import pallas as pl
from jax.experimental.pallas import tpu as pltpu
from jax.sharding import PartitionSpec as P

HEAD_DIM = 64
GROUPS = 32
EDGE = 48


highest = lax.Precision.HIGHEST
norm_eps = 1e-05
masked_score = -1e30
edge_margin = 56
high = lax.Precision.HIGH
margin = 64
I, H, T = "items", "height", "tensor"
IH = (I, H)
E0 = "bc,bn->cn"
E1 = "bhqk,bkhd->bqhd"
E2 = "bhqk,bqhd->bkhd"
E3 = "bqhd,bkhd->bhqk"
E4 = "bqhd,bqhd->bhq"
E5 = "bsc,bsjf->cjf"
E6 = "bsc,cjf->bsjf"
E7 = "bsjf,cjf->bsc"
E8 = "bsk,bsn->kn"
E9 = "bsk,kn->bsn"
E10 = "bsn,kn->bsk"
QK, PV, PQ = "qhd,khd->hqk", "hqk,khd->qhd", "hqk,qhd->khd"


def padded_2(block, sides, width):
    for axis, dim in sides:
        count = lax.axis_size(axis)
        forward = [(i, i + 1) for i in range(count - 1)]
        backward = [(target, source) for source, target in forward]
        low = lax.ppermute(
            lax.slice_in_dim(block, block.shape[dim] - width, None, axis=dim), axis, forward
        )
        high = lax.ppermute(lax.slice_in_dim(block, 0, width, axis=dim), axis, backward)
        block = jnp.concatenate([low, block, high], axis=dim)
    return block


def grid_shape(bucket):
    strip_rows = jnp.where(bucket == 0, 8, jnp.where(bucket == 1, 6, 5)).astype(jnp.int32)
    strip_width = jnp.where(bucket == 0, 32, jnp.where(bucket == 1, 40, 48)).astype(jnp.int32)
    return (strip_rows, strip_width)


def tokens_dot(values, weight):
    return jnp.einsum(E9, values, weight, precision=highest)


def tokens_back(grad_values, weight):
    return jnp.einsum(E10, grad_values, weight, precision=highest)


def tokens_grad(values, grad_values):
    return jnp.einsum(E8, values, grad_values, precision=highest)


def tensor_sum(values):
    return lax.psum(values, T)


def expand_groups(stat, size_group):
    return jnp.repeat(stat, size_group, axis=1)[:, None, :]


def group_stats(values, valid_col, group_count, counts):
    item_count, slot_count, channels = values.shape
    size_group = channels // group_count
    grouped = (values * valid_col).reshape(item_count, slot_count, group_count, size_group)
    sum_values = jnp.sum(grouped, axis=(1, 3))
    sum_squares = jnp.sum(grouped * grouped, axis=(1, 3))
    sum_values, sum_squares = lax.psum((sum_values, sum_squares), H)
    mean_val = sum_values / counts[:, None]
    var_val = sum_squares / counts[:, None] - mean_val * mean_val
    return (
        expand_groups(mean_val, size_group),
        expand_groups(lax.rsqrt(var_val + norm_eps), size_group),
    )


def group_back(grad_out, centred, inv_std, gain_vector, valid_col, group_count, counts):
    item_count, slot_count, channels = grad_out.shape
    size_group = channels // group_count
    scaled = grad_out * gain_vector * valid_col
    sum_first = jnp.sum(
        scaled.reshape(item_count, slot_count, group_count, size_group), axis=(1, 3)
    )
    sum_second = jnp.sum(
        (scaled * centred).reshape(item_count, slot_count, group_count, size_group), axis=(1, 3)
    )
    sum_first, sum_second = lax.psum((sum_first, sum_second), H)
    mean_first = expand_groups(sum_first / counts[:, None], size_group)
    mean_second = expand_groups(sum_second / counts[:, None], size_group)
    grad_in = inv_std * (scaled - mean_first - centred * mean_second) * valid_col
    return (grad_in, jnp.sum(grad_out * centred, axis=(0, 1)))


def layer_norm(values, gain_vector):
    mean_val = jnp.mean(values, axis=-1, keepdims=True)
    var_val = jnp.mean(values * values, axis=-1, keepdims=True) - mean_val * mean_val
    inv_std = lax.rsqrt(var_val + norm_eps)
    centred = (values - mean_val) * inv_std
    return (centred * gain_vector, centred, inv_std)


def layer_back(grad_out, centred, inv_std, gain_vector):
    scaled = grad_out * gain_vector
    grad_in = inv_std * (
        scaled
        - jnp.mean(scaled, axis=-1, keepdims=True)
        - centred * jnp.mean(scaled * centred, axis=-1, keepdims=True)
    )
    return (grad_in, jnp.sum(grad_out * centred, axis=(0, 1)))


def edge_rows(values, strip_rows, strip_width):
    item_count, slot_count, channels = values.shape
    position = jnp.arange(EDGE, dtype=jnp.int32)

    def edge_one_item(item_vals, rows_here, width_here):
        keep_mask = (position < width_here)[:, None].astype(jnp.float32)
        padded = jnp.concatenate([item_vals, jnp.zeros((EDGE, channels), jnp.float32)], axis=0)
        top_row = item_vals[:EDGE] * keep_mask
        bottom_row = (
            lax.dynamic_slice_in_dim(padded, (rows_here - 1) * width_here, EDGE, 0) * keep_mask
        )
        return jnp.stack([top_row, bottom_row])

    return jax.vmap(edge_one_item)(values, strip_rows, strip_width)


def neighbour_stack(values, strip_rows, strip_width):
    edge_pair = edge_rows(values, strip_rows, strip_width)
    beside_all = padded_2(edge_pair, ((H, 1),), 1)
    item_count, slot_count, channels = values.shape
    position = jnp.arange(slot_count, dtype=jnp.int32)

    def neighbour_one_item(item_vals, item_around, rows_here, width_here):
        cell_span = rows_here * width_here
        extended = jnp.zeros((2 * edge_margin + slot_count, channels), jnp.float32)
        extended = lax.dynamic_update_slice_in_dim(
            extended, item_around[0], edge_margin - width_here, 0
        )
        extended = lax.dynamic_update_slice_in_dim(extended, item_vals, edge_margin, 0)
        extended = lax.dynamic_update_slice_in_dim(
            extended, item_around[3], edge_margin + cell_span, 0
        )
        column = position % width_here
        shifted_list = []
        for row_step in (-1, 0, 1):
            for col_step in (-1, 0, 1):
                shifted = lax.dynamic_slice_in_dim(
                    extended, edge_margin + row_step * width_here + col_step, slot_count, 0
                )
                keep_mask = (
                    (column + col_step >= 0)
                    & (column + col_step < width_here)
                    & (position < cell_span)
                )
                shifted_list.append(shifted * keep_mask[:, None].astype(jnp.float32))
        return jnp.stack(shifted_list, axis=1)

    return jax.vmap(neighbour_one_item)(values, beside_all, strip_rows, strip_width)


def conv_apply(neighbours, weight):
    item_count, slot_count = (neighbours.shape[0], neighbours.shape[1])
    flattened = neighbours.reshape(item_count, slot_count, -1)
    return tokens_dot(flattened, weight.reshape(-1, weight.shape[3]))


def conv_input_grad(neighbours_grad, weight):
    flipped = jnp.transpose(weight[::-1, ::-1], (0, 1, 3, 2))
    return conv_apply(neighbours_grad, flipped)


def conv_weight_grad(neighbours, grad_out, weight_shape):
    flattened = neighbours.reshape(neighbours.shape[0], neighbours.shape[1], -1)
    return tokens_grad(flattened, grad_out).reshape(weight_shape)


def time_features(timestep, channels):
    half_width = channels // 2
    frequency = jnp.exp(-math.log(10000.0) * jnp.arange(half_width, dtype=jnp.float32) / half_width)
    angles = timestep.astype(jnp.float32)[:, None] * frequency[None, :]
    return jnp.concatenate([jnp.cos(angles), jnp.sin(angles)], axis=1)


def exact_gelu(values):
    return jax.nn.gelu(values, approximate=False)


def head_split(values, heads_here):
    return values.reshape(
        values.shape[0], values.shape[1], heads_here, values.shape[2] // heads_here
    )


def score_block(queries, keys_all, key_valid, heads_here):
    head_size = queries.shape[2] // heads_here
    scores = jnp.einsum(
        E3,
        head_split(queries, heads_here),
        head_split(keys_all, heads_here),
        precision=highest,
    ) * (1.0 / math.sqrt(head_size))
    return jnp.where(key_valid[:, None, None, :], scores, masked_score)


def attend(queries, keys_all, values_all, key_valid, heads_here):
    scores = score_block(queries, keys_all, key_valid, heads_here)
    row_peak = jnp.max(scores, axis=-1, keepdims=True)
    exponent = jnp.exp(scores - row_peak)
    row_total = jnp.sum(exponent, axis=-1, keepdims=True)
    soft_weights = exponent / row_total
    attended = jnp.einsum(
        E1, soft_weights, head_split(values_all, heads_here), precision=highest
    )
    return (attended.reshape(queries.shape), row_peak + jnp.log(row_total))


def attend_back(
    queries, keys_all, values_all, key_valid, heads_here, attended, log_total, grad_attended
):
    head_size = queries.shape[2] // heads_here
    scaling = 1.0 / math.sqrt(head_size)
    soft_weights = jnp.exp(score_block(queries, keys_all, key_valid, heads_here) - log_total)
    grad_heads = head_split(grad_attended, heads_here)
    grad_soft = jnp.einsum(
        E3, grad_heads, head_split(values_all, heads_here), precision=highest
    )
    row_delta = jnp.einsum(
        E4, grad_heads, head_split(attended, heads_here), precision=highest
    )
    grad_scores = soft_weights * (grad_soft - row_delta[..., None])
    grad_query = (
        jnp.einsum(
            E1, grad_scores, head_split(keys_all, heads_here), precision=highest
        )
        * scaling
    )
    grad_key = (
        jnp.einsum(
            E2, grad_scores, head_split(queries, heads_here), precision=highest
        )
        * scaling
    )
    grad_value = jnp.einsum(E2, soft_weights, grad_heads, precision=highest)
    return (
        grad_query.reshape(queries.shape),
        grad_key.reshape(keys_all.shape),
        grad_value.reshape(values_all.shape),
    )


def shards(
    hidden,
    text_states,
    bucket,
    timestep,
    gain_in,
    conv_first,
    time_weight,
    gain_mid,
    conv_second,
    gain_attn_norm,
    proj_in,
    gain_self,
    query_self,
    key_self,
    value_self,
    out_self,
    gain_cross,
    query_cross,
    key_cross,
    value_cross,
    out_cross,
    gain_ff,
    ff_in,
    ff_out,
    proj_out,
    cotangent,
):
    item_count, slot_count, channels = hidden.shape
    local_width = gain_mid.shape[0]
    local_groups = GROUPS * local_width // channels
    heads_here = local_width // HEAD_DIM
    height_count = lax.axis_size(H)
    width_ih = lax.axis_size(I) * lax.axis_size(H)
    offset = lax.axis_index(T) * local_width
    strip_rows, strip_width = grid_shape(bucket)
    cell_span = strip_rows * strip_width
    position = jnp.arange(slot_count, dtype=jnp.int32)
    valid_mask = position[None, :] < cell_span[:, None]
    valid_col = valid_mask[:, :, None].astype(jnp.float32)
    full_counts = (height_count * cell_span * (channels // GROUPS)).astype(jnp.float32)
    key_valid = jnp.tile(valid_mask, (1, height_count))
    text_valid = jnp.ones((item_count, text_states.shape[1]), dtype=bool)
    resnet_full = (
        lax.all_gather(gain_in, IH, axis=0, tiled=True),
        lax.all_gather(conv_first, IH, axis=2, tiled=True),
        lax.all_gather(time_weight, IH, axis=0, tiled=True),
        lax.all_gather(conv_second, IH, axis=3, tiled=True),
    )
    block_full = (
        lax.all_gather(proj_in, IH, axis=1, tiled=True),
        lax.all_gather(gain_self, IH, axis=0, tiled=True),
        lax.all_gather(query_self, IH, axis=0, tiled=True),
        lax.all_gather(key_self, IH, axis=0, tiled=True),
        lax.all_gather(value_self, IH, axis=0, tiled=True),
        lax.all_gather(out_self, IH, axis=1, tiled=True),
        lax.all_gather(gain_cross, IH, axis=0, tiled=True),
        lax.all_gather(query_cross, IH, axis=0, tiled=True),
        lax.all_gather(key_cross, IH, axis=0, tiled=True),
        lax.all_gather(value_cross, IH, axis=0, tiled=True),
        lax.all_gather(out_cross, IH, axis=1, tiled=True),
        lax.all_gather(gain_ff, IH, axis=0, tiled=True),
        lax.all_gather(ff_in, IH, axis=0, tiled=True),
        lax.all_gather(ff_out, IH, axis=1, tiled=True),
        lax.all_gather(proj_out, IH, axis=0, tiled=True),
    )
    gain_in_full, conv_first_full, time_full, conv_second_full = resnet_full
    (
        proj_in_full,
        gain_self_full,
        query_self_full,
        key_self_full,
        value_self_full,
        out_self_full,
        gain_cross_full,
        query_cross_full,
        key_cross_full,
        value_cross_full,
        out_cross_full,
        gain_ff_full,
        ff_in_full,
        ff_out_full,
        proj_out_full,
    ) = block_full
    source = hidden * valid_col
    mean_one, inv_one = group_stats(source, valid_col, GROUPS, full_counts)
    centred_one = (source - mean_one) * inv_one * valid_col
    norm_one = centred_one * gain_in_full
    act_one, silu_pull_one = jax.vjp(jax.nn.silu, norm_one)
    stack_one = neighbour_stack(act_one, strip_rows, strip_width)
    silu_features = jax.nn.silu(time_features(timestep, channels))
    time_term = jnp.dot(
        silu_features, time_full, precision=highest, preferred_element_type=jnp.float32
    )
    conv_one = (conv_apply(stack_one, conv_first_full) + time_term[:, None, :]) * valid_col
    mean_two, inv_two = group_stats(conv_one, valid_col, local_groups, full_counts)
    centred_two = (conv_one - mean_two) * inv_two * valid_col
    norm_two = centred_two * gain_mid
    act_two, silu_pull_two = jax.vjp(jax.nn.silu, norm_two)
    stack_two = neighbour_stack(act_two, strip_rows, strip_width)
    conv_two = tensor_sum(conv_apply(stack_two, conv_second_full)) * valid_col
    residual = source + conv_two
    residual_local = lax.dynamic_slice_in_dim(residual, offset, local_width, 2)
    mean_three, inv_three = group_stats(residual_local, valid_col, local_groups, full_counts)
    centred_three = (residual_local - mean_three) * inv_three * valid_col
    norm_three = centred_three * gain_attn_norm
    projected = tensor_sum(tokens_dot(norm_three, proj_in_full))
    normed_self, centred_self, inv_self = layer_norm(projected, gain_self_full)
    queries = tokens_dot(normed_self, query_self_full)
    keys_here = tokens_dot(normed_self, key_self_full)
    values_here = tokens_dot(normed_self, value_self_full)
    keys_all, values_all = (
        lax.all_gather(keys_here, H, axis=1, tiled=True),
        lax.all_gather(values_here, H, axis=1, tiled=True),
    )
    attn_self, total_self = attend(queries, keys_all, values_all, key_valid, heads_here)
    after_self = projected + tensor_sum(tokens_dot(attn_self, out_self_full))
    normed_cross, centred_cross, inv_cross = layer_norm(after_self, gain_cross_full)
    queries_cross = tokens_dot(normed_cross, query_cross_full)
    keys_text = tokens_dot(text_states, key_cross_full)
    values_text = tokens_dot(text_states, value_cross_full)
    attn_cross, total_cross = attend(queries_cross, keys_text, values_text, text_valid, heads_here)
    after_cross = after_self + tensor_sum(tokens_dot(attn_cross, out_cross_full))
    normed_ff, centred_ff, inv_ff = layer_norm(after_cross, gain_ff_full)
    hidden_ff = jnp.einsum(E6, normed_ff, ff_in_full, precision=highest)
    value_half = hidden_ff[:, :, 0]
    gate_act, gelu_pull = jax.vjp(exact_gelu, hidden_ff[:, :, 1])
    ff_act = value_half * gate_act
    after_ff = after_cross + tensor_sum(tokens_dot(ff_act, ff_out_full))
    output = (residual_local + tokens_dot(after_ff, proj_out_full)) * valid_col
    (
        proj_in_back,
        gain_self_back,
        query_self_back,
        key_self_back,
        value_self_back,
        out_self_back,
        gain_cross_back,
        query_cross_back,
        key_cross_back,
        value_cross_back,
        out_cross_back,
        gain_ff_back,
        ff_in_back,
        ff_out_back,
        proj_out_back,
    ) = block_full
    grad_local = cotangent * valid_col
    grad_proj_out = tokens_grad(after_ff, grad_local)
    grad_after_ff = tensor_sum(tokens_back(grad_local, proj_out_back))
    grad_ff_out = tokens_grad(ff_act, grad_after_ff)
    grad_ff_act = tokens_back(grad_after_ff, ff_out_back)
    grad_value_half = grad_ff_act * gate_act
    grad_gate_half = gelu_pull(grad_ff_act * value_half)[0]
    grad_hidden_ff = jnp.stack([grad_value_half, grad_gate_half], axis=2)
    grad_ff_in = jnp.einsum(E5, normed_ff, grad_hidden_ff, precision=highest)
    grad_normed_ff = tensor_sum(
        jnp.einsum(E7, grad_hidden_ff, ff_in_back, precision=highest)
    )
    back_ff, grad_gain_ff = layer_back(grad_normed_ff, centred_ff, inv_ff, gain_ff_back)
    grad_after_cross = grad_after_ff + back_ff
    grad_out_cross = tokens_grad(attn_cross, grad_after_cross)
    grad_attn_cross = tokens_back(grad_after_cross, out_cross_back)
    grad_queries_cross, grad_keys_text, grad_values_text = attend_back(
        queries_cross,
        keys_text,
        values_text,
        text_valid,
        heads_here,
        attn_cross,
        total_cross,
        grad_attn_cross,
    )
    grad_query_cross = tokens_grad(normed_cross, grad_queries_cross)
    grad_key_cross = tokens_grad(text_states, grad_keys_text)
    grad_value_cross = tokens_grad(text_states, grad_values_text)
    grad_normed_cross = tensor_sum(tokens_back(grad_queries_cross, query_cross_back))
    back_cross, grad_gain_cross = layer_back(
        grad_normed_cross, centred_cross, inv_cross, gain_cross_back
    )
    grad_after_self = grad_after_cross + back_cross
    grad_out_self = tokens_grad(attn_self, grad_after_self)
    grad_attn_self = tokens_back(grad_after_self, out_self_back)
    grad_queries, grad_keys_all, grad_values_all = attend_back(
        queries, keys_all, values_all, key_valid, heads_here, attn_self, total_self, grad_attn_self
    )
    grad_keys_here, grad_values_here = (
        lax.psum_scatter(grad_keys_all, H, scatter_dimension=1, tiled=True),
        lax.psum_scatter(grad_values_all, H, scatter_dimension=1, tiled=True),
    )
    grad_query_self = tokens_grad(normed_self, grad_queries)
    grad_key_self = tokens_grad(normed_self, grad_keys_here)
    grad_value_self = tokens_grad(normed_self, grad_values_here)
    grad_normed_self = tensor_sum(
        tokens_back(grad_queries, query_self_back)
        + tokens_back(grad_keys_here, key_self_back)
        + tokens_back(grad_values_here, value_self_back)
    )
    back_self, grad_gain_self = layer_back(grad_normed_self, centred_self, inv_self, gain_self_back)
    grad_projected = grad_after_self + back_self
    grad_proj_in = tokens_grad(norm_three, grad_projected)
    grad_norm_three = tokens_back(grad_projected, proj_in_back)
    back_three, grad_gain_attn = group_back(
        grad_norm_three,
        centred_three,
        inv_three,
        gain_attn_norm,
        valid_col,
        local_groups,
        full_counts,
    )
    grad_residual_local = grad_local + back_three
    block_grads = (
        lax.psum_scatter(grad_proj_in, IH, scatter_dimension=1, tiled=True),
        lax.psum_scatter(
            jnp.tile(grad_gain_attn, width_ih), IH, scatter_dimension=0, tiled=True
        ),
        lax.psum_scatter(grad_gain_self, IH, scatter_dimension=0, tiled=True),
        lax.psum_scatter(grad_query_self, IH, scatter_dimension=0, tiled=True),
        lax.psum_scatter(grad_key_self, IH, scatter_dimension=0, tiled=True),
        lax.psum_scatter(grad_value_self, IH, scatter_dimension=0, tiled=True),
        lax.psum_scatter(grad_out_self, IH, scatter_dimension=1, tiled=True),
        lax.psum_scatter(grad_gain_cross, IH, scatter_dimension=0, tiled=True),
        lax.psum_scatter(grad_query_cross, IH, scatter_dimension=0, tiled=True),
        lax.psum_scatter(grad_key_cross, IH, scatter_dimension=0, tiled=True),
        lax.psum_scatter(grad_value_cross, IH, scatter_dimension=0, tiled=True),
        lax.psum_scatter(grad_out_cross, IH, scatter_dimension=1, tiled=True),
        lax.psum_scatter(grad_gain_ff, IH, scatter_dimension=0, tiled=True),
        lax.psum_scatter(grad_ff_in, IH, scatter_dimension=0, tiled=True),
        lax.psum_scatter(grad_ff_out, IH, scatter_dimension=1, tiled=True),
        lax.psum_scatter(grad_proj_out, IH, scatter_dimension=0, tiled=True),
    )
    gain_in_back, conv_first_back, time_back, conv_second_back = resnet_full
    grad_residual = lax.all_gather(grad_residual_local, T, axis=2, tiled=True)
    grad_conv_second = conv_weight_grad(stack_two, grad_residual, conv_second_back.shape)
    stack_grad_two = neighbour_stack(grad_residual, strip_rows, strip_width)
    grad_act_two = conv_input_grad(stack_grad_two, conv_second_back)
    grad_norm_two = silu_pull_two(grad_act_two)[0]
    grad_conv_one, grad_gain_mid = group_back(
        grad_norm_two, centred_two, inv_two, gain_mid, valid_col, local_groups, full_counts
    )
    grad_time_term = jnp.sum(grad_conv_one, axis=1)
    grad_time_weight = jnp.einsum(E0, silu_features, grad_time_term, precision=highest)
    grad_conv_first = conv_weight_grad(stack_one, grad_conv_one, conv_first_back.shape)
    stack_grad_one = neighbour_stack(grad_conv_one, strip_rows, strip_width)
    grad_act_one = tensor_sum(conv_input_grad(stack_grad_one, conv_first_back))
    grad_norm_one = silu_pull_one(grad_act_one)[0]
    back_one, grad_gain_in = group_back(
        grad_norm_one, centred_one, inv_one, gain_in_back, valid_col, GROUPS, full_counts
    )
    grad_hidden = (grad_residual + back_one) * valid_col
    resnet_grads = (
        lax.psum_scatter(grad_gain_in, IH, scatter_dimension=0, tiled=True),
        lax.psum_scatter(grad_conv_first, IH, scatter_dimension=2, tiled=True),
        lax.psum_scatter(grad_time_weight, IH, scatter_dimension=0, tiled=True),
        lax.psum_scatter(
            jnp.tile(grad_gain_mid, width_ih), IH, scatter_dimension=0, tiled=True
        ),
        lax.psum_scatter(grad_conv_second, IH, scatter_dimension=3, tiled=True),
    )
    return (
        output,
        grad_hidden,
        resnet_grads[0],
        resnet_grads[1],
        resnet_grads[2],
        resnet_grads[3],
        resnet_grads[4],
        block_grads[1],
        block_grads[0],
        block_grads[2],
        block_grads[3],
        block_grads[4],
        block_grads[5],
        block_grads[6],
        block_grads[7],
        block_grads[8],
        block_grads[9],
        block_grads[10],
        block_grads[11],
        block_grads[12],
        block_grads[13],
        block_grads[14],
        block_grads[15],
    )


def mm(left, right, left_dim, right_dim):
    return lax.dot_general(
        left,
        right,
        (((left_dim,), (right_dim,)), ((), ())),
        precision=high,
        preferred_element_type=jnp.float32,
    )


def swap(values):
    return lax.ppermute(values, I, [(0, 1), (1, 0)])


def flip(values, step):
    return lax.ppermute(values, H, [(s, s ^ step) for s in range(4)])


def turn(values, step):
    return lax.ppermute(values, T, [(s, (s + step) % 4) for s in range(4)])


def z_pieces(values):
    return [values] + [turn(values, 4 - j) for j in (1, 2, 3)]


def total_of(pieces):
    return (pieces[0] + pieces[1]) + (pieces[2] + pieces[3])


def z_received(pieces):
    return [pieces[0]] + [turn(pieces[j], j) for j in (1, 2, 3)]


def z_all(values):
    return lax.all_to_all(values, T, 0, 0)


def z_spread(values):
    return z_all(jnp.broadcast_to(values[None], (4,) + values.shape))


def folded(values):
    values = jnp.pad(values, ((0, 3), (0, 0)))
    return jnp.concatenate([values[:40], values[40:]], axis=1)


def unfolded(values):
    return jnp.concatenate([values[:, :640], values[:37, 640:]], axis=0)


def h_collect(pieces):
    total = pieces[0]
    for j in (1, 2, 3):
        total = total + flip(pieces[j], j)
    return total


def h_sum(values):
    pair = values + flip(values, 1)
    return pair + flip(pair, 2)


def pick(values, index, axis=0):
    return lax.dynamic_index_in_dim(values, index, axis, keepdims=False)


def plane_sum(own):
    part = h_collect([own[j] for j in range(4)])
    pieces = [part] + [flip(part, j) for j in (1, 2, 3)]
    return pieces + [swap(piece) for piece in pieces], part


def plane_exchange(packed):
    return lax.all_to_all(packed, IH, 0, 0)


IMAGE_ROWS = 1152
TAP_ROWS = range(16, 1136, 160)


def halves(values):
    top = values.astype(jnp.bfloat16)
    return top, (values - top.astype(jnp.float32)).astype(jnp.bfloat16)


def dot_halves(left, right, left_dim, right_dim):
    def one(a, b):
        return lax.dot_general(
            a, b, (((left_dim,), (right_dim,)), ((), ())), preferred_element_type=jnp.float32
        )

    return one(left[0], right[0]) + (one(left[0], right[1]) + one(left[1], right[0]))


def marks_of(marks, b):
    return marks[2 * b], marks[2 * b + 1]


def row_mask(span, rows, columns):
    return (lax.broadcasted_iota(jnp.int32, (rows, columns), 0) < span).astype(jnp.float32)


def unpack_quarter(packed):
    rest = jnp.concatenate([packed[64:80, 32 * g : 32 * g + 32] for g in range(4)], axis=0)
    return jnp.concatenate([packed[:64], rest], axis=1)


def put_quarter(out, place, values, row=0):
    out[place, row : row + 64, :] = values[:, :128]
    for g in range(4):
        out[place, row + 64 : row + 80, 32 * g : 32 * g + 32] = values[
            16 * g : 16 * g + 16, 128:160
        ]


def unpack_strip(packed):
    rest = jnp.concatenate([packed[256:320, 64 * g : 64 * g + 64] for g in range(4)], axis=0)
    return jnp.concatenate([packed[:256], rest], axis=1)


def put_packed_strip(out, place, values):
    out[place, 0:256, :] = values[:, :256]
    for g in range(4):
        out[place, 256:320, 64 * g : 64 * g + 64] = values[64 * g : 64 * g + 64, 256:320]


def put_strip(image, b, strip, span, values):
    at = pl.multiple_of(margin + strip * span, 8)
    image[b, pl.ds(at, 240)] = values[:240]

    @pl.when(span == 256)
    def _():
        image[b, pl.ds(pl.multiple_of(at + 240, 8), 16)] = values[240:]


def put_cells(image, b, strip, span, q, values):
    at = pl.multiple_of(margin + strip * span + q * 64, 8)
    image[b, pl.ds(at, 48)] = values[:48]

    @pl.when((q < 3) | (span == 256))
    def _():
        image[b, pl.ds(pl.multiple_of(at + 48, 8), 16)] = values[48:]


def quarter_mask(span, q):
    row = lax.broadcasted_iota(jnp.int32, (64, 160), 0) + q * 64
    return (row < span).astype(jnp.float32)


def widen(wide, image, b, width, sign):
    channels = image.shape[2]
    width_f = width.astype(jnp.float32)
    for base in TAP_ROWS:
        row = lax.broadcasted_iota(jnp.int32, (160, channels), 0).astype(jnp.float32)
        cell = row + float(base - margin)
        column = cell - width_f * jnp.floor((cell + 0.5) / width_f)
        for j in range(3):
            step = sign * (j - 1)
            values = image[b, base + step : base + step + 160, :]
            if step < 0:
                values = jnp.where(column > 0.5, values, 0.0)
            if step > 0:
                values = jnp.where(column < width_f - 1.5, values, 0.0)
            wide[base : base + 160, j * channels : (j + 1) * channels] = values


def split_weight(weight, top, low):
    for k in range(3):
        rows = weight.shape[0] // 3
        first, second = halves(weight[k * rows : (k + 1) * rows, :])
        top[k * rows : (k + 1) * rows, :] = first
        low[k * rows : (k + 1) * rows, :] = second


def split_weight_turned(weight, top, low):
    for tap in range(9):
        first, second = halves(weight[160 * tap : 160 * tap + 160, :].T)
        top[320 * tap : 320 * tap + 320, :] = first
        low[320 * tap : 320 * tap + 320, :] = second


def conv_strip(wide, top, low, strip, span, width, sign):
    rows = top.shape[0] // 3
    total = None
    for i in range(3):
        at = pl.multiple_of(margin + strip * span + sign * (i - 1) * width, 8)
        taps = halves(wide[pl.ds(at, 256), :])
        part = dot_halves(
            taps, (top[i * rows : (i + 1) * rows, :], low[i * rows : (i + 1) * rows, :]), 1, 0
        )
        total = part if total is None else total + part
    return total * row_mask(span, 256, total.shape[1])


def group_rows(sums):
    channels = sums.shape[1]
    lane = lax.broadcasted_iota(jnp.int32, (1, channels), 1)
    result = jnp.zeros((1, channels), jnp.float32)
    for g in range(channels // 40):
        inside = (lane >= 40 * g) & (lane < 40 * g + 40)
        result = jnp.where(inside, jnp.sum(jnp.where(inside, sums, 0.0)), result)
    return result


def group_row_stats(total, squares, span):
    count = (span * 160).astype(jnp.float32)
    mean = group_rows(total) / count
    var = group_rows(squares) / count - mean * mean
    return mean, lax.rsqrt(var + norm_eps)


def column_sum(values):
    return jnp.sum(values, axis=0, keepdims=True)


def first_kernel(
    marks, source, gain, tau, weight, own, other, image, stats, wide, top, low, cells
):
    item, h = marks[4], marks[5]
    split_weight(weight, top, low)
    image[...] = jnp.zeros_like(image)
    for b, out in ((0, own), (1, other)):
        span, width = marks_of(marks, b)
        base = (item ^ b) * 4
        total = jnp.zeros((1, 160), jnp.float32)
        squares = jnp.zeros((1, 160), jnp.float32)
        for k in range(4):
            for q in range(4):
                values = unpack_quarter(source[base + k, 80 * q : 80 * q + 80, :])
                cells[k, 64 * q : 64 * q + 64, :] = values
                total = total + column_sum(values)
                squares = squares + column_sum(values * values)
        mean, inv = group_row_stats(total, squares, span)
        stats[b, 0:1, :] = mean
        stats[b, 1:2, :] = inv
        for k in range(4):
            norm = (cells[k] - mean) * inv * row_mask(span, 256, 160) * gain[...]
            put_strip(image, b, k, span, norm * jax.nn.sigmoid(norm))
        widen(wide, image, b, width, 1)
        added = tau[b : b + 1, :]

        def step(k, _):
            conv = conv_strip(wide, top, low, k, span, width, 1)
            put_packed_strip(out, k ^ h, conv + added * row_mask(span, 256, 320))
            return 0

        lax.fori_loop(0, 4, step, 0)


def put_quarters(outs, tile, place, t):
    for j in range(4):
        at = pl.multiple_of(lax.rem(t + j, 4) * 64, 8)
        put_quarter(outs[j], place, tile[pl.ds(at, 64), :])


def second_kernel(marks, *refs):
    strips, gain, weight = refs[:8], refs[8], refs[9]
    outs, image, stats = refs[10:14], refs[14], refs[15]
    wide, top, low, tile = refs[16:]
    item, h, t = marks[4], marks[5], marks[6]
    split_weight_turned(weight, top, low)
    image[...] = jnp.zeros_like(image)
    for b in range(2):
        span, width = marks_of(marks, b)
        total = jnp.zeros((1, 320), jnp.float32)
        squares = jnp.zeros((1, 320), jnp.float32)
        for j in range(4):
            values = unpack_strip(strips[4 * b + j][...])
            total = total + column_sum(values)
            squares = squares + column_sum(values * values)
        mean, inv = group_row_stats(total, squares, span)
        stats[b, 0:1, :] = mean
        stats[b, 1:2, :] = inv
        for j in range(4):
            values = unpack_strip(strips[4 * b + j][...])
            norm = (values - mean) * inv * row_mask(span, 256, 320) * gain[...]
            put_strip(image, b, h ^ j, span, norm * jax.nn.sigmoid(norm))
        widen(wide, image, b, width, 1)

        def step(k, _):
            tile[...] = conv_strip(wide, top, low, k, span, width, 1)
            put_quarters(outs, tile, (item ^ b) * 4 + k, t)
            return 0

        lax.fori_loop(0, 4, step, 0)


def second_back_kernel(marks, *refs):
    quarters, weight = refs[:4], refs[4]
    own, other, image = refs[5:8]
    wide, top, low = refs[8:]
    item, h, t = marks[4], marks[5], marks[6]
    split_weight(weight, top, low)
    image[...] = jnp.zeros_like(image)
    for b, out in ((0, own), (1, other)):
        span, width = marks_of(marks, b)

        def fill(k, _):
            for j in range(4):
                values = unpack_quarter(quarters[j][(item ^ b) * 4 + k])
                put_cells(image, b, k, span, lax.rem(t + j, 4), values)
            return 0

        lax.fori_loop(0, 4, fill, 0)
        widen(wide, image, b, width, -1)

        def step(k, _):
            put_packed_strip(out, k ^ h, conv_strip(wide, top, low, k, span, width, -1))
            return 0

        lax.fori_loop(0, 4, step, 0)


def first_back_kernel(marks, *refs):
    grads, strips, gain, stats, weight = refs[:8], refs[8:16], refs[16], refs[17], refs[18]
    outs, image, sums, grad_gain = refs[19:23], refs[23], refs[24], refs[25]
    wide, top, low, tile, scaled_at, centred_at = refs[26:]
    item, h, t = marks[4], marks[5], marks[6]
    split_weight_turned(weight, top, low)
    image[...] = jnp.zeros_like(image)
    gain_total = jnp.zeros((1, 320), jnp.float32)
    for b in range(2):
        span, width = marks_of(marks, b)
        mean, inv = stats[b, 0:1, :], stats[b, 1:2, :]
        first = jnp.zeros((1, 320), jnp.float32)
        second = jnp.zeros((1, 320), jnp.float32)
        for j in range(4):
            values = unpack_strip(strips[4 * b + j][...])
            centred = (values - mean) * inv * row_mask(span, 256, 320)
            norm = centred * gain[...]
            gate = jax.nn.sigmoid(norm)
            grad_norm = unpack_strip(grads[4 * b + j][...]) * gate * (1.0 + norm * (1.0 - gate))
            scaled = grad_norm * gain[...]
            first = first + column_sum(scaled)
            second = second + column_sum(scaled * centred)
            gain_total = gain_total + column_sum(grad_norm * centred)
            scaled_at[j] = scaled
            centred_at[j] = centred
        count = (span * 160).astype(jnp.float32)
        first = group_rows(first) / count
        second = group_rows(second) / count
        tau_total = jnp.zeros((1, 320), jnp.float32)
        for j in range(4):
            grad = inv * row_mask(span, 256, 320) * (
                scaled_at[j] - first - centred_at[j] * second
            )
            tau_total = tau_total + column_sum(grad)
            put_strip(image, b, h ^ j, span, grad)
        sums[b : b + 1, :] = tau_total
        widen(wide, image, b, width, -1)

        def step(k, _):
            tile[...] = conv_strip(wide, top, low, k, span, width, -1)
            put_quarters(outs, tile, (item ^ b) * 4 + k, t)
            return 0

        lax.fori_loop(0, 4, step, 0)
    grad_gain[...] = gain_total


def conv_weight_kernel(sign, marks, image, cells, out, wide):
    out[...] = jnp.zeros_like(out)
    for b in range(2):
        _, width = marks_of(marks, b)
        widen(wide, image, b, width, sign)
        for i in range(3):

            def step(c, _):
                at = pl.multiple_of(margin + c * 256 + sign * (i - 1) * width, 8)
                taps = halves(wide[pl.ds(at, 256), :].T)
                values = halves(cells[b, pl.ds(pl.multiple_of(margin + c * 256, 8), 256), :])
                part = dot_halves(taps, values, 1, 0)
                for j in range(3):
                    out[3 * i + j] += part[160 * j : 160 * j + 160]
                return 0

            lax.fori_loop(0, 4, step, 0)


def wide_halves(values):
    top, low = halves(values)
    return jnp.concatenate([top, top, low], axis=1)


def other_halves(values):
    top, low = halves(values)
    return jnp.concatenate([top, low, top], axis=1)


def dot_last(left, right):
    return lax.dot_general(
        left, right, (((1,), (1,)), ((), ())), preferred_element_type=jnp.float32
    )


def dot_pair(left, values):
    top, low = halves(values)
    both = jnp.dot(left[0], jnp.concatenate([top, low], axis=1), preferred_element_type=jnp.float32)
    return (both[:, :64] + both[:, 64:]) + jnp.dot(
        left[1], top, preferred_element_type=jnp.float32
    )


def scores_turned(marks, queries, pieces, head, j):
    at = 64 * head
    keys = pieces[j][:, at : at + 64]
    scores = dot_last(wide_halves(keys), other_halves(queries[:, at : at + 64])) * 0.125
    slot = lax.broadcasted_iota(jnp.int32, (256, 256), 0) + marks[6] * 64
    slot = jnp.where(slot >= 256, slot - 256, slot)
    return jnp.where(slot < marks[0], scores, masked_score)


def attend_kernel(marks, qkv, *refs):
    pieces, out, totals, held = refs[:4], refs[4], refs[5], refs[6]
    totals[...] = jnp.zeros_like(totals)
    for head in range(5):
        peak = None
        for j in range(4):
            scores = scores_turned(marks, qkv, pieces, head, j)
            held[256 * j : 256 * j + 256, :] = scores
            here = jnp.max(scores, axis=0, keepdims=True)
            peak = here if peak is None else jnp.maximum(peak, here)
        total = jnp.zeros((1, 256), jnp.float32)
        attended = jnp.zeros((64, 256), jnp.float32)
        for j in range(4):
            exponent = jnp.exp(held[256 * j : 256 * j + 256, :] - peak)
            total = total + column_sum(exponent)
            values = halves(pieces[j][:, 320 + 64 * head : 384 + 64 * head].T)
            first, second = halves(exponent)
            both = jnp.dot(
                jnp.concatenate(values, axis=0), first, preferred_element_type=jnp.float32
            )
            attended = attended + (
                (both[:64] + both[64:])
                + jnp.dot(values[0], second, preferred_element_type=jnp.float32)
            )
        out[:, 64 * head : 64 * head + 64] = (attended / total).T
        totals[head : head + 1, :] = peak + jnp.log(total)


def attend_back_kernel(marks, qkv, *refs):
    pieces, totals, attended, grad = refs[:4], refs[4], refs[5], refs[6]
    grad_query, outs = refs[7], refs[8:12]
    for head in range(5):
        at = 64 * head
        grad_out = grad[:, at : at + 64]
        queries = qkv[:, at : at + 64]
        delta = column_sum((grad_out * attended[:, at : at + 64]).T)
        total = totals[head : head + 1, :]
        grad_other = other_halves(grad_out)
        query_grad = jnp.zeros((64, 256), jnp.float32)
        for j in range(4):
            weights = jnp.exp(scores_turned(marks, qkv, pieces, head, j) - total)
            values = pieces[j][:, 320 + at : 384 + at]
            grad_scores = weights * (dot_last(wide_halves(values), grad_other) - delta)
            outs[j][:, 320 + at : 384 + at] = dot_pair(halves(weights), grad_out)
            first, second = halves(grad_scores)
            outs[j][:, at : at + 64] = dot_pair((first, second), queries) * 0.125
            keys = halves(pieces[j][:, at : at + 64].T)
            both = jnp.dot(
                jnp.concatenate(keys, axis=0), first, preferred_element_type=jnp.float32
            )
            query_grad = query_grad + (
                (both[:64] + both[64:])
                + jnp.dot(keys[0], second, preferred_element_type=jnp.float32)
            )
        grad_query[:, at : at + 64] = query_grad.T * 0.125


def pack_kernel(marks, values, out):
    for q in range(values.shape[0] // 64):
        for k in range(8):
            part = values[64 * q : 64 * q + 64, 160 * k : 160 * k + 160]
            put_quarter(out, k, part, 80 * q)


def unpack_kernel(marks, packed, plain):
    for k in range(8):
        plain[:, 160 * k : 160 * k + 160] = unpack_quarter(packed[k, 0:80, :])


def unpack_norm_kernel(marks, packed, gain, scaled, plain):
    for k in range(8):
        centred = unpack_quarter(packed[k, 0:80, :])
        mean = jnp.concatenate([packed[k, 80:81, :], packed[k, 81:82, 0:32]], axis=1)
        inv = jnp.concatenate([packed[k, 82:83, :], packed[k, 83:84, 0:32]], axis=1)
        at = slice(160 * k, 160 * k + 160)
        scaled[:, at] = centred * gain[:, at]
        plain[:, at] = centred * (1.0 / inv) + mean


def cotangent_kernel(marks, pieces, total, out, whole):
    total[...] = (pieces[0, :, :1280] + pieces[1, :, :1280]) + (
        pieces[2, :, :1280] + pieces[3, :, :1280]
    )
    for part in range(4):
        whole[:, 320 * part : 320 * part + 320] = pieces[part, :, 1280:1600]
    for k in range(8):
        put_quarter(out, k, whole[:, 160 * k : 160 * k + 160])


def third_kernel(marks, *refs):
    pieces, out, gain = refs[:4], refs[4], refs[5]
    for first in range(4):

        @pl.when(marks[6] == first)
        def _():
            for j in range(4):
                at = (first + j) % 4 * 320
                gain[:, at : at + 320] = pieces[j][160:161, 0:320]
                for m in range(3):
                    out[:, 1280 * m + at : 1280 * m + at + 320] = pieces[j][
                        0:160, 320 * m : 320 * m + 320
                    ]


def text_kernel(marks, pieces, rows, keys, values):
    for part in range(4):
        at = pl.multiple_of(lax.rem(part - marks[6] + 4, 4) * 64, 8)
        rows[pl.ds(at, 64), :] = pieces[part, 0:64, :]
        lanes = slice(320 * part, 320 * part + 320)
        keys[0:40, lanes] = pieces[part, 64:104, 0:320]
        values[0:40, lanes] = pieces[part, 64:104, 320:640]
        keys[40:77, lanes] = pieces[part, 64:101, 640:960]
        values[40:77, lanes] = pieces[part, 64:101, 960:1280]


def text_grad_kernel(marks, rows, keys, values, out):
    for part in range(4):
        at = pl.multiple_of(lax.rem(part - marks[6] + 4, 4) * 64, 8)
        out[part, 0:64, :] = rows[pl.ds(at, 64), :]
        lanes = slice(320 * part, 320 * part + 320)
        out[part, 64:104, 0:320] = keys[0:40, lanes]
        out[part, 64:104, 320:640] = values[0:40, lanes]
        out[part, 64:101, 640:960] = keys[40:77, lanes]
        out[part, 64:101, 960:1280] = values[40:77, lanes]
        out[part, 101:104, 640:1280] = jnp.zeros((3, 640), jnp.float32)


def rows_kernel(marks, *refs):
    pieces, out = refs[:4], refs[4]
    for j in range(4):
        at = pl.multiple_of(lax.rem(marks[6] + j, 4) * 64, 8)
        out[pl.ds(at, 64), :] = pieces[j][...]


def residual_kernel(marks, source, first, second, third, fourth, out, sums):
    t = marks[6]
    at = pl.multiple_of(t * 80, 8)
    sums[...] = jnp.zeros_like(sums)
    for b in range(2):
        for k in range(4):
            place = 4 * b + k
            packed = source[place, pl.ds(at, 80), :] + (
                (first[place] + second[place]) + (third[place] + fourth[place])
            )
            out[place] = packed
            values = unpack_quarter(packed)
            sums[2 * b : 2 * b + 1, :] += column_sum(values)
            sums[2 * b + 1 : 2 * b + 2, :] += column_sum(values * values)


def span_of_item(marks, b):
    return jnp.where(marks[4] == b, marks[0], marks[2])


def norm_kernel(marks, residual, first, second, third, fourth, out, stats):
    total = (first[...] + second[...]) + (third[...] + fourth[...])
    for b in range(2):
        span = span_of_item(marks, b)
        mean, inv = group_row_stats(
            total[2 * b : 2 * b + 1, :], total[2 * b + 1 : 2 * b + 2, :], span
        )
        stats[2 * b : 2 * b + 1, :] = mean
        stats[2 * b + 1 : 2 * b + 2, :] = inv
        for k in range(4):
            values = unpack_quarter(residual[4 * b + k])
            centred = (values - mean) * inv * quarter_mask(span, marks[6])
            put_quarter(out, 4 * b + k, centred)
            out[4 * b + k, 80:88, :] = jnp.zeros((8, 128), jnp.float32)
            for row, value in ((80, mean), (82, inv)):
                out[4 * b + k, row : row + 1, :] = value[:, :128]
                out[4 * b + k, row + 1 : row + 2, 0:32] = value[:, 128:]


def centred_of(marks, residual, stats, b, k):
    values = unpack_quarter(residual[4 * b + k])
    mean, inv = stats[2 * b : 2 * b + 1, :], stats[2 * b + 1 : 2 * b + 2, :]
    return (values - mean) * inv * quarter_mask(span_of_item(marks, b), marks[6])


def norm_sums_kernel(marks, grad, residual, stats, gain, sums):
    sums[...] = jnp.zeros_like(sums)
    for b in range(2):
        for k in range(4):
            centred = centred_of(marks, residual, stats, b, k)
            values = unpack_quarter(grad[4 * b + k])
            scaled = values * gain[...]
            sums[3 * b : 3 * b + 1, :] += column_sum(scaled)
            sums[3 * b + 1 : 3 * b + 2, :] += column_sum(scaled * centred)
            sums[3 * b + 2 : 3 * b + 3, :] += column_sum(values * centred)


def sum_in_order(pieces, t):
    total = None
    for part in range(4):
        j = lax.rem(part - t + 4, 4)
        value = jnp.where(
            j < 2,
            jnp.where(j == 0, pieces[0][...], pieces[1][...]),
            jnp.where(j == 2, pieces[2][...], pieces[3][...]),
        )
        total = value if total is None else total + value
    return total


def norm_back_kernel(marks, *refs):
    grad, residual, stats, gain, base = refs[:5]
    pieces, out, grad_gain = refs[5:9], refs[9], refs[10]
    total = sum_in_order(pieces, marks[6])
    grad_gain[...] = jnp.zeros_like(grad_gain)
    grad_gain[0:1, :] = total[2:3, :] + total[5:6, :]
    for b in range(2):
        span = span_of_item(marks, b)
        count = (span * 160).astype(jnp.float32)
        first = group_rows(total[3 * b : 3 * b + 1, :]) / count
        second = group_rows(total[3 * b + 1 : 3 * b + 2, :]) / count
        inv = stats[2 * b + 1 : 2 * b + 2, :]
        for k in range(4):
            centred = centred_of(marks, residual, stats, b, k)
            scaled = unpack_quarter(grad[4 * b + k]) * gain[...]
            values = inv * quarter_mask(span, marks[6]) * (scaled - first - centred * second)
            put_quarter(out, 4 * b + k, values + unpack_quarter(base[4 * b + k]))


def input_sums_kernel(marks, source, gain, stats, *refs):
    pieces, out, sums = refs[:4], refs[4], refs[5]
    at = pl.multiple_of(marks[6] * 80, 8)
    sums[...] = jnp.zeros_like(sums)
    for b in range(2):
        span = span_of_item(marks, b)
        mine = marks[4] ^ b
        mean, inv = stats[mine, 0:1, :], stats[mine, 1:2, :]
        for k in range(4):
            place = 4 * b + k
            values = unpack_quarter(source[place, pl.ds(at, 80), :])
            centred = (values - mean) * inv * quarter_mask(span, marks[6])
            norm = centred * gain[...]
            gate = jax.nn.sigmoid(norm)
            packed = (pieces[0][place] + pieces[1][place]) + (pieces[2][place] + pieces[3][place])
            grad = unpack_quarter(packed) * gate * (1.0 + norm * (1.0 - gate))
            put_quarter(out, place, grad)
            scaled = grad * gain[...]
            sums[3 * b : 3 * b + 1, :] += column_sum(scaled)
            sums[3 * b + 1 : 3 * b + 2, :] += column_sum(scaled * centred)
            sums[3 * b + 2 : 3 * b + 3, :] += column_sum(grad * centred)


def input_back_kernel(marks, grad, source, gain, stats, base, extra, *refs):
    pieces, out, grad_gain = refs[:4], refs[4], refs[5]
    at = pl.multiple_of(marks[6] * 80, 8)
    total = sum_in_order(pieces, marks[6])
    grad_gain[...] = jnp.zeros_like(grad_gain)
    grad_gain[0:1, :] = total[2:3, :] + total[5:6, :]
    for b in range(2):
        span = span_of_item(marks, b)
        count = (span * 160).astype(jnp.float32)
        first = group_rows(total[3 * b : 3 * b + 1, :]) / count
        second = group_rows(total[3 * b + 1 : 3 * b + 2, :]) / count
        mine = marks[4] ^ b
        mean, inv = stats[mine, 0:1, :], stats[mine, 1:2, :]
        for k in range(4):
            place = 4 * b + k
            keep = quarter_mask(span, marks[6])
            centred = (unpack_quarter(source[place, pl.ds(at, 80), :]) - mean) * inv * keep
            scaled = unpack_quarter(grad[place]) * gain[...]
            values = inv * keep * (scaled - first - centred * second)
            put_quarter(out, place, values + unpack_quarter(base[place]))
            out[place, 80:88, :] = extra[place]


def run_kernel(body, marks, inputs, outs, scratch, flops):
    in_smem = pl.BlockSpec(memory_space=pltpu.SMEM)
    in_vmem = pl.BlockSpec(memory_space=pltpu.VMEM)
    return pl.pallas_call(
        body,
        out_shape=[jax.ShapeDtypeStruct(shape, jnp.float32) for shape in outs],
        in_specs=[in_smem] + [in_vmem] * len(inputs),
        out_specs=[in_vmem] * len(outs),
        scratch_shapes=[pltpu.VMEM(shape, kind) for shape, kind in scratch],
        compiler_params=pltpu.CompilerParams(vmem_limit_bytes=56 * 1024 * 1024),
        cost_estimate=pl.CostEstimate(
            flops=flops, bytes_accessed=10 * 1024 * 1024, transcendentals=0
        ),
    )(marks, *inputs)


def weight_kernel(plan, *refs):
    count = 1 + max(which for block in plan for _, _, which in block)
    lefts, right, out = refs[:count], refs[count], refs[-1]
    tokens = right.shape[0]
    for number, block in enumerate(plan):

        @pl.when(pl.program_id(0) == number)
        def _():
            for begin, columns, which in block:
                top, low = halves(right[:, begin : begin + columns])
                if tokens <= 64:
                    stacked = jnp.concatenate([top, low, top], axis=0)
                for m in range(0, 1280, 256):
                    cells = lefts[which][:, m : m + 256].T
                    if tokens <= 64:
                        first, second = halves(cells)
                        first = jnp.concatenate([first, first, second], axis=1)
                        part = jnp.dot(first, stacked, preferred_element_type=jnp.float32)
                    else:
                        part = dot_halves(halves(cells), (top, low), 1, 0)
                    out[m : m + 256, begin : begin + columns] = part


def weight_grads(plan, lefts, right, first=0, blocks=None, into=None):
    tokens = right.shape[0]
    blocks = blocks or len(plan)
    in_specs = [pl.BlockSpec((tokens, 1280), lambda i: (0, 0))] * len(lefts)
    in_specs.append(pl.BlockSpec((tokens, 1280), lambda i: (0, i)))
    inputs, alias = (*lefts, right), {}
    if into is not None:
        in_specs.append(pl.BlockSpec(memory_space=pl.ANY))
        alias = {len(inputs): 0}
        inputs = (*inputs, into)
    return pl.pallas_call(
        functools.partial(weight_kernel, plan),
        out_shape=jax.ShapeDtypeStruct((1280, 1280 * blocks), jnp.float32),
        grid=(len(plan),),
        in_specs=in_specs,
        out_specs=pl.BlockSpec((1280, 1280), lambda i: (0, i + first)),
        input_output_aliases=alias,
        compiler_params=pltpu.CompilerParams(vmem_limit_bytes=48 * 1024 * 1024),
        cost_estimate=pl.CostEstimate(
            flops=6 * tokens * 1280 * 1280 * len(plan),
            bytes_accessed=7 * 1024 * 1024 * len(plan),
            transcendentals=0,
        ),
    )(*inputs)


def after(values, *events):
    return lax.optimization_barrier((values,) + events)[0]


def together(*values):
    return lax.optimization_barrier(values)


def small(body, marks, inputs, outs, scratch=()):
    return run_kernel(body, marks, inputs, outs, scratch, 4 * 1024 * 1024)


CONV_FLOPS = 6 * 2048 * 1440 * 320


def first_conv(marks, source, gain, tau, weight):
    f32, b16 = jnp.float32, jnp.bfloat16
    return run_kernel(
        first_kernel,
        marks,
        (source, gain, tau, weight),
        [(4, 320, 256), (4, 320, 256), (2, IMAGE_ROWS, 160), (2, 8, 160)],
        [
            ((IMAGE_ROWS, 480), f32),
            ((1440, 320), b16),
            ((1440, 320), b16),
            ((4, 256, 160), f32),
        ],
        CONV_FLOPS,
    )


def second_conv(marks, strips, gain, weight):
    f32, b16 = jnp.float32, jnp.bfloat16
    return run_kernel(
        second_kernel,
        marks,
        (*strips, gain, weight),
        [(8, 80, 128)] * 4 + [(2, IMAGE_ROWS, 320), (2, 8, 320)],
        [
            ((IMAGE_ROWS, 960), f32),
            ((2880, 160), b16),
            ((2880, 160), b16),
            ((256, 160), f32),
        ],
        CONV_FLOPS,
    )


def second_conv_back(marks, quarters, weight):
    f32, b16 = jnp.float32, jnp.bfloat16
    return run_kernel(
        second_back_kernel,
        marks,
        (*quarters, weight),
        [(4, 320, 256), (4, 320, 256), (2, IMAGE_ROWS, 160)],
        [((IMAGE_ROWS, 480), f32), ((1440, 320), b16), ((1440, 320), b16)],
        CONV_FLOPS,
    )


def first_conv_back(marks, grads, strips, gain, stats, weight):
    f32, b16 = jnp.float32, jnp.bfloat16
    return run_kernel(
        first_back_kernel,
        marks,
        (*grads, *strips, gain, stats, weight),
        [(8, 80, 128)] * 4 + [(2, IMAGE_ROWS, 320), (2, 320), (1, 320)],
        [
            ((IMAGE_ROWS, 960), f32),
            ((2880, 160), b16),
            ((2880, 160), b16),
            ((256, 160), f32),
            ((4, 256, 320), f32),
            ((4, 256, 320), f32),
        ],
        CONV_FLOPS,
    )


def conv_weight(marks, image, cells, sign):
    return run_kernel(
        functools.partial(conv_weight_kernel, sign),
        marks,
        (image, cells),
        [(9, 160, 320)],
        [((IMAGE_ROWS, 480), jnp.float32)],
        CONV_FLOPS,
    )[0]


def heads_of(values, count):
    return values.reshape(values.shape[0], count, HEAD_DIM)


def ein(form, left, right):
    return jnp.einsum(form, left, right, precision=high, preferred_element_type=jnp.float32)


def soft_attend(queries, keys, values, key_valid, count):
    scores = ein(QK, heads_of(queries, count), heads_of(keys, count)) * (1.0 / math.sqrt(HEAD_DIM))
    if key_valid is not None:
        scores = jnp.where(key_valid[None, None, :], scores, masked_score)
    exponent = jnp.exp(scores - jnp.max(scores, axis=-1, keepdims=True))
    weights = exponent / jnp.sum(exponent, axis=-1, keepdims=True)
    attended = ein(PV, weights, heads_of(values, count))
    return attended.reshape(queries.shape), weights


def soft_back(queries, keys, values, count, weights, attended, grad_out):
    scaling = 1.0 / math.sqrt(HEAD_DIM)
    grad_heads = heads_of(grad_out, count)
    grad_soft = ein(QK, grad_heads, heads_of(values, count))
    delta = jnp.sum(grad_heads * heads_of(attended, count), axis=-1).T
    grad_scores = weights * (grad_soft - delta[..., None])
    grad_query = ein(PV, grad_scores, heads_of(keys, count)) * scaling
    grad_key = ein(PQ, grad_scores, heads_of(queries, count)) * scaling
    grad_value = ein(PQ, weights, grad_heads)
    return (
        grad_query.reshape(queries.shape),
        grad_key.reshape(keys.shape),
        grad_value.reshape(values.shape),
    )


def layer_grad(grad_out, centred, inv_std, gain_vector):
    scaled = grad_out * gain_vector
    grad_in = inv_std * (
        scaled
        - jnp.mean(scaled, axis=-1, keepdims=True)
        - centred * jnp.mean(scaled * centred, axis=-1, keepdims=True)
    )
    return grad_in, jnp.sum(grad_out * centred, axis=0)


def layer_forward(values, gain_vector):
    mean_val = jnp.mean(values, axis=-1, keepdims=True)
    var_val = jnp.mean(values * values, axis=-1, keepdims=True) - mean_val * mean_val
    inv_std = lax.rsqrt(var_val + norm_eps)
    centred = (values - mean_val) * inv_std
    return centred * gain_vector, centred, inv_std


def gather_plane(block):
    return lax.all_gather(block, IH, axis=0, tiled=True)


def scatter_plane(block):
    return lax.psum_scatter(block, IH, scatter_dimension=0, tiled=True)


def grid_cells(bucket):
    strip_rows, strip_width = grid_shape(bucket)
    return strip_rows * strip_width


def fast_shards(
    hidden,
    text_states,
    bucket,
    timestep,
    gain_in,
    conv_first,
    time_weight,
    gain_mid,
    conv_second,
    gain_attn_norm,
    proj_in,
    gain_self,
    query_self,
    key_self,
    value_self,
    out_self,
    gain_cross,
    query_cross,
    key_cross,
    value_cross,
    out_cross,
    gain_ff,
    ff_in,
    ff_out,
    proj_out,
    cotangent,
):
    item, h, t = lax.axis_index(I), lax.axis_index(H), lax.axis_index(T)
    block = item * 4 + h
    width, wide = 160, 320
    channels = 1280

    def rows_of(values):
        return [values[64 * j : 64 * j + 64] for j in range(4)]

    own_span = grid_cells(bucket[0])
    slot = jnp.arange(256, dtype=jnp.int32)
    own_valid = (slot < own_span).astype(jnp.float32)[:, None]
    both = jnp.stack([bucket[0], timestep[0]]).astype(jnp.float32)
    both_other = swap(both)
    times = jnp.stack([both[1], both_other[1]])
    other_rows, other_width = grid_shape(both_other[0].astype(jnp.int32))
    own_rows, own_width = grid_shape(bucket[0])
    marks = jnp.stack(
        [own_span, own_width, other_rows * other_width, other_width, item, h, t]
    ).astype(jnp.int32)

    (source,) = small(pack_kernel, marks, (hidden[0] * own_valid,), [(8, 320, 128)])
    source = plane_exchange(source)
    gains = jnp.stack([gain_self, gain_cross, gain_ff], axis=1)
    attn_full = gather_plane(
        jnp.concatenate(
            [
                query_self,
                key_self,
                value_self,
                proj_out,
                out_self.T,
                jnp.pad(gains, ((0, 0), (0, 125))),
            ],
            axis=1,
        )
    )
    qkv_full = attn_full[:, :960]
    proj_out_full = attn_full[:, 960:1280]
    out_self_full = attn_full[:, 1280:1600]
    gain_rows = attn_full[:, 1600:1603].T
    gain_self_full, gain_cross_full, gain_ff_full = (gain_rows[k : k + 1] for k in range(3))

    own_third = jnp.concatenate([proj_in.T, query_cross, out_cross.T], axis=1)
    own_third = jnp.concatenate(
        [own_third, jnp.pad(gain_attn_norm[None, :], ((0, 7), (0, 640)))], axis=0
    )
    third_pieces = z_pieces(own_third)

    features = jax.nn.silu(time_features(times, channels))
    own_features = lax.dynamic_slice_in_dim(features, block * width, width, 1)
    tau = mm(own_features, time_weight, 1, 0)
    second_weight = conv_second.transpose(0, 1, 3, 2).reshape(9 * width, wide)
    own_one, other_one, image_one, stats_one = first_conv(
        marks, source, gain_in[None, :], tau, conv_first.reshape(9 * width, wide)
    )
    own_one, other_one, *third_pieces = together(own_one, other_one, *third_pieces)
    own_one = own_one + swap(other_one)
    strips_one, part = plane_sum(own_one)
    third, gain_attn_full = small(
        third_kernel, marks, after(third_pieces, part), [(160, 3840), (1, channels)]
    )
    third_full = gather_plane(third)
    proj_in_full = third_full[:, :1280]
    query_cross_full = third_full[:, 1280:2560]
    out_cross_full = third_full[:, 2560:]
    ff_block = jnp.concatenate([ff_in.reshape(160, 2560), ff_out.T], axis=1)
    ff_full = gather_plane(after(ff_block, part))
    ff_in_full = ff_full[:, :2560]
    ff_out_full = ff_full[:, 2560:]
    cot = after(cotangent[0] * own_valid, own_one)
    grad_ff_part = mm(cot, proj_out_full, 1, 1)
    cot_pieces = z_all(jnp.concatenate([grad_ff_part, cot], axis=1).reshape(4, 64, channels + wide))
    *strips_one, cot_pieces = together(*strips_one, cot_pieces)

    *conv_two, image_two, stats_two = second_conv(
        marks, strips_one, gain_mid[None, :], second_weight
    )
    conv_two_pieces = z_received(conv_two)

    event = conv_two[0]
    grad_after_ff, cot_packed = small(
        cotangent_kernel,
        marks,
        (after(cot_pieces, event),),
        [(64, channels), (8, 80, 128)],
        [((64, channels), jnp.float32)],
    )
    cot_q = plane_exchange(cot_packed)
    text_here = after(text_states[0], event)
    text_own = lax.dynamic_slice_in_dim(text_here, block * 256, 256, 1)
    text_other = swap(lax.dynamic_slice_in_dim(text_here, ((1 - item) * 4 + h) * 256, 256, 1))
    text_weight = jnp.concatenate([key_cross, value_cross], axis=1)
    text_part = mm(text_own, text_weight, 1, 0) + swap(mm(text_other, text_weight, 1, 0))

    residual_q, sums = small(
        residual_kernel, marks, (source, *conv_two_pieces), [(8, 80, 128), (8, width)]
    )
    centred_three, stats_three = small(
        norm_kernel, marks, (residual_q, *z_pieces(sums)), [(8, 88, 128), (8, width)]
    )
    norm_three, residual_s = small(
        unpack_norm_kernel,
        marks,
        (plane_exchange(centred_three), gain_attn_full),
        [(64, channels), (64, channels)],
    )
    projected = mm(norm_three, proj_in_full, 1, 1)

    normed_self, centred_self, inv_self = layer_forward(projected, gain_self_full)
    normed_pieces = z_pieces(normed_self)
    text_sum = h_sum(after(text_part, normed_self))
    *normed_pieces, text_sum, cot_q = together(*normed_pieces, text_sum, cot_q)
    normed_self_all = jnp.concatenate(normed_pieces, axis=0)
    qkv = mm(normed_self_all, qkv_full, 1, 0)
    own_kv = qkv[:, wide:]
    kv_pieces = [own_kv] + [flip(own_kv, j) for j in (1, 2, 3)]
    text_sum, grad_here = after((text_sum, grad_after_ff), own_kv)
    side_pieces = z_spread(jnp.concatenate([grad_here, folded(text_sum)], axis=0))
    *kv_pieces, side_pieces = together(*kv_pieces, side_pieces)
    attn_self, totals_self = small(
        attend_kernel,
        marks,
        (qkv, *kv_pieces),
        [(256, wide), (8, 256)],
        [((1024, 256), jnp.float32)],
    )
    self_part = mm(attn_self, out_self_full, 1, 1)
    self_pieces = z_received(rows_of(self_part))
    self_sum = total_of(self_pieces)
    event = self_pieces[1]
    grad_after_ff_all, keys_text, values_text = small(
        text_kernel,
        marks,
        (after(side_pieces, event),),
        [(256, channels), (77, channels), (77, channels)],
    )
    grad_ff_act = mm(grad_after_ff_all, ff_out_full, 1, 0)
    self_sum, grad_ff_act, keys_text, values_text = together(
        self_sum, grad_ff_act, keys_text, values_text
    )
    after_self = projected + self_sum

    normed_cross, centred_cross, inv_cross = layer_forward(after_self, gain_cross_full)
    queries_cross = mm(normed_cross, query_cross_full, 1, 0)
    attn_cross, weights_cross = soft_attend(queries_cross, keys_text, values_text, None, 20)
    after_cross = after_self + mm(attn_cross, out_cross_full, 1, 1)

    normed_ff, centred_ff, inv_ff = layer_forward(after_cross, gain_ff_full)
    normed_ff_all = jnp.concatenate(z_pieces(normed_ff), axis=0)
    hidden_ff = mm(normed_ff_all, ff_in_full, 1, 0)
    value_half, gate_half = hidden_ff[:, :channels], hidden_ff[:, channels:]
    phi = 0.5 * (1.0 + lax.erf(gate_half * math.sqrt(0.5)))
    slope = phi + gate_half * jnp.exp(-0.5 * gate_half * gate_half) * (1.0 / math.sqrt(2 * math.pi))
    gate_act = gate_half * phi
    ff_act = value_half * gate_act
    grad_value = grad_ff_act * gate_act
    grad_gate = grad_ff_act * value_half * slope
    grad_hidden_ff = jnp.concatenate([grad_value, grad_gate], axis=1)
    grad_normed_part = mm(grad_hidden_ff, ff_in_full, 1, 1)
    normed_pieces = z_received(rows_of(grad_normed_part))
    grad_normed_ff = total_of(normed_pieces)
    ff_right = jnp.concatenate(after([grad_hidden_ff, ff_act], normed_pieces[1]), axis=1)
    ff_grads = weight_grads(
        (((0, 1280, 0),), ((0, 1280, 0),), ((0, 1280, 1),)),
        (normed_ff_all, grad_after_ff_all),
        ff_right,
        0,
        5,
    )
    grad_normed_ff, ff_grads = together(grad_normed_ff, ff_grads)

    back_ff, grad_gain_ff = layer_grad(grad_normed_ff, centred_ff, inv_ff, gain_ff_full)
    grad_after_cross = grad_after_ff + back_ff
    grad_attn_cross = mm(grad_after_cross, out_cross_full, 1, 0)
    grad_queries_cross, grad_keys_text, grad_values_text = soft_back(
        queries_cross, keys_text, values_text, 20, weights_cross, attn_cross, grad_attn_cross
    )
    grad_normed_cross = mm(grad_queries_cross, query_cross_full, 1, 1)
    back_cross, grad_gain_cross = layer_grad(
        grad_normed_cross, centred_cross, inv_cross, gain_cross_full
    )
    grad_after_self = grad_after_cross + back_cross
    grad_pieces = z_pieces(grad_after_self)
    cross_right = after((grad_queries_cross, attn_cross), grad_pieces[1])
    cross_right = jnp.concatenate(
        [side[:, wide * k : wide * k + wide] for k in range(4) for side in cross_right], axis=1
    )
    cross_grads = weight_grads(
        (((0, 320, 0), (320, 320, 1), (640, 320, 0), (960, 320, 1)),) * 2,
        (normed_cross, grad_after_cross),
        cross_right,
        3,
        5,
        ff_grads,
    )
    ff_here, grad_keys_text, grad_values_text = after(
        (ff_act, grad_keys_text, grad_values_text), grad_pieces[1]
    )
    out_part = mm(ff_here, ff_out_full, 1, 1)
    (side_grads,) = small(
        text_grad_kernel,
        marks,
        (out_part, grad_keys_text, grad_values_text),
        [(4, 104, channels)],
    )
    *grad_pieces, cross_grads, side_grads = together(*grad_pieces, cross_grads, side_grads)
    side_grads = z_all(side_grads)
    ff_grads = scatter_plane(cross_grads)
    ff_grads, cross_grads = ff_grads[:, :3840], ff_grads[:, 3840:]

    grad_after_self_all = jnp.concatenate(grad_pieces, axis=0)
    grad_attn_self = mm(grad_after_self_all, out_self_full, 1, 0)
    grad_queries, *kv_pieces = small(
        attend_back_kernel,
        marks,
        (qkv, *kv_pieces, totals_self, attn_self, grad_attn_self),
        [(256, wide)] + [(256, 2 * wide)] * 4,
    )
    kv_pieces = kv_pieces[:1] + [flip(kv_pieces[j], j) for j in (1, 2, 3)]
    grad_kv = total_of(kv_pieces)
    grad_qkv = jnp.concatenate([grad_queries, grad_kv], axis=1)
    grad_normed_part = mm(grad_qkv, qkv_full, 1, 1)
    normed_pieces = z_received(rows_of(grad_normed_part))
    grad_normed_self = total_of(normed_pieces)
    grad_normed_self, side_grads = together(grad_normed_self, side_grads)
    back_self, grad_gain_self = layer_grad(grad_normed_self, centred_self, inv_self, gain_self_full)
    grad_projected = grad_after_self + back_self
    grad_norm_three = mm(grad_projected, proj_in_full, 1, 0)

    (grad_three,) = small(pack_kernel, marks, (grad_norm_three,), [(8, 80, 128)])
    grad_three_q = plane_exchange(grad_three)
    side_grads = jnp.sum(after(side_grads, grad_three), axis=0)
    out_sum, text_grads = side_grads[:64], side_grads[64:]
    text_grads = text_grads + flip(text_grads, 1)
    attn_right = jnp.concatenate(
        [
            jnp.concatenate([grad_qkv, attn_self], axis=1),
            jnp.pad(norm_three, ((0, 192), (0, 0))),
        ],
        axis=1,
    )
    attn_grads = weight_grads(
        (((0, 960, 0), (960, 320, 1)), ((0, 1280, 2),)),
        (
            normed_self_all,
            grad_after_self_all,
            jnp.pad(grad_projected, ((0, 192), (0, 0))),
        ),
        after(attn_right, grad_three),
    )
    grad_three_q, attn_grads, text_grads = together(grad_three_q, attn_grads, text_grads)
    attn_grads = scatter_plane(attn_grads)
    gain_block = lax.dynamic_slice_in_dim(gain_attn_full, block * width, width, 1)
    (sums,) = small(
        norm_sums_kernel, marks, (grad_three_q, residual_q, stats_three, gain_block), [(8, width)]
    )
    grad_residual_q, grad_gain_three = small(
        norm_back_kernel,
        marks,
        (grad_three_q, residual_q, stats_three, gain_block, cot_q, *z_pieces(sums)),
        [(8, 80, 128), (8, width)],
    )

    residual_pieces = z_pieces(grad_residual_q)
    text_grads = after(text_grads, grad_residual_q)
    text_grads = text_grads + flip(text_grads, 2)
    *residual_pieces, text_grads = together(*residual_pieces, text_grads)
    own_two, other_two, image_back = second_conv_back(marks, residual_pieces, second_weight)
    own_two = own_two + swap(other_two)
    grad_act_two, part = plane_sum(own_two)
    side = jnp.concatenate(
        [
            jnp.broadcast_to((after_cross + out_sum)[None], (4, 64, channels)),
            jnp.moveaxis(residual_s.reshape(64, 4, wide), 1, 0),
        ],
        axis=2,
    )
    gain_rows = jnp.stack([grad_gain_self, grad_gain_cross, grad_gain_ff])
    gain_rows = jnp.broadcast_to(jnp.pad(gain_rows, ((0, 5), (0, wide)))[None], (4, 8, 1600))
    side = z_all(after(jnp.concatenate([side, gain_rows], axis=1), own_two))
    side_here = after(side, part)
    after_ff_all = side_here[:, :64, :channels].reshape(256, channels)
    residual_all = side_here[:, :64, channels:].reshape(256, wide)
    gain_sums = jnp.sum(side_here[:, 64:67, :channels], axis=0)
    cross_cut = after(cross_grads, part)
    cross_cut = jnp.stack([cross_cut[:, 640 * k : 640 * k + 640] for k in range(4)])
    *grad_act_two, after_ff_all, gain_sums, residual_all, cross_cut = together(
        *grad_act_two, after_ff_all, gain_sums, residual_all, cross_cut
    )
    cross_shares = z_all(cross_cut)

    *grad_act_one, image_grad, grad_tau, grad_gain_mid = first_conv_back(
        marks,
        grad_act_two,
        strips_one,
        gain_mid[None, :],
        stats_two,
        conv_first.reshape(9 * width, wide),
    )
    grad_act_pieces = z_received(grad_act_one)
    image_grad, text_grads = after((image_grad, text_grads), grad_act_pieces[1])
    text_other_grads = swap(text_grads)
    grad_conv_first = conv_weight(marks, image_one, image_grad, 1)
    cross_shares, after_ff_here = after((cross_shares, after_ff_all), grad_act_pieces[1])
    cross_shares = jnp.sum(cross_shares, axis=0)
    grad_proj_out = mm(after_ff_here, cot, 0, 0)
    *grad_act_pieces, grad_conv_first, cross_shares, grad_proj_out, text_other_grads = together(
        *grad_act_pieces, grad_conv_first, cross_shares, grad_proj_out, text_other_grads
    )
    text_grads, text_other_grads = unfolded(text_grads), unfolded(text_other_grads)
    grad_proj_out = grad_proj_out.reshape(2, 4, width, wide)
    grad_proj_own = pick(grad_proj_out, item) + swap(pick(grad_proj_out, 1 - item))
    grad_conv_first = grad_conv_first.reshape(3, 3, width, wide)
    extra = jnp.concatenate(
        [
            jnp.broadcast_to(grad_gain_three[0], (8, 1, width)),
            jnp.moveaxis(gain_sums.reshape(3, 8, width), 1, 0),
        ],
        axis=1,
    )
    extra = jnp.concatenate(
        [extra[:, :, :128], jnp.pad(extra[:, :, 128:], ((0, 0), (0, 0), (0, 96)))], axis=1
    )
    grad_input_q, sums = small(
        input_sums_kernel,
        marks,
        (source, gain_in[None, :], stats_one, *grad_act_pieces),
        [(8, 80, 128), (8, width)],
    )
    moved, grad_gain_in = small(
        input_back_kernel,
        marks,
        (
            grad_input_q,
            source,
            gain_in[None, :],
            stats_one,
            grad_residual_q,
            extra,
            *z_pieces(sums),
        ),
        [(8, 88, 128), (8, width)],
    )
    received = plane_exchange(moved)
    grad_proj_own, image_back = after((grad_proj_own, image_back), moved)
    grad_conv_second = conv_weight(marks, image_back, image_two, -1)
    grad_proj_out = h_collect([pick(grad_proj_own, h ^ j) for j in range(4)])
    received, grad_conv_second, grad_proj_out = together(
        received, grad_conv_second, grad_proj_out
    )
    grad_conv_second = grad_conv_second.reshape(3, 3, width, wide).transpose(0, 1, 3, 2)
    attn_grads = after(attn_grads, received)
    proj_cut = attn_grads[:, 1280:].reshape(width, 4, wide)
    proj_pieces = z_received([pick(proj_cut, lax.rem(t + j, 4), 1) for j in range(4)])
    (grad_hidden,) = small(unpack_kernel, marks, (received,), [(64, channels)])
    hidden_pieces = z_pieces(grad_hidden)
    text_own, text_other, own_features, after_ff_all = after(
        (text_own, text_other, own_features, after_ff_all), hidden_pieces[1]
    )
    output = residual_all + mm(after_ff_all, proj_out_full, 1, 0)
    output = output * own_valid
    grad_text_weight = mm(text_own, text_grads, 0, 0) + mm(text_other, text_other_grads, 0, 0)
    grad_time_weight = mm(own_features, grad_tau, 0, 0)
    (grad_hidden,) = small(rows_kernel, marks, hidden_pieces, [(256, channels)])
    proj_share = total_of(proj_pieces)
    extra = jnp.concatenate([received[:, 80:84, :], received[:, 84:88, :32]], axis=2)
    grad_gain_attn = lax.dynamic_slice_in_dim(extra[:, 0].reshape(channels), t * wide, wide, 0)
    gain_sums = jnp.sum(extra[:, 1:], axis=0)

    return (
        output[None],
        grad_hidden[None],
        grad_gain_in[0],
        grad_conv_first,
        grad_time_weight,
        grad_gain_mid[0],
        grad_conv_second,
        grad_gain_attn,
        proj_share.T,
        gain_sums[0],
        attn_grads[:, :320],
        attn_grads[:, 320:640],
        attn_grads[:, 640:960],
        attn_grads[:, 960:1280].T,
        gain_sums[1],
        cross_shares[:, :320],
        grad_text_weight[:, :wide],
        grad_text_weight[:, wide:],
        cross_shares[:, 320:].T,
        gain_sums[2],
        ff_grads[:, :2560].reshape(width, 2, channels),
        ff_grads[:, 2560:].T,
        grad_proj_out,
    )


def solution(mesh):
    placed = (
        P(I, H, None),
        P(I, None, None),
        P(I),
        P(I),
        P(IH),
        P(None, None, IH, T),
        P(IH, T),
        P(T),
        P(None, None, T, IH),
        P(T),
        P(T, IH),
        P(IH),
        P(IH, T),
        P(IH, T),
        P(IH, T),
        P(T, IH),
        P(IH),
        P(IH, T),
        P(IH, T),
        P(IH, T),
        P(T, IH),
        P(IH),
        P(IH, None, T),
        P(T, IH),
        P(IH, T),
        P(I, H, T),
    )
    sizes = (mesh.shape[I], mesh.shape[H], mesh.shape[T])
    body = fast_shards if sizes == (2, 4, 4) else shards
    return jax.shard_map(
        body,
        mesh=mesh,
        in_specs=placed,
        out_specs=(
            P(I, H, T),
            P(I, H, None),
            P(IH),
            P(None, None, IH, T),
            P(IH, T),
            P(T),
            P(None, None, T, IH),
            P(T),
            P(T, IH),
            P(IH),
            P(IH, T),
            P(IH, T),
            P(IH, T),
            P(T, IH),
            P(IH),
            P(IH, T),
            P(IH, T),
            P(IH, T),
            P(T, IH),
            P(IH),
            P(IH, None, T),
            P(T, IH),
            P(IH, T),
        ),
        check_vma=False,
    )
```

```python
import functools
import math

import jax
import jax.numpy as jnp
from jax import lax
from jax.experimental import pallas as pl
from jax.experimental.pallas import tpu as pltpu
from jax.sharding import PartitionSpec as P

HEAD_DIM = 64
GROUPS = 32
EDGE = 48


highest = lax.Precision.HIGHEST
norm_eps = 1e-05
masked_score = -1e30
edge_margin = 56
high = lax.Precision.HIGH
margin = 64
I, H, T = "items", "height", "tensor"
IH = (I, H)
E0 = "bc,bn->cn"
E1 = "bhqk,bkhd->bqhd"
E2 = "bhqk,bqhd->bkhd"
E3 = "bqhd,bkhd->bhqk"
E4 = "bqhd,bqhd->bhq"
E5 = "bsc,bsjf->cjf"
E6 = "bsc,cjf->bsjf"
E7 = "bsjf,cjf->bsc"
E8 = "bsk,bsn->kn"
E9 = "bsk,kn->bsn"
E10 = "bsn,kn->bsk"
QK, PV, PQ = "qhd,khd->hqk", "hqk,khd->qhd", "hqk,qhd->khd"


def padded_2(block, sides, width):
    for axis, dim in sides:
        count = lax.axis_size(axis)
        forward = [(i, i + 1) for i in range(count - 1)]
        backward = [(target, source) for source, target in forward]
        low = lax.ppermute(
            lax.slice_in_dim(block, block.shape[dim] - width, None, axis=dim), axis, forward
        )
        high = lax.ppermute(lax.slice_in_dim(block, 0, width, axis=dim), axis, backward)
        block = jnp.concatenate([low, block, high], axis=dim)
    return block


def grid_shape(bucket):
    strip_rows = jnp.where(bucket == 0, 8, jnp.where(bucket == 1, 6, 5)).astype(jnp.int32)
    strip_width = jnp.where(bucket == 0, 32, jnp.where(bucket == 1, 40, 48)).astype(jnp.int32)
    return (strip_rows, strip_width)


def tokens_dot(values, weight):
    return jnp.einsum(E9, values, weight, precision=highest)


def tokens_back(grad_values, weight):
    return jnp.einsum(E10, grad_values, weight, precision=highest)


def tokens_grad(values, grad_values):
    return jnp.einsum(E8, values, grad_values, precision=highest)


def tensor_sum(values):
    return lax.psum(values, T)


def expand_groups(stat, size_group):
    return jnp.repeat(stat, size_group, axis=1)[:, None, :]


def group_stats(values, valid_col, group_count, counts):
    item_count, slot_count, channels = values.shape
    size_group = channels // group_count
    grouped = (values * valid_col).reshape(item_count, slot_count, group_count, size_group)
    sum_values = jnp.sum(grouped, axis=(1, 3))
    sum_squares = jnp.sum(grouped * grouped, axis=(1, 3))
    sum_values, sum_squares = lax.psum((sum_values, sum_squares), H)
    mean_val = sum_values / counts[:, None]
    var_val = sum_squares / counts[:, None] - mean_val * mean_val
    return (
        expand_groups(mean_val, size_group),
        expand_groups(lax.rsqrt(var_val + norm_eps), size_group),
    )


def group_back(grad_out, centred, inv_std, gain_vector, valid_col, group_count, counts):
    item_count, slot_count, channels = grad_out.shape
    size_group = channels // group_count
    scaled = grad_out * gain_vector * valid_col
    sum_first = jnp.sum(
        scaled.reshape(item_count, slot_count, group_count, size_group), axis=(1, 3)
    )
    sum_second = jnp.sum(
        (scaled * centred).reshape(item_count, slot_count, group_count, size_group), axis=(1, 3)
    )
    sum_first, sum_second = lax.psum((sum_first, sum_second), H)
    mean_first = expand_groups(sum_first / counts[:, None], size_group)
    mean_second = expand_groups(sum_second / counts[:, None], size_group)
    grad_in = inv_std * (scaled - mean_first - centred * mean_second) * valid_col
    return (grad_in, jnp.sum(grad_out * centred, axis=(0, 1)))


def layer_norm(values, gain_vector):
    mean_val = jnp.mean(values, axis=-1, keepdims=True)
    var_val = jnp.mean(values * values, axis=-1, keepdims=True) - mean_val * mean_val
    inv_std = lax.rsqrt(var_val + norm_eps)
    centred = (values - mean_val) * inv_std
    return (centred * gain_vector, centred, inv_std)


def layer_back(grad_out, centred, inv_std, gain_vector):
    scaled = grad_out * gain_vector
    grad_in = inv_std * (
        scaled
        - jnp.mean(scaled, axis=-1, keepdims=True)
        - centred * jnp.mean(scaled * centred, axis=-1, keepdims=True)
    )
    return (grad_in, jnp.sum(grad_out * centred, axis=(0, 1)))


def edge_rows(values, strip_rows, strip_width):
    item_count, slot_count, channels = values.shape
    position = jnp.arange(EDGE, dtype=jnp.int32)

    def edge_one_item(item_vals, rows_here, width_here):
        keep_mask = (position < width_here)[:, None].astype(jnp.float32)
        padded = jnp.concatenate([item_vals, jnp.zeros((EDGE, channels), jnp.float32)], axis=0)
        top_row = item_vals[:EDGE] * keep_mask
        bottom_row = (
            lax.dynamic_slice_in_dim(padded, (rows_here - 1) * width_here, EDGE, 0) * keep_mask
        )
        return jnp.stack([top_row, bottom_row])

    return jax.vmap(edge_one_item)(values, strip_rows, strip_width)


def neighbour_stack(values, strip_rows, strip_width):
    edge_pair = edge_rows(values, strip_rows, strip_width)
    beside_all = padded_2(edge_pair, ((H, 1),), 1)
    item_count, slot_count, channels = values.shape
    position = jnp.arange(slot_count, dtype=jnp.int32)

    def neighbour_one_item(item_vals, item_around, rows_here, width_here):
        cell_span = rows_here * width_here
        extended = jnp.zeros((2 * edge_margin + slot_count, channels), jnp.float32)
        extended = lax.dynamic_update_slice_in_dim(
            extended, item_around[0], edge_margin - width_here, 0
        )
        extended = lax.dynamic_update_slice_in_dim(extended, item_vals, edge_margin, 0)
        extended = lax.dynamic_update_slice_in_dim(
            extended, item_around[3], edge_margin + cell_span, 0
        )
        column = position % width_here
        shifted_list = []
        for row_step in (-1, 0, 1):
            for col_step in (-1, 0, 1):
                shifted = lax.dynamic_slice_in_dim(
                    extended, edge_margin + row_step * width_here + col_step, slot_count, 0
                )
                keep_mask = (
                    (column + col_step >= 0)
                    & (column + col_step < width_here)
                    & (position < cell_span)
                )
                shifted_list.append(shifted * keep_mask[:, None].astype(jnp.float32))
        return jnp.stack(shifted_list, axis=1)

    return jax.vmap(neighbour_one_item)(values, beside_all, strip_rows, strip_width)


def conv_apply(neighbours, weight):
    item_count, slot_count = (neighbours.shape[0], neighbours.shape[1])
    flattened = neighbours.reshape(item_count, slot_count, -1)
    return tokens_dot(flattened, weight.reshape(-1, weight.shape[3]))


def conv_input_grad(neighbours_grad, weight):
    flipped = jnp.transpose(weight[::-1, ::-1], (0, 1, 3, 2))
    return conv_apply(neighbours_grad, flipped)


def conv_weight_grad(neighbours, grad_out, weight_shape):
    flattened = neighbours.reshape(neighbours.shape[0], neighbours.shape[1], -1)
    return tokens_grad(flattened, grad_out).reshape(weight_shape)


def time_features(timestep, channels):
    half_width = channels // 2
    frequency = jnp.exp(-math.log(10000.0) * jnp.arange(half_width, dtype=jnp.float32) / half_width)
    angles = timestep.astype(jnp.float32)[:, None] * frequency[None, :]
    return jnp.concatenate([jnp.cos(angles), jnp.sin(angles)], axis=1)


def exact_gelu(values):
    return jax.nn.gelu(values, approximate=False)


def head_split(values, heads_here):
    return values.reshape(
        values.shape[0], values.shape[1], heads_here, values.shape[2] // heads_here
    )


def score_block(queries, keys_all, key_valid, heads_here):
    head_size = queries.shape[2] // heads_here
    scores = jnp.einsum(
        E3,
        head_split(queries, heads_here),
        head_split(keys_all, heads_here),
        precision=highest,
    ) * (1.0 / math.sqrt(head_size))
    return jnp.where(key_valid[:, None, None, :], scores, masked_score)


def attend(queries, keys_all, values_all, key_valid, heads_here):
    scores = score_block(queries, keys_all, key_valid, heads_here)
    row_peak = jnp.max(scores, axis=-1, keepdims=True)
    exponent = jnp.exp(scores - row_peak)
    row_total = jnp.sum(exponent, axis=-1, keepdims=True)
    soft_weights = exponent / row_total
    attended = jnp.einsum(
        E1, soft_weights, head_split(values_all, heads_here), precision=highest
    )
    return (attended.reshape(queries.shape), row_peak + jnp.log(row_total))


def attend_back(
    queries, keys_all, values_all, key_valid, heads_here, attended, log_total, grad_attended
):
    head_size = queries.shape[2] // heads_here
    scaling = 1.0 / math.sqrt(head_size)
    soft_weights = jnp.exp(score_block(queries, keys_all, key_valid, heads_here) - log_total)
    grad_heads = head_split(grad_attended, heads_here)
    grad_soft = jnp.einsum(
        E3, grad_heads, head_split(values_all, heads_here), precision=highest
    )
    row_delta = jnp.einsum(
        E4, grad_heads, head_split(attended, heads_here), precision=highest
    )
    grad_scores = soft_weights * (grad_soft - row_delta[..., None])
    grad_query = (
        jnp.einsum(
            E1, grad_scores, head_split(keys_all, heads_here), precision=highest
        )
        * scaling
    )
    grad_key = (
        jnp.einsum(
            E2, grad_scores, head_split(queries, heads_here), precision=highest
        )
        * scaling
    )
    grad_value = jnp.einsum(E2, soft_weights, grad_heads, precision=highest)
    return (
        grad_query.reshape(queries.shape),
        grad_key.reshape(keys_all.shape),
        grad_value.reshape(values_all.shape),
    )


def shards(
    hidden,
    text_states,
    bucket,
    timestep,
    gain_in,
    conv_first,
    time_weight,
    gain_mid,
    conv_second,
    gain_attn_norm,
    proj_in,
    gain_self,
    query_self,
    key_self,
    value_self,
    out_self,
    gain_cross,
    query_cross,
    key_cross,
    value_cross,
    out_cross,
    gain_ff,
    ff_in,
    ff_out,
    proj_out,
    cotangent,
):
    item_count, slot_count, channels = hidden.shape
    local_width = gain_mid.shape[0]
    local_groups = GROUPS * local_width // channels
    heads_here = local_width // HEAD_DIM
    height_count = lax.axis_size(H)
    width_ih = lax.axis_size(I) * lax.axis_size(H)
    offset = lax.axis_index(T) * local_width
    strip_rows, strip_width = grid_shape(bucket)
    cell_span = strip_rows * strip_width
    position = jnp.arange(slot_count, dtype=jnp.int32)
    valid_mask = position[None, :] < cell_span[:, None]
    valid_col = valid_mask[:, :, None].astype(jnp.float32)
    full_counts = (height_count * cell_span * (channels // GROUPS)).astype(jnp.float32)
    key_valid = jnp.tile(valid_mask, (1, height_count))
    text_valid = jnp.ones((item_count, text_states.shape[1]), dtype=bool)
    resnet_full = (
        lax.all_gather(gain_in, IH, axis=0, tiled=True),
        lax.all_gather(conv_first, IH, axis=2, tiled=True),
        lax.all_gather(time_weight, IH, axis=0, tiled=True),
        lax.all_gather(conv_second, IH, axis=3, tiled=True),
    )
    block_full = (
        lax.all_gather(proj_in, IH, axis=1, tiled=True),
        lax.all_gather(gain_self, IH, axis=0, tiled=True),
        lax.all_gather(query_self, IH, axis=0, tiled=True),
        lax.all_gather(key_self, IH, axis=0, tiled=True),
        lax.all_gather(value_self, IH, axis=0, tiled=True),
        lax.all_gather(out_self, IH, axis=1, tiled=True),
        lax.all_gather(gain_cross, IH, axis=0, tiled=True),
        lax.all_gather(query_cross, IH, axis=0, tiled=True),
        lax.all_gather(key_cross, IH, axis=0, tiled=True),
        lax.all_gather(value_cross, IH, axis=0, tiled=True),
        lax.all_gather(out_cross, IH, axis=1, tiled=True),
        lax.all_gather(gain_ff, IH, axis=0, tiled=True),
        lax.all_gather(ff_in, IH, axis=0, tiled=True),
        lax.all_gather(ff_out, IH, axis=1, tiled=True),
        lax.all_gather(proj_out, IH, axis=0, tiled=True),
    )
    gain_in_full, conv_first_full, time_full, conv_second_full = resnet_full
    (
        proj_in_full,
        gain_self_full,
        query_self_full,
        key_self_full,
        value_self_full,
        out_self_full,
        gain_cross_full,
        query_cross_full,
        key_cross_full,
        value_cross_full,
        out_cross_full,
        gain_ff_full,
        ff_in_full,
        ff_out_full,
        proj_out_full,
    ) = block_full
    source = hidden * valid_col
    mean_one, inv_one = group_stats(source, valid_col, GROUPS, full_counts)
    centred_one = (source - mean_one) * inv_one * valid_col
    norm_one = centred_one * gain_in_full
    act_one, silu_pull_one = jax.vjp(jax.nn.silu, norm_one)
    stack_one = neighbour_stack(act_one, strip_rows, strip_width)
    silu_features = jax.nn.silu(time_features(timestep, channels))
    time_term = jnp.dot(
        silu_features, time_full, precision=highest, preferred_element_type=jnp.float32
    )
    conv_one = (conv_apply(stack_one, conv_first_full) + time_term[:, None, :]) * valid_col
    mean_two, inv_two = group_stats(conv_one, valid_col, local_groups, full_counts)
    centred_two = (conv_one - mean_two) * inv_two * valid_col
    norm_two = centred_two * gain_mid
    act_two, silu_pull_two = jax.vjp(jax.nn.silu, norm_two)
    stack_two = neighbour_stack(act_two, strip_rows, strip_width)
    conv_two = tensor_sum(conv_apply(stack_two, conv_second_full)) * valid_col
    residual = source + conv_two
    residual_local = lax.dynamic_slice_in_dim(residual, offset, local_width, 2)
    mean_three, inv_three = group_stats(residual_local, valid_col, local_groups, full_counts)
    centred_three = (residual_local - mean_three) * inv_three * valid_col
    norm_three = centred_three * gain_attn_norm
    projected = tensor_sum(tokens_dot(norm_three, proj_in_full))
    normed_self, centred_self, inv_self = layer_norm(projected, gain_self_full)
    queries = tokens_dot(normed_self, query_self_full)
    keys_here = tokens_dot(normed_self, key_self_full)
    values_here = tokens_dot(normed_self, value_self_full)
    keys_all, values_all = (
        lax.all_gather(keys_here, H, axis=1, tiled=True),
        lax.all_gather(values_here, H, axis=1, tiled=True),
    )
    attn_self, total_self = attend(queries, keys_all, values_all, key_valid, heads_here)
    after_self = projected + tensor_sum(tokens_dot(attn_self, out_self_full))
    normed_cross, centred_cross, inv_cross = layer_norm(after_self, gain_cross_full)
    queries_cross = tokens_dot(normed_cross, query_cross_full)
    keys_text = tokens_dot(text_states, key_cross_full)
    values_text = tokens_dot(text_states, value_cross_full)
    attn_cross, total_cross = attend(queries_cross, keys_text, values_text, text_valid, heads_here)
    after_cross = after_self + tensor_sum(tokens_dot(attn_cross, out_cross_full))
    normed_ff, centred_ff, inv_ff = layer_norm(after_cross, gain_ff_full)
    hidden_ff = jnp.einsum(E6, normed_ff, ff_in_full, precision=highest)
    value_half = hidden_ff[:, :, 0]
    gate_act, gelu_pull = jax.vjp(exact_gelu, hidden_ff[:, :, 1])
    ff_act = value_half * gate_act
    after_ff = after_cross + tensor_sum(tokens_dot(ff_act, ff_out_full))
    output = (residual_local + tokens_dot(after_ff, proj_out_full)) * valid_col
    (
        proj_in_back,
        gain_self_back,
        query_self_back,
        key_self_back,
        value_self_back,
        out_self_back,
        gain_cross_back,
        query_cross_back,
        key_cross_back,
        value_cross_back,
        out_cross_back,
        gain_ff_back,
        ff_in_back,
        ff_out_back,
        proj_out_back,
    ) = block_full
    grad_local = cotangent * valid_col
    grad_proj_out = tokens_grad(after_ff, grad_local)
    grad_after_ff = tensor_sum(tokens_back(grad_local, proj_out_back))
    grad_ff_out = tokens_grad(ff_act, grad_after_ff)
    grad_ff_act = tokens_back(grad_after_ff, ff_out_back)
    grad_value_half = grad_ff_act * gate_act
    grad_gate_half = gelu_pull(grad_ff_act * value_half)[0]
    grad_hidden_ff = jnp.stack([grad_value_half, grad_gate_half], axis=2)
    grad_ff_in = jnp.einsum(E5, normed_ff, grad_hidden_ff, precision=highest)
    grad_normed_ff = tensor_sum(
        jnp.einsum(E7, grad_hidden_ff, ff_in_back, precision=highest)
    )
    back_ff, grad_gain_ff = layer_back(grad_normed_ff, centred_ff, inv_ff, gain_ff_back)
    grad_after_cross = grad_after_ff + back_ff
    grad_out_cross = tokens_grad(attn_cross, grad_after_cross)
    grad_attn_cross = tokens_back(grad_after_cross, out_cross_back)
    grad_queries_cross, grad_keys_text, grad_values_text = attend_back(
        queries_cross,
        keys_text,
        values_text,
        text_valid,
        heads_here,
        attn_cross,
        total_cross,
        grad_attn_cross,
    )
    grad_query_cross = tokens_grad(normed_cross, grad_queries_cross)
    grad_key_cross = tokens_grad(text_states, grad_keys_text)
    grad_value_cross = tokens_grad(text_states, grad_values_text)
    grad_normed_cross = tensor_sum(tokens_back(grad_queries_cross, query_cross_back))
    back_cross, grad_gain_cross = layer_back(
        grad_normed_cross, centred_cross, inv_cross, gain_cross_back
    )
    grad_after_self = grad_after_cross + back_cross
    grad_out_self = tokens_grad(attn_self, grad_after_self)
    grad_attn_self = tokens_back(grad_after_self, out_self_back)
    grad_queries, grad_keys_all, grad_values_all = attend_back(
        queries, keys_all, values_all, key_valid, heads_here, attn_self, total_self, grad_attn_self
    )
    grad_keys_here, grad_values_here = (
        lax.psum_scatter(grad_keys_all, H, scatter_dimension=1, tiled=True),
        lax.psum_scatter(grad_values_all, H, scatter_dimension=1, tiled=True),
    )
    grad_query_self = tokens_grad(normed_self, grad_queries)
    grad_key_self = tokens_grad(normed_self, grad_keys_here)
    grad_value_self = tokens_grad(normed_self, grad_values_here)
    grad_normed_self = tensor_sum(
        tokens_back(grad_queries, query_self_back)
        + tokens_back(grad_keys_here, key_self_back)
        + tokens_back(grad_values_here, value_self_back)
    )
    back_self, grad_gain_self = layer_back(grad_normed_self, centred_self, inv_self, gain_self_back)
    grad_projected = grad_after_self + back_self
    grad_proj_in = tokens_grad(norm_three, grad_projected)
    grad_norm_three = tokens_back(grad_projected, proj_in_back)
    back_three, grad_gain_attn = group_back(
        grad_norm_three,
        centred_three,
        inv_three,
        gain_attn_norm,
        valid_col,
        local_groups,
        full_counts,
    )
    grad_residual_local = grad_local + back_three
    block_grads = (
        lax.psum_scatter(grad_proj_in, IH, scatter_dimension=1, tiled=True),
        lax.psum_scatter(
            jnp.tile(grad_gain_attn, width_ih), IH, scatter_dimension=0, tiled=True
        ),
        lax.psum_scatter(grad_gain_self, IH, scatter_dimension=0, tiled=True),
        lax.psum_scatter(grad_query_self, IH, scatter_dimension=0, tiled=True),
        lax.psum_scatter(grad_key_self, IH, scatter_dimension=0, tiled=True),
        lax.psum_scatter(grad_value_self, IH, scatter_dimension=0, tiled=True),
        lax.psum_scatter(grad_out_self, IH, scatter_dimension=1, tiled=True),
        lax.psum_scatter(grad_gain_cross, IH, scatter_dimension=0, tiled=True),
        lax.psum_scatter(grad_query_cross, IH, scatter_dimension=0, tiled=True),
        lax.psum_scatter(grad_key_cross, IH, scatter_dimension=0, tiled=True),
        lax.psum_scatter(grad_value_cross, IH, scatter_dimension=0, tiled=True),
        lax.psum_scatter(grad_out_cross, IH, scatter_dimension=1, tiled=True),
        lax.psum_scatter(grad_gain_ff, IH, scatter_dimension=0, tiled=True),
        lax.psum_scatter(grad_ff_in, IH, scatter_dimension=0, tiled=True),
        lax.psum_scatter(grad_ff_out, IH, scatter_dimension=1, tiled=True),
        lax.psum_scatter(grad_proj_out, IH, scatter_dimension=0, tiled=True),
    )
    gain_in_back, conv_first_back, time_back, conv_second_back = resnet_full
    grad_residual = lax.all_gather(grad_residual_local, T, axis=2, tiled=True)
    grad_conv_second = conv_weight_grad(stack_two, grad_residual, conv_second_back.shape)
    stack_grad_two = neighbour_stack(grad_residual, strip_rows, strip_width)
    grad_act_two = conv_input_grad(stack_grad_two, conv_second_back)
    grad_norm_two = silu_pull_two(grad_act_two)[0]
    grad_conv_one, grad_gain_mid = group_back(
        grad_norm_two, centred_two, inv_two, gain_mid, valid_col, local_groups, full_counts
    )
    grad_time_term = jnp.sum(grad_conv_one, axis=1)
    grad_time_weight = jnp.einsum(E0, silu_features, grad_time_term, precision=highest)
    grad_conv_first = conv_weight_grad(stack_one, grad_conv_one, conv_first_back.shape)
    stack_grad_one = neighbour_stack(grad_conv_one, strip_rows, strip_width)
    grad_act_one = tensor_sum(conv_input_grad(stack_grad_one, conv_first_back))
    grad_norm_one = silu_pull_one(grad_act_one)[0]
    back_one, grad_gain_in = group_back(
        grad_norm_one, centred_one, inv_one, gain_in_back, valid_col, GROUPS, full_counts
    )
    grad_hidden = (grad_residual + back_one) * valid_col
    resnet_grads = (
        lax.psum_scatter(grad_gain_in, IH, scatter_dimension=0, tiled=True),
        lax.psum_scatter(grad_conv_first, IH, scatter_dimension=2, tiled=True),
        lax.psum_scatter(grad_time_weight, IH, scatter_dimension=0, tiled=True),
        lax.psum_scatter(
            jnp.tile(grad_gain_mid, width_ih), IH, scatter_dimension=0, tiled=True
        ),
        lax.psum_scatter(grad_conv_second, IH, scatter_dimension=3, tiled=True),
    )
    return (
        output,
        grad_hidden,
        resnet_grads[0],
        resnet_grads[1],
        resnet_grads[2],
        resnet_grads[3],
        resnet_grads[4],
        block_grads[1],
        block_grads[0],
        block_grads[2],
        block_grads[3],
        block_grads[4],
        block_grads[5],
        block_grads[6],
        block_grads[7],
        block_grads[8],
        block_grads[9],
        block_grads[10],
        block_grads[11],
        block_grads[12],
        block_grads[13],
        block_grads[14],
        block_grads[15],
    )


def mm(left, right, left_dim, right_dim):
    return lax.dot_general(
        left,
        right,
        (((left_dim,), (right_dim,)), ((), ())),
        precision=high,
        preferred_element_type=jnp.float32,
    )


def swap(values):
    return lax.ppermute(values, I, [(0, 1), (1, 0)])


def flip(values, step):
    return lax.ppermute(values, H, [(s, s ^ step) for s in range(4)])


def turn(values, step):
    return lax.ppermute(values, T, [(s, (s + step) % 4) for s in range(4)])


def z_pieces(values):
    return [values] + [turn(values, 4 - j) for j in (1, 2, 3)]


def total_of(pieces):
    return (pieces[0] + pieces[1]) + (pieces[2] + pieces[3])


def z_received(pieces):
    return [pieces[0]] + [turn(pieces[j], j) for j in (1, 2, 3)]


def z_all(values):
    return lax.all_to_all(values, T, 0, 0)


def z_spread(values):
    return z_all(jnp.broadcast_to(values[None], (4,) + values.shape))


def folded(values):
    values = jnp.pad(values, ((0, 3), (0, 0)))
    return jnp.concatenate([values[:40], values[40:]], axis=1)


def unfolded(values):
    return jnp.concatenate([values[:, :640], values[:37, 640:]], axis=0)


def h_collect(pieces):
    total = pieces[0]
    for j in (1, 2, 3):
        total = total + flip(pieces[j], j)
    return total


def h_sum(values):
    pair = values + flip(values, 1)
    return pair + flip(pair, 2)


def pick(values, index, axis=0):
    return lax.dynamic_index_in_dim(values, index, axis, keepdims=False)


def plane_sum(own):
    part = h_collect([own[j] for j in range(4)])
    pieces = [part] + [flip(part, j) for j in (1, 2, 3)]
    return pieces + [swap(piece) for piece in pieces], part


def plane_exchange(packed):
    return lax.all_to_all(packed, IH, 0, 0)


IMAGE_ROWS = 1152
TAP_ROWS = range(16, 1136, 160)


def halves(values):
    top = values.astype(jnp.bfloat16)
    return top, (values - top.astype(jnp.float32)).astype(jnp.bfloat16)


def dot_halves(left, right, left_dim, right_dim):
    def one(a, b):
        return lax.dot_general(
            a, b, (((left_dim,), (right_dim,)), ((), ())), preferred_element_type=jnp.float32
        )

    return one(left[0], right[0]) + (one(left[0], right[1]) + one(left[1], right[0]))


def marks_of(marks, b):
    return marks[2 * b], marks[2 * b + 1]


def row_mask(span, rows, columns):
    return (lax.broadcasted_iota(jnp.int32, (rows, columns), 0) < span).astype(jnp.float32)


def unpack_quarter(packed):
    rest = jnp.concatenate([packed[64:80, 32 * g : 32 * g + 32] for g in range(4)], axis=0)
    return jnp.concatenate([packed[:64], rest], axis=1)


def put_quarter(out, place, values, row=0):
    out[place, row : row + 64, :] = values[:, :128]
    for g in range(4):
        out[place, row + 64 : row + 80, 32 * g : 32 * g + 32] = values[
            16 * g : 16 * g + 16, 128:160
        ]


def unpack_strip(packed):
    rest = jnp.concatenate([packed[256:320, 64 * g : 64 * g + 64] for g in range(4)], axis=0)
    return jnp.concatenate([packed[:256], rest], axis=1)


def put_packed_strip(out, place, values):
    out[place, 0:256, :] = values[:, :256]
    for g in range(4):
        out[place, 256:320, 64 * g : 64 * g + 64] = values[64 * g : 64 * g + 64, 256:320]


def put_strip(image, b, strip, span, values):
    at = pl.multiple_of(margin + strip * span, 8)
    image[b, pl.ds(at, 240)] = values[:240]

    @pl.when(span == 256)
    def _():
        image[b, pl.ds(pl.multiple_of(at + 240, 8), 16)] = values[240:]


def put_cells(image, b, strip, span, q, values):
    at = pl.multiple_of(margin + strip * span + q * 64, 8)
    image[b, pl.ds(at, 48)] = values[:48]

    @pl.when((q < 3) | (span == 256))
    def _():
        image[b, pl.ds(pl.multiple_of(at + 48, 8), 16)] = values[48:]


def quarter_mask(span, q):
    row = lax.broadcasted_iota(jnp.int32, (64, 160), 0) + q * 64
    return (row < span).astype(jnp.float32)


def widen(wide, image, b, width, sign):
    channels = image.shape[2]
    width_f = width.astype(jnp.float32)
    for base in TAP_ROWS:
        row = lax.broadcasted_iota(jnp.int32, (160, channels), 0).astype(jnp.float32)
        cell = row + float(base - margin)
        column = cell - width_f * jnp.floor((cell + 0.5) / width_f)
        for j in range(3):
            step = sign * (j - 1)
            values = image[b, base + step : base + step + 160, :]
            if step < 0:
                values = jnp.where(column > 0.5, values, 0.0)
            if step > 0:
                values = jnp.where(column < width_f - 1.5, values, 0.0)
            wide[base : base + 160, j * channels : (j + 1) * channels] = values


def split_weight(weight, top, low):
    for k in range(3):
        rows = weight.shape[0] // 3
        first, second = halves(weight[k * rows : (k + 1) * rows, :])
        top[k * rows : (k + 1) * rows, :] = first
        low[k * rows : (k + 1) * rows, :] = second


def split_weight_turned(weight, top, low):
    for tap in range(9):
        first, second = halves(weight[160 * tap : 160 * tap + 160, :].T)
        top[320 * tap : 320 * tap + 320, :] = first
        low[320 * tap : 320 * tap + 320, :] = second


def conv_strip(wide, top, low, strip, span, width, sign):
    rows = top.shape[0] // 3
    total = None
    for i in range(3):
        at = pl.multiple_of(margin + strip * span + sign * (i - 1) * width, 8)
        taps = halves(wide[pl.ds(at, 256), :])
        part = dot_halves(
            taps, (top[i * rows : (i + 1) * rows, :], low[i * rows : (i + 1) * rows, :]), 1, 0
        )
        total = part if total is None else total + part
    return total * row_mask(span, 256, total.shape[1])


def group_rows(sums):
    channels = sums.shape[1]
    lane = lax.broadcasted_iota(jnp.int32, (1, channels), 1)
    result = jnp.zeros((1, channels), jnp.float32)
    for g in range(channels // 40):
        inside = (lane >= 40 * g) & (lane < 40 * g + 40)
        result = jnp.where(inside, jnp.sum(jnp.where(inside, sums, 0.0)), result)
    return result


def group_row_stats(total, squares, span):
    count = (span * 160).astype(jnp.float32)
    mean = group_rows(total) / count
    var = group_rows(squares) / count - mean * mean
    return mean, lax.rsqrt(var + norm_eps)


def column_sum(values):
    return jnp.sum(values, axis=0, keepdims=True)


def first_kernel(
    marks, source, gain, tau, weight, own, other, image, stats, wide, top, low, cells
):
    item, h = marks[4], marks[5]
    split_weight(weight, top, low)
    image[...] = jnp.zeros_like(image)
    for b, out in ((0, own), (1, other)):
        span, width = marks_of(marks, b)
        base = (item ^ b) * 4
        total = jnp.zeros((1, 160), jnp.float32)
        squares = jnp.zeros((1, 160), jnp.float32)
        for k in range(4):
            for q in range(4):
                values = unpack_quarter(source[base + k, 80 * q : 80 * q + 80, :])
                cells[k, 64 * q : 64 * q + 64, :] = values
                total = total + column_sum(values)
                squares = squares + column_sum(values * values)
        mean, inv = group_row_stats(total, squares, span)
        stats[b, 0:1, :] = mean
        stats[b, 1:2, :] = inv
        for k in range(4):
            norm = (cells[k] - mean) * inv * row_mask(span, 256, 160) * gain[...]
            put_strip(image, b, k, span, norm * jax.nn.sigmoid(norm))
        widen(wide, image, b, width, 1)
        added = tau[b : b + 1, :]

        def step(k, _):
            conv = conv_strip(wide, top, low, k, span, width, 1)
            put_packed_strip(out, k ^ h, conv + added * row_mask(span, 256, 320))
            return 0

        lax.fori_loop(0, 4, step, 0)


def put_quarters(outs, tile, place, t):
    for j in range(4):
        at = pl.multiple_of(lax.rem(t + j, 4) * 64, 8)
        put_quarter(outs[j], place, tile[pl.ds(at, 64), :])


def second_kernel(marks, *refs):
    strips, gain, weight = refs[:8], refs[8], refs[9]
    outs, image, stats = refs[10:14], refs[14], refs[15]
    wide, top, low, tile = refs[16:]
    item, h, t = marks[4], marks[5], marks[6]
    split_weight_turned(weight, top, low)
    image[...] = jnp.zeros_like(image)
    for b in range(2):
        span, width = marks_of(marks, b)
        total = jnp.zeros((1, 320), jnp.float32)
        squares = jnp.zeros((1, 320), jnp.float32)
        for j in range(4):
            values = unpack_strip(strips[4 * b + j][...])
            total = total + column_sum(values)
            squares = squares + column_sum(values * values)
        mean, inv = group_row_stats(total, squares, span)
        stats[b, 0:1, :] = mean
        stats[b, 1:2, :] = inv
        for j in range(4):
            values = unpack_strip(strips[4 * b + j][...])
            norm = (values - mean) * inv * row_mask(span, 256, 320) * gain[...]
            put_strip(image, b, h ^ j, span, norm * jax.nn.sigmoid(norm))
        widen(wide, image, b, width, 1)

        def step(k, _):
            tile[...] = conv_strip(wide, top, low, k, span, width, 1)
            put_quarters(outs, tile, (item ^ b) * 4 + k, t)
            return 0

        lax.fori_loop(0, 4, step, 0)


def second_back_kernel(marks, *refs):
    quarters, weight = refs[:4], refs[4]
    own, other, image = refs[5:8]
    wide, top, low = refs[8:]
    item, h, t = marks[4], marks[5], marks[6]
    split_weight(weight, top, low)
    image[...] = jnp.zeros_like(image)
    for b, out in ((0, own), (1, other)):
        span, width = marks_of(marks, b)

        def fill(k, _):
            for j in range(4):
                values = unpack_quarter(quarters[j][(item ^ b) * 4 + k])
                put_cells(image, b, k, span, lax.rem(t + j, 4), values)
            return 0

        lax.fori_loop(0, 4, fill, 0)
        widen(wide, image, b, width, -1)

        def step(k, _):
            put_packed_strip(out, k ^ h, conv_strip(wide, top, low, k, span, width, -1))
            return 0

        lax.fori_loop(0, 4, step, 0)


def first_back_kernel(marks, *refs):
    grads, strips, gain, stats, weight = refs[:8], refs[8:16], refs[16], refs[17], refs[18]
    outs, image, sums, grad_gain = refs[19:23], refs[23], refs[24], refs[25]
    wide, top, low, tile, scaled_at, centred_at = refs[26:]
    item, h, t = marks[4], marks[5], marks[6]
    split_weight_turned(weight, top, low)
    image[...] = jnp.zeros_like(image)
    gain_total = jnp.zeros((1, 320), jnp.float32)
    for b in range(2):
        span, width = marks_of(marks, b)
        mean, inv = stats[b, 0:1, :], stats[b, 1:2, :]
        first = jnp.zeros((1, 320), jnp.float32)
        second = jnp.zeros((1, 320), jnp.float32)
        for j in range(4):
            values = unpack_strip(strips[4 * b + j][...])
            centred = (values - mean) * inv * row_mask(span, 256, 320)
            norm = centred * gain[...]
            gate = jax.nn.sigmoid(norm)
            grad_norm = unpack_strip(grads[4 * b + j][...]) * gate * (1.0 + norm * (1.0 - gate))
            scaled = grad_norm * gain[...]
            first = first + column_sum(scaled)
            second = second + column_sum(scaled * centred)
            gain_total = gain_total + column_sum(grad_norm * centred)
            scaled_at[j] = scaled
            centred_at[j] = centred
        count = (span * 160).astype(jnp.float32)
        first = group_rows(first) / count
        second = group_rows(second) / count
        tau_total = jnp.zeros((1, 320), jnp.float32)
        for j in range(4):
            grad = inv * row_mask(span, 256, 320) * (
                scaled_at[j] - first - centred_at[j] * second
            )
            tau_total = tau_total + column_sum(grad)
            put_strip(image, b, h ^ j, span, grad)
        sums[b : b + 1, :] = tau_total
        widen(wide, image, b, width, -1)

        def step(k, _):
            tile[...] = conv_strip(wide, top, low, k, span, width, -1)
            put_quarters(outs, tile, (item ^ b) * 4 + k, t)
            return 0

        lax.fori_loop(0, 4, step, 0)
    grad_gain[...] = gain_total


def conv_weight_kernel(sign, marks, image, cells, out, wide):
    out[...] = jnp.zeros_like(out)
    for b in range(2):
        _, width = marks_of(marks, b)
        widen(wide, image, b, width, sign)
        for i in range(3):

            def step(c, _):
                at = pl.multiple_of(margin + c * 256 + sign * (i - 1) * width, 8)
                taps = halves(wide[pl.ds(at, 256), :].T)
                values = halves(cells[b, pl.ds(pl.multiple_of(margin + c * 256, 8), 256), :])
                part = dot_halves(taps, values, 1, 0)
                for j in range(3):
                    out[3 * i + j] += part[160 * j : 160 * j + 160]
                return 0

            lax.fori_loop(0, 4, step, 0)


def wide_halves(values):
    top, low = halves(values)
    return jnp.concatenate([top, top, low], axis=1)


def other_halves(values):
    top, low = halves(values)
    return jnp.concatenate([top, low, top], axis=1)


def dot_last(left, right):
    return lax.dot_general(
        left, right, (((1,), (1,)), ((), ())), preferred_element_type=jnp.float32
    )


def dot_pair(left, values):
    top, low = halves(values)
    both = jnp.dot(left[0], jnp.concatenate([top, low], axis=1), preferred_element_type=jnp.float32)
    return (both[:, :64] + both[:, 64:]) + jnp.dot(
        left[1], top, preferred_element_type=jnp.float32
    )


def scores_turned(marks, queries, pieces, head, j):
    at = 64 * head
    keys = pieces[j][:, at : at + 64]
    scores = dot_last(wide_halves(keys), other_halves(queries[:, at : at + 64])) * 0.125
    slot = lax.broadcasted_iota(jnp.int32, (256, 256), 0) + marks[6] * 64
    slot = jnp.where(slot >= 256, slot - 256, slot)
    return jnp.where(slot < marks[0], scores, masked_score)


def attend_kernel(marks, qkv, *refs):
    pieces, out, totals, held = refs[:4], refs[4], refs[5], refs[6]
    totals[...] = jnp.zeros_like(totals)
    for head in range(5):
        peak = None
        for j in range(4):
            scores = scores_turned(marks, qkv, pieces, head, j)
            held[256 * j : 256 * j + 256, :] = scores
            here = jnp.max(scores, axis=0, keepdims=True)
            peak = here if peak is None else jnp.maximum(peak, here)
        total = jnp.zeros((1, 256), jnp.float32)
        attended = jnp.zeros((64, 256), jnp.float32)
        for j in range(4):
            exponent = jnp.exp(held[256 * j : 256 * j + 256, :] - peak)
            total = total + column_sum(exponent)
            values = halves(pieces[j][:, 320 + 64 * head : 384 + 64 * head].T)
            first, second = halves(exponent)
            both = jnp.dot(
                jnp.concatenate(values, axis=0), first, preferred_element_type=jnp.float32
            )
            attended = attended + (
                (both[:64] + both[64:])
                + jnp.dot(values[0], second, preferred_element_type=jnp.float32)
            )
        out[:, 64 * head : 64 * head + 64] = (attended / total).T
        totals[head : head + 1, :] = peak + jnp.log(total)


def attend_back_kernel(marks, qkv, *refs):
    pieces, totals, attended, grad = refs[:4], refs[4], refs[5], refs[6]
    grad_query, outs = refs[7], refs[8:12]
    for head in range(5):
        at = 64 * head
        grad_out = grad[:, at : at + 64]
        queries = qkv[:, at : at + 64]
        delta = column_sum((grad_out * attended[:, at : at + 64]).T)
        total = totals[head : head + 1, :]
        grad_other = other_halves(grad_out)
        query_grad = jnp.zeros((64, 256), jnp.float32)
        for j in range(4):
            weights = jnp.exp(scores_turned(marks, qkv, pieces, head, j) - total)
            values = pieces[j][:, 320 + at : 384 + at]
            grad_scores = weights * (dot_last(wide_halves(values), grad_other) - delta)
            outs[j][:, 320 + at : 384 + at] = dot_pair(halves(weights), grad_out)
            first, second = halves(grad_scores)
            outs[j][:, at : at + 64] = dot_pair((first, second), queries) * 0.125
            keys = halves(pieces[j][:, at : at + 64].T)
            both = jnp.dot(
                jnp.concatenate(keys, axis=0), first, preferred_element_type=jnp.float32
            )
            query_grad = query_grad + (
                (both[:64] + both[64:])
                + jnp.dot(keys[0], second, preferred_element_type=jnp.float32)
            )
        grad_query[:, at : at + 64] = query_grad.T * 0.125


def pack_kernel(marks, values, out):
    for q in range(values.shape[0] // 64):
        for k in range(8):
            part = values[64 * q : 64 * q + 64, 160 * k : 160 * k + 160]
            put_quarter(out, k, part, 80 * q)


def unpack_kernel(marks, packed, plain):
    for k in range(8):
        plain[:, 160 * k : 160 * k + 160] = unpack_quarter(packed[k, 0:80, :])


def unpack_norm_kernel(marks, packed, gain, scaled, plain):
    for k in range(8):
        centred = unpack_quarter(packed[k, 0:80, :])
        mean = jnp.concatenate([packed[k, 80:81, :], packed[k, 81:82, 0:32]], axis=1)
        inv = jnp.concatenate([packed[k, 82:83, :], packed[k, 83:84, 0:32]], axis=1)
        at = slice(160 * k, 160 * k + 160)
        scaled[:, at] = centred * gain[:, at]
        plain[:, at] = centred * (1.0 / inv) + mean


def cotangent_kernel(marks, pieces, total, out, whole):
    total[...] = (pieces[0, :, :1280] + pieces[1, :, :1280]) + (
        pieces[2, :, :1280] + pieces[3, :, :1280]
    )
    for part in range(4):
        whole[:, 320 * part : 320 * part + 320] = pieces[part, :, 1280:1600]
    for k in range(8):
        put_quarter(out, k, whole[:, 160 * k : 160 * k + 160])


def third_kernel(marks, *refs):
    pieces, out, gain = refs[:4], refs[4], refs[5]
    for first in range(4):

        @pl.when(marks[6] == first)
        def _():
            for j in range(4):
                at = (first + j) % 4 * 320
                gain[:, at : at + 320] = pieces[j][160:161, 0:320]
                for m in range(3):
                    out[:, 1280 * m + at : 1280 * m + at + 320] = pieces[j][
                        0:160, 320 * m : 320 * m + 320
                    ]


def text_kernel(marks, pieces, rows, keys, values):
    for part in range(4):
        at = pl.multiple_of(lax.rem(part - marks[6] + 4, 4) * 64, 8)
        rows[pl.ds(at, 64), :] = pieces[part, 0:64, :]
        lanes = slice(320 * part, 320 * part + 320)
        keys[0:40, lanes] = pieces[part, 64:104, 0:320]
        values[0:40, lanes] = pieces[part, 64:104, 320:640]
        keys[40:77, lanes] = pieces[part, 64:101, 640:960]
        values[40:77, lanes] = pieces[part, 64:101, 960:1280]


def text_grad_kernel(marks, keys, values, *outs):
    for first in range(4):

        @pl.when(marks[6] == first)
        def _():
            for j in range(4):
                at = (first + j) % 4 * 320
                lanes = slice(at, at + 320)
                outs[j][:, 0:320] = keys[0:40, lanes]
                outs[j][:, 320:640] = values[0:40, lanes]
                outs[j][0:37, 640:960] = keys[40:77, lanes]
                outs[j][0:37, 960:1280] = values[40:77, lanes]
                outs[j][37:40, 640:1280] = jnp.zeros((3, 640), jnp.float32)


def rows_kernel(marks, *refs):
    pieces, out = refs[:4], refs[4]
    for j in range(4):
        at = pl.multiple_of(lax.rem(marks[6] + j, 4) * 64, 8)
        out[pl.ds(at, 64), :] = pieces[j][...]


def residual_kernel(marks, source, first, second, third, fourth, out, sums):
    t = marks[6]
    at = pl.multiple_of(t * 80, 8)
    sums[...] = jnp.zeros_like(sums)
    for b in range(2):
        for k in range(4):
            place = 4 * b + k
            packed = source[place, pl.ds(at, 80), :] + (
                (first[place] + second[place]) + (third[place] + fourth[place])
            )
            out[place] = packed
            values = unpack_quarter(packed)
            sums[2 * b : 2 * b + 1, :] += column_sum(values)
            sums[2 * b + 1 : 2 * b + 2, :] += column_sum(values * values)


def span_of_item(marks, b):
    return jnp.where(marks[4] == b, marks[0], marks[2])


def norm_kernel(marks, residual, first, second, third, fourth, out, stats):
    total = (first[...] + second[...]) + (third[...] + fourth[...])
    for b in range(2):
        span = span_of_item(marks, b)
        mean, inv = group_row_stats(
            total[2 * b : 2 * b + 1, :], total[2 * b + 1 : 2 * b + 2, :], span
        )
        stats[2 * b : 2 * b + 1, :] = mean
        stats[2 * b + 1 : 2 * b + 2, :] = inv
        for k in range(4):
            values = unpack_quarter(residual[4 * b + k])
            centred = (values - mean) * inv * quarter_mask(span, marks[6])
            put_quarter(out, 4 * b + k, centred)
            out[4 * b + k, 80:88, :] = jnp.zeros((8, 128), jnp.float32)
            for row, value in ((80, mean), (82, inv)):
                out[4 * b + k, row : row + 1, :] = value[:, :128]
                out[4 * b + k, row + 1 : row + 2, 0:32] = value[:, 128:]


def centred_of(marks, residual, stats, b, k):
    values = unpack_quarter(residual[4 * b + k])
    mean, inv = stats[2 * b : 2 * b + 1, :], stats[2 * b + 1 : 2 * b + 2, :]
    return (values - mean) * inv * quarter_mask(span_of_item(marks, b), marks[6])


def norm_sums_kernel(marks, grad, residual, stats, gain, sums):
    sums[...] = jnp.zeros_like(sums)
    for b in range(2):
        for k in range(4):
            centred = centred_of(marks, residual, stats, b, k)
            values = unpack_quarter(grad[4 * b + k])
            scaled = values * gain[...]
            sums[3 * b : 3 * b + 1, :] += column_sum(scaled)
            sums[3 * b + 1 : 3 * b + 2, :] += column_sum(scaled * centred)
            sums[3 * b + 2 : 3 * b + 3, :] += column_sum(values * centred)


def sum_in_order(pieces, t):
    total = None
    for part in range(4):
        j = lax.rem(part - t + 4, 4)
        value = jnp.where(
            j < 2,
            jnp.where(j == 0, pieces[0][...], pieces[1][...]),
            jnp.where(j == 2, pieces[2][...], pieces[3][...]),
        )
        total = value if total is None else total + value
    return total


def norm_back_kernel(marks, *refs):
    grad, residual, stats, gain, base = refs[:5]
    pieces, out, grad_gain = refs[5:9], refs[9], refs[10]
    total = sum_in_order(pieces, marks[6])
    grad_gain[...] = jnp.zeros_like(grad_gain)
    grad_gain[0:1, :] = total[2:3, :] + total[5:6, :]
    for b in range(2):
        span = span_of_item(marks, b)
        count = (span * 160).astype(jnp.float32)
        first = group_rows(total[3 * b : 3 * b + 1, :]) / count
        second = group_rows(total[3 * b + 1 : 3 * b + 2, :]) / count
        inv = stats[2 * b + 1 : 2 * b + 2, :]
        for k in range(4):
            centred = centred_of(marks, residual, stats, b, k)
            scaled = unpack_quarter(grad[4 * b + k]) * gain[...]
            values = inv * quarter_mask(span, marks[6]) * (scaled - first - centred * second)
            put_quarter(out, 4 * b + k, values + unpack_quarter(base[4 * b + k]))


def input_sums_kernel(marks, source, gain, stats, *refs):
    pieces, out, sums = refs[:4], refs[4], refs[5]
    at = pl.multiple_of(marks[6] * 80, 8)
    sums[...] = jnp.zeros_like(sums)
    for b in range(2):
        span = span_of_item(marks, b)
        mine = marks[4] ^ b
        mean, inv = stats[mine, 0:1, :], stats[mine, 1:2, :]
        for k in range(4):
            place = 4 * b + k
            values = unpack_quarter(source[place, pl.ds(at, 80), :])
            centred = (values - mean) * inv * quarter_mask(span, marks[6])
            norm = centred * gain[...]
            gate = jax.nn.sigmoid(norm)
            packed = (pieces[0][place] + pieces[1][place]) + (pieces[2][place] + pieces[3][place])
            grad = unpack_quarter(packed) * gate * (1.0 + norm * (1.0 - gate))
            put_quarter(out, place, grad)
            scaled = grad * gain[...]
            sums[3 * b : 3 * b + 1, :] += column_sum(scaled)
            sums[3 * b + 1 : 3 * b + 2, :] += column_sum(scaled * centred)
            sums[3 * b + 2 : 3 * b + 3, :] += column_sum(grad * centred)


def input_back_kernel(marks, grad, source, gain, stats, base, extra, *refs):
    pieces, out, grad_gain = refs[:4], refs[4], refs[5]
    at = pl.multiple_of(marks[6] * 80, 8)
    total = sum_in_order(pieces, marks[6])
    grad_gain[...] = jnp.zeros_like(grad_gain)
    grad_gain[0:1, :] = total[2:3, :] + total[5:6, :]
    for b in range(2):
        span = span_of_item(marks, b)
        count = (span * 160).astype(jnp.float32)
        first = group_rows(total[3 * b : 3 * b + 1, :]) / count
        second = group_rows(total[3 * b + 1 : 3 * b + 2, :]) / count
        mine = marks[4] ^ b
        mean, inv = stats[mine, 0:1, :], stats[mine, 1:2, :]
        for k in range(4):
            place = 4 * b + k
            keep = quarter_mask(span, marks[6])
            centred = (unpack_quarter(source[place, pl.ds(at, 80), :]) - mean) * inv * keep
            scaled = unpack_quarter(grad[place]) * gain[...]
            values = inv * keep * (scaled - first - centred * second)
            put_quarter(out, place, values + unpack_quarter(base[place]))
            out[place, 80:88, :] = extra[place]


def run_kernel(body, marks, inputs, outs, scratch, flops):
    in_smem = pl.BlockSpec(memory_space=pltpu.SMEM)
    in_vmem = pl.BlockSpec(memory_space=pltpu.VMEM)
    return pl.pallas_call(
        body,
        out_shape=[jax.ShapeDtypeStruct(shape, jnp.float32) for shape in outs],
        in_specs=[in_smem] + [in_vmem] * len(inputs),
        out_specs=[in_vmem] * len(outs),
        scratch_shapes=[pltpu.VMEM(shape, kind) for shape, kind in scratch],
        compiler_params=pltpu.CompilerParams(vmem_limit_bytes=56 * 1024 * 1024),
        cost_estimate=pl.CostEstimate(
            flops=flops, bytes_accessed=10 * 1024 * 1024, transcendentals=0
        ),
    )(marks, *inputs)


def weight_kernel(plan, *refs):
    count = 1 + max(which for block in plan for _, _, which in block)
    lefts, right, out = refs[:count], refs[count], refs[-1]
    tokens = right.shape[0]
    for number, block in enumerate(plan):

        @pl.when(pl.program_id(0) == number)
        def _():
            for begin, columns, which in block:
                top, low = halves(right[:, begin : begin + columns])
                if tokens <= 64:
                    stacked = jnp.concatenate([top, low, top], axis=0)
                for m in range(0, 1280, 256):
                    cells = lefts[which][:, m : m + 256].T
                    if tokens <= 64:
                        first, second = halves(cells)
                        first = jnp.concatenate([first, first, second], axis=1)
                        part = jnp.dot(first, stacked, preferred_element_type=jnp.float32)
                    else:
                        part = dot_halves(halves(cells), (top, low), 1, 0)
                    out[m : m + 256, begin : begin + columns] = part


def weight_grads(plan, lefts, right, first=0, blocks=None, into=None):
    tokens = right.shape[0]
    blocks = blocks or len(plan)
    in_specs = [pl.BlockSpec((tokens, 1280), lambda i: (0, 0))] * len(lefts)
    in_specs.append(pl.BlockSpec((tokens, 1280), lambda i: (0, i)))
    inputs, alias = (*lefts, right), {}
    if into is not None:
        in_specs.append(pl.BlockSpec(memory_space=pl.ANY))
        alias = {len(inputs): 0}
        inputs = (*inputs, into)
    return pl.pallas_call(
        functools.partial(weight_kernel, plan),
        out_shape=jax.ShapeDtypeStruct((1280, 1280 * blocks), jnp.float32),
        grid=(len(plan),),
        in_specs=in_specs,
        out_specs=pl.BlockSpec((1280, 1280), lambda i: (0, i + first)),
        input_output_aliases=alias,
        compiler_params=pltpu.CompilerParams(vmem_limit_bytes=48 * 1024 * 1024),
        cost_estimate=pl.CostEstimate(
            flops=6 * tokens * 1280 * 1280 * len(plan),
            bytes_accessed=7 * 1024 * 1024 * len(plan),
            transcendentals=0,
        ),
    )(*inputs)


def after(values, *events):
    return lax.optimization_barrier((values,) + events)[0]


def together(*values):
    return lax.optimization_barrier(values)


def small(body, marks, inputs, outs, scratch=()):
    return run_kernel(body, marks, inputs, outs, scratch, 4 * 1024 * 1024)


CONV_FLOPS = 6 * 2048 * 1440 * 320


def first_conv(marks, source, gain, tau, weight):
    f32, b16 = jnp.float32, jnp.bfloat16
    return run_kernel(
        first_kernel,
        marks,
        (source, gain, tau, weight),
        [(4, 320, 256), (4, 320, 256), (2, IMAGE_ROWS, 160), (2, 8, 160)],
        [
            ((IMAGE_ROWS, 480), f32),
            ((1440, 320), b16),
            ((1440, 320), b16),
            ((4, 256, 160), f32),
        ],
        CONV_FLOPS,
    )


def second_conv(marks, strips, gain, weight):
    f32, b16 = jnp.float32, jnp.bfloat16
    return run_kernel(
        second_kernel,
        marks,
        (*strips, gain, weight),
        [(8, 80, 128)] * 4 + [(2, IMAGE_ROWS, 320), (2, 8, 320)],
        [
            ((IMAGE_ROWS, 960), f32),
            ((2880, 160), b16),
            ((2880, 160), b16),
            ((256, 160), f32),
        ],
        CONV_FLOPS,
    )


def second_conv_back(marks, quarters, weight):
    f32, b16 = jnp.float32, jnp.bfloat16
    return run_kernel(
        second_back_kernel,
        marks,
        (*quarters, weight),
        [(4, 320, 256), (4, 320, 256), (2, IMAGE_ROWS, 160)],
        [((IMAGE_ROWS, 480), f32), ((1440, 320), b16), ((1440, 320), b16)],
        CONV_FLOPS,
    )


def first_conv_back(marks, grads, strips, gain, stats, weight):
    f32, b16 = jnp.float32, jnp.bfloat16
    return run_kernel(
        first_back_kernel,
        marks,
        (*grads, *strips, gain, stats, weight),
        [(8, 80, 128)] * 4 + [(2, IMAGE_ROWS, 320), (2, 320), (1, 320)],
        [
            ((IMAGE_ROWS, 960), f32),
            ((2880, 160), b16),
            ((2880, 160), b16),
            ((256, 160), f32),
            ((4, 256, 320), f32),
            ((4, 256, 320), f32),
        ],
        CONV_FLOPS,
    )


def conv_weight(marks, image, cells, sign):
    return run_kernel(
        functools.partial(conv_weight_kernel, sign),
        marks,
        (image, cells),
        [(9, 160, 320)],
        [((IMAGE_ROWS, 480), jnp.float32)],
        CONV_FLOPS,
    )[0]


def heads_of(values, count):
    return values.reshape(values.shape[0], count, HEAD_DIM)


def ein(form, left, right):
    return jnp.einsum(form, left, right, precision=high, preferred_element_type=jnp.float32)


def soft_attend(queries, keys, values, key_valid, count):
    scores = ein(QK, heads_of(queries, count), heads_of(keys, count)) * (1.0 / math.sqrt(HEAD_DIM))
    if key_valid is not None:
        scores = jnp.where(key_valid[None, None, :], scores, masked_score)
    exponent = jnp.exp(scores - jnp.max(scores, axis=-1, keepdims=True))
    weights = exponent / jnp.sum(exponent, axis=-1, keepdims=True)
    attended = ein(PV, weights, heads_of(values, count))
    return attended.reshape(queries.shape), weights


def soft_back(queries, keys, values, count, weights, attended, grad_out):
    scaling = 1.0 / math.sqrt(HEAD_DIM)
    grad_heads = heads_of(grad_out, count)
    grad_soft = ein(QK, grad_heads, heads_of(values, count))
    delta = jnp.sum(grad_heads * heads_of(attended, count), axis=-1).T
    grad_scores = weights * (grad_soft - delta[..., None])
    grad_query = ein(PV, grad_scores, heads_of(keys, count)) * scaling
    grad_key = ein(PQ, grad_scores, heads_of(queries, count)) * scaling
    grad_value = ein(PQ, weights, grad_heads)
    return (
        grad_query.reshape(queries.shape),
        grad_key.reshape(keys.shape),
        grad_value.reshape(values.shape),
    )


def layer_grad(grad_out, centred, inv_std, gain_vector):
    scaled = grad_out * gain_vector
    grad_in = inv_std * (
        scaled
        - jnp.mean(scaled, axis=-1, keepdims=True)
        - centred * jnp.mean(scaled * centred, axis=-1, keepdims=True)
    )
    return grad_in, jnp.sum(grad_out * centred, axis=0)


def layer_forward(values, gain_vector):
    mean_val = jnp.mean(values, axis=-1, keepdims=True)
    var_val = jnp.mean(values * values, axis=-1, keepdims=True) - mean_val * mean_val
    inv_std = lax.rsqrt(var_val + norm_eps)
    centred = (values - mean_val) * inv_std
    return centred * gain_vector, centred, inv_std


def gather_plane(block):
    return lax.all_gather(block, IH, axis=0, tiled=True)


def scatter_plane(block):
    return lax.psum_scatter(block, IH, scatter_dimension=0, tiled=True)


def grid_cells(bucket):
    strip_rows, strip_width = grid_shape(bucket)
    return strip_rows * strip_width


def fast_shards(
    hidden,
    text_states,
    bucket,
    timestep,
    gain_in,
    conv_first,
    time_weight,
    gain_mid,
    conv_second,
    gain_attn_norm,
    proj_in,
    gain_self,
    query_self,
    key_self,
    value_self,
    out_self,
    gain_cross,
    query_cross,
    key_cross,
    value_cross,
    out_cross,
    gain_ff,
    ff_in,
    ff_out,
    proj_out,
    cotangent,
):
    item, h, t = lax.axis_index(I), lax.axis_index(H), lax.axis_index(T)
    block = item * 4 + h
    width, wide = 160, 320
    channels = 1280

    def rows_of(values):
        return [values[64 * j : 64 * j + 64] for j in range(4)]

    own_span = grid_cells(bucket[0])
    slot = jnp.arange(256, dtype=jnp.int32)
    own_valid = (slot < own_span).astype(jnp.float32)[:, None]
    both = jnp.stack([bucket[0], timestep[0]]).astype(jnp.float32)
    both_other = swap(both)
    times = jnp.stack([both[1], both_other[1]])
    other_rows, other_width = grid_shape(both_other[0].astype(jnp.int32))
    own_rows, own_width = grid_shape(bucket[0])
    marks = jnp.stack(
        [own_span, own_width, other_rows * other_width, other_width, item, h, t]
    ).astype(jnp.int32)

    (source,) = small(pack_kernel, marks, (hidden[0] * own_valid,), [(8, 320, 128)])
    source = plane_exchange(source)
    gains = jnp.stack([gain_self, gain_cross, gain_ff], axis=1)
    attn_full = gather_plane(
        jnp.concatenate(
            [
                query_self,
                key_self,
                value_self,
                proj_out,
                out_self.T,
                jnp.pad(gains, ((0, 0), (0, 125))),
            ],
            axis=1,
        )
    )
    qkv_full = attn_full[:, :960]
    proj_out_full = attn_full[:, 960:1280]
    out_self_full = attn_full[:, 1280:1600]
    gain_rows = attn_full[:, 1600:1603].T
    gain_self_full, gain_cross_full, gain_ff_full = (gain_rows[k : k + 1] for k in range(3))

    own_third = jnp.concatenate([proj_in.T, query_cross, out_cross.T], axis=1)
    own_third = jnp.concatenate(
        [own_third, jnp.pad(gain_attn_norm[None, :], ((0, 7), (0, 640)))], axis=0
    )
    third_pieces = z_pieces(own_third)

    features = jax.nn.silu(time_features(times, channels))
    own_features = lax.dynamic_slice_in_dim(features, block * width, width, 1)
    tau = mm(own_features, time_weight, 1, 0)
    second_weight = conv_second.transpose(0, 1, 3, 2).reshape(9 * width, wide)
    own_one, other_one, image_one, stats_one = first_conv(
        marks, source, gain_in[None, :], tau, conv_first.reshape(9 * width, wide)
    )
    own_one, other_one, *third_pieces = together(own_one, other_one, *third_pieces)
    own_one = own_one + swap(other_one)
    strips_one, part = plane_sum(own_one)
    third, gain_attn_full = small(
        third_kernel, marks, after(third_pieces, part), [(160, 3840), (1, channels)]
    )
    third_full = gather_plane(third)
    proj_in_full = third_full[:, :1280]
    query_cross_full = third_full[:, 1280:2560]
    out_cross_full = third_full[:, 2560:]
    ff_block = jnp.concatenate([ff_in.reshape(160, 2560), ff_out.T], axis=1)
    ff_full = gather_plane(after(ff_block, third))
    ff_in_full = ff_full[:, :2560]
    ff_out_full = ff_full[:, 2560:]
    cot = after(cotangent[0] * own_valid, own_one)
    grad_ff_part = mm(cot, proj_out_full, 1, 1)
    cot_pieces = z_all(jnp.concatenate([grad_ff_part, cot], axis=1).reshape(4, 64, channels + wide))
    *strips_one, cot_pieces = together(*strips_one, cot_pieces)

    *conv_two, image_two, stats_two = second_conv(
        marks, strips_one, gain_mid[None, :], second_weight
    )
    conv_two_pieces = z_received(conv_two)

    event = conv_two[0]
    grad_after_ff, cot_packed = small(
        cotangent_kernel,
        marks,
        (after(cot_pieces, event),),
        [(64, channels), (8, 80, 128)],
        [((64, channels), jnp.float32)],
    )
    cot_q = plane_exchange(cot_packed)
    text_here = after(text_states[0], event)
    text_own = lax.dynamic_slice_in_dim(text_here, block * 256, 256, 1)
    text_other = swap(lax.dynamic_slice_in_dim(text_here, ((1 - item) * 4 + h) * 256, 256, 1))
    text_weight = jnp.concatenate([key_cross, value_cross], axis=1)
    text_part = mm(text_own, text_weight, 1, 0) + swap(mm(text_other, text_weight, 1, 0))

    residual_q, sums = small(
        residual_kernel, marks, (source, *conv_two_pieces), [(8, 80, 128), (8, width)]
    )
    centred_three, stats_three = small(
        norm_kernel, marks, (residual_q, *z_pieces(sums)), [(8, 88, 128), (8, width)]
    )
    norm_three, residual_s = small(
        unpack_norm_kernel,
        marks,
        (plane_exchange(centred_three), gain_attn_full),
        [(64, channels), (64, channels)],
    )
    projected = mm(norm_three, proj_in_full, 1, 1)

    normed_self, centred_self, inv_self = layer_forward(projected, gain_self_full)
    normed_pieces = z_pieces(normed_self)
    text_sum = h_sum(after(text_part, normed_self))
    *normed_pieces, text_sum, cot_q = together(*normed_pieces, text_sum, cot_q)
    normed_self_all = jnp.concatenate(normed_pieces, axis=0)
    qkv = mm(normed_self_all, qkv_full, 1, 0)
    own_kv = qkv[:, wide:]
    kv_pieces = [own_kv] + [flip(own_kv, j) for j in (1, 2, 3)]
    text_sum, grad_here = after((text_sum, grad_after_ff), own_kv)
    side_pieces = z_spread(jnp.concatenate([grad_here, folded(text_sum)], axis=0))
    *kv_pieces, side_pieces = together(*kv_pieces, side_pieces)
    attn_self, totals_self = small(
        attend_kernel,
        marks,
        (qkv, *kv_pieces),
        [(256, wide), (8, 256)],
        [((1024, 256), jnp.float32)],
    )
    self_part = mm(attn_self, out_self_full, 1, 1)
    self_pieces = z_received(rows_of(self_part))
    self_sum = total_of(self_pieces)
    event = self_pieces[1]
    grad_after_ff_all, keys_text, values_text = small(
        text_kernel,
        marks,
        (after(side_pieces, event),),
        [(256, channels), (77, channels), (77, channels)],
    )
    grad_ff_act = mm(grad_after_ff_all, ff_out_full, 1, 0)
    self_sum, grad_ff_act, keys_text, values_text = together(
        self_sum, grad_ff_act, keys_text, values_text
    )
    after_self = projected + self_sum

    normed_cross, centred_cross, inv_cross = layer_forward(after_self, gain_cross_full)
    queries_cross = mm(normed_cross, query_cross_full, 1, 0)
    attn_cross, weights_cross = soft_attend(queries_cross, keys_text, values_text, None, 20)
    after_cross = after_self + mm(attn_cross, out_cross_full, 1, 1)

    normed_ff, centred_ff, inv_ff = layer_forward(after_cross, gain_ff_full)
    normed_ff_all = jnp.concatenate(z_pieces(normed_ff), axis=0)
    hidden_ff = mm(normed_ff_all, ff_in_full, 1, 0)
    value_half, gate_half = hidden_ff[:, :channels], hidden_ff[:, channels:]
    phi = 0.5 * (1.0 + lax.erf(gate_half * math.sqrt(0.5)))
    slope = phi + gate_half * jnp.exp(-0.5 * gate_half * gate_half) * (1.0 / math.sqrt(2 * math.pi))
    gate_act = gate_half * phi
    ff_act = value_half * gate_act
    grad_value = grad_ff_act * gate_act
    grad_gate = grad_ff_act * value_half * slope
    grad_hidden_ff = jnp.concatenate([grad_value, grad_gate], axis=1)
    grad_normed_part = mm(grad_hidden_ff, ff_in_full, 1, 1)
    normed_pieces = z_received(rows_of(grad_normed_part))
    grad_normed_ff = total_of(normed_pieces)
    ff_right = jnp.concatenate(after([grad_hidden_ff, ff_act], normed_pieces[1]), axis=1)
    ff_grads = weight_grads(
        (((0, 1280, 0),), ((0, 1280, 0),), ((0, 1280, 1),)),
        (normed_ff_all, grad_after_ff_all),
        ff_right,
        0,
        5,
    )
    out_part = mm(after(ff_act, normed_pieces[1]), ff_out_full, 1, 1)
    grad_normed_ff, ff_grads, out_part = together(grad_normed_ff, ff_grads, out_part)

    back_ff, grad_gain_ff = layer_grad(grad_normed_ff, centred_ff, inv_ff, gain_ff_full)
    grad_after_cross = grad_after_ff + back_ff
    grad_attn_cross = mm(grad_after_cross, out_cross_full, 1, 0)
    grad_queries_cross, grad_keys_text, grad_values_text = soft_back(
        queries_cross, keys_text, values_text, 20, weights_cross, attn_cross, grad_attn_cross
    )
    grad_normed_cross = mm(grad_queries_cross, query_cross_full, 1, 1)
    back_cross, grad_gain_cross = layer_grad(
        grad_normed_cross, centred_cross, inv_cross, gain_cross_full
    )
    grad_after_self = grad_after_cross + back_cross
    grad_pieces = z_pieces(grad_after_self)
    cross_right = after((grad_queries_cross, attn_cross), grad_pieces[1])
    cross_right = jnp.concatenate(
        [side[:, wide * k : wide * k + wide] for k in range(4) for side in cross_right], axis=1
    )
    cross_grads = weight_grads(
        (((0, 320, 0), (320, 320, 1), (640, 320, 0), (960, 320, 1)),) * 2,
        (normed_cross, grad_after_cross),
        cross_right,
        3,
        5,
        ff_grads,
    )
    *grad_pieces, cross_grads = together(*grad_pieces, cross_grads)
    out_turned = jnp.concatenate([out_part, out_part], axis=0)
    out_turned = lax.dynamic_slice_in_dim(out_turned, lax.rem(4 - t, 4) * 64, 256, 0)
    out_sum = z_all(after(out_turned, grad_after_self).reshape(4, 64, channels))
    ff_grads = scatter_plane(cross_grads)
    ff_grads, cross_grads = ff_grads[:, :3840], ff_grads[:, 3840:]

    grad_after_self_all = jnp.concatenate(grad_pieces, axis=0)
    grad_attn_self = mm(grad_after_self_all, out_self_full, 1, 0)
    grad_queries, *kv_pieces = small(
        attend_back_kernel,
        marks,
        (qkv, *kv_pieces, totals_self, attn_self, grad_attn_self),
        [(256, wide)] + [(256, 2 * wide)] * 4,
    )
    kv_pieces = kv_pieces[:1] + [flip(kv_pieces[j], j) for j in (1, 2, 3)]
    grad_kv = total_of(kv_pieces)
    grad_qkv = jnp.concatenate([grad_queries, grad_kv], axis=1)
    grad_normed_part = mm(grad_qkv, qkv_full, 1, 1)
    normed_pieces = z_received(rows_of(grad_normed_part))
    grad_normed_self = total_of(normed_pieces)
    text_grads = small(
        text_grad_kernel,
        marks,
        after((grad_keys_text, grad_values_text), normed_pieces[1]),
        [(40, channels)] * 4,
    )
    grad_normed_self, out_sum, *text_grads = together(grad_normed_self, out_sum, *text_grads)
    back_self, grad_gain_self = layer_grad(grad_normed_self, centred_self, inv_self, gain_self_full)
    grad_projected = grad_after_self + back_self
    grad_norm_three = mm(grad_projected, proj_in_full, 1, 0)

    (grad_three,) = small(pack_kernel, marks, (grad_norm_three,), [(8, 80, 128)])
    grad_three_q = plane_exchange(grad_three)
    out_sum = jnp.sum(after(out_sum, grad_three), axis=0)
    text_grads = total_of(z_received(text_grads))
    attn_right = jnp.concatenate(
        [
            jnp.concatenate([grad_qkv, attn_self], axis=1),
            jnp.pad(norm_three, ((0, 192), (0, 0))),
        ],
        axis=1,
    )
    attn_grads = weight_grads(
        (((0, 960, 0), (960, 320, 1)), ((0, 1280, 2),)),
        (
            normed_self_all,
            grad_after_self_all,
            jnp.pad(grad_projected, ((0, 192), (0, 0))),
        ),
        after(attn_right, grad_three),
    )
    grad_three_q, attn_grads, text_grads = together(grad_three_q, attn_grads, text_grads)
    attn_grads = scatter_plane(attn_grads)
    gain_block = lax.dynamic_slice_in_dim(gain_attn_full, block * width, width, 1)
    (sums,) = small(
        norm_sums_kernel, marks, (grad_three_q, residual_q, stats_three, gain_block), [(8, width)]
    )
    grad_residual_q, grad_gain_three = small(
        norm_back_kernel,
        marks,
        (grad_three_q, residual_q, stats_three, gain_block, cot_q, *z_pieces(sums)),
        [(8, 80, 128), (8, width)],
    )

    residual_pieces = z_pieces(grad_residual_q)
    text_grads = after(text_grads, grad_residual_q)
    text_grads = text_grads + flip(text_grads, 1)
    *residual_pieces, text_grads = together(*residual_pieces, text_grads)
    own_two, other_two, image_back = second_conv_back(marks, residual_pieces, second_weight)
    own_two = own_two + swap(other_two)
    grad_act_two, part = plane_sum(own_two)
    side = jnp.concatenate(
        [
            jnp.broadcast_to((after_cross + out_sum)[None], (4, 64, channels)),
            jnp.moveaxis(residual_s.reshape(64, 4, wide), 1, 0),
        ],
        axis=2,
    )
    gain_rows = jnp.stack([grad_gain_self, grad_gain_cross, grad_gain_ff])
    gain_rows = jnp.broadcast_to(jnp.pad(gain_rows, ((0, 5), (0, wide)))[None], (4, 8, 1600))
    side = z_all(after(jnp.concatenate([side, gain_rows], axis=1), own_two))
    side_here = after(side, part)
    after_ff_all = side_here[:, :64, :channels].reshape(256, channels)
    residual_all = side_here[:, :64, channels:].reshape(256, wide)
    gain_sums = jnp.sum(side_here[:, 64:67, :channels], axis=0)
    cross_cut = after(cross_grads, part)
    cross_cut = jnp.stack([cross_cut[:, 640 * k : 640 * k + 640] for k in range(4)])
    *grad_act_two, after_ff_all, gain_sums, residual_all, cross_cut = together(
        *grad_act_two, after_ff_all, gain_sums, residual_all, cross_cut
    )
    cross_shares = z_all(cross_cut)

    *grad_act_one, image_grad, grad_tau, grad_gain_mid = first_conv_back(
        marks,
        grad_act_two,
        strips_one,
        gain_mid[None, :],
        stats_two,
        conv_first.reshape(9 * width, wide),
    )
    grad_act_pieces = z_received(grad_act_one)
    image_grad, text_grads = after((image_grad, text_grads), grad_act_pieces[1])
    text_grads = text_grads + flip(text_grads, 2)
    grad_conv_first = conv_weight(marks, image_one, image_grad, 1)
    cross_shares = jnp.sum(after(cross_shares, grad_act_pieces[1]), axis=0)
    *grad_act_pieces, grad_conv_first, cross_shares, text_grads = together(
        *grad_act_pieces, grad_conv_first, cross_shares, text_grads
    )
    grad_conv_first = grad_conv_first.reshape(3, 3, width, wide)
    extra = jnp.concatenate(
        [
            jnp.broadcast_to(grad_gain_three[0], (8, 1, width)),
            jnp.moveaxis(gain_sums.reshape(3, 8, width), 1, 0),
        ],
        axis=1,
    )
    extra = jnp.concatenate(
        [extra[:, :, :128], jnp.pad(extra[:, :, 128:], ((0, 0), (0, 0), (0, 96)))], axis=1
    )
    grad_input_q, sums = small(
        input_sums_kernel,
        marks,
        (source, gain_in[None, :], stats_one, *grad_act_pieces),
        [(8, 80, 128), (8, width)],
    )
    moved, grad_gain_in = small(
        input_back_kernel,
        marks,
        (
            grad_input_q,
            source,
            gain_in[None, :],
            stats_one,
            grad_residual_q,
            extra,
            *z_pieces(sums),
        ),
        [(8, 88, 128), (8, width)],
    )
    received = plane_exchange(moved)
    attn_grads, text_grads = after((attn_grads, text_grads), moved)
    text_other_grads = swap(text_grads)
    proj_cut = attn_grads[:, 1280:].reshape(width, 4, wide)
    proj_share = total_of(z_received([pick(proj_cut, lax.rem(t + j, 4), 1) for j in range(4)]))
    received, proj_share, text_other_grads = together(received, proj_share, text_other_grads)
    text_grads, text_other_grads = unfolded(text_grads), unfolded(text_other_grads)
    (grad_hidden,) = small(unpack_kernel, marks, (received,), [(64, channels)])
    hidden_pieces = z_pieces(grad_hidden)
    after_ff_all, image_back = after((after_ff_all, image_back), grad_hidden)
    grad_proj_out = mm(after_ff_all, cot, 0, 0).reshape(2, 4, width, wide)
    grad_proj_own = pick(grad_proj_out, item) + swap(pick(grad_proj_out, 1 - item))
    grad_proj_out = h_collect([pick(grad_proj_own, h ^ j) for j in range(4)])
    grad_conv_second = conv_weight(marks, image_back, image_two, -1)
    *hidden_pieces, grad_conv_second = together(*hidden_pieces, grad_conv_second)
    grad_conv_second = grad_conv_second.reshape(3, 3, width, wide).transpose(0, 1, 3, 2)
    output = residual_all + mm(after_ff_all, proj_out_full, 1, 0)
    output = output * own_valid
    grad_text_weight = mm(text_own, text_grads, 0, 0) + mm(text_other, text_other_grads, 0, 0)
    grad_time_weight = mm(own_features, grad_tau, 0, 0)
    (grad_hidden,) = small(rows_kernel, marks, hidden_pieces, [(256, channels)])
    extra = jnp.concatenate([received[:, 80:84, :], received[:, 84:88, :32]], axis=2)
    grad_gain_attn = lax.dynamic_slice_in_dim(extra[:, 0].reshape(channels), t * wide, wide, 0)
    gain_sums = jnp.sum(extra[:, 1:], axis=0)

    return (
        output[None],
        grad_hidden[None],
        grad_gain_in[0],
        grad_conv_first,
        grad_time_weight,
        grad_gain_mid[0],
        grad_conv_second,
        grad_gain_attn,
        proj_share.T,
        gain_sums[0],
        attn_grads[:, :320],
        attn_grads[:, 320:640],
        attn_grads[:, 640:960],
        attn_grads[:, 960:1280].T,
        gain_sums[1],
        cross_shares[:, :320],
        grad_text_weight[:, :wide],
        grad_text_weight[:, wide:],
        cross_shares[:, 320:].T,
        gain_sums[2],
        ff_grads[:, :2560].reshape(width, 2, channels),
        ff_grads[:, 2560:].T,
        grad_proj_out,
    )


def solution(mesh):
    placed = (
        P(I, H, None),
        P(I, None, None),
        P(I),
        P(I),
        P(IH),
        P(None, None, IH, T),
        P(IH, T),
        P(T),
        P(None, None, T, IH),
        P(T),
        P(T, IH),
        P(IH),
        P(IH, T),
        P(IH, T),
        P(IH, T),
        P(T, IH),
        P(IH),
        P(IH, T),
        P(IH, T),
        P(IH, T),
        P(T, IH),
        P(IH),
        P(IH, None, T),
        P(T, IH),
        P(IH, T),
        P(I, H, T),
    )
    sizes = (mesh.shape[I], mesh.shape[H], mesh.shape[T])
    body = fast_shards if sizes == (2, 4, 4) else shards
    return jax.shard_map(
        body,
        mesh=mesh,
        in_specs=placed,
        out_specs=(
            P(I, H, T),
            P(I, H, None),
            P(IH),
            P(None, None, IH, T),
            P(IH, T),
            P(T),
            P(None, None, T, IH),
            P(T),
            P(T, IH),
            P(IH),
            P(IH, T),
            P(IH, T),
            P(IH, T),
            P(T, IH),
            P(IH),
            P(IH, T),
            P(IH, T),
            P(IH, T),
            P(T, IH),
            P(IH),
            P(IH, None, T),
            P(T, IH),
            P(IH, T),
        ),
        check_vma=False,
    )
```

```python
import functools
import math

import jax
import jax.numpy as jnp
from jax import lax
from jax.experimental import pallas as pl
from jax.experimental.pallas import tpu as pltpu
from jax.sharding import PartitionSpec as P

HEAD_DIM = 64
GROUPS = 32
EDGE = 48


highest = lax.Precision.HIGHEST
norm_eps = 1e-05
masked_score = -1e30
edge_margin = 56
high = lax.Precision.HIGH
margin = 64
I, H, T = "items", "height", "tensor"
IH = (I, H)
E0 = "bc,bn->cn"
E1 = "bhqk,bkhd->bqhd"
E2 = "bhqk,bqhd->bkhd"
E3 = "bqhd,bkhd->bhqk"
E4 = "bqhd,bqhd->bhq"
E5 = "bsc,bsjf->cjf"
E6 = "bsc,cjf->bsjf"
E7 = "bsjf,cjf->bsc"
E8 = "bsk,bsn->kn"
E9 = "bsk,kn->bsn"
E10 = "bsn,kn->bsk"
QK, PV, PQ = "qhd,khd->hqk", "hqk,khd->qhd", "hqk,qhd->khd"


def padded_2(block, sides, width):
    for axis, dim in sides:
        count = lax.axis_size(axis)
        forward = [(i, i + 1) for i in range(count - 1)]
        backward = [(target, source) for source, target in forward]
        low = lax.ppermute(
            lax.slice_in_dim(block, block.shape[dim] - width, None, axis=dim), axis, forward
        )
        high = lax.ppermute(lax.slice_in_dim(block, 0, width, axis=dim), axis, backward)
        block = jnp.concatenate([low, block, high], axis=dim)
    return block


def grid_shape(bucket):
    strip_rows = jnp.where(bucket == 0, 8, jnp.where(bucket == 1, 6, 5)).astype(jnp.int32)
    strip_width = jnp.where(bucket == 0, 32, jnp.where(bucket == 1, 40, 48)).astype(jnp.int32)
    return (strip_rows, strip_width)


def tokens_dot(values, weight):
    return jnp.einsum(E9, values, weight, precision=highest)


def tokens_back(grad_values, weight):
    return jnp.einsum(E10, grad_values, weight, precision=highest)


def tokens_grad(values, grad_values):
    return jnp.einsum(E8, values, grad_values, precision=highest)


def tensor_sum(values):
    return lax.psum(values, T)


def expand_groups(stat, size_group):
    return jnp.repeat(stat, size_group, axis=1)[:, None, :]


def group_stats(values, valid_col, group_count, counts):
    item_count, slot_count, channels = values.shape
    size_group = channels // group_count
    grouped = (values * valid_col).reshape(item_count, slot_count, group_count, size_group)
    sum_values = jnp.sum(grouped, axis=(1, 3))
    sum_squares = jnp.sum(grouped * grouped, axis=(1, 3))
    sum_values, sum_squares = lax.psum((sum_values, sum_squares), H)
    mean_val = sum_values / counts[:, None]
    var_val = sum_squares / counts[:, None] - mean_val * mean_val
    return (
        expand_groups(mean_val, size_group),
        expand_groups(lax.rsqrt(var_val + norm_eps), size_group),
    )


def group_back(grad_out, centred, inv_std, gain_vector, valid_col, group_count, counts):
    item_count, slot_count, channels = grad_out.shape
    size_group = channels // group_count
    scaled = grad_out * gain_vector * valid_col
    sum_first = jnp.sum(
        scaled.reshape(item_count, slot_count, group_count, size_group), axis=(1, 3)
    )
    sum_second = jnp.sum(
        (scaled * centred).reshape(item_count, slot_count, group_count, size_group), axis=(1, 3)
    )
    sum_first, sum_second = lax.psum((sum_first, sum_second), H)
    mean_first = expand_groups(sum_first / counts[:, None], size_group)
    mean_second = expand_groups(sum_second / counts[:, None], size_group)
    grad_in = inv_std * (scaled - mean_first - centred * mean_second) * valid_col
    return (grad_in, jnp.sum(grad_out * centred, axis=(0, 1)))


def layer_norm(values, gain_vector):
    mean_val = jnp.mean(values, axis=-1, keepdims=True)
    var_val = jnp.mean(values * values, axis=-1, keepdims=True) - mean_val * mean_val
    inv_std = lax.rsqrt(var_val + norm_eps)
    centred = (values - mean_val) * inv_std
    return (centred * gain_vector, centred, inv_std)


def layer_back(grad_out, centred, inv_std, gain_vector):
    scaled = grad_out * gain_vector
    grad_in = inv_std * (
        scaled
        - jnp.mean(scaled, axis=-1, keepdims=True)
        - centred * jnp.mean(scaled * centred, axis=-1, keepdims=True)
    )
    return (grad_in, jnp.sum(grad_out * centred, axis=(0, 1)))


def edge_rows(values, strip_rows, strip_width):
    item_count, slot_count, channels = values.shape
    position = jnp.arange(EDGE, dtype=jnp.int32)

    def edge_one_item(item_vals, rows_here, width_here):
        keep_mask = (position < width_here)[:, None].astype(jnp.float32)
        padded = jnp.concatenate([item_vals, jnp.zeros((EDGE, channels), jnp.float32)], axis=0)
        top_row = item_vals[:EDGE] * keep_mask
        bottom_row = (
            lax.dynamic_slice_in_dim(padded, (rows_here - 1) * width_here, EDGE, 0) * keep_mask
        )
        return jnp.stack([top_row, bottom_row])

    return jax.vmap(edge_one_item)(values, strip_rows, strip_width)


def neighbour_stack(values, strip_rows, strip_width):
    edge_pair = edge_rows(values, strip_rows, strip_width)
    beside_all = padded_2(edge_pair, ((H, 1),), 1)
    item_count, slot_count, channels = values.shape
    position = jnp.arange(slot_count, dtype=jnp.int32)

    def neighbour_one_item(item_vals, item_around, rows_here, width_here):
        cell_span = rows_here * width_here
        extended = jnp.zeros((2 * edge_margin + slot_count, channels), jnp.float32)
        extended = lax.dynamic_update_slice_in_dim(
            extended, item_around[0], edge_margin - width_here, 0
        )
        extended = lax.dynamic_update_slice_in_dim(extended, item_vals, edge_margin, 0)
        extended = lax.dynamic_update_slice_in_dim(
            extended, item_around[3], edge_margin + cell_span, 0
        )
        column = position % width_here
        shifted_list = []
        for row_step in (-1, 0, 1):
            for col_step in (-1, 0, 1):
                shifted = lax.dynamic_slice_in_dim(
                    extended, edge_margin + row_step * width_here + col_step, slot_count, 0
                )
                keep_mask = (
                    (column + col_step >= 0)
                    & (column + col_step < width_here)
                    & (position < cell_span)
                )
                shifted_list.append(shifted * keep_mask[:, None].astype(jnp.float32))
        return jnp.stack(shifted_list, axis=1)

    return jax.vmap(neighbour_one_item)(values, beside_all, strip_rows, strip_width)


def conv_apply(neighbours, weight):
    item_count, slot_count = (neighbours.shape[0], neighbours.shape[1])
    flattened = neighbours.reshape(item_count, slot_count, -1)
    return tokens_dot(flattened, weight.reshape(-1, weight.shape[3]))


def conv_input_grad(neighbours_grad, weight):
    flipped = jnp.transpose(weight[::-1, ::-1], (0, 1, 3, 2))
    return conv_apply(neighbours_grad, flipped)


def conv_weight_grad(neighbours, grad_out, weight_shape):
    flattened = neighbours.reshape(neighbours.shape[0], neighbours.shape[1], -1)
    return tokens_grad(flattened, grad_out).reshape(weight_shape)


def time_features(timestep, channels):
    half_width = channels // 2
    frequency = jnp.exp(-math.log(10000.0) * jnp.arange(half_width, dtype=jnp.float32) / half_width)
    angles = timestep.astype(jnp.float32)[:, None] * frequency[None, :]
    return jnp.concatenate([jnp.cos(angles), jnp.sin(angles)], axis=1)


def exact_gelu(values):
    return jax.nn.gelu(values, approximate=False)


def head_split(values, heads_here):
    return values.reshape(
        values.shape[0], values.shape[1], heads_here, values.shape[2] // heads_here
    )


def score_block(queries, keys_all, key_valid, heads_here):
    head_size = queries.shape[2] // heads_here
    scores = jnp.einsum(
        E3,
        head_split(queries, heads_here),
        head_split(keys_all, heads_here),
        precision=highest,
    ) * (1.0 / math.sqrt(head_size))
    return jnp.where(key_valid[:, None, None, :], scores, masked_score)


def attend(queries, keys_all, values_all, key_valid, heads_here):
    scores = score_block(queries, keys_all, key_valid, heads_here)
    row_peak = jnp.max(scores, axis=-1, keepdims=True)
    exponent = jnp.exp(scores - row_peak)
    row_total = jnp.sum(exponent, axis=-1, keepdims=True)
    soft_weights = exponent / row_total
    attended = jnp.einsum(
        E1, soft_weights, head_split(values_all, heads_here), precision=highest
    )
    return (attended.reshape(queries.shape), row_peak + jnp.log(row_total))


def attend_back(
    queries, keys_all, values_all, key_valid, heads_here, attended, log_total, grad_attended
):
    head_size = queries.shape[2] // heads_here
    scaling = 1.0 / math.sqrt(head_size)
    soft_weights = jnp.exp(score_block(queries, keys_all, key_valid, heads_here) - log_total)
    grad_heads = head_split(grad_attended, heads_here)
    grad_soft = jnp.einsum(
        E3, grad_heads, head_split(values_all, heads_here), precision=highest
    )
    row_delta = jnp.einsum(
        E4, grad_heads, head_split(attended, heads_here), precision=highest
    )
    grad_scores = soft_weights * (grad_soft - row_delta[..., None])
    grad_query = (
        jnp.einsum(
            E1, grad_scores, head_split(keys_all, heads_here), precision=highest
        )
        * scaling
    )
    grad_key = (
        jnp.einsum(
            E2, grad_scores, head_split(queries, heads_here), precision=highest
        )
        * scaling
    )
    grad_value = jnp.einsum(E2, soft_weights, grad_heads, precision=highest)
    return (
        grad_query.reshape(queries.shape),
        grad_key.reshape(keys_all.shape),
        grad_value.reshape(values_all.shape),
    )


def shards(
    hidden,
    text_states,
    bucket,
    timestep,
    gain_in,
    conv_first,
    time_weight,
    gain_mid,
    conv_second,
    gain_attn_norm,
    proj_in,
    gain_self,
    query_self,
    key_self,
    value_self,
    out_self,
    gain_cross,
    query_cross,
    key_cross,
    value_cross,
    out_cross,
    gain_ff,
    ff_in,
    ff_out,
    proj_out,
    cotangent,
):
    item_count, slot_count, channels = hidden.shape
    local_width = gain_mid.shape[0]
    local_groups = GROUPS * local_width // channels
    heads_here = local_width // HEAD_DIM
    height_count = lax.axis_size(H)
    width_ih = lax.axis_size(I) * lax.axis_size(H)
    offset = lax.axis_index(T) * local_width
    strip_rows, strip_width = grid_shape(bucket)
    cell_span = strip_rows * strip_width
    position = jnp.arange(slot_count, dtype=jnp.int32)
    valid_mask = position[None, :] < cell_span[:, None]
    valid_col = valid_mask[:, :, None].astype(jnp.float32)
    full_counts = (height_count * cell_span * (channels // GROUPS)).astype(jnp.float32)
    key_valid = jnp.tile(valid_mask, (1, height_count))
    text_valid = jnp.ones((item_count, text_states.shape[1]), dtype=bool)
    resnet_full = (
        lax.all_gather(gain_in, IH, axis=0, tiled=True),
        lax.all_gather(conv_first, IH, axis=2, tiled=True),
        lax.all_gather(time_weight, IH, axis=0, tiled=True),
        lax.all_gather(conv_second, IH, axis=3, tiled=True),
    )
    block_full = (
        lax.all_gather(proj_in, IH, axis=1, tiled=True),
        lax.all_gather(gain_self, IH, axis=0, tiled=True),
        lax.all_gather(query_self, IH, axis=0, tiled=True),
        lax.all_gather(key_self, IH, axis=0, tiled=True),
        lax.all_gather(value_self, IH, axis=0, tiled=True),
        lax.all_gather(out_self, IH, axis=1, tiled=True),
        lax.all_gather(gain_cross, IH, axis=0, tiled=True),
        lax.all_gather(query_cross, IH, axis=0, tiled=True),
        lax.all_gather(key_cross, IH, axis=0, tiled=True),
        lax.all_gather(value_cross, IH, axis=0, tiled=True),
        lax.all_gather(out_cross, IH, axis=1, tiled=True),
        lax.all_gather(gain_ff, IH, axis=0, tiled=True),
        lax.all_gather(ff_in, IH, axis=0, tiled=True),
        lax.all_gather(ff_out, IH, axis=1, tiled=True),
        lax.all_gather(proj_out, IH, axis=0, tiled=True),
    )
    gain_in_full, conv_first_full, time_full, conv_second_full = resnet_full
    (
        proj_in_full,
        gain_self_full,
        query_self_full,
        key_self_full,
        value_self_full,
        out_self_full,
        gain_cross_full,
        query_cross_full,
        key_cross_full,
        value_cross_full,
        out_cross_full,
        gain_ff_full,
        ff_in_full,
        ff_out_full,
        proj_out_full,
    ) = block_full
    source = hidden * valid_col
    mean_one, inv_one = group_stats(source, valid_col, GROUPS, full_counts)
    centred_one = (source - mean_one) * inv_one * valid_col
    norm_one = centred_one * gain_in_full
    act_one, silu_pull_one = jax.vjp(jax.nn.silu, norm_one)
    stack_one = neighbour_stack(act_one, strip_rows, strip_width)
    silu_features = jax.nn.silu(time_features(timestep, channels))
    time_term = jnp.dot(
        silu_features, time_full, precision=highest, preferred_element_type=jnp.float32
    )
    conv_one = (conv_apply(stack_one, conv_first_full) + time_term[:, None, :]) * valid_col
    mean_two, inv_two = group_stats(conv_one, valid_col, local_groups, full_counts)
    centred_two = (conv_one - mean_two) * inv_two * valid_col
    norm_two = centred_two * gain_mid
    act_two, silu_pull_two = jax.vjp(jax.nn.silu, norm_two)
    stack_two = neighbour_stack(act_two, strip_rows, strip_width)
    conv_two = tensor_sum(conv_apply(stack_two, conv_second_full)) * valid_col
    residual = source + conv_two
    residual_local = lax.dynamic_slice_in_dim(residual, offset, local_width, 2)
    mean_three, inv_three = group_stats(residual_local, valid_col, local_groups, full_counts)
    centred_three = (residual_local - mean_three) * inv_three * valid_col
    norm_three = centred_three * gain_attn_norm
    projected = tensor_sum(tokens_dot(norm_three, proj_in_full))
    normed_self, centred_self, inv_self = layer_norm(projected, gain_self_full)
    queries = tokens_dot(normed_self, query_self_full)
    keys_here = tokens_dot(normed_self, key_self_full)
    values_here = tokens_dot(normed_self, value_self_full)
    keys_all, values_all = (
        lax.all_gather(keys_here, H, axis=1, tiled=True),
        lax.all_gather(values_here, H, axis=1, tiled=True),
    )
    attn_self, total_self = attend(queries, keys_all, values_all, key_valid, heads_here)
    after_self = projected + tensor_sum(tokens_dot(attn_self, out_self_full))
    normed_cross, centred_cross, inv_cross = layer_norm(after_self, gain_cross_full)
    queries_cross = tokens_dot(normed_cross, query_cross_full)
    keys_text = tokens_dot(text_states, key_cross_full)
    values_text = tokens_dot(text_states, value_cross_full)
    attn_cross, total_cross = attend(queries_cross, keys_text, values_text, text_valid, heads_here)
    after_cross = after_self + tensor_sum(tokens_dot(attn_cross, out_cross_full))
    normed_ff, centred_ff, inv_ff = layer_norm(after_cross, gain_ff_full)
    hidden_ff = jnp.einsum(E6, normed_ff, ff_in_full, precision=highest)
    value_half = hidden_ff[:, :, 0]
    gate_act, gelu_pull = jax.vjp(exact_gelu, hidden_ff[:, :, 1])
    ff_act = value_half * gate_act
    after_ff = after_cross + tensor_sum(tokens_dot(ff_act, ff_out_full))
    output = (residual_local + tokens_dot(after_ff, proj_out_full)) * valid_col
    (
        proj_in_back,
        gain_self_back,
        query_self_back,
        key_self_back,
        value_self_back,
        out_self_back,
        gain_cross_back,
        query_cross_back,
        key_cross_back,
        value_cross_back,
        out_cross_back,
        gain_ff_back,
        ff_in_back,
        ff_out_back,
        proj_out_back,
    ) = block_full
    grad_local = cotangent * valid_col
    grad_proj_out = tokens_grad(after_ff, grad_local)
    grad_after_ff = tensor_sum(tokens_back(grad_local, proj_out_back))
    grad_ff_out = tokens_grad(ff_act, grad_after_ff)
    grad_ff_act = tokens_back(grad_after_ff, ff_out_back)
    grad_value_half = grad_ff_act * gate_act
    grad_gate_half = gelu_pull(grad_ff_act * value_half)[0]
    grad_hidden_ff = jnp.stack([grad_value_half, grad_gate_half], axis=2)
    grad_ff_in = jnp.einsum(E5, normed_ff, grad_hidden_ff, precision=highest)
    grad_normed_ff = tensor_sum(
        jnp.einsum(E7, grad_hidden_ff, ff_in_back, precision=highest)
    )
    back_ff, grad_gain_ff = layer_back(grad_normed_ff, centred_ff, inv_ff, gain_ff_back)
    grad_after_cross = grad_after_ff + back_ff
    grad_out_cross = tokens_grad(attn_cross, grad_after_cross)
    grad_attn_cross = tokens_back(grad_after_cross, out_cross_back)
    grad_queries_cross, grad_keys_text, grad_values_text = attend_back(
        queries_cross,
        keys_text,
        values_text,
        text_valid,
        heads_here,
        attn_cross,
        total_cross,
        grad_attn_cross,
    )
    grad_query_cross = tokens_grad(normed_cross, grad_queries_cross)
    grad_key_cross = tokens_grad(text_states, grad_keys_text)
    grad_value_cross = tokens_grad(text_states, grad_values_text)
    grad_normed_cross = tensor_sum(tokens_back(grad_queries_cross, query_cross_back))
    back_cross, grad_gain_cross = layer_back(
        grad_normed_cross, centred_cross, inv_cross, gain_cross_back
    )
    grad_after_self = grad_after_cross + back_cross
    grad_out_self = tokens_grad(attn_self, grad_after_self)
    grad_attn_self = tokens_back(grad_after_self, out_self_back)
    grad_queries, grad_keys_all, grad_values_all = attend_back(
        queries, keys_all, values_all, key_valid, heads_here, attn_self, total_self, grad_attn_self
    )
    grad_keys_here, grad_values_here = (
        lax.psum_scatter(grad_keys_all, H, scatter_dimension=1, tiled=True),
        lax.psum_scatter(grad_values_all, H, scatter_dimension=1, tiled=True),
    )
    grad_query_self = tokens_grad(normed_self, grad_queries)
    grad_key_self = tokens_grad(normed_self, grad_keys_here)
    grad_value_self = tokens_grad(normed_self, grad_values_here)
    grad_normed_self = tensor_sum(
        tokens_back(grad_queries, query_self_back)
        + tokens_back(grad_keys_here, key_self_back)
        + tokens_back(grad_values_here, value_self_back)
    )
    back_self, grad_gain_self = layer_back(grad_normed_self, centred_self, inv_self, gain_self_back)
    grad_projected = grad_after_self + back_self
    grad_proj_in = tokens_grad(norm_three, grad_projected)
    grad_norm_three = tokens_back(grad_projected, proj_in_back)
    back_three, grad_gain_attn = group_back(
        grad_norm_three,
        centred_three,
        inv_three,
        gain_attn_norm,
        valid_col,
        local_groups,
        full_counts,
    )
    grad_residual_local = grad_local + back_three
    block_grads = (
        lax.psum_scatter(grad_proj_in, IH, scatter_dimension=1, tiled=True),
        lax.psum_scatter(
            jnp.tile(grad_gain_attn, width_ih), IH, scatter_dimension=0, tiled=True
        ),
        lax.psum_scatter(grad_gain_self, IH, scatter_dimension=0, tiled=True),
        lax.psum_scatter(grad_query_self, IH, scatter_dimension=0, tiled=True),
        lax.psum_scatter(grad_key_self, IH, scatter_dimension=0, tiled=True),
        lax.psum_scatter(grad_value_self, IH, scatter_dimension=0, tiled=True),
        lax.psum_scatter(grad_out_self, IH, scatter_dimension=1, tiled=True),
        lax.psum_scatter(grad_gain_cross, IH, scatter_dimension=0, tiled=True),
        lax.psum_scatter(grad_query_cross, IH, scatter_dimension=0, tiled=True),
        lax.psum_scatter(grad_key_cross, IH, scatter_dimension=0, tiled=True),
        lax.psum_scatter(grad_value_cross, IH, scatter_dimension=0, tiled=True),
        lax.psum_scatter(grad_out_cross, IH, scatter_dimension=1, tiled=True),
        lax.psum_scatter(grad_gain_ff, IH, scatter_dimension=0, tiled=True),
        lax.psum_scatter(grad_ff_in, IH, scatter_dimension=0, tiled=True),
        lax.psum_scatter(grad_ff_out, IH, scatter_dimension=1, tiled=True),
        lax.psum_scatter(grad_proj_out, IH, scatter_dimension=0, tiled=True),
    )
    gain_in_back, conv_first_back, time_back, conv_second_back = resnet_full
    grad_residual = lax.all_gather(grad_residual_local, T, axis=2, tiled=True)
    grad_conv_second = conv_weight_grad(stack_two, grad_residual, conv_second_back.shape)
    stack_grad_two = neighbour_stack(grad_residual, strip_rows, strip_width)
    grad_act_two = conv_input_grad(stack_grad_two, conv_second_back)
    grad_norm_two = silu_pull_two(grad_act_two)[0]
    grad_conv_one, grad_gain_mid = group_back(
        grad_norm_two, centred_two, inv_two, gain_mid, valid_col, local_groups, full_counts
    )
    grad_time_term = jnp.sum(grad_conv_one, axis=1)
    grad_time_weight = jnp.einsum(E0, silu_features, grad_time_term, precision=highest)
    grad_conv_first = conv_weight_grad(stack_one, grad_conv_one, conv_first_back.shape)
    stack_grad_one = neighbour_stack(grad_conv_one, strip_rows, strip_width)
    grad_act_one = tensor_sum(conv_input_grad(stack_grad_one, conv_first_back))
    grad_norm_one = silu_pull_one(grad_act_one)[0]
    back_one, grad_gain_in = group_back(
        grad_norm_one, centred_one, inv_one, gain_in_back, valid_col, GROUPS, full_counts
    )
    grad_hidden = (grad_residual + back_one) * valid_col
    resnet_grads = (
        lax.psum_scatter(grad_gain_in, IH, scatter_dimension=0, tiled=True),
        lax.psum_scatter(grad_conv_first, IH, scatter_dimension=2, tiled=True),
        lax.psum_scatter(grad_time_weight, IH, scatter_dimension=0, tiled=True),
        lax.psum_scatter(
            jnp.tile(grad_gain_mid, width_ih), IH, scatter_dimension=0, tiled=True
        ),
        lax.psum_scatter(grad_conv_second, IH, scatter_dimension=3, tiled=True),
    )
    return (
        output,
        grad_hidden,
        resnet_grads[0],
        resnet_grads[1],
        resnet_grads[2],
        resnet_grads[3],
        resnet_grads[4],
        block_grads[1],
        block_grads[0],
        block_grads[2],
        block_grads[3],
        block_grads[4],
        block_grads[5],
        block_grads[6],
        block_grads[7],
        block_grads[8],
        block_grads[9],
        block_grads[10],
        block_grads[11],
        block_grads[12],
        block_grads[13],
        block_grads[14],
        block_grads[15],
    )


def mm(left, right, left_dim, right_dim):
    return lax.dot_general(
        left,
        right,
        (((left_dim,), (right_dim,)), ((), ())),
        precision=high,
        preferred_element_type=jnp.float32,
    )


def swap(values):
    return lax.ppermute(values, I, [(0, 1), (1, 0)])


def flip(values, step):
    return lax.ppermute(values, H, [(s, s ^ step) for s in range(4)])


def turn(values, step):
    return lax.ppermute(values, T, [(s, (s + step) % 4) for s in range(4)])


def z_pieces(values):
    return [values] + [turn(values, 4 - j) for j in (1, 2, 3)]


def total_of(pieces):
    return (pieces[0] + pieces[1]) + (pieces[2] + pieces[3])


def z_received(pieces):
    return [pieces[0]] + [turn(pieces[j], j) for j in (1, 2, 3)]


def z_all(values):
    return lax.all_to_all(values, T, 0, 0)


def z_spread(values):
    return z_all(jnp.broadcast_to(values[None], (4,) + values.shape))


def folded(values):
    values = jnp.pad(values, ((0, 3), (0, 0)))
    return jnp.concatenate([values[:40], values[40:]], axis=1)


def unfolded(values):
    return jnp.concatenate([values[:, :640], values[:37, 640:]], axis=0)


def h_collect(pieces):
    total = pieces[0]
    for j in (1, 2, 3):
        total = total + flip(pieces[j], j)
    return total


def h_sum(values):
    pair = values + flip(values, 1)
    return pair + flip(pair, 2)


def pick(values, index, axis=0):
    return lax.dynamic_index_in_dim(values, index, axis, keepdims=False)


def plane_sum(own):
    part = h_collect([own[j] for j in range(4)])
    pieces = [part] + [flip(part, j) for j in (1, 2, 3)]
    return pieces + [swap(piece) for piece in pieces], part


def plane_exchange(packed):
    return lax.all_to_all(packed, IH, 0, 0)


IMAGE_ROWS = 1152
TAP_ROWS = range(16, 1136, 160)


def halves(values):
    top = values.astype(jnp.bfloat16)
    return top, (values - top.astype(jnp.float32)).astype(jnp.bfloat16)


def dot_halves(left, right, left_dim, right_dim):
    def one(a, b):
        return lax.dot_general(
            a, b, (((left_dim,), (right_dim,)), ((), ())), preferred_element_type=jnp.float32
        )

    return one(left[0], right[0]) + (one(left[0], right[1]) + one(left[1], right[0]))


def marks_of(marks, b):
    return marks[2 * b], marks[2 * b + 1]


def row_mask(span, rows, columns):
    return (lax.broadcasted_iota(jnp.int32, (rows, columns), 0) < span).astype(jnp.float32)


def unpack_quarter(packed):
    rest = jnp.concatenate([packed[64:80, 32 * g : 32 * g + 32] for g in range(4)], axis=0)
    return jnp.concatenate([packed[:64], rest], axis=1)


def put_quarter(out, place, values, row=0):
    out[place, row : row + 64, :] = values[:, :128]
    for g in range(4):
        out[place, row + 64 : row + 80, 32 * g : 32 * g + 32] = values[
            16 * g : 16 * g + 16, 128:160
        ]


def unpack_strip(packed):
    rest = jnp.concatenate([packed[256:320, 64 * g : 64 * g + 64] for g in range(4)], axis=0)
    return jnp.concatenate([packed[:256], rest], axis=1)


def put_packed_strip(out, place, values):
    out[place, 0:256, :] = values[:, :256]
    for g in range(4):
        out[place, 256:320, 64 * g : 64 * g + 64] = values[64 * g : 64 * g + 64, 256:320]


def put_strip(image, b, strip, span, values):
    at = pl.multiple_of(margin + strip * span, 8)
    image[b, pl.ds(at, 240)] = values[:240]

    @pl.when(span == 256)
    def _():
        image[b, pl.ds(pl.multiple_of(at + 240, 8), 16)] = values[240:]


def put_cells(image, b, strip, span, q, values):
    at = pl.multiple_of(margin + strip * span + q * 64, 8)
    image[b, pl.ds(at, 48)] = values[:48]

    @pl.when((q < 3) | (span == 256))
    def _():
        image[b, pl.ds(pl.multiple_of(at + 48, 8), 16)] = values[48:]


def quarter_mask(span, q):
    row = lax.broadcasted_iota(jnp.int32, (64, 160), 0) + q * 64
    return (row < span).astype(jnp.float32)


def widen(wide, image, b, width, sign):
    channels = image.shape[2]
    width_f = width.astype(jnp.float32)
    for base in TAP_ROWS:
        row = lax.broadcasted_iota(jnp.int32, (160, channels), 0).astype(jnp.float32)
        cell = row + float(base - margin)
        column = cell - width_f * jnp.floor((cell + 0.5) / width_f)
        for j in range(3):
            step = sign * (j - 1)
            values = image[b, base + step : base + step + 160, :]
            if step < 0:
                values = jnp.where(column > 0.5, values, 0.0)
            if step > 0:
                values = jnp.where(column < width_f - 1.5, values, 0.0)
            wide[base : base + 160, j * channels : (j + 1) * channels] = values


def split_weight(weight, top, low):
    for k in range(3):
        rows = weight.shape[0] // 3
        first, second = halves(weight[k * rows : (k + 1) * rows, :])
        top[k * rows : (k + 1) * rows, :] = first
        low[k * rows : (k + 1) * rows, :] = second


def split_weight_turned(weight, top, low):
    for tap in range(9):
        first, second = halves(weight[160 * tap : 160 * tap + 160, :].T)
        top[320 * tap : 320 * tap + 320, :] = first
        low[320 * tap : 320 * tap + 320, :] = second


def conv_strip(wide, top, low, strip, span, width, sign):
    rows = top.shape[0] // 3
    total = None
    for i in range(3):
        at = pl.multiple_of(margin + strip * span + sign * (i - 1) * width, 8)
        taps = halves(wide[pl.ds(at, 256), :])
        part = dot_halves(
            taps, (top[i * rows : (i + 1) * rows, :], low[i * rows : (i + 1) * rows, :]), 1, 0
        )
        total = part if total is None else total + part
    return total * row_mask(span, 256, total.shape[1])


def group_rows(sums):
    channels = sums.shape[1]
    lane = lax.broadcasted_iota(jnp.int32, (1, channels), 1)
    result = jnp.zeros((1, channels), jnp.float32)
    for g in range(channels // 40):
        inside = (lane >= 40 * g) & (lane < 40 * g + 40)
        result = jnp.where(inside, jnp.sum(jnp.where(inside, sums, 0.0)), result)
    return result


def group_row_stats(total, squares, span):
    count = (span * 160).astype(jnp.float32)
    mean = group_rows(total) / count
    var = group_rows(squares) / count - mean * mean
    return mean, lax.rsqrt(var + norm_eps)


def column_sum(values):
    return jnp.sum(values, axis=0, keepdims=True)


def first_kernel(
    marks, source, gain, tau, weight, own, other, image, stats, wide, top, low, cells
):
    item, h = marks[4], marks[5]
    split_weight(weight, top, low)
    image[...] = jnp.zeros_like(image)
    for b, out in ((0, own), (1, other)):
        span, width = marks_of(marks, b)
        base = (item ^ b) * 4
        total = jnp.zeros((1, 160), jnp.float32)
        squares = jnp.zeros((1, 160), jnp.float32)
        for k in range(4):
            for q in range(4):
                values = unpack_quarter(source[base + k, 80 * q : 80 * q + 80, :])
                cells[k, 64 * q : 64 * q + 64, :] = values
                total = total + column_sum(values)
                squares = squares + column_sum(values * values)
        mean, inv = group_row_stats(total, squares, span)
        stats[b, 0:1, :] = mean
        stats[b, 1:2, :] = inv
        for k in range(4):
            norm = (cells[k] - mean) * inv * row_mask(span, 256, 160) * gain[...]
            put_strip(image, b, k, span, norm * jax.nn.sigmoid(norm))
        widen(wide, image, b, width, 1)
        added = tau[b : b + 1, :]

        def step(k, _):
            conv = conv_strip(wide, top, low, k, span, width, 1)
            put_packed_strip(out, k ^ h, conv + added * row_mask(span, 256, 320))
            return 0

        lax.fori_loop(0, 4, step, 0)


def put_quarters(outs, tile, place, t):
    for j in range(4):
        at = pl.multiple_of(lax.rem(t + j, 4) * 64, 8)
        put_quarter(outs[j], place, tile[pl.ds(at, 64), :])


def second_kernel(marks, *refs):
    strips, gain, weight = refs[:8], refs[8], refs[9]
    outs, image, stats = refs[10:14], refs[14], refs[15]
    wide, top, low, tile = refs[16:]
    item, h, t = marks[4], marks[5], marks[6]
    split_weight_turned(weight, top, low)
    image[...] = jnp.zeros_like(image)
    for b in range(2):
        span, width = marks_of(marks, b)
        total = jnp.zeros((1, 320), jnp.float32)
        squares = jnp.zeros((1, 320), jnp.float32)
        for j in range(4):
            values = unpack_strip(strips[4 * b + j][...])
            total = total + column_sum(values)
            squares = squares + column_sum(values * values)
        mean, inv = group_row_stats(total, squares, span)
        stats[b, 0:1, :] = mean
        stats[b, 1:2, :] = inv
        for j in range(4):
            values = unpack_strip(strips[4 * b + j][...])
            norm = (values - mean) * inv * row_mask(span, 256, 320) * gain[...]
            put_strip(image, b, h ^ j, span, norm * jax.nn.sigmoid(norm))
        widen(wide, image, b, width, 1)

        def step(k, _):
            tile[...] = conv_strip(wide, top, low, k, span, width, 1)
            put_quarters(outs, tile, (item ^ b) * 4 + k, t)
            return 0

        lax.fori_loop(0, 4, step, 0)


def second_back_kernel(marks, *refs):
    quarters, weight = refs[:4], refs[4]
    own, other, image = refs[5:8]
    wide, top, low = refs[8:]
    item, h, t = marks[4], marks[5], marks[6]
    split_weight(weight, top, low)
    image[...] = jnp.zeros_like(image)
    for b, out in ((0, own), (1, other)):
        span, width = marks_of(marks, b)

        def fill(k, _):
            for j in range(4):
                values = unpack_quarter(quarters[j][(item ^ b) * 4 + k])
                put_cells(image, b, k, span, lax.rem(t + j, 4), values)
            return 0

        lax.fori_loop(0, 4, fill, 0)
        widen(wide, image, b, width, -1)

        def step(k, _):
            put_packed_strip(out, k ^ h, conv_strip(wide, top, low, k, span, width, -1))
            return 0

        lax.fori_loop(0, 4, step, 0)


def first_back_kernel(marks, *refs):
    grads, strips, gain, stats, weight = refs[:8], refs[8:16], refs[16], refs[17], refs[18]
    outs, image, sums, grad_gain = refs[19:23], refs[23], refs[24], refs[25]
    wide, top, low, tile, scaled_at, centred_at = refs[26:]
    item, h, t = marks[4], marks[5], marks[6]
    split_weight_turned(weight, top, low)
    image[...] = jnp.zeros_like(image)
    gain_total = jnp.zeros((1, 320), jnp.float32)
    for b in range(2):
        span, width = marks_of(marks, b)
        mean, inv = stats[b, 0:1, :], stats[b, 1:2, :]
        first = jnp.zeros((1, 320), jnp.float32)
        second = jnp.zeros((1, 320), jnp.float32)
        for j in range(4):
            values = unpack_strip(strips[4 * b + j][...])
            centred = (values - mean) * inv * row_mask(span, 256, 320)
            norm = centred * gain[...]
            gate = jax.nn.sigmoid(norm)
            grad_norm = unpack_strip(grads[4 * b + j][...]) * gate * (1.0 + norm * (1.0 - gate))
            scaled = grad_norm * gain[...]
            first = first + column_sum(scaled)
            second = second + column_sum(scaled * centred)
            gain_total = gain_total + column_sum(grad_norm * centred)
            scaled_at[j] = scaled
            centred_at[j] = centred
        count = (span * 160).astype(jnp.float32)
        first = group_rows(first) / count
        second = group_rows(second) / count
        tau_total = jnp.zeros((1, 320), jnp.float32)
        for j in range(4):
            grad = inv * row_mask(span, 256, 320) * (
                scaled_at[j] - first - centred_at[j] * second
            )
            tau_total = tau_total + column_sum(grad)
            put_strip(image, b, h ^ j, span, grad)
        sums[b : b + 1, :] = tau_total
        widen(wide, image, b, width, -1)

        def step(k, _):
            tile[...] = conv_strip(wide, top, low, k, span, width, -1)
            put_quarters(outs, tile, (item ^ b) * 4 + k, t)
            return 0

        lax.fori_loop(0, 4, step, 0)
    grad_gain[...] = gain_total


def conv_weight_kernel(sign, marks, image, cells, out, wide):
    out[...] = jnp.zeros_like(out)
    for b in range(2):
        _, width = marks_of(marks, b)
        widen(wide, image, b, width, sign)
        for i in range(3):

            def step(c, _):
                at = pl.multiple_of(margin + c * 256 + sign * (i - 1) * width, 8)
                taps = halves(wide[pl.ds(at, 256), :].T)
                values = halves(cells[b, pl.ds(pl.multiple_of(margin + c * 256, 8), 256), :])
                part = dot_halves(taps, values, 1, 0)
                for j in range(3):
                    out[3 * i + j] += part[160 * j : 160 * j + 160]
                return 0

            lax.fori_loop(0, 4, step, 0)


def wide_halves(values):
    top, low = halves(values)
    return jnp.concatenate([top, top, low], axis=1)


def other_halves(values):
    top, low = halves(values)
    return jnp.concatenate([top, low, top], axis=1)


def dot_last(left, right):
    return lax.dot_general(
        left, right, (((1,), (1,)), ((), ())), preferred_element_type=jnp.float32
    )


def dot_pair(left, values):
    top, low = halves(values)
    both = jnp.dot(left[0], jnp.concatenate([top, low], axis=1), preferred_element_type=jnp.float32)
    return (both[:, :64] + both[:, 64:]) + jnp.dot(
        left[1], top, preferred_element_type=jnp.float32
    )


def scores_turned(marks, queries, pieces, head, j):
    at = 64 * head
    keys = pieces[j][:, at : at + 64]
    scores = dot_last(wide_halves(keys), other_halves(queries[:, at : at + 64])) * 0.125
    slot = lax.broadcasted_iota(jnp.int32, (256, 256), 0) + marks[6] * 64
    slot = jnp.where(slot >= 256, slot - 256, slot)
    return jnp.where(slot < marks[0], scores, masked_score)


def attend_kernel(marks, qkv, *refs):
    pieces, out, totals, held = refs[:4], refs[4], refs[5], refs[6]
    totals[...] = jnp.zeros_like(totals)
    for head in range(5):
        peak = None
        for j in range(4):
            scores = scores_turned(marks, qkv, pieces, head, j)
            held[256 * j : 256 * j + 256, :] = scores
            here = jnp.max(scores, axis=0, keepdims=True)
            peak = here if peak is None else jnp.maximum(peak, here)
        total = jnp.zeros((1, 256), jnp.float32)
        attended = jnp.zeros((64, 256), jnp.float32)
        for j in range(4):
            exponent = jnp.exp(held[256 * j : 256 * j + 256, :] - peak)
            total = total + column_sum(exponent)
            values = halves(pieces[j][:, 320 + 64 * head : 384 + 64 * head].T)
            first, second = halves(exponent)
            both = jnp.dot(
                jnp.concatenate(values, axis=0), first, preferred_element_type=jnp.float32
            )
            attended = attended + (
                (both[:64] + both[64:])
                + jnp.dot(values[0], second, preferred_element_type=jnp.float32)
            )
        out[:, 64 * head : 64 * head + 64] = (attended / total).T
        totals[head : head + 1, :] = peak + jnp.log(total)


def attend_back_kernel(marks, qkv, *refs):
    pieces, totals, attended, grad = refs[:4], refs[4], refs[5], refs[6]
    grad_query, outs = refs[7], refs[8:12]
    for head in range(5):
        at = 64 * head
        grad_out = grad[:, at : at + 64]
        queries = qkv[:, at : at + 64]
        delta = column_sum((grad_out * attended[:, at : at + 64]).T)
        total = totals[head : head + 1, :]
        grad_other = other_halves(grad_out)
        query_grad = jnp.zeros((64, 256), jnp.float32)
        for j in range(4):
            weights = jnp.exp(scores_turned(marks, qkv, pieces, head, j) - total)
            values = pieces[j][:, 320 + at : 384 + at]
            grad_scores = weights * (dot_last(wide_halves(values), grad_other) - delta)
            outs[j][:, 320 + at : 384 + at] = dot_pair(halves(weights), grad_out)
            first, second = halves(grad_scores)
            outs[j][:, at : at + 64] = dot_pair((first, second), queries) * 0.125
            keys = halves(pieces[j][:, at : at + 64].T)
            both = jnp.dot(
                jnp.concatenate(keys, axis=0), first, preferred_element_type=jnp.float32
            )
            query_grad = query_grad + (
                (both[:64] + both[64:])
                + jnp.dot(keys[0], second, preferred_element_type=jnp.float32)
            )
        grad_query[:, at : at + 64] = query_grad.T * 0.125


def pack_kernel(marks, values, out):
    for q in range(values.shape[0] // 64):
        for k in range(8):
            part = values[64 * q : 64 * q + 64, 160 * k : 160 * k + 160]
            put_quarter(out, k, part, 80 * q)


def unpack_kernel(marks, packed, plain):
    for k in range(8):
        plain[:, 160 * k : 160 * k + 160] = unpack_quarter(packed[k, 0:80, :])


def unpack_norm_kernel(marks, packed, gain, scaled, plain):
    for k in range(8):
        centred = unpack_quarter(packed[k, 0:80, :])
        mean = jnp.concatenate([packed[k, 80:81, :], packed[k, 81:82, 0:32]], axis=1)
        inv = jnp.concatenate([packed[k, 82:83, :], packed[k, 83:84, 0:32]], axis=1)
        at = slice(160 * k, 160 * k + 160)
        scaled[:, at] = centred * gain[:, at]
        plain[:, at] = centred * (1.0 / inv) + mean


def cotangent_kernel(marks, pieces, total, out, whole):
    total[...] = (pieces[0, :, :1280] + pieces[1, :, :1280]) + (
        pieces[2, :, :1280] + pieces[3, :, :1280]
    )
    for part in range(4):
        whole[:, 320 * part : 320 * part + 320] = pieces[part, :, 1280:1600]
    for k in range(8):
        put_quarter(out, k, whole[:, 160 * k : 160 * k + 160])


def third_kernel(marks, *refs):
    pieces, out, gain = refs[:4], refs[4], refs[5]
    for first in range(4):

        @pl.when(marks[6] == first)
        def _():
            for j in range(4):
                at = (first + j) % 4 * 320
                gain[:, at : at + 320] = pieces[j][160:161, 0:320]
                for m in range(3):
                    out[:, 1280 * m + at : 1280 * m + at + 320] = pieces[j][
                        0:160, 320 * m : 320 * m + 320
                    ]


def text_kernel(marks, pieces, rows, keys, values):
    for part in range(4):
        at = pl.multiple_of(lax.rem(part - marks[6] + 4, 4) * 64, 8)
        rows[pl.ds(at, 64), :] = pieces[part, 0:64, :]
        lanes = slice(320 * part, 320 * part + 320)
        keys[0:40, lanes] = pieces[part, 64:104, 0:320]
        values[0:40, lanes] = pieces[part, 64:104, 320:640]
        keys[40:77, lanes] = pieces[part, 64:101, 640:960]
        values[40:77, lanes] = pieces[part, 64:101, 960:1280]


def text_grad_kernel(marks, keys, values, *outs):
    for first in range(4):

        @pl.when(marks[6] == first)
        def _():
            for j in range(4):
                at = (first + j) % 4 * 320
                lanes = slice(at, at + 320)
                outs[j][:, 0:320] = keys[0:40, lanes]
                outs[j][:, 320:640] = values[0:40, lanes]
                outs[j][0:37, 640:960] = keys[40:77, lanes]
                outs[j][0:37, 960:1280] = values[40:77, lanes]
                outs[j][37:40, 640:1280] = jnp.zeros((3, 640), jnp.float32)


def rows_kernel(marks, *refs):
    pieces, out = refs[:4], refs[4]
    for j in range(4):
        at = pl.multiple_of(lax.rem(marks[6] + j, 4) * 64, 8)
        out[pl.ds(at, 64), :] = pieces[j][...]


def residual_kernel(marks, source, first, second, third, fourth, out, sums):
    t = marks[6]
    at = pl.multiple_of(t * 80, 8)
    sums[...] = jnp.zeros_like(sums)
    for b in range(2):
        for k in range(4):
            place = 4 * b + k
            packed = source[place, pl.ds(at, 80), :] + (
                (first[place] + second[place]) + (third[place] + fourth[place])
            )
            out[place] = packed
            values = unpack_quarter(packed)
            sums[2 * b : 2 * b + 1, :] += column_sum(values)
            sums[2 * b + 1 : 2 * b + 2, :] += column_sum(values * values)


def span_of_item(marks, b):
    return jnp.where(marks[4] == b, marks[0], marks[2])


def norm_kernel(marks, residual, first, second, third, fourth, out, stats):
    total = (first[...] + second[...]) + (third[...] + fourth[...])
    for b in range(2):
        span = span_of_item(marks, b)
        mean, inv = group_row_stats(
            total[2 * b : 2 * b + 1, :], total[2 * b + 1 : 2 * b + 2, :], span
        )
        stats[2 * b : 2 * b + 1, :] = mean
        stats[2 * b + 1 : 2 * b + 2, :] = inv
        for k in range(4):
            values = unpack_quarter(residual[4 * b + k])
            centred = (values - mean) * inv * quarter_mask(span, marks[6])
            put_quarter(out, 4 * b + k, centred)
            out[4 * b + k, 80:88, :] = jnp.zeros((8, 128), jnp.float32)
            for row, value in ((80, mean), (82, inv)):
                out[4 * b + k, row : row + 1, :] = value[:, :128]
                out[4 * b + k, row + 1 : row + 2, 0:32] = value[:, 128:]


def centred_of(marks, residual, stats, b, k):
    values = unpack_quarter(residual[4 * b + k])
    mean, inv = stats[2 * b : 2 * b + 1, :], stats[2 * b + 1 : 2 * b + 2, :]
    return (values - mean) * inv * quarter_mask(span_of_item(marks, b), marks[6])


def norm_sums_kernel(marks, grad, residual, stats, gain, sums):
    sums[...] = jnp.zeros_like(sums)
    for b in range(2):
        for k in range(4):
            centred = centred_of(marks, residual, stats, b, k)
            values = unpack_quarter(grad[4 * b + k])
            scaled = values * gain[...]
            sums[3 * b : 3 * b + 1, :] += column_sum(scaled)
            sums[3 * b + 1 : 3 * b + 2, :] += column_sum(scaled * centred)
            sums[3 * b + 2 : 3 * b + 3, :] += column_sum(values * centred)


def sum_in_order(pieces, t):
    total = None
    for part in range(4):
        j = lax.rem(part - t + 4, 4)
        value = jnp.where(
            j < 2,
            jnp.where(j == 0, pieces[0][...], pieces[1][...]),
            jnp.where(j == 2, pieces[2][...], pieces[3][...]),
        )
        total = value if total is None else total + value
    return total


def norm_back_kernel(marks, *refs):
    grad, residual, stats, gain, base = refs[:5]
    pieces, out, grad_gain = refs[5:9], refs[9], refs[10]
    total = sum_in_order(pieces, marks[6])
    grad_gain[...] = jnp.zeros_like(grad_gain)
    grad_gain[0:1, :] = total[2:3, :] + total[5:6, :]
    for b in range(2):
        span = span_of_item(marks, b)
        count = (span * 160).astype(jnp.float32)
        first = group_rows(total[3 * b : 3 * b + 1, :]) / count
        second = group_rows(total[3 * b + 1 : 3 * b + 2, :]) / count
        inv = stats[2 * b + 1 : 2 * b + 2, :]
        for k in range(4):
            centred = centred_of(marks, residual, stats, b, k)
            scaled = unpack_quarter(grad[4 * b + k]) * gain[...]
            values = inv * quarter_mask(span, marks[6]) * (scaled - first - centred * second)
            put_quarter(out, 4 * b + k, values + unpack_quarter(base[4 * b + k]))


def input_sums_kernel(marks, source, gain, stats, *refs):
    pieces, out, sums = refs[:4], refs[4], refs[5]
    at = pl.multiple_of(marks[6] * 80, 8)
    sums[...] = jnp.zeros_like(sums)
    for b in range(2):
        span = span_of_item(marks, b)
        mine = marks[4] ^ b
        mean, inv = stats[mine, 0:1, :], stats[mine, 1:2, :]
        for k in range(4):
            place = 4 * b + k
            values = unpack_quarter(source[place, pl.ds(at, 80), :])
            centred = (values - mean) * inv * quarter_mask(span, marks[6])
            norm = centred * gain[...]
            gate = jax.nn.sigmoid(norm)
            packed = (pieces[0][place] + pieces[1][place]) + (pieces[2][place] + pieces[3][place])
            grad = unpack_quarter(packed) * gate * (1.0 + norm * (1.0 - gate))
            put_quarter(out, place, grad)
            scaled = grad * gain[...]
            sums[3 * b : 3 * b + 1, :] += column_sum(scaled)
            sums[3 * b + 1 : 3 * b + 2, :] += column_sum(scaled * centred)
            sums[3 * b + 2 : 3 * b + 3, :] += column_sum(grad * centred)


def input_back_kernel(marks, grad, source, gain, stats, base, extra, *refs):
    pieces, out, grad_gain = refs[:4], refs[4], refs[5]
    at = pl.multiple_of(marks[6] * 80, 8)
    total = sum_in_order(pieces, marks[6])
    grad_gain[...] = jnp.zeros_like(grad_gain)
    grad_gain[0:1, :] = total[2:3, :] + total[5:6, :]
    for b in range(2):
        span = span_of_item(marks, b)
        count = (span * 160).astype(jnp.float32)
        first = group_rows(total[3 * b : 3 * b + 1, :]) / count
        second = group_rows(total[3 * b + 1 : 3 * b + 2, :]) / count
        mine = marks[4] ^ b
        mean, inv = stats[mine, 0:1, :], stats[mine, 1:2, :]
        for k in range(4):
            place = 4 * b + k
            keep = quarter_mask(span, marks[6])
            centred = (unpack_quarter(source[place, pl.ds(at, 80), :]) - mean) * inv * keep
            scaled = unpack_quarter(grad[place]) * gain[...]
            values = inv * keep * (scaled - first - centred * second)
            put_quarter(out, place, values + unpack_quarter(base[place]))
            out[place, 80:88, :] = extra[place]


def run_kernel(body, marks, inputs, outs, scratch, flops):
    in_smem = pl.BlockSpec(memory_space=pltpu.SMEM)
    in_vmem = pl.BlockSpec(memory_space=pltpu.VMEM)
    return pl.pallas_call(
        body,
        out_shape=[jax.ShapeDtypeStruct(shape, jnp.float32) for shape in outs],
        in_specs=[in_smem] + [in_vmem] * len(inputs),
        out_specs=[in_vmem] * len(outs),
        scratch_shapes=[pltpu.VMEM(shape, kind) for shape, kind in scratch],
        compiler_params=pltpu.CompilerParams(vmem_limit_bytes=56 * 1024 * 1024),
        cost_estimate=pl.CostEstimate(
            flops=flops, bytes_accessed=10 * 1024 * 1024, transcendentals=0
        ),
    )(marks, *inputs)


def weight_kernel(plan, *refs):
    count = 1 + max(which for block in plan for _, _, which in block)
    lefts, right, out = refs[:count], refs[count], refs[-1]
    tokens = right.shape[0]
    for number, block in enumerate(plan):

        @pl.when(pl.program_id(0) == number)
        def _():
            for begin, columns, which in block:
                top, low = halves(right[:, begin : begin + columns])
                if tokens <= 64:
                    stacked = jnp.concatenate([top, low, top], axis=0)
                for m in range(0, 1280, 256):
                    cells = lefts[which][:, m : m + 256].T
                    if tokens <= 64:
                        first, second = halves(cells)
                        first = jnp.concatenate([first, first, second], axis=1)
                        part = jnp.dot(first, stacked, preferred_element_type=jnp.float32)
                    else:
                        part = dot_halves(halves(cells), (top, low), 1, 0)
                    out[m : m + 256, begin : begin + columns] = part


def weight_grads(plan, lefts, right, first=0, blocks=None, into=None):
    tokens = right.shape[0]
    blocks = blocks or len(plan)
    in_specs = [pl.BlockSpec((tokens, 1280), lambda i: (0, 0))] * len(lefts)
    in_specs.append(pl.BlockSpec((tokens, 1280), lambda i: (0, i)))
    inputs, alias = (*lefts, right), {}
    if into is not None:
        in_specs.append(pl.BlockSpec(memory_space=pl.ANY))
        alias = {len(inputs): 0}
        inputs = (*inputs, into)
    return pl.pallas_call(
        functools.partial(weight_kernel, plan),
        out_shape=jax.ShapeDtypeStruct((1280, 1280 * blocks), jnp.float32),
        grid=(len(plan),),
        in_specs=in_specs,
        out_specs=pl.BlockSpec((1280, 1280), lambda i: (0, i + first)),
        input_output_aliases=alias,
        compiler_params=pltpu.CompilerParams(vmem_limit_bytes=48 * 1024 * 1024),
        cost_estimate=pl.CostEstimate(
            flops=6 * tokens * 1280 * 1280 * len(plan),
            bytes_accessed=7 * 1024 * 1024 * len(plan),
            transcendentals=0,
        ),
    )(*inputs)


def after(values, *events):
    return lax.optimization_barrier((values,) + events)[0]


def together(*values):
    return lax.optimization_barrier(values)


def small(body, marks, inputs, outs, scratch=()):
    return run_kernel(body, marks, inputs, outs, scratch, 4 * 1024 * 1024)


CONV_FLOPS = 6 * 2048 * 1440 * 320


def first_conv(marks, source, gain, tau, weight):
    f32, b16 = jnp.float32, jnp.bfloat16
    return run_kernel(
        first_kernel,
        marks,
        (source, gain, tau, weight),
        [(4, 320, 256), (4, 320, 256), (2, IMAGE_ROWS, 160), (2, 8, 160)],
        [
            ((IMAGE_ROWS, 480), f32),
            ((1440, 320), b16),
            ((1440, 320), b16),
            ((4, 256, 160), f32),
        ],
        CONV_FLOPS,
    )


def second_conv(marks, strips, gain, weight):
    f32, b16 = jnp.float32, jnp.bfloat16
    return run_kernel(
        second_kernel,
        marks,
        (*strips, gain, weight),
        [(8, 80, 128)] * 4 + [(2, IMAGE_ROWS, 320), (2, 8, 320)],
        [
            ((IMAGE_ROWS, 960), f32),
            ((2880, 160), b16),
            ((2880, 160), b16),
            ((256, 160), f32),
        ],
        CONV_FLOPS,
    )


def second_conv_back(marks, quarters, weight):
    f32, b16 = jnp.float32, jnp.bfloat16
    return run_kernel(
        second_back_kernel,
        marks,
        (*quarters, weight),
        [(4, 320, 256), (4, 320, 256), (2, IMAGE_ROWS, 160)],
        [((IMAGE_ROWS, 480), f32), ((1440, 320), b16), ((1440, 320), b16)],
        CONV_FLOPS,
    )


def first_conv_back(marks, grads, strips, gain, stats, weight):
    f32, b16 = jnp.float32, jnp.bfloat16
    return run_kernel(
        first_back_kernel,
        marks,
        (*grads, *strips, gain, stats, weight),
        [(8, 80, 128)] * 4 + [(2, IMAGE_ROWS, 320), (2, 320), (1, 320)],
        [
            ((IMAGE_ROWS, 960), f32),
            ((2880, 160), b16),
            ((2880, 160), b16),
            ((256, 160), f32),
            ((4, 256, 320), f32),
            ((4, 256, 320), f32),
        ],
        CONV_FLOPS,
    )


def conv_weight(marks, image, cells, sign):
    return run_kernel(
        functools.partial(conv_weight_kernel, sign),
        marks,
        (image, cells),
        [(9, 160, 320)],
        [((IMAGE_ROWS, 480), jnp.float32)],
        CONV_FLOPS,
    )[0]


def heads_of(values, count):
    return values.reshape(values.shape[0], count, HEAD_DIM)


def ein(form, left, right):
    return jnp.einsum(form, left, right, precision=high, preferred_element_type=jnp.float32)


def soft_attend(queries, keys, values, key_valid, count):
    scores = ein(QK, heads_of(queries, count), heads_of(keys, count)) * (1.0 / math.sqrt(HEAD_DIM))
    if key_valid is not None:
        scores = jnp.where(key_valid[None, None, :], scores, masked_score)
    exponent = jnp.exp(scores - jnp.max(scores, axis=-1, keepdims=True))
    weights = exponent / jnp.sum(exponent, axis=-1, keepdims=True)
    attended = ein(PV, weights, heads_of(values, count))
    return attended.reshape(queries.shape), weights


def soft_back(queries, keys, values, count, weights, attended, grad_out):
    scaling = 1.0 / math.sqrt(HEAD_DIM)
    grad_heads = heads_of(grad_out, count)
    grad_soft = ein(QK, grad_heads, heads_of(values, count))
    delta = jnp.sum(grad_heads * heads_of(attended, count), axis=-1).T
    grad_scores = weights * (grad_soft - delta[..., None])
    grad_query = ein(PV, grad_scores, heads_of(keys, count)) * scaling
    grad_key = ein(PQ, grad_scores, heads_of(queries, count)) * scaling
    grad_value = ein(PQ, weights, grad_heads)
    return (
        grad_query.reshape(queries.shape),
        grad_key.reshape(keys.shape),
        grad_value.reshape(values.shape),
    )


def layer_grad(grad_out, centred, inv_std, gain_vector):
    scaled = grad_out * gain_vector
    grad_in = inv_std * (
        scaled
        - jnp.mean(scaled, axis=-1, keepdims=True)
        - centred * jnp.mean(scaled * centred, axis=-1, keepdims=True)
    )
    return grad_in, jnp.sum(grad_out * centred, axis=0)


def layer_forward(values, gain_vector):
    mean_val = jnp.mean(values, axis=-1, keepdims=True)
    var_val = jnp.mean(values * values, axis=-1, keepdims=True) - mean_val * mean_val
    inv_std = lax.rsqrt(var_val + norm_eps)
    centred = (values - mean_val) * inv_std
    return centred * gain_vector, centred, inv_std


def gather_plane(block):
    return lax.all_gather(block, IH, axis=0, tiled=True)


def scatter_plane(block):
    return lax.psum_scatter(block, IH, scatter_dimension=0, tiled=True)


def grid_cells(bucket):
    strip_rows, strip_width = grid_shape(bucket)
    return strip_rows * strip_width


def fast_shards(
    hidden,
    text_states,
    bucket,
    timestep,
    gain_in,
    conv_first,
    time_weight,
    gain_mid,
    conv_second,
    gain_attn_norm,
    proj_in,
    gain_self,
    query_self,
    key_self,
    value_self,
    out_self,
    gain_cross,
    query_cross,
    key_cross,
    value_cross,
    out_cross,
    gain_ff,
    ff_in,
    ff_out,
    proj_out,
    cotangent,
):
    item, h, t = lax.axis_index(I), lax.axis_index(H), lax.axis_index(T)
    block = item * 4 + h
    width, wide = 160, 320
    channels = 1280

    def rows_of(values):
        return [values[64 * j : 64 * j + 64] for j in range(4)]

    own_span = grid_cells(bucket[0])
    slot = jnp.arange(256, dtype=jnp.int32)
    own_valid = (slot < own_span).astype(jnp.float32)[:, None]
    both = jnp.stack([bucket[0], timestep[0]]).astype(jnp.float32)
    both_other = swap(both)
    times = jnp.stack([both[1], both_other[1]])
    other_rows, other_width = grid_shape(both_other[0].astype(jnp.int32))
    own_rows, own_width = grid_shape(bucket[0])
    marks = jnp.stack(
        [own_span, own_width, other_rows * other_width, other_width, item, h, t]
    ).astype(jnp.int32)

    (source,) = small(pack_kernel, marks, (hidden[0] * own_valid,), [(8, 320, 128)])
    source = plane_exchange(source)
    gains = jnp.stack([gain_self, gain_cross, gain_ff], axis=1)
    attn_full = gather_plane(
        jnp.concatenate(
            [
                query_self,
                key_self,
                value_self,
                proj_out,
                out_self.T,
                jnp.pad(gains, ((0, 0), (0, 125))),
            ],
            axis=1,
        )
    )
    qkv_full = attn_full[:, :960]
    proj_out_full = attn_full[:, 960:1280]
    out_self_full = attn_full[:, 1280:1600]
    gain_rows = attn_full[:, 1600:1603].T
    gain_self_full, gain_cross_full, gain_ff_full = (gain_rows[k : k + 1] for k in range(3))

    own_third = jnp.concatenate([proj_in.T, query_cross, out_cross.T], axis=1)
    own_third = jnp.concatenate(
        [own_third, jnp.pad(gain_attn_norm[None, :], ((0, 7), (0, 640)))], axis=0
    )
    third_pieces = [own_third, turn(own_third, 3), turn(own_third[:, :512], 2), turn(own_third, 1)]

    features = jax.nn.silu(time_features(times, channels))
    own_features = lax.dynamic_slice_in_dim(features, block * width, width, 1)
    tau = mm(own_features, time_weight, 1, 0)
    second_weight = conv_second.transpose(0, 1, 3, 2).reshape(9 * width, wide)
    own_one, other_one, image_one, stats_one = first_conv(
        marks, source, gain_in[None, :], tau, conv_first.reshape(9 * width, wide)
    )
    own_one, other_one, *third_pieces = together(own_one, other_one, *third_pieces)
    own_one = own_one + swap(other_one)
    strips_one, part = plane_sum(own_one)
    third_rest = turn(own_third[:, 512:], 2)
    third_pieces[2] = jnp.concatenate([third_pieces[2], third_rest], axis=1)
    third, gain_attn_full = small(
        third_kernel, marks, after(third_pieces, part), [(160, 3840), (1, channels)]
    )
    third_full = gather_plane(third)
    proj_in_full = third_full[:, :1280]
    query_cross_full = third_full[:, 1280:2560]
    out_cross_full = third_full[:, 2560:]
    ff_block = jnp.concatenate([ff_in.reshape(160, 2560), ff_out.T], axis=1)
    ff_full = gather_plane(after(ff_block, third))
    ff_in_full = ff_full[:, :2560]
    ff_out_full = ff_full[:, 2560:]
    cot = after(cotangent[0] * own_valid, own_one)
    grad_ff_part = mm(cot, proj_out_full, 1, 1)
    cot_pieces = z_all(jnp.concatenate([grad_ff_part, cot], axis=1).reshape(4, 64, channels + wide))
    *strips_one, cot_pieces = together(*strips_one, cot_pieces)

    *conv_two, image_two, stats_two = second_conv(
        marks, strips_one, gain_mid[None, :], second_weight
    )
    conv_two_pieces = z_received(conv_two)

    event = conv_two[0]
    grad_after_ff, cot_packed = small(
        cotangent_kernel,
        marks,
        (after(cot_pieces, event),),
        [(64, channels), (8, 80, 128)],
        [((64, channels), jnp.float32)],
    )
    cot_q = plane_exchange(cot_packed)
    text_here = after(text_states[0], event)
    text_own = lax.dynamic_slice_in_dim(text_here, block * 256, 256, 1)
    text_other = swap(lax.dynamic_slice_in_dim(text_here, ((1 - item) * 4 + h) * 256, 256, 1))
    text_weight = jnp.concatenate([key_cross, value_cross], axis=1)
    text_part = mm(text_own, text_weight, 1, 0) + swap(mm(text_other, text_weight, 1, 0))

    residual_q, sums = small(
        residual_kernel, marks, (source, *conv_two_pieces), [(8, 80, 128), (8, width)]
    )
    centred_three, stats_three = small(
        norm_kernel, marks, (residual_q, *z_pieces(sums)), [(8, 88, 128), (8, width)]
    )
    norm_three, residual_s = small(
        unpack_norm_kernel,
        marks,
        (plane_exchange(centred_three), gain_attn_full),
        [(64, channels), (64, channels)],
    )
    projected = mm(norm_three, proj_in_full, 1, 1)

    normed_self, centred_self, inv_self = layer_forward(projected, gain_self_full)
    normed_pieces = z_pieces(normed_self)
    text_sum = h_sum(after(text_part, normed_self))
    *normed_pieces, text_sum, cot_q = together(*normed_pieces, text_sum, cot_q)
    normed_self_all = jnp.concatenate(normed_pieces, axis=0)
    qkv = mm(normed_self_all, qkv_full, 1, 0)
    own_kv = qkv[:, wide:]
    kv_pieces = [own_kv] + [flip(own_kv, j) for j in (1, 2, 3)]
    text_sum, grad_here = after((text_sum, grad_after_ff), own_kv)
    side_pieces = z_spread(jnp.concatenate([grad_here, folded(text_sum)], axis=0))
    *kv_pieces, side_pieces = together(*kv_pieces, side_pieces)
    attn_self, totals_self = small(
        attend_kernel,
        marks,
        (qkv, *kv_pieces),
        [(256, wide), (8, 256)],
        [((1024, 256), jnp.float32)],
    )
    self_part = mm(attn_self, out_self_full, 1, 1)
    self_pieces = z_received(rows_of(self_part))
    self_sum = total_of(self_pieces)
    event = self_pieces[1]
    grad_after_ff_all, keys_text, values_text = small(
        text_kernel,
        marks,
        (after(side_pieces, event),),
        [(256, channels), (77, channels), (77, channels)],
    )
    grad_ff_act = mm(grad_after_ff_all, ff_out_full, 1, 0)
    self_sum, grad_ff_act, keys_text, values_text = together(
        self_sum, grad_ff_act, keys_text, values_text
    )
    after_self = projected + self_sum

    normed_cross, centred_cross, inv_cross = layer_forward(after_self, gain_cross_full)
    queries_cross = mm(normed_cross, query_cross_full, 1, 0)
    attn_cross, weights_cross = soft_attend(queries_cross, keys_text, values_text, None, 20)
    after_cross = after_self + mm(attn_cross, out_cross_full, 1, 1)

    normed_ff, centred_ff, inv_ff = layer_forward(after_cross, gain_ff_full)
    normed_ff_all = jnp.concatenate(z_pieces(normed_ff), axis=0)
    hidden_ff = mm(normed_ff_all, ff_in_full, 1, 0)
    value_half, gate_half = hidden_ff[:, :channels], hidden_ff[:, channels:]
    phi = 0.5 * (1.0 + lax.erf(gate_half * math.sqrt(0.5)))
    slope = phi + gate_half * jnp.exp(-0.5 * gate_half * gate_half) * (1.0 / math.sqrt(2 * math.pi))
    gate_act = gate_half * phi
    ff_act = value_half * gate_act
    grad_value = grad_ff_act * gate_act
    grad_gate = grad_ff_act * value_half * slope
    grad_hidden_ff = jnp.concatenate([grad_value, grad_gate], axis=1)
    grad_normed_part = mm(grad_hidden_ff, ff_in_full, 1, 1)
    normed_pieces = z_received(rows_of(grad_normed_part))
    grad_normed_ff = total_of(normed_pieces)
    ff_right = jnp.concatenate(after([grad_hidden_ff, ff_act], normed_pieces[1]), axis=1)
    ff_grads = weight_grads(
        (((0, 1280, 0),), ((0, 1280, 0),), ((0, 1280, 1),)),
        (normed_ff_all, grad_after_ff_all),
        ff_right,
        0,
        5,
    )
    out_part = mm(after(ff_act, normed_pieces[1]), ff_out_full, 1, 1)
    grad_normed_ff, ff_grads, out_part = together(grad_normed_ff, ff_grads, out_part)

    back_ff, grad_gain_ff = layer_grad(grad_normed_ff, centred_ff, inv_ff, gain_ff_full)
    grad_after_cross = grad_after_ff + back_ff
    grad_attn_cross = mm(grad_after_cross, out_cross_full, 1, 0)
    grad_queries_cross, grad_keys_text, grad_values_text = soft_back(
        queries_cross, keys_text, values_text, 20, weights_cross, attn_cross, grad_attn_cross
    )
    grad_normed_cross = mm(grad_queries_cross, query_cross_full, 1, 1)
    back_cross, grad_gain_cross = layer_grad(
        grad_normed_cross, centred_cross, inv_cross, gain_cross_full
    )
    grad_after_self = grad_after_cross + back_cross
    grad_pieces = z_pieces(grad_after_self)
    cross_right = after((grad_queries_cross, attn_cross), grad_pieces[1])
    cross_right = jnp.concatenate(
        [side[:, wide * k : wide * k + wide] for k in range(4) for side in cross_right], axis=1
    )
    cross_grads = weight_grads(
        (((0, 320, 0), (320, 320, 1), (640, 320, 0), (960, 320, 1)),) * 2,
        (normed_cross, grad_after_cross),
        cross_right,
        3,
        5,
        ff_grads,
    )
    *grad_pieces, cross_grads = together(*grad_pieces, cross_grads)
    out_turned = jnp.concatenate([out_part, out_part], axis=0)
    out_turned = lax.dynamic_slice_in_dim(out_turned, lax.rem(4 - t, 4) * 64, 256, 0)
    out_sum = z_all(after(out_turned, grad_after_self).reshape(4, 64, channels))
    ff_grads = scatter_plane(cross_grads)
    ff_grads, cross_grads = ff_grads[:, :3840], ff_grads[:, 3840:]

    grad_after_self_all = jnp.concatenate(grad_pieces, axis=0)
    grad_attn_self = mm(grad_after_self_all, out_self_full, 1, 0)
    grad_queries, *kv_pieces = small(
        attend_back_kernel,
        marks,
        (qkv, *kv_pieces, totals_self, attn_self, grad_attn_self),
        [(256, wide)] + [(256, 2 * wide)] * 4,
    )
    kv_pieces = kv_pieces[:1] + [flip(kv_pieces[j], j) for j in (1, 2, 3)]
    grad_kv = total_of(kv_pieces)
    grad_qkv = jnp.concatenate([grad_queries, grad_kv], axis=1)
    grad_normed_part = mm(grad_qkv, qkv_full, 1, 1)
    normed_pieces = z_received(rows_of(grad_normed_part))
    grad_normed_self = total_of(normed_pieces)
    text_grads = small(
        text_grad_kernel,
        marks,
        after((grad_keys_text, grad_values_text), normed_pieces[1]),
        [(40, channels)] * 4,
    )
    grad_normed_self, out_sum, *text_grads = together(grad_normed_self, out_sum, *text_grads)
    back_self, grad_gain_self = layer_grad(grad_normed_self, centred_self, inv_self, gain_self_full)
    grad_projected = grad_after_self + back_self
    grad_norm_three = mm(grad_projected, proj_in_full, 1, 0)

    (grad_three,) = small(pack_kernel, marks, (grad_norm_three,), [(8, 80, 128)])
    grad_three_q = plane_exchange(grad_three)
    out_sum = jnp.sum(after(out_sum, grad_three), axis=0)
    text_grads = total_of(z_received(after(text_grads, grad_three)))
    attn_right = jnp.concatenate(
        [
            jnp.concatenate([grad_qkv, attn_self], axis=1),
            jnp.pad(norm_three, ((0, 192), (0, 0))),
        ],
        axis=1,
    )
    attn_grads = weight_grads(
        (((0, 960, 0), (960, 320, 1)), ((0, 1280, 2),)),
        (
            normed_self_all,
            grad_after_self_all,
            jnp.pad(grad_projected, ((0, 192), (0, 0))),
        ),
        after(attn_right, grad_three),
    )
    grad_three_q, attn_grads, text_grads = together(grad_three_q, attn_grads, text_grads)
    attn_grads = scatter_plane(attn_grads)
    gain_block = lax.dynamic_slice_in_dim(gain_attn_full, block * width, width, 1)
    (sums,) = small(
        norm_sums_kernel, marks, (grad_three_q, residual_q, stats_three, gain_block), [(8, width)]
    )
    grad_residual_q, grad_gain_three = small(
        norm_back_kernel,
        marks,
        (grad_three_q, residual_q, stats_three, gain_block, cot_q, *z_pieces(sums)),
        [(8, 80, 128), (8, width)],
    )

    residual_pieces = z_pieces(grad_residual_q)
    text_grads = after(text_grads, grad_residual_q)
    text_grads = text_grads + flip(text_grads, 1)
    *residual_pieces, text_grads = together(*residual_pieces, text_grads)
    own_two, other_two, image_back = second_conv_back(marks, residual_pieces, second_weight)
    own_two = own_two + swap(other_two)
    grad_act_two, part = plane_sum(own_two)
    side = jnp.concatenate(
        [
            jnp.broadcast_to((after_cross + out_sum)[None], (4, 64, channels)),
            jnp.moveaxis(residual_s.reshape(64, 4, wide), 1, 0),
        ],
        axis=2,
    )
    gain_rows = jnp.stack([grad_gain_self, grad_gain_cross, grad_gain_ff])
    gain_rows = jnp.broadcast_to(jnp.pad(gain_rows, ((0, 5), (0, wide)))[None], (4, 8, 1600))
    side = z_all(after(jnp.concatenate([side, gain_rows], axis=1), own_two))
    side_here = after(side, part)
    after_ff_all = side_here[:, :64, :channels].reshape(256, channels)
    residual_all = side_here[:, :64, channels:].reshape(256, wide)
    gain_sums = jnp.sum(side_here[:, 64:67, :channels], axis=0)
    *grad_act_two, after_ff_all, gain_sums, residual_all = together(
        *grad_act_two, after_ff_all, gain_sums, residual_all
    )

    *grad_act_one, image_grad, grad_tau, grad_gain_mid = first_conv_back(
        marks,
        grad_act_two,
        strips_one,
        gain_mid[None, :],
        stats_two,
        conv_first.reshape(9 * width, wide),
    )
    grad_act_pieces = z_received(grad_act_one)
    image_grad, text_grads = after((image_grad, text_grads), grad_act_pieces[1])
    text_grads = text_grads + flip(text_grads, 2)
    grad_conv_first = conv_weight(marks, image_one, image_grad, 1)
    cross_cut = after(cross_grads, grad_act_pieces[1])
    cross_cut = [
        lax.dynamic_slice_in_dim(cross_cut, lax.rem(t + j, 4) * 640, 640, 1) for j in range(4)
    ]
    *grad_act_pieces, grad_conv_first, text_grads, cross_cut = together(
        *grad_act_pieces, grad_conv_first, text_grads, cross_cut
    )
    grad_conv_first = grad_conv_first.reshape(3, 3, width, wide)
    extra = jnp.concatenate(
        [
            jnp.broadcast_to(grad_gain_three[0], (8, 1, width)),
            jnp.moveaxis(gain_sums.reshape(3, 8, width), 1, 0),
        ],
        axis=1,
    )
    extra = jnp.concatenate(
        [extra[:, :, :128], jnp.pad(extra[:, :, 128:], ((0, 0), (0, 0), (0, 96)))], axis=1
    )
    grad_input_q, sums = small(
        input_sums_kernel,
        marks,
        (source, gain_in[None, :], stats_one, *grad_act_pieces),
        [(8, 80, 128), (8, width)],
    )
    cross_shares = total_of(z_received(after(cross_cut, grad_input_q)))
    moved, grad_gain_in = small(
        input_back_kernel,
        marks,
        (
            grad_input_q,
            source,
            gain_in[None, :],
            stats_one,
            grad_residual_q,
            extra,
            *z_pieces(sums),
        ),
        [(8, 88, 128), (8, width)],
    )
    received = plane_exchange(moved)
    text_grads, image_back, after_ff_here, attn_grads = after(
        (text_grads, image_back, after_ff_all, attn_grads), moved
    )
    proj_cut = attn_grads[:, 1280:].reshape(width, 4, wide)
    proj_share = total_of(z_received([pick(proj_cut, lax.rem(t + j, 4), 1) for j in range(4)]))
    text_other_grads = swap(text_grads)
    grad_proj_out = mm(after_ff_here, cot, 0, 0).reshape(2, 4, width, wide)
    grad_proj_own = pick(grad_proj_out, item) + swap(pick(grad_proj_out, 1 - item))
    grad_conv_second = conv_weight(marks, image_back, image_two, -1)
    received, cross_shares, proj_share, text_other_grads, grad_proj_own, grad_conv_second = together(
        received, cross_shares, proj_share, text_other_grads, grad_proj_own, grad_conv_second
    )
    grad_conv_second = grad_conv_second.reshape(3, 3, width, wide).transpose(0, 1, 3, 2)
    text_grads, text_other_grads = unfolded(text_grads), unfolded(text_other_grads)
    (grad_hidden,) = small(unpack_kernel, marks, (received,), [(64, channels)])
    hidden_pieces = z_pieces(grad_hidden)
    after_ff_all, grad_proj_own = after((after_ff_all, grad_proj_own), grad_hidden)
    grad_proj_out = h_collect([pick(grad_proj_own, h ^ j) for j in range(4)])
    output = residual_all + mm(after_ff_all, proj_out_full, 1, 0)
    output = output * own_valid
    grad_text_weight = mm(text_own, text_grads, 0, 0) + mm(text_other, text_other_grads, 0, 0)
    grad_time_weight = mm(own_features, grad_tau, 0, 0)
    (grad_hidden,) = small(rows_kernel, marks, hidden_pieces, [(256, channels)])
    extra = jnp.concatenate([received[:, 80:84, :], received[:, 84:88, :32]], axis=2)
    grad_gain_attn = lax.dynamic_slice_in_dim(extra[:, 0].reshape(channels), t * wide, wide, 0)
    gain_sums = jnp.sum(extra[:, 1:], axis=0)

    return (
        output[None],
        grad_hidden[None],
        grad_gain_in[0],
        grad_conv_first,
        grad_time_weight,
        grad_gain_mid[0],
        grad_conv_second,
        grad_gain_attn,
        proj_share.T,
        gain_sums[0],
        attn_grads[:, :320],
        attn_grads[:, 320:640],
        attn_grads[:, 640:960],
        attn_grads[:, 960:1280].T,
        gain_sums[1],
        cross_shares[:, :320],
        grad_text_weight[:, :wide],
        grad_text_weight[:, wide:],
        cross_shares[:, 320:].T,
        gain_sums[2],
        ff_grads[:, :2560].reshape(width, 2, channels),
        ff_grads[:, 2560:].T,
        grad_proj_out,
    )


def solution(mesh):
    placed = (
        P(I, H, None),
        P(I, None, None),
        P(I),
        P(I),
        P(IH),
        P(None, None, IH, T),
        P(IH, T),
        P(T),
        P(None, None, T, IH),
        P(T),
        P(T, IH),
        P(IH),
        P(IH, T),
        P(IH, T),
        P(IH, T),
        P(T, IH),
        P(IH),
        P(IH, T),
        P(IH, T),
        P(IH, T),
        P(T, IH),
        P(IH),
        P(IH, None, T),
        P(T, IH),
        P(IH, T),
        P(I, H, T),
    )
    sizes = (mesh.shape[I], mesh.shape[H], mesh.shape[T])
    body = fast_shards if sizes == (2, 4, 4) else shards
    return jax.shard_map(
        body,
        mesh=mesh,
        in_specs=placed,
        out_specs=(
            P(I, H, T),
            P(I, H, None),
            P(IH),
            P(None, None, IH, T),
            P(IH, T),
            P(T),
            P(None, None, T, IH),
            P(T),
            P(T, IH),
            P(IH),
            P(IH, T),
            P(IH, T),
            P(IH, T),
            P(T, IH),
            P(IH),
            P(IH, T),
            P(IH, T),
            P(IH, T),
            P(T, IH),
            P(IH),
            P(IH, None, T),
            P(T, IH),
            P(IH, T),
        ),
        check_vma=False,
    )
```

```python
import functools
import math

import jax
import jax.numpy as jnp
from jax import lax
from jax.experimental import pallas as pl
from jax.experimental.pallas import tpu as pltpu
from jax.sharding import PartitionSpec as P

HEAD_DIM = 64
GROUPS = 32
EDGE = 48


highest = lax.Precision.HIGHEST
norm_eps = 1e-05
masked_score = -1e30
edge_margin = 56
high = lax.Precision.HIGH
margin = 64
I, H, T = "items", "height", "tensor"
IH = (I, H)
E0 = "bc,bn->cn"
E1 = "bhqk,bkhd->bqhd"
E2 = "bhqk,bqhd->bkhd"
E3 = "bqhd,bkhd->bhqk"
E4 = "bqhd,bqhd->bhq"
E5 = "bsc,bsjf->cjf"
E6 = "bsc,cjf->bsjf"
E7 = "bsjf,cjf->bsc"
E8 = "bsk,bsn->kn"
E9 = "bsk,kn->bsn"
E10 = "bsn,kn->bsk"
QK, PV, PQ = "qhd,khd->hqk", "hqk,khd->qhd", "hqk,qhd->khd"


def padded_2(block, sides, width):
    for axis, dim in sides:
        count = lax.axis_size(axis)
        forward = [(i, i + 1) for i in range(count - 1)]
        backward = [(target, source) for source, target in forward]
        low = lax.ppermute(
            lax.slice_in_dim(block, block.shape[dim] - width, None, axis=dim), axis, forward
        )
        high = lax.ppermute(lax.slice_in_dim(block, 0, width, axis=dim), axis, backward)
        block = jnp.concatenate([low, block, high], axis=dim)
    return block


def grid_shape(bucket):
    strip_rows = jnp.where(bucket == 0, 8, jnp.where(bucket == 1, 6, 5)).astype(jnp.int32)
    strip_width = jnp.where(bucket == 0, 32, jnp.where(bucket == 1, 40, 48)).astype(jnp.int32)
    return (strip_rows, strip_width)


def tokens_dot(values, weight):
    return jnp.einsum(E9, values, weight, precision=highest)


def tokens_back(grad_values, weight):
    return jnp.einsum(E10, grad_values, weight, precision=highest)


def tokens_grad(values, grad_values):
    return jnp.einsum(E8, values, grad_values, precision=highest)


def tensor_sum(values):
    return lax.psum(values, T)


def expand_groups(stat, size_group):
    return jnp.repeat(stat, size_group, axis=1)[:, None, :]


def group_stats(values, valid_col, group_count, counts):
    item_count, slot_count, channels = values.shape
    size_group = channels // group_count
    grouped = (values * valid_col).reshape(item_count, slot_count, group_count, size_group)
    sum_values = jnp.sum(grouped, axis=(1, 3))
    sum_squares = jnp.sum(grouped * grouped, axis=(1, 3))
    sum_values, sum_squares = lax.psum((sum_values, sum_squares), H)
    mean_val = sum_values / counts[:, None]
    var_val = sum_squares / counts[:, None] - mean_val * mean_val
    return (
        expand_groups(mean_val, size_group),
        expand_groups(lax.rsqrt(var_val + norm_eps), size_group),
    )


def group_back(grad_out, centred, inv_std, gain_vector, valid_col, group_count, counts):
    item_count, slot_count, channels = grad_out.shape
    size_group = channels // group_count
    scaled = grad_out * gain_vector * valid_col
    sum_first = jnp.sum(
        scaled.reshape(item_count, slot_count, group_count, size_group), axis=(1, 3)
    )
    sum_second = jnp.sum(
        (scaled * centred).reshape(item_count, slot_count, group_count, size_group), axis=(1, 3)
    )
    sum_first, sum_second = lax.psum((sum_first, sum_second), H)
    mean_first = expand_groups(sum_first / counts[:, None], size_group)
    mean_second = expand_groups(sum_second / counts[:, None], size_group)
    grad_in = inv_std * (scaled - mean_first - centred * mean_second) * valid_col
    return (grad_in, jnp.sum(grad_out * centred, axis=(0, 1)))


def layer_norm(values, gain_vector):
    mean_val = jnp.mean(values, axis=-1, keepdims=True)
    var_val = jnp.mean(values * values, axis=-1, keepdims=True) - mean_val * mean_val
    inv_std = lax.rsqrt(var_val + norm_eps)
    centred = (values - mean_val) * inv_std
    return (centred * gain_vector, centred, inv_std)


def layer_back(grad_out, centred, inv_std, gain_vector):
    scaled = grad_out * gain_vector
    grad_in = inv_std * (
        scaled
        - jnp.mean(scaled, axis=-1, keepdims=True)
        - centred * jnp.mean(scaled * centred, axis=-1, keepdims=True)
    )
    return (grad_in, jnp.sum(grad_out * centred, axis=(0, 1)))


def edge_rows(values, strip_rows, strip_width):
    item_count, slot_count, channels = values.shape
    position = jnp.arange(EDGE, dtype=jnp.int32)

    def edge_one_item(item_vals, rows_here, width_here):
        keep_mask = (position < width_here)[:, None].astype(jnp.float32)
        padded = jnp.concatenate([item_vals, jnp.zeros((EDGE, channels), jnp.float32)], axis=0)
        top_row = item_vals[:EDGE] * keep_mask
        bottom_row = (
            lax.dynamic_slice_in_dim(padded, (rows_here - 1) * width_here, EDGE, 0) * keep_mask
        )
        return jnp.stack([top_row, bottom_row])

    return jax.vmap(edge_one_item)(values, strip_rows, strip_width)


def neighbour_stack(values, strip_rows, strip_width):
    edge_pair = edge_rows(values, strip_rows, strip_width)
    beside_all = padded_2(edge_pair, ((H, 1),), 1)
    item_count, slot_count, channels = values.shape
    position = jnp.arange(slot_count, dtype=jnp.int32)

    def neighbour_one_item(item_vals, item_around, rows_here, width_here):
        cell_span = rows_here * width_here
        extended = jnp.zeros((2 * edge_margin + slot_count, channels), jnp.float32)
        extended = lax.dynamic_update_slice_in_dim(
            extended, item_around[0], edge_margin - width_here, 0
        )
        extended = lax.dynamic_update_slice_in_dim(extended, item_vals, edge_margin, 0)
        extended = lax.dynamic_update_slice_in_dim(
            extended, item_around[3], edge_margin + cell_span, 0
        )
        column = position % width_here
        shifted_list = []
        for row_step in (-1, 0, 1):
            for col_step in (-1, 0, 1):
                shifted = lax.dynamic_slice_in_dim(
                    extended, edge_margin + row_step * width_here + col_step, slot_count, 0
                )
                keep_mask = (
                    (column + col_step >= 0)
                    & (column + col_step < width_here)
                    & (position < cell_span)
                )
                shifted_list.append(shifted * keep_mask[:, None].astype(jnp.float32))
        return jnp.stack(shifted_list, axis=1)

    return jax.vmap(neighbour_one_item)(values, beside_all, strip_rows, strip_width)


def conv_apply(neighbours, weight):
    item_count, slot_count = (neighbours.shape[0], neighbours.shape[1])
    flattened = neighbours.reshape(item_count, slot_count, -1)
    return tokens_dot(flattened, weight.reshape(-1, weight.shape[3]))


def conv_input_grad(neighbours_grad, weight):
    flipped = jnp.transpose(weight[::-1, ::-1], (0, 1, 3, 2))
    return conv_apply(neighbours_grad, flipped)


def conv_weight_grad(neighbours, grad_out, weight_shape):
    flattened = neighbours.reshape(neighbours.shape[0], neighbours.shape[1], -1)
    return tokens_grad(flattened, grad_out).reshape(weight_shape)


def time_features(timestep, channels):
    half_width = channels // 2
    frequency = jnp.exp(-math.log(10000.0) * jnp.arange(half_width, dtype=jnp.float32) / half_width)
    angles = timestep.astype(jnp.float32)[:, None] * frequency[None, :]
    return jnp.concatenate([jnp.cos(angles), jnp.sin(angles)], axis=1)


def exact_gelu(values):
    return jax.nn.gelu(values, approximate=False)


def head_split(values, heads_here):
    return values.reshape(
        values.shape[0], values.shape[1], heads_here, values.shape[2] // heads_here
    )


def score_block(queries, keys_all, key_valid, heads_here):
    head_size = queries.shape[2] // heads_here
    scores = jnp.einsum(
        E3,
        head_split(queries, heads_here),
        head_split(keys_all, heads_here),
        precision=highest,
    ) * (1.0 / math.sqrt(head_size))
    return jnp.where(key_valid[:, None, None, :], scores, masked_score)


def attend(queries, keys_all, values_all, key_valid, heads_here):
    scores = score_block(queries, keys_all, key_valid, heads_here)
    row_peak = jnp.max(scores, axis=-1, keepdims=True)
    exponent = jnp.exp(scores - row_peak)
    row_total = jnp.sum(exponent, axis=-1, keepdims=True)
    soft_weights = exponent / row_total
    attended = jnp.einsum(
        E1, soft_weights, head_split(values_all, heads_here), precision=highest
    )
    return (attended.reshape(queries.shape), row_peak + jnp.log(row_total))


def attend_back(
    queries, keys_all, values_all, key_valid, heads_here, attended, log_total, grad_attended
):
    head_size = queries.shape[2] // heads_here
    scaling = 1.0 / math.sqrt(head_size)
    soft_weights = jnp.exp(score_block(queries, keys_all, key_valid, heads_here) - log_total)
    grad_heads = head_split(grad_attended, heads_here)
    grad_soft = jnp.einsum(
        E3, grad_heads, head_split(values_all, heads_here), precision=highest
    )
    row_delta = jnp.einsum(
        E4, grad_heads, head_split(attended, heads_here), precision=highest
    )
    grad_scores = soft_weights * (grad_soft - row_delta[..., None])
    grad_query = (
        jnp.einsum(
            E1, grad_scores, head_split(keys_all, heads_here), precision=highest
        )
        * scaling
    )
    grad_key = (
        jnp.einsum(
            E2, grad_scores, head_split(queries, heads_here), precision=highest
        )
        * scaling
    )
    grad_value = jnp.einsum(E2, soft_weights, grad_heads, precision=highest)
    return (
        grad_query.reshape(queries.shape),
        grad_key.reshape(keys_all.shape),
        grad_value.reshape(values_all.shape),
    )


def shards(
    hidden,
    text_states,
    bucket,
    timestep,
    gain_in,
    conv_first,
    time_weight,
    gain_mid,
    conv_second,
    gain_attn_norm,
    proj_in,
    gain_self,
    query_self,
    key_self,
    value_self,
    out_self,
    gain_cross,
    query_cross,
    key_cross,
    value_cross,
    out_cross,
    gain_ff,
    ff_in,
    ff_out,
    proj_out,
    cotangent,
):
    item_count, slot_count, channels = hidden.shape
    local_width = gain_mid.shape[0]
    local_groups = GROUPS * local_width // channels
    heads_here = local_width // HEAD_DIM
    height_count = lax.axis_size(H)
    width_ih = lax.axis_size(I) * lax.axis_size(H)
    offset = lax.axis_index(T) * local_width
    strip_rows, strip_width = grid_shape(bucket)
    cell_span = strip_rows * strip_width
    position = jnp.arange(slot_count, dtype=jnp.int32)
    valid_mask = position[None, :] < cell_span[:, None]
    valid_col = valid_mask[:, :, None].astype(jnp.float32)
    full_counts = (height_count * cell_span * (channels // GROUPS)).astype(jnp.float32)
    key_valid = jnp.tile(valid_mask, (1, height_count))
    text_valid = jnp.ones((item_count, text_states.shape[1]), dtype=bool)
    resnet_full = (
        lax.all_gather(gain_in, IH, axis=0, tiled=True),
        lax.all_gather(conv_first, IH, axis=2, tiled=True),
        lax.all_gather(time_weight, IH, axis=0, tiled=True),
        lax.all_gather(conv_second, IH, axis=3, tiled=True),
    )
    block_full = (
        lax.all_gather(proj_in, IH, axis=1, tiled=True),
        lax.all_gather(gain_self, IH, axis=0, tiled=True),
        lax.all_gather(query_self, IH, axis=0, tiled=True),
        lax.all_gather(key_self, IH, axis=0, tiled=True),
        lax.all_gather(value_self, IH, axis=0, tiled=True),
        lax.all_gather(out_self, IH, axis=1, tiled=True),
        lax.all_gather(gain_cross, IH, axis=0, tiled=True),
        lax.all_gather(query_cross, IH, axis=0, tiled=True),
        lax.all_gather(key_cross, IH, axis=0, tiled=True),
        lax.all_gather(value_cross, IH, axis=0, tiled=True),
        lax.all_gather(out_cross, IH, axis=1, tiled=True),
        lax.all_gather(gain_ff, IH, axis=0, tiled=True),
        lax.all_gather(ff_in, IH, axis=0, tiled=True),
        lax.all_gather(ff_out, IH, axis=1, tiled=True),
        lax.all_gather(proj_out, IH, axis=0, tiled=True),
    )
    gain_in_full, conv_first_full, time_full, conv_second_full = resnet_full
    (
        proj_in_full,
        gain_self_full,
        query_self_full,
        key_self_full,
        value_self_full,
        out_self_full,
        gain_cross_full,
        query_cross_full,
        key_cross_full,
        value_cross_full,
        out_cross_full,
        gain_ff_full,
        ff_in_full,
        ff_out_full,
        proj_out_full,
    ) = block_full
    source = hidden * valid_col
    mean_one, inv_one = group_stats(source, valid_col, GROUPS, full_counts)
    centred_one = (source - mean_one) * inv_one * valid_col
    norm_one = centred_one * gain_in_full
    act_one, silu_pull_one = jax.vjp(jax.nn.silu, norm_one)
    stack_one = neighbour_stack(act_one, strip_rows, strip_width)
    silu_features = jax.nn.silu(time_features(timestep, channels))
    time_term = jnp.dot(
        silu_features, time_full, precision=highest, preferred_element_type=jnp.float32
    )
    conv_one = (conv_apply(stack_one, conv_first_full) + time_term[:, None, :]) * valid_col
    mean_two, inv_two = group_stats(conv_one, valid_col, local_groups, full_counts)
    centred_two = (conv_one - mean_two) * inv_two * valid_col
    norm_two = centred_two * gain_mid
    act_two, silu_pull_two = jax.vjp(jax.nn.silu, norm_two)
    stack_two = neighbour_stack(act_two, strip_rows, strip_width)
    conv_two = tensor_sum(conv_apply(stack_two, conv_second_full)) * valid_col
    residual = source + conv_two
    residual_local = lax.dynamic_slice_in_dim(residual, offset, local_width, 2)
    mean_three, inv_three = group_stats(residual_local, valid_col, local_groups, full_counts)
    centred_three = (residual_local - mean_three) * inv_three * valid_col
    norm_three = centred_three * gain_attn_norm
    projected = tensor_sum(tokens_dot(norm_three, proj_in_full))
    normed_self, centred_self, inv_self = layer_norm(projected, gain_self_full)
    queries = tokens_dot(normed_self, query_self_full)
    keys_here = tokens_dot(normed_self, key_self_full)
    values_here = tokens_dot(normed_self, value_self_full)
    keys_all, values_all = (
        lax.all_gather(keys_here, H, axis=1, tiled=True),
        lax.all_gather(values_here, H, axis=1, tiled=True),
    )
    attn_self, total_self = attend(queries, keys_all, values_all, key_valid, heads_here)
    after_self = projected + tensor_sum(tokens_dot(attn_self, out_self_full))
    normed_cross, centred_cross, inv_cross = layer_norm(after_self, gain_cross_full)
    queries_cross = tokens_dot(normed_cross, query_cross_full)
    keys_text = tokens_dot(text_states, key_cross_full)
    values_text = tokens_dot(text_states, value_cross_full)
    attn_cross, total_cross = attend(queries_cross, keys_text, values_text, text_valid, heads_here)
    after_cross = after_self + tensor_sum(tokens_dot(attn_cross, out_cross_full))
    normed_ff, centred_ff, inv_ff = layer_norm(after_cross, gain_ff_full)
    hidden_ff = jnp.einsum(E6, normed_ff, ff_in_full, precision=highest)
    value_half = hidden_ff[:, :, 0]
    gate_act, gelu_pull = jax.vjp(exact_gelu, hidden_ff[:, :, 1])
    ff_act = value_half * gate_act
    after_ff = after_cross + tensor_sum(tokens_dot(ff_act, ff_out_full))
    output = (residual_local + tokens_dot(after_ff, proj_out_full)) * valid_col
    (
        proj_in_back,
        gain_self_back,
        query_self_back,
        key_self_back,
        value_self_back,
        out_self_back,
        gain_cross_back,
        query_cross_back,
        key_cross_back,
        value_cross_back,
        out_cross_back,
        gain_ff_back,
        ff_in_back,
        ff_out_back,
        proj_out_back,
    ) = block_full
    grad_local = cotangent * valid_col
    grad_proj_out = tokens_grad(after_ff, grad_local)
    grad_after_ff = tensor_sum(tokens_back(grad_local, proj_out_back))
    grad_ff_out = tokens_grad(ff_act, grad_after_ff)
    grad_ff_act = tokens_back(grad_after_ff, ff_out_back)
    grad_value_half = grad_ff_act * gate_act
    grad_gate_half = gelu_pull(grad_ff_act * value_half)[0]
    grad_hidden_ff = jnp.stack([grad_value_half, grad_gate_half], axis=2)
    grad_ff_in = jnp.einsum(E5, normed_ff, grad_hidden_ff, precision=highest)
    grad_normed_ff = tensor_sum(
        jnp.einsum(E7, grad_hidden_ff, ff_in_back, precision=highest)
    )
    back_ff, grad_gain_ff = layer_back(grad_normed_ff, centred_ff, inv_ff, gain_ff_back)
    grad_after_cross = grad_after_ff + back_ff
    grad_out_cross = tokens_grad(attn_cross, grad_after_cross)
    grad_attn_cross = tokens_back(grad_after_cross, out_cross_back)
    grad_queries_cross, grad_keys_text, grad_values_text = attend_back(
        queries_cross,
        keys_text,
        values_text,
        text_valid,
        heads_here,
        attn_cross,
        total_cross,
        grad_attn_cross,
    )
    grad_query_cross = tokens_grad(normed_cross, grad_queries_cross)
    grad_key_cross = tokens_grad(text_states, grad_keys_text)
    grad_value_cross = tokens_grad(text_states, grad_values_text)
    grad_normed_cross = tensor_sum(tokens_back(grad_queries_cross, query_cross_back))
    back_cross, grad_gain_cross = layer_back(
        grad_normed_cross, centred_cross, inv_cross, gain_cross_back
    )
    grad_after_self = grad_after_cross + back_cross
    grad_out_self = tokens_grad(attn_self, grad_after_self)
    grad_attn_self = tokens_back(grad_after_self, out_self_back)
    grad_queries, grad_keys_all, grad_values_all = attend_back(
        queries, keys_all, values_all, key_valid, heads_here, attn_self, total_self, grad_attn_self
    )
    grad_keys_here, grad_values_here = (
        lax.psum_scatter(grad_keys_all, H, scatter_dimension=1, tiled=True),
        lax.psum_scatter(grad_values_all, H, scatter_dimension=1, tiled=True),
    )
    grad_query_self = tokens_grad(normed_self, grad_queries)
    grad_key_self = tokens_grad(normed_self, grad_keys_here)
    grad_value_self = tokens_grad(normed_self, grad_values_here)
    grad_normed_self = tensor_sum(
        tokens_back(grad_queries, query_self_back)
        + tokens_back(grad_keys_here, key_self_back)
        + tokens_back(grad_values_here, value_self_back)
    )
    back_self, grad_gain_self = layer_back(grad_normed_self, centred_self, inv_self, gain_self_back)
    grad_projected = grad_after_self + back_self
    grad_proj_in = tokens_grad(norm_three, grad_projected)
    grad_norm_three = tokens_back(grad_projected, proj_in_back)
    back_three, grad_gain_attn = group_back(
        grad_norm_three,
        centred_three,
        inv_three,
        gain_attn_norm,
        valid_col,
        local_groups,
        full_counts,
    )
    grad_residual_local = grad_local + back_three
    block_grads = (
        lax.psum_scatter(grad_proj_in, IH, scatter_dimension=1, tiled=True),
        lax.psum_scatter(
            jnp.tile(grad_gain_attn, width_ih), IH, scatter_dimension=0, tiled=True
        ),
        lax.psum_scatter(grad_gain_self, IH, scatter_dimension=0, tiled=True),
        lax.psum_scatter(grad_query_self, IH, scatter_dimension=0, tiled=True),
        lax.psum_scatter(grad_key_self, IH, scatter_dimension=0, tiled=True),
        lax.psum_scatter(grad_value_self, IH, scatter_dimension=0, tiled=True),
        lax.psum_scatter(grad_out_self, IH, scatter_dimension=1, tiled=True),
        lax.psum_scatter(grad_gain_cross, IH, scatter_dimension=0, tiled=True),
        lax.psum_scatter(grad_query_cross, IH, scatter_dimension=0, tiled=True),
        lax.psum_scatter(grad_key_cross, IH, scatter_dimension=0, tiled=True),
        lax.psum_scatter(grad_value_cross, IH, scatter_dimension=0, tiled=True),
        lax.psum_scatter(grad_out_cross, IH, scatter_dimension=1, tiled=True),
        lax.psum_scatter(grad_gain_ff, IH, scatter_dimension=0, tiled=True),
        lax.psum_scatter(grad_ff_in, IH, scatter_dimension=0, tiled=True),
        lax.psum_scatter(grad_ff_out, IH, scatter_dimension=1, tiled=True),
        lax.psum_scatter(grad_proj_out, IH, scatter_dimension=0, tiled=True),
    )
    gain_in_back, conv_first_back, time_back, conv_second_back = resnet_full
    grad_residual = lax.all_gather(grad_residual_local, T, axis=2, tiled=True)
    grad_conv_second = conv_weight_grad(stack_two, grad_residual, conv_second_back.shape)
    stack_grad_two = neighbour_stack(grad_residual, strip_rows, strip_width)
    grad_act_two = conv_input_grad(stack_grad_two, conv_second_back)
    grad_norm_two = silu_pull_two(grad_act_two)[0]
    grad_conv_one, grad_gain_mid = group_back(
        grad_norm_two, centred_two, inv_two, gain_mid, valid_col, local_groups, full_counts
    )
    grad_time_term = jnp.sum(grad_conv_one, axis=1)
    grad_time_weight = jnp.einsum(E0, silu_features, grad_time_term, precision=highest)
    grad_conv_first = conv_weight_grad(stack_one, grad_conv_one, conv_first_back.shape)
    stack_grad_one = neighbour_stack(grad_conv_one, strip_rows, strip_width)
    grad_act_one = tensor_sum(conv_input_grad(stack_grad_one, conv_first_back))
    grad_norm_one = silu_pull_one(grad_act_one)[0]
    back_one, grad_gain_in = group_back(
        grad_norm_one, centred_one, inv_one, gain_in_back, valid_col, GROUPS, full_counts
    )
    grad_hidden = (grad_residual + back_one) * valid_col
    resnet_grads = (
        lax.psum_scatter(grad_gain_in, IH, scatter_dimension=0, tiled=True),
        lax.psum_scatter(grad_conv_first, IH, scatter_dimension=2, tiled=True),
        lax.psum_scatter(grad_time_weight, IH, scatter_dimension=0, tiled=True),
        lax.psum_scatter(
            jnp.tile(grad_gain_mid, width_ih), IH, scatter_dimension=0, tiled=True
        ),
        lax.psum_scatter(grad_conv_second, IH, scatter_dimension=3, tiled=True),
    )
    return (
        output,
        grad_hidden,
        resnet_grads[0],
        resnet_grads[1],
        resnet_grads[2],
        resnet_grads[3],
        resnet_grads[4],
        block_grads[1],
        block_grads[0],
        block_grads[2],
        block_grads[3],
        block_grads[4],
        block_grads[5],
        block_grads[6],
        block_grads[7],
        block_grads[8],
        block_grads[9],
        block_grads[10],
        block_grads[11],
        block_grads[12],
        block_grads[13],
        block_grads[14],
        block_grads[15],
    )


def mm(left, right, left_dim, right_dim):
    return lax.dot_general(
        left,
        right,
        (((left_dim,), (right_dim,)), ((), ())),
        precision=high,
        preferred_element_type=jnp.float32,
    )


def swap(values):
    return lax.ppermute(values, I, [(0, 1), (1, 0)])


def flip(values, step):
    return lax.ppermute(values, H, [(s, s ^ step) for s in range(4)])


def turn(values, step):
    return lax.ppermute(values, T, [(s, (s + step) % 4) for s in range(4)])


def z_pieces(values):
    return [values] + [turn(values, 4 - j) for j in (1, 2, 3)]


def total_of(pieces):
    return (pieces[0] + pieces[1]) + (pieces[2] + pieces[3])


def z_received(pieces):
    return [pieces[0]] + [turn(pieces[j], j) for j in (1, 2, 3)]


def z_all(values):
    return lax.all_to_all(values, T, 0, 0)


def z_spread(values):
    return z_all(jnp.broadcast_to(values[None], (4,) + values.shape))


def folded(values):
    values = jnp.pad(values, ((0, 3), (0, 0)))
    return jnp.concatenate([values[:40], values[40:]], axis=1)


def unfolded(values):
    return jnp.concatenate([values[:, :640], values[:37, 640:]], axis=0)


def h_collect(pieces):
    total = pieces[0]
    for j in (1, 2, 3):
        total = total + flip(pieces[j], j)
    return total


def h_sum(values):
    pair = values + flip(values, 1)
    return pair + flip(pair, 2)


def pick(values, index, axis=0):
    return lax.dynamic_index_in_dim(values, index, axis, keepdims=False)


def plane_sum(own):
    part = h_collect([own[j] for j in range(4)])
    pieces = [part] + [flip(part, j) for j in (1, 2, 3)]
    return pieces + [swap(piece) for piece in pieces], part


def plane_exchange(packed):
    return lax.all_to_all(packed, IH, 0, 0)


IMAGE_ROWS = 1152
TAP_ROWS = range(16, 1136, 160)


def halves(values):
    top = values.astype(jnp.bfloat16)
    return top, (values - top.astype(jnp.float32)).astype(jnp.bfloat16)


def dot_halves(left, right, left_dim, right_dim):
    def one(a, b):
        return lax.dot_general(
            a, b, (((left_dim,), (right_dim,)), ((), ())), preferred_element_type=jnp.float32
        )

    return one(left[0], right[0]) + (one(left[0], right[1]) + one(left[1], right[0]))


def marks_of(marks, b):
    return marks[2 * b], marks[2 * b + 1]


def row_mask(span, rows, columns):
    return (lax.broadcasted_iota(jnp.int32, (rows, columns), 0) < span).astype(jnp.float32)


def unpack_quarter(packed):
    rest = jnp.concatenate([packed[64:80, 32 * g : 32 * g + 32] for g in range(4)], axis=0)
    return jnp.concatenate([packed[:64], rest], axis=1)


def put_quarter(out, place, values, row=0):
    out[place, row : row + 64, :] = values[:, :128]
    for g in range(4):
        out[place, row + 64 : row + 80, 32 * g : 32 * g + 32] = values[
            16 * g : 16 * g + 16, 128:160
        ]


def unpack_strip(packed):
    rest = jnp.concatenate([packed[256:320, 64 * g : 64 * g + 64] for g in range(4)], axis=0)
    return jnp.concatenate([packed[:256], rest], axis=1)


def put_packed_strip(out, place, values):
    out[place, 0:256, :] = values[:, :256]
    for g in range(4):
        out[place, 256:320, 64 * g : 64 * g + 64] = values[64 * g : 64 * g + 64, 256:320]


def put_strip(image, b, strip, span, values):
    at = pl.multiple_of(margin + strip * span, 8)
    image[b, pl.ds(at, 240)] = values[:240]

    @pl.when(span == 256)
    def _():
        image[b, pl.ds(pl.multiple_of(at + 240, 8), 16)] = values[240:]


def put_cells(image, b, strip, span, q, values):
    at = pl.multiple_of(margin + strip * span + q * 64, 8)
    image[b, pl.ds(at, 48)] = values[:48]

    @pl.when((q < 3) | (span == 256))
    def _():
        image[b, pl.ds(pl.multiple_of(at + 48, 8), 16)] = values[48:]


def quarter_mask(span, q):
    row = lax.broadcasted_iota(jnp.int32, (64, 160), 0) + q * 64
    return (row < span).astype(jnp.float32)


def widen(wide, image, b, width, sign):
    channels = image.shape[2]
    width_f = width.astype(jnp.float32)
    for base in TAP_ROWS:
        row = lax.broadcasted_iota(jnp.int32, (160, channels), 0).astype(jnp.float32)
        cell = row + float(base - margin)
        column = cell - width_f * jnp.floor((cell + 0.5) / width_f)
        for j in range(3):
            step = sign * (j - 1)
            values = image[b, base + step : base + step + 160, :]
            if step < 0:
                values = jnp.where(column > 0.5, values, 0.0)
            if step > 0:
                values = jnp.where(column < width_f - 1.5, values, 0.0)
            wide[base : base + 160, j * channels : (j + 1) * channels] = values


def split_weight(weight, top, low):
    for k in range(3):
        rows = weight.shape[0] // 3
        first, second = halves(weight[k * rows : (k + 1) * rows, :])
        top[k * rows : (k + 1) * rows, :] = first
        low[k * rows : (k + 1) * rows, :] = second


def split_weight_turned(weight, top, low):
    for tap in range(9):
        first, second = halves(weight[160 * tap : 160 * tap + 160, :].T)
        top[320 * tap : 320 * tap + 320, :] = first
        low[320 * tap : 320 * tap + 320, :] = second


def conv_strip(wide, top, low, strip, span, width, sign):
    rows = top.shape[0] // 3
    total = None
    for i in range(3):
        at = pl.multiple_of(margin + strip * span + sign * (i - 1) * width, 8)
        taps = halves(wide[pl.ds(at, 256), :])
        part = dot_halves(
            taps, (top[i * rows : (i + 1) * rows, :], low[i * rows : (i + 1) * rows, :]), 1, 0
        )
        total = part if total is None else total + part
    return total * row_mask(span, 256, total.shape[1])


def group_rows(sums):
    channels = sums.shape[1]
    lane = lax.broadcasted_iota(jnp.int32, (1, channels), 1)
    result = jnp.zeros((1, channels), jnp.float32)
    for g in range(channels // 40):
        inside = (lane >= 40 * g) & (lane < 40 * g + 40)
        result = jnp.where(inside, jnp.sum(jnp.where(inside, sums, 0.0)), result)
    return result


def group_row_stats(total, squares, span):
    count = (span * 160).astype(jnp.float32)
    mean = group_rows(total) / count
    var = group_rows(squares) / count - mean * mean
    return mean, lax.rsqrt(var + norm_eps)


def column_sum(values):
    return jnp.sum(values, axis=0, keepdims=True)


def first_kernel(
    marks, source, gain, tau, weight, own, other, image, stats, wide, top, low, cells
):
    item, h = marks[4], marks[5]
    split_weight(weight, top, low)
    image[...] = jnp.zeros_like(image)
    for b, out in ((0, own), (1, other)):
        span, width = marks_of(marks, b)
        base = (item ^ b) * 4
        total = jnp.zeros((1, 160), jnp.float32)
        squares = jnp.zeros((1, 160), jnp.float32)
        for k in range(4):
            for q in range(4):
                values = unpack_quarter(source[base + k, 80 * q : 80 * q + 80, :])
                cells[k, 64 * q : 64 * q + 64, :] = values
                total = total + column_sum(values)
                squares = squares + column_sum(values * values)
        mean, inv = group_row_stats(total, squares, span)
        stats[b, 0:1, :] = mean
        stats[b, 1:2, :] = inv
        for k in range(4):
            norm = (cells[k] - mean) * inv * row_mask(span, 256, 160) * gain[...]
            put_strip(image, b, k, span, norm * jax.nn.sigmoid(norm))
        widen(wide, image, b, width, 1)
        added = tau[b : b + 1, :]

        def step(k, _):
            conv = conv_strip(wide, top, low, k, span, width, 1)
            put_packed_strip(out, k ^ h, conv + added * row_mask(span, 256, 320))
            return 0

        lax.fori_loop(0, 4, step, 0)


def put_quarters(outs, tile, place, t):
    for j in range(4):
        at = pl.multiple_of(lax.rem(t + j, 4) * 64, 8)
        put_quarter(outs[j], place, tile[pl.ds(at, 64), :])


def second_kernel(marks, *refs):
    strips, gain, weight = refs[:8], refs[8], refs[9]
    outs, image, stats = refs[10:14], refs[14], refs[15]
    wide, top, low, tile = refs[16:]
    item, h, t = marks[4], marks[5], marks[6]
    split_weight_turned(weight, top, low)
    image[...] = jnp.zeros_like(image)
    for b in range(2):
        span, width = marks_of(marks, b)
        total = jnp.zeros((1, 320), jnp.float32)
        squares = jnp.zeros((1, 320), jnp.float32)
        for j in range(4):
            values = unpack_strip(strips[4 * b + j][...])
            total = total + column_sum(values)
            squares = squares + column_sum(values * values)
        mean, inv = group_row_stats(total, squares, span)
        stats[b, 0:1, :] = mean
        stats[b, 1:2, :] = inv
        for j in range(4):
            values = unpack_strip(strips[4 * b + j][...])
            norm = (values - mean) * inv * row_mask(span, 256, 320) * gain[...]
            put_strip(image, b, h ^ j, span, norm * jax.nn.sigmoid(norm))
        widen(wide, image, b, width, 1)

        def step(k, _):
            tile[...] = conv_strip(wide, top, low, k, span, width, 1)
            put_quarters(outs, tile, (item ^ b) * 4 + k, t)
            return 0

        lax.fori_loop(0, 4, step, 0)


def second_back_kernel(marks, *refs):
    quarters, weight = refs[:4], refs[4]
    own, other, image = refs[5:8]
    wide, top, low = refs[8:]
    item, h, t = marks[4], marks[5], marks[6]
    split_weight(weight, top, low)
    image[...] = jnp.zeros_like(image)
    for b, out in ((0, own), (1, other)):
        span, width = marks_of(marks, b)

        def fill(k, _):
            for j in range(4):
                values = unpack_quarter(quarters[j][(item ^ b) * 4 + k])
                put_cells(image, b, k, span, lax.rem(t + j, 4), values)
            return 0

        lax.fori_loop(0, 4, fill, 0)
        widen(wide, image, b, width, -1)

        def step(k, _):
            put_packed_strip(out, k ^ h, conv_strip(wide, top, low, k, span, width, -1))
            return 0

        lax.fori_loop(0, 4, step, 0)


def first_back_kernel(marks, *refs):
    grads, strips, gain, stats, weight = refs[:8], refs[8:16], refs[16], refs[17], refs[18]
    outs, image, sums, grad_gain = refs[19:23], refs[23], refs[24], refs[25]
    wide, top, low, tile, scaled_at, centred_at = refs[26:]
    item, h, t = marks[4], marks[5], marks[6]
    split_weight_turned(weight, top, low)
    image[...] = jnp.zeros_like(image)
    gain_total = jnp.zeros((1, 320), jnp.float32)
    for b in range(2):
        span, width = marks_of(marks, b)
        mean, inv = stats[b, 0:1, :], stats[b, 1:2, :]
        first = jnp.zeros((1, 320), jnp.float32)
        second = jnp.zeros((1, 320), jnp.float32)
        for j in range(4):
            values = unpack_strip(strips[4 * b + j][...])
            centred = (values - mean) * inv * row_mask(span, 256, 320)
            norm = centred * gain[...]
            gate = jax.nn.sigmoid(norm)
            grad_norm = unpack_strip(grads[4 * b + j][...]) * gate * (1.0 + norm * (1.0 - gate))
            scaled = grad_norm * gain[...]
            first = first + column_sum(scaled)
            second = second + column_sum(scaled * centred)
            gain_total = gain_total + column_sum(grad_norm * centred)
            scaled_at[j] = scaled
            centred_at[j] = centred
        count = (span * 160).astype(jnp.float32)
        first = group_rows(first) / count
        second = group_rows(second) / count
        tau_total = jnp.zeros((1, 320), jnp.float32)
        for j in range(4):
            grad = inv * row_mask(span, 256, 320) * (
                scaled_at[j] - first - centred_at[j] * second
            )
            tau_total = tau_total + column_sum(grad)
            put_strip(image, b, h ^ j, span, grad)
        sums[b : b + 1, :] = tau_total
        widen(wide, image, b, width, -1)

        def step(k, _):
            tile[...] = conv_strip(wide, top, low, k, span, width, -1)
            put_quarters(outs, tile, (item ^ b) * 4 + k, t)
            return 0

        lax.fori_loop(0, 4, step, 0)
    grad_gain[...] = gain_total


def conv_weight_kernel(sign, marks, image, cells, out, wide):
    out[...] = jnp.zeros_like(out)
    for b in range(2):
        _, width = marks_of(marks, b)
        widen(wide, image, b, width, sign)
        for i in range(3):

            def step(c, _):
                at = pl.multiple_of(margin + c * 256 + sign * (i - 1) * width, 8)
                taps = halves(wide[pl.ds(at, 256), :].T)
                values = halves(cells[b, pl.ds(pl.multiple_of(margin + c * 256, 8), 256), :])
                part = dot_halves(taps, values, 1, 0)
                for j in range(3):
                    out[3 * i + j] += part[160 * j : 160 * j + 160]
                return 0

            lax.fori_loop(0, 4, step, 0)


def wide_halves(values):
    top, low = halves(values)
    return jnp.concatenate([top, top, low], axis=1)


def other_halves(values):
    top, low = halves(values)
    return jnp.concatenate([top, low, top], axis=1)


def dot_last(left, right):
    return lax.dot_general(
        left, right, (((1,), (1,)), ((), ())), preferred_element_type=jnp.float32
    )


def dot_pair(left, values):
    top, low = halves(values)
    both = jnp.dot(left[0], jnp.concatenate([top, low], axis=1), preferred_element_type=jnp.float32)
    return (both[:, :64] + both[:, 64:]) + jnp.dot(
        left[1], top, preferred_element_type=jnp.float32
    )


def scores_turned(marks, queries, pieces, head, j):
    at = 64 * head
    keys = pieces[j][:, at : at + 64]
    scores = dot_last(wide_halves(keys), other_halves(queries[:, at : at + 64])) * 0.125
    slot = lax.broadcasted_iota(jnp.int32, (256, 256), 0) + marks[6] * 64
    slot = jnp.where(slot >= 256, slot - 256, slot)
    return jnp.where(slot < marks[0], scores, masked_score)


def attend_kernel(marks, qkv, *refs):
    pieces, out, totals, held = refs[:4], refs[4], refs[5], refs[6]
    totals[...] = jnp.zeros_like(totals)
    for head in range(5):
        peak = None
        for j in range(4):
            scores = scores_turned(marks, qkv, pieces, head, j)
            held[256 * j : 256 * j + 256, :] = scores
            here = jnp.max(scores, axis=0, keepdims=True)
            peak = here if peak is None else jnp.maximum(peak, here)
        total = jnp.zeros((1, 256), jnp.float32)
        attended = jnp.zeros((64, 256), jnp.float32)
        for j in range(4):
            exponent = jnp.exp(held[256 * j : 256 * j + 256, :] - peak)
            total = total + column_sum(exponent)
            values = halves(pieces[j][:, 320 + 64 * head : 384 + 64 * head].T)
            first, second = halves(exponent)
            both = jnp.dot(
                jnp.concatenate(values, axis=0), first, preferred_element_type=jnp.float32
            )
            attended = attended + (
                (both[:64] + both[64:])
                + jnp.dot(values[0], second, preferred_element_type=jnp.float32)
            )
        out[:, 64 * head : 64 * head + 64] = (attended / total).T
        totals[head : head + 1, :] = peak + jnp.log(total)


def attend_back_kernel(marks, qkv, *refs):
    pieces, totals, attended, grad = refs[:4], refs[4], refs[5], refs[6]
    grad_query, outs = refs[7], refs[8:12]
    for head in range(5):
        at = 64 * head
        grad_out = grad[:, at : at + 64]
        queries = qkv[:, at : at + 64]
        delta = column_sum((grad_out * attended[:, at : at + 64]).T)
        total = totals[head : head + 1, :]
        grad_other = other_halves(grad_out)
        query_grad = jnp.zeros((64, 256), jnp.float32)
        for j in range(4):
            weights = jnp.exp(scores_turned(marks, qkv, pieces, head, j) - total)
            values = pieces[j][:, 320 + at : 384 + at]
            grad_scores = weights * (dot_last(wide_halves(values), grad_other) - delta)
            outs[j][:, 320 + at : 384 + at] = dot_pair(halves(weights), grad_out)
            first, second = halves(grad_scores)
            outs[j][:, at : at + 64] = dot_pair((first, second), queries) * 0.125
            keys = halves(pieces[j][:, at : at + 64].T)
            both = jnp.dot(
                jnp.concatenate(keys, axis=0), first, preferred_element_type=jnp.float32
            )
            query_grad = query_grad + (
                (both[:64] + both[64:])
                + jnp.dot(keys[0], second, preferred_element_type=jnp.float32)
            )
        grad_query[:, at : at + 64] = query_grad.T * 0.125


def pack_kernel(marks, values, out):
    for q in range(values.shape[0] // 64):
        for k in range(8):
            part = values[64 * q : 64 * q + 64, 160 * k : 160 * k + 160]
            put_quarter(out, k, part, 80 * q)


def unpack_kernel(marks, packed, plain):
    for k in range(8):
        plain[:, 160 * k : 160 * k + 160] = unpack_quarter(packed[k, 0:80, :])


def unpack_norm_kernel(marks, packed, gain, scaled, plain):
    for k in range(8):
        centred = unpack_quarter(packed[k, 0:80, :])
        mean = jnp.concatenate([packed[k, 80:81, :], packed[k, 81:82, 0:32]], axis=1)
        inv = jnp.concatenate([packed[k, 82:83, :], packed[k, 83:84, 0:32]], axis=1)
        at = slice(160 * k, 160 * k + 160)
        scaled[:, at] = centred * gain[:, at]
        plain[:, at] = centred * (1.0 / inv) + mean


def cotangent_kernel(marks, pieces, total, out, whole):
    total[...] = (pieces[0, :, :1280] + pieces[1, :, :1280]) + (
        pieces[2, :, :1280] + pieces[3, :, :1280]
    )
    for part in range(4):
        whole[:, 320 * part : 320 * part + 320] = pieces[part, :, 1280:1600]
    for k in range(8):
        put_quarter(out, k, whole[:, 160 * k : 160 * k + 160])


def third_kernel(marks, *refs):
    pieces, out, gain = refs[:4], refs[4], refs[5]
    for first in range(4):

        @pl.when(marks[6] == first)
        def _():
            for j in range(4):
                at = (first + j) % 4 * 320
                gain[:, at : at + 320] = pieces[j][160:161, 0:320]
                for m in range(3):
                    out[:, 1280 * m + at : 1280 * m + at + 320] = pieces[j][
                        0:160, 320 * m : 320 * m + 320
                    ]


def text_kernel(marks, pieces, rows, keys, values):
    for part in range(4):
        at = pl.multiple_of(lax.rem(part - marks[6] + 4, 4) * 64, 8)
        rows[pl.ds(at, 64), :] = pieces[part, 0:64, :]
        lanes = slice(320 * part, 320 * part + 320)
        keys[0:40, lanes] = pieces[part, 64:104, 0:320]
        values[0:40, lanes] = pieces[part, 64:104, 320:640]
        keys[40:77, lanes] = pieces[part, 64:101, 640:960]
        values[40:77, lanes] = pieces[part, 64:101, 960:1280]


def text_grad_kernel(marks, keys, values, *outs):
    for first in range(4):

        @pl.when(marks[6] == first)
        def _():
            for j in range(4):
                at = (first + j) % 4 * 320
                lanes = slice(at, at + 320)
                outs[j][:, 0:320] = keys[0:40, lanes]
                outs[j][:, 320:640] = values[0:40, lanes]
                outs[j][0:37, 640:960] = keys[40:77, lanes]
                outs[j][0:37, 960:1280] = values[40:77, lanes]
                outs[j][37:40, 640:1280] = jnp.zeros((3, 640), jnp.float32)


def rows_kernel(marks, *refs):
    pieces, out = refs[:4], refs[4]
    for j in range(4):
        at = pl.multiple_of(lax.rem(marks[6] + j, 4) * 64, 8)
        out[pl.ds(at, 64), :] = pieces[j][...]


def residual_kernel(marks, source, first, second, third, fourth, out, sums):
    t = marks[6]
    at = pl.multiple_of(t * 80, 8)
    sums[...] = jnp.zeros_like(sums)
    for b in range(2):
        for k in range(4):
            place = 4 * b + k
            packed = source[place, pl.ds(at, 80), :] + (
                (first[place] + second[place]) + (third[place] + fourth[place])
            )
            out[place] = packed
            values = unpack_quarter(packed)
            sums[2 * b : 2 * b + 1, :] += column_sum(values)
            sums[2 * b + 1 : 2 * b + 2, :] += column_sum(values * values)


def span_of_item(marks, b):
    return jnp.where(marks[4] == b, marks[0], marks[2])


def norm_kernel(marks, residual, first, second, third, fourth, out, stats):
    total = (first[...] + second[...]) + (third[...] + fourth[...])
    for b in range(2):
        span = span_of_item(marks, b)
        mean, inv = group_row_stats(
            total[2 * b : 2 * b + 1, :], total[2 * b + 1 : 2 * b + 2, :], span
        )
        stats[2 * b : 2 * b + 1, :] = mean
        stats[2 * b + 1 : 2 * b + 2, :] = inv
        for k in range(4):
            values = unpack_quarter(residual[4 * b + k])
            centred = (values - mean) * inv * quarter_mask(span, marks[6])
            put_quarter(out, 4 * b + k, centred)
            out[4 * b + k, 80:88, :] = jnp.zeros((8, 128), jnp.float32)
            for row, value in ((80, mean), (82, inv)):
                out[4 * b + k, row : row + 1, :] = value[:, :128]
                out[4 * b + k, row + 1 : row + 2, 0:32] = value[:, 128:]


def centred_of(marks, residual, stats, b, k):
    values = unpack_quarter(residual[4 * b + k])
    mean, inv = stats[2 * b : 2 * b + 1, :], stats[2 * b + 1 : 2 * b + 2, :]
    return (values - mean) * inv * quarter_mask(span_of_item(marks, b), marks[6])


def norm_sums_kernel(marks, grad, residual, stats, gain, sums):
    sums[...] = jnp.zeros_like(sums)
    for b in range(2):
        for k in range(4):
            centred = centred_of(marks, residual, stats, b, k)
            values = unpack_quarter(grad[4 * b + k])
            scaled = values * gain[...]
            sums[3 * b : 3 * b + 1, :] += column_sum(scaled)
            sums[3 * b + 1 : 3 * b + 2, :] += column_sum(scaled * centred)
            sums[3 * b + 2 : 3 * b + 3, :] += column_sum(values * centred)


def sum_in_order(pieces, t):
    total = None
    for part in range(4):
        j = lax.rem(part - t + 4, 4)
        value = jnp.where(
            j < 2,
            jnp.where(j == 0, pieces[0][...], pieces[1][...]),
            jnp.where(j == 2, pieces[2][...], pieces[3][...]),
        )
        total = value if total is None else total + value
    return total


def norm_back_kernel(marks, *refs):
    grad, residual, stats, gain, base = refs[:5]
    pieces, out, grad_gain = refs[5:9], refs[9], refs[10]
    total = sum_in_order(pieces, marks[6])
    grad_gain[...] = jnp.zeros_like(grad_gain)
    grad_gain[0:1, :] = total[2:3, :] + total[5:6, :]
    for b in range(2):
        span = span_of_item(marks, b)
        count = (span * 160).astype(jnp.float32)
        first = group_rows(total[3 * b : 3 * b + 1, :]) / count
        second = group_rows(total[3 * b + 1 : 3 * b + 2, :]) / count
        inv = stats[2 * b + 1 : 2 * b + 2, :]
        for k in range(4):
            centred = centred_of(marks, residual, stats, b, k)
            scaled = unpack_quarter(grad[4 * b + k]) * gain[...]
            values = inv * quarter_mask(span, marks[6]) * (scaled - first - centred * second)
            put_quarter(out, 4 * b + k, values + unpack_quarter(base[4 * b + k]))


def input_sums_kernel(marks, source, gain, stats, *refs):
    pieces, out, sums = refs[:4], refs[4], refs[5]
    at = pl.multiple_of(marks[6] * 80, 8)
    sums[...] = jnp.zeros_like(sums)
    for b in range(2):
        span = span_of_item(marks, b)
        mine = marks[4] ^ b
        mean, inv = stats[mine, 0:1, :], stats[mine, 1:2, :]
        for k in range(4):
            place = 4 * b + k
            values = unpack_quarter(source[place, pl.ds(at, 80), :])
            centred = (values - mean) * inv * quarter_mask(span, marks[6])
            norm = centred * gain[...]
            gate = jax.nn.sigmoid(norm)
            packed = (pieces[0][place] + pieces[1][place]) + (pieces[2][place] + pieces[3][place])
            grad = unpack_quarter(packed) * gate * (1.0 + norm * (1.0 - gate))
            put_quarter(out, place, grad)
            scaled = grad * gain[...]
            sums[3 * b : 3 * b + 1, :] += column_sum(scaled)
            sums[3 * b + 1 : 3 * b + 2, :] += column_sum(scaled * centred)
            sums[3 * b + 2 : 3 * b + 3, :] += column_sum(grad * centred)


def input_back_kernel(marks, grad, source, gain, stats, base, extra, *refs):
    pieces, out, grad_gain = refs[:4], refs[4], refs[5]
    at = pl.multiple_of(marks[6] * 80, 8)
    total = sum_in_order(pieces, marks[6])
    grad_gain[...] = jnp.zeros_like(grad_gain)
    grad_gain[0:1, :] = total[2:3, :] + total[5:6, :]
    for b in range(2):
        span = span_of_item(marks, b)
        count = (span * 160).astype(jnp.float32)
        first = group_rows(total[3 * b : 3 * b + 1, :]) / count
        second = group_rows(total[3 * b + 1 : 3 * b + 2, :]) / count
        mine = marks[4] ^ b
        mean, inv = stats[mine, 0:1, :], stats[mine, 1:2, :]
        for k in range(4):
            place = 4 * b + k
            keep = quarter_mask(span, marks[6])
            centred = (unpack_quarter(source[place, pl.ds(at, 80), :]) - mean) * inv * keep
            scaled = unpack_quarter(grad[place]) * gain[...]
            values = inv * keep * (scaled - first - centred * second)
            put_quarter(out, place, values + unpack_quarter(base[place]))
            out[place, 80:88, :] = extra[place]


def run_kernel(body, marks, inputs, outs, scratch, flops):
    in_smem = pl.BlockSpec(memory_space=pltpu.SMEM)
    in_vmem = pl.BlockSpec(memory_space=pltpu.VMEM)
    return pl.pallas_call(
        body,
        out_shape=[jax.ShapeDtypeStruct(shape, jnp.float32) for shape in outs],
        in_specs=[in_smem] + [in_vmem] * len(inputs),
        out_specs=[in_vmem] * len(outs),
        scratch_shapes=[pltpu.VMEM(shape, kind) for shape, kind in scratch],
        compiler_params=pltpu.CompilerParams(vmem_limit_bytes=56 * 1024 * 1024),
        cost_estimate=pl.CostEstimate(
            flops=flops, bytes_accessed=10 * 1024 * 1024, transcendentals=0
        ),
    )(marks, *inputs)


def weight_kernel(plan, *refs):
    count = 1 + max(which for block in plan for _, _, which in block)
    lefts, right, out = refs[:count], refs[count], refs[-1]
    tokens = right.shape[0]
    for number, block in enumerate(plan):

        @pl.when(pl.program_id(0) == number)
        def _():
            for begin, columns, which in block:
                top, low = halves(right[:, begin : begin + columns])
                if tokens <= 64:
                    stacked = jnp.concatenate([top, low, top], axis=0)
                for m in range(0, 1280, 256):
                    cells = lefts[which][:, m : m + 256].T
                    if tokens <= 64:
                        first, second = halves(cells)
                        first = jnp.concatenate([first, first, second], axis=1)
                        part = jnp.dot(first, stacked, preferred_element_type=jnp.float32)
                    else:
                        part = dot_halves(halves(cells), (top, low), 1, 0)
                    out[m : m + 256, begin : begin + columns] = part


def weight_grads(plan, lefts, right, first=0, blocks=None, into=None):
    tokens = right.shape[0]
    blocks = blocks or len(plan)
    in_specs = [pl.BlockSpec((tokens, 1280), lambda i: (0, 0))] * len(lefts)
    in_specs.append(pl.BlockSpec((tokens, 1280), lambda i: (0, i)))
    inputs, alias = (*lefts, right), {}
    if into is not None:
        in_specs.append(pl.BlockSpec(memory_space=pl.ANY))
        alias = {len(inputs): 0}
        inputs = (*inputs, into)
    return pl.pallas_call(
        functools.partial(weight_kernel, plan),
        out_shape=jax.ShapeDtypeStruct((1280, 1280 * blocks), jnp.float32),
        grid=(len(plan),),
        in_specs=in_specs,
        out_specs=pl.BlockSpec((1280, 1280), lambda i: (0, i + first)),
        input_output_aliases=alias,
        compiler_params=pltpu.CompilerParams(vmem_limit_bytes=48 * 1024 * 1024),
        cost_estimate=pl.CostEstimate(
            flops=6 * tokens * 1280 * 1280 * len(plan),
            bytes_accessed=7 * 1024 * 1024 * len(plan),
            transcendentals=0,
        ),
    )(*inputs)


def after(values, *events):
    return lax.optimization_barrier((values,) + events)[0]


def together(*values):
    return lax.optimization_barrier(values)


def small(body, marks, inputs, outs, scratch=()):
    return run_kernel(body, marks, inputs, outs, scratch, 4 * 1024 * 1024)


CONV_FLOPS = 6 * 2048 * 1440 * 320


def first_conv(marks, source, gain, tau, weight):
    f32, b16 = jnp.float32, jnp.bfloat16
    return run_kernel(
        first_kernel,
        marks,
        (source, gain, tau, weight),
        [(4, 320, 256), (4, 320, 256), (2, IMAGE_ROWS, 160), (2, 8, 160)],
        [
            ((IMAGE_ROWS, 480), f32),
            ((1440, 320), b16),
            ((1440, 320), b16),
            ((4, 256, 160), f32),
        ],
        CONV_FLOPS,
    )


def second_conv(marks, strips, gain, weight):
    f32, b16 = jnp.float32, jnp.bfloat16
    return run_kernel(
        second_kernel,
        marks,
        (*strips, gain, weight),
        [(8, 80, 128)] * 4 + [(2, IMAGE_ROWS, 320), (2, 8, 320)],
        [
            ((IMAGE_ROWS, 960), f32),
            ((2880, 160), b16),
            ((2880, 160), b16),
            ((256, 160), f32),
        ],
        CONV_FLOPS,
    )


def second_conv_back(marks, quarters, weight):
    f32, b16 = jnp.float32, jnp.bfloat16
    return run_kernel(
        second_back_kernel,
        marks,
        (*quarters, weight),
        [(4, 320, 256), (4, 320, 256), (2, IMAGE_ROWS, 160)],
        [((IMAGE_ROWS, 480), f32), ((1440, 320), b16), ((1440, 320), b16)],
        CONV_FLOPS,
    )


def first_conv_back(marks, grads, strips, gain, stats, weight):
    f32, b16 = jnp.float32, jnp.bfloat16
    return run_kernel(
        first_back_kernel,
        marks,
        (*grads, *strips, gain, stats, weight),
        [(8, 80, 128)] * 4 + [(2, IMAGE_ROWS, 320), (2, 320), (1, 320)],
        [
            ((IMAGE_ROWS, 960), f32),
            ((2880, 160), b16),
            ((2880, 160), b16),
            ((256, 160), f32),
            ((4, 256, 320), f32),
            ((4, 256, 320), f32),
        ],
        CONV_FLOPS,
    )


def conv_weight(marks, image, cells, sign):
    return run_kernel(
        functools.partial(conv_weight_kernel, sign),
        marks,
        (image, cells),
        [(9, 160, 320)],
        [((IMAGE_ROWS, 480), jnp.float32)],
        CONV_FLOPS,
    )[0]


def heads_of(values, count):
    return values.reshape(values.shape[0], count, HEAD_DIM)


def ein(form, left, right):
    return jnp.einsum(form, left, right, precision=high, preferred_element_type=jnp.float32)


def soft_attend(queries, keys, values, key_valid, count):
    scores = ein(QK, heads_of(queries, count), heads_of(keys, count)) * (1.0 / math.sqrt(HEAD_DIM))
    if key_valid is not None:
        scores = jnp.where(key_valid[None, None, :], scores, masked_score)
    exponent = jnp.exp(scores - jnp.max(scores, axis=-1, keepdims=True))
    weights = exponent / jnp.sum(exponent, axis=-1, keepdims=True)
    attended = ein(PV, weights, heads_of(values, count))
    return attended.reshape(queries.shape), weights


def soft_back(queries, keys, values, count, weights, attended, grad_out):
    scaling = 1.0 / math.sqrt(HEAD_DIM)
    grad_heads = heads_of(grad_out, count)
    grad_soft = ein(QK, grad_heads, heads_of(values, count))
    delta = jnp.sum(grad_heads * heads_of(attended, count), axis=-1).T
    grad_scores = weights * (grad_soft - delta[..., None])
    grad_query = ein(PV, grad_scores, heads_of(keys, count)) * scaling
    grad_key = ein(PQ, grad_scores, heads_of(queries, count)) * scaling
    grad_value = ein(PQ, weights, grad_heads)
    return (
        grad_query.reshape(queries.shape),
        grad_key.reshape(keys.shape),
        grad_value.reshape(values.shape),
    )


def layer_grad(grad_out, centred, inv_std, gain_vector):
    scaled = grad_out * gain_vector
    grad_in = inv_std * (
        scaled
        - jnp.mean(scaled, axis=-1, keepdims=True)
        - centred * jnp.mean(scaled * centred, axis=-1, keepdims=True)
    )
    return grad_in, jnp.sum(grad_out * centred, axis=0)


def layer_forward(values, gain_vector):
    mean_val = jnp.mean(values, axis=-1, keepdims=True)
    var_val = jnp.mean(values * values, axis=-1, keepdims=True) - mean_val * mean_val
    inv_std = lax.rsqrt(var_val + norm_eps)
    centred = (values - mean_val) * inv_std
    return centred * gain_vector, centred, inv_std


def gather_plane(block):
    return lax.all_gather(block, IH, axis=0, tiled=True)


def scatter_plane(block):
    return lax.psum_scatter(block, IH, scatter_dimension=0, tiled=True)


def grid_cells(bucket):
    strip_rows, strip_width = grid_shape(bucket)
    return strip_rows * strip_width


def fast_shards(
    hidden,
    text_states,
    bucket,
    timestep,
    gain_in,
    conv_first,
    time_weight,
    gain_mid,
    conv_second,
    gain_attn_norm,
    proj_in,
    gain_self,
    query_self,
    key_self,
    value_self,
    out_self,
    gain_cross,
    query_cross,
    key_cross,
    value_cross,
    out_cross,
    gain_ff,
    ff_in,
    ff_out,
    proj_out,
    cotangent,
):
    item, h, t = lax.axis_index(I), lax.axis_index(H), lax.axis_index(T)
    block = item * 4 + h
    width, wide = 160, 320
    channels = 1280

    def rows_of(values):
        return [values[64 * j : 64 * j + 64] for j in range(4)]

    own_span = grid_cells(bucket[0])
    slot = jnp.arange(256, dtype=jnp.int32)
    own_valid = (slot < own_span).astype(jnp.float32)[:, None]
    both = jnp.stack([bucket[0], timestep[0]]).astype(jnp.float32)
    both_other = swap(both)
    times = jnp.stack([both[1], both_other[1]])
    other_rows, other_width = grid_shape(both_other[0].astype(jnp.int32))
    own_rows, own_width = grid_shape(bucket[0])
    marks = jnp.stack(
        [own_span, own_width, other_rows * other_width, other_width, item, h, t]
    ).astype(jnp.int32)

    (source,) = small(pack_kernel, marks, (hidden[0] * own_valid,), [(8, 320, 128)])
    source = plane_exchange(source)
    gains = jnp.stack([gain_self, gain_cross, gain_ff], axis=1)
    attn_full = gather_plane(
        jnp.concatenate(
            [
                query_self,
                key_self,
                value_self,
                proj_out,
                out_self.T,
                jnp.pad(gains, ((0, 0), (0, 125))),
            ],
            axis=1,
        )
    )
    qkv_full = attn_full[:, :960]
    proj_out_full = attn_full[:, 960:1280]
    out_self_full = attn_full[:, 1280:1600]
    gain_rows = attn_full[:, 1600:1603].T
    gain_self_full, gain_cross_full, gain_ff_full = (gain_rows[k : k + 1] for k in range(3))

    own_third = jnp.concatenate([proj_in.T, query_cross, out_cross.T], axis=1)
    own_third = jnp.concatenate(
        [own_third, jnp.pad(gain_attn_norm[None, :], ((0, 7), (0, 640)))], axis=0
    )
    third_pieces = [own_third, turn(own_third, 3), turn(own_third[:, :512], 2), turn(own_third, 1)]

    features = jax.nn.silu(time_features(times, channels))
    own_features = lax.dynamic_slice_in_dim(features, block * width, width, 1)
    tau = mm(own_features, time_weight, 1, 0)
    second_weight = conv_second.transpose(0, 1, 3, 2).reshape(9 * width, wide)
    own_one, other_one, image_one, stats_one = first_conv(
        marks, source, gain_in[None, :], tau, conv_first.reshape(9 * width, wide)
    )
    own_one, other_one, *third_pieces = together(own_one, other_one, *third_pieces)
    own_one = own_one + swap(other_one)
    strips_one, part = plane_sum(own_one)
    third_rest = turn(own_third[:, 512:], 2)
    third_pieces[2] = jnp.concatenate([third_pieces[2], third_rest], axis=1)
    third, gain_attn_full = small(
        third_kernel, marks, after(third_pieces, part), [(160, 3840), (1, channels)]
    )
    third_full = gather_plane(third)
    proj_in_full = third_full[:, :1280]
    query_cross_full = third_full[:, 1280:2560]
    out_cross_full = third_full[:, 2560:]
    ff_out_full = gather_plane(after(ff_out.T, third))
    cot = after(cotangent[0] * own_valid, own_one)
    grad_ff_part = mm(cot, proj_out_full, 1, 1)
    cot_pieces = z_all(jnp.concatenate([grad_ff_part, cot], axis=1).reshape(4, 64, channels + wide))
    *strips_one, cot_pieces = together(*strips_one, cot_pieces)

    *conv_two, image_two, stats_two = second_conv(
        marks, strips_one, gain_mid[None, :], second_weight
    )
    conv_two_pieces = z_received(conv_two)

    event = conv_two[0]
    grad_after_ff, cot_packed = small(
        cotangent_kernel,
        marks,
        (after(cot_pieces, event),),
        [(64, channels), (8, 80, 128)],
        [((64, channels), jnp.float32)],
    )
    cot_q = plane_exchange(cot_packed)
    text_here = after(text_states[0], event)
    text_own = lax.dynamic_slice_in_dim(text_here, block * 256, 256, 1)
    text_other = swap(lax.dynamic_slice_in_dim(text_here, ((1 - item) * 4 + h) * 256, 256, 1))
    text_weight = jnp.concatenate([key_cross, value_cross], axis=1)
    text_part = mm(text_own, text_weight, 1, 0) + swap(mm(text_other, text_weight, 1, 0))

    residual_q, sums = small(
        residual_kernel, marks, (source, *conv_two_pieces), [(8, 80, 128), (8, width)]
    )
    centred_three, stats_three = small(
        norm_kernel, marks, (residual_q, *z_pieces(sums)), [(8, 88, 128), (8, width)]
    )
    norm_three, residual_s = small(
        unpack_norm_kernel,
        marks,
        (plane_exchange(centred_three), gain_attn_full),
        [(64, channels), (64, channels)],
    )
    projected = mm(norm_three, proj_in_full, 1, 1)

    normed_self, centred_self, inv_self = layer_forward(projected, gain_self_full)
    normed_pieces = z_pieces(normed_self)
    text_sum = h_sum(after(text_part, normed_self))
    *normed_pieces, text_sum, cot_q = together(*normed_pieces, text_sum, cot_q)
    normed_self_all = jnp.concatenate(normed_pieces, axis=0)
    qkv = mm(normed_self_all, qkv_full, 1, 0)
    own_kv = qkv[:, wide:]
    kv_pieces = [own_kv] + [flip(own_kv, j) for j in (1, 2, 3)]
    text_sum, grad_here = after((text_sum, grad_after_ff), own_kv)
    side_pieces = z_spread(jnp.concatenate([grad_here, folded(text_sum)], axis=0))
    *kv_pieces, side_pieces = together(*kv_pieces, side_pieces)
    attn_self, totals_self = small(
        attend_kernel,
        marks,
        (qkv, *kv_pieces),
        [(256, wide), (8, 256)],
        [((1024, 256), jnp.float32)],
    )
    ff_in_full = gather_plane(after(ff_in.reshape(160, 2560), attn_self))
    self_part = mm(attn_self, out_self_full, 1, 1)
    self_pieces = z_received(rows_of(self_part))
    self_sum = total_of(self_pieces)
    event = self_pieces[1]
    grad_after_ff_all, keys_text, values_text = small(
        text_kernel,
        marks,
        (after(side_pieces, event),),
        [(256, channels), (77, channels), (77, channels)],
    )
    grad_ff_act = mm(grad_after_ff_all, ff_out_full, 1, 0)
    self_sum, grad_ff_act, keys_text, values_text = together(
        self_sum, grad_ff_act, keys_text, values_text
    )
    after_self = projected + self_sum

    normed_cross, centred_cross, inv_cross = layer_forward(after_self, gain_cross_full)
    queries_cross = mm(normed_cross, query_cross_full, 1, 0)
    attn_cross, weights_cross = soft_attend(queries_cross, keys_text, values_text, None, 20)
    after_cross = after_self + mm(attn_cross, out_cross_full, 1, 1)

    normed_ff, centred_ff, inv_ff = layer_forward(after_cross, gain_ff_full)
    normed_ff_all = jnp.concatenate(z_pieces(normed_ff), axis=0)
    hidden_ff = mm(normed_ff_all, ff_in_full, 1, 0)
    value_half, gate_half = hidden_ff[:, :channels], hidden_ff[:, channels:]
    phi = 0.5 * (1.0 + lax.erf(gate_half * math.sqrt(0.5)))
    slope = phi + gate_half * jnp.exp(-0.5 * gate_half * gate_half) * (1.0 / math.sqrt(2 * math.pi))
    gate_act = gate_half * phi
    ff_act = value_half * gate_act
    grad_value = grad_ff_act * gate_act
    grad_gate = grad_ff_act * value_half * slope
    grad_hidden_ff = jnp.concatenate([grad_value, grad_gate], axis=1)
    grad_normed_part = mm(grad_hidden_ff, ff_in_full, 1, 1)
    normed_pieces = z_received(rows_of(grad_normed_part))
    grad_normed_ff = total_of(normed_pieces)
    ff_right = jnp.concatenate(after([grad_hidden_ff, ff_act], normed_pieces[1]), axis=1)
    ff_grads = weight_grads(
        (((0, 1280, 0),), ((0, 1280, 0),), ((0, 1280, 1),)),
        (normed_ff_all, grad_after_ff_all),
        ff_right,
        0,
        5,
    )
    out_part = mm(after(ff_act, normed_pieces[1]), ff_out_full, 1, 1)
    grad_normed_ff, ff_grads, out_part = together(grad_normed_ff, ff_grads, out_part)

    back_ff, grad_gain_ff = layer_grad(grad_normed_ff, centred_ff, inv_ff, gain_ff_full)
    grad_after_cross = grad_after_ff + back_ff
    grad_attn_cross = mm(grad_after_cross, out_cross_full, 1, 0)
    grad_queries_cross, grad_keys_text, grad_values_text = soft_back(
        queries_cross, keys_text, values_text, 20, weights_cross, attn_cross, grad_attn_cross
    )
    grad_normed_cross = mm(grad_queries_cross, query_cross_full, 1, 1)
    back_cross, grad_gain_cross = layer_grad(
        grad_normed_cross, centred_cross, inv_cross, gain_cross_full
    )
    grad_after_self = grad_after_cross + back_cross
    grad_pieces = z_pieces(grad_after_self)
    cross_right = after((grad_queries_cross, attn_cross), grad_pieces[1])
    cross_right = jnp.concatenate(
        [side[:, wide * k : wide * k + wide] for k in range(4) for side in cross_right], axis=1
    )
    cross_grads = weight_grads(
        (((0, 320, 0), (320, 320, 1), (640, 320, 0), (960, 320, 1)),) * 2,
        (normed_cross, grad_after_cross),
        cross_right,
        3,
        5,
        ff_grads,
    )
    *grad_pieces, cross_grads = together(*grad_pieces, cross_grads)
    out_turned = jnp.concatenate([out_part, out_part], axis=0)
    out_turned = lax.dynamic_slice_in_dim(out_turned, lax.rem(4 - t, 4) * 64, 256, 0)
    out_sum = z_all(after(out_turned, grad_after_self).reshape(4, 64, channels))
    ff_grads = scatter_plane(cross_grads)
    ff_grads, cross_grads = ff_grads[:, :3840], ff_grads[:, 3840:]

    grad_after_self_all = jnp.concatenate(grad_pieces, axis=0)
    grad_attn_self = mm(grad_after_self_all, out_self_full, 1, 0)
    grad_queries, *kv_pieces = small(
        attend_back_kernel,
        marks,
        (qkv, *kv_pieces, totals_self, attn_self, grad_attn_self),
        [(256, wide)] + [(256, 2 * wide)] * 4,
    )
    kv_pieces = kv_pieces[:1] + [flip(kv_pieces[j], j) for j in (1, 2, 3)]
    grad_kv = total_of(kv_pieces)
    grad_qkv = jnp.concatenate([grad_queries, grad_kv], axis=1)
    grad_normed_part = mm(grad_qkv, qkv_full, 1, 1)
    normed_pieces = z_received(rows_of(grad_normed_part))
    grad_normed_self = total_of(normed_pieces)
    text_grads = small(
        text_grad_kernel,
        marks,
        after((grad_keys_text, grad_values_text), normed_pieces[1]),
        [(40, channels)] * 4,
    )
    grad_normed_self, out_sum, *text_grads = together(grad_normed_self, out_sum, *text_grads)
    back_self, grad_gain_self = layer_grad(grad_normed_self, centred_self, inv_self, gain_self_full)
    grad_projected = grad_after_self + back_self
    grad_norm_three = mm(grad_projected, proj_in_full, 1, 0)

    (grad_three,) = small(pack_kernel, marks, (grad_norm_three,), [(8, 80, 128)])
    grad_three_q = plane_exchange(grad_three)
    out_sum = jnp.sum(after(out_sum, grad_three), axis=0)
    text_grads = total_of(z_received(after(text_grads, grad_three)))
    grad_three_q, text_grads = together(grad_three_q, text_grads)
    gain_block = lax.dynamic_slice_in_dim(gain_attn_full, block * width, width, 1)
    (sums,) = small(
        norm_sums_kernel, marks, (grad_three_q, residual_q, stats_three, gain_block), [(8, width)]
    )
    grad_residual_q, grad_gain_three = small(
        norm_back_kernel,
        marks,
        (grad_three_q, residual_q, stats_three, gain_block, cot_q, *z_pieces(sums)),
        [(8, 80, 128), (8, width)],
    )

    residual_pieces = z_pieces(grad_residual_q)
    text_grads = after(text_grads, grad_residual_q)
    text_grads = text_grads + flip(text_grads, 1)
    attn_right = jnp.concatenate(
        [
            jnp.concatenate([grad_qkv, attn_self], axis=1),
            jnp.pad(norm_three, ((0, 192), (0, 0))),
        ],
        axis=1,
    )
    attn_grads = weight_grads(
        (((0, 960, 0), (960, 320, 1)), ((0, 1280, 2),)),
        (
            normed_self_all,
            grad_after_self_all,
            jnp.pad(grad_projected, ((0, 192), (0, 0))),
        ),
        after(attn_right, residual_pieces[1]),
    )
    *residual_pieces, text_grads, attn_grads = together(*residual_pieces, text_grads, attn_grads)
    attn_grads = scatter_plane(attn_grads)
    own_two, other_two, image_back = second_conv_back(marks, residual_pieces, second_weight)
    own_two = own_two + swap(other_two)
    grad_act_two, part = plane_sum(own_two)
    side = jnp.concatenate(
        [
            jnp.broadcast_to((after_cross + out_sum)[None], (4, 64, channels)),
            jnp.moveaxis(residual_s.reshape(64, 4, wide), 1, 0),
        ],
        axis=2,
    )
    gain_rows = jnp.stack([grad_gain_self, grad_gain_cross, grad_gain_ff])
    gain_rows = jnp.broadcast_to(jnp.pad(gain_rows, ((0, 5), (0, wide)))[None], (4, 8, 1600))
    side = z_all(after(jnp.concatenate([side, gain_rows], axis=1), own_two))
    side_here = after(side, part)
    after_ff_all = side_here[:, :64, :channels].reshape(256, channels)
    residual_all = side_here[:, :64, channels:].reshape(256, wide)
    gain_sums = jnp.sum(side_here[:, 64:67, :channels], axis=0)
    *grad_act_two, after_ff_all, gain_sums, residual_all = together(
        *grad_act_two, after_ff_all, gain_sums, residual_all
    )

    *grad_act_one, image_grad, grad_tau, grad_gain_mid = first_conv_back(
        marks,
        grad_act_two,
        strips_one,
        gain_mid[None, :],
        stats_two,
        conv_first.reshape(9 * width, wide),
    )
    grad_act_pieces = z_received(grad_act_one)
    image_grad, text_grads = after((image_grad, text_grads), grad_act_pieces[1])
    text_grads = text_grads + flip(text_grads, 2)
    grad_conv_first = conv_weight(marks, image_one, image_grad, 1)
    cross_cut = after(cross_grads, grad_act_pieces[1])
    cross_cut = [
        lax.dynamic_slice_in_dim(cross_cut, lax.rem(t + j, 4) * 640, 640, 1) for j in range(4)
    ]
    *grad_act_pieces, grad_conv_first, text_grads, cross_cut = together(
        *grad_act_pieces, grad_conv_first, text_grads, cross_cut
    )
    grad_conv_first = grad_conv_first.reshape(3, 3, width, wide)
    extra = jnp.concatenate(
        [
            jnp.broadcast_to(grad_gain_three[0], (8, 1, width)),
            jnp.moveaxis(gain_sums.reshape(3, 8, width), 1, 0),
        ],
        axis=1,
    )
    extra = jnp.concatenate(
        [extra[:, :, :128], jnp.pad(extra[:, :, 128:], ((0, 0), (0, 0), (0, 96)))], axis=1
    )
    grad_input_q, sums = small(
        input_sums_kernel,
        marks,
        (source, gain_in[None, :], stats_one, *grad_act_pieces),
        [(8, 80, 128), (8, width)],
    )
    cross_shares = total_of(z_received(after(cross_cut, grad_input_q)))
    moved, grad_gain_in = small(
        input_back_kernel,
        marks,
        (
            grad_input_q,
            source,
            gain_in[None, :],
            stats_one,
            grad_residual_q,
            extra,
            *z_pieces(sums),
        ),
        [(8, 88, 128), (8, width)],
    )
    received = plane_exchange(moved)
    text_grads, image_back, after_ff_here, attn_grads = after(
        (text_grads, image_back, after_ff_all, attn_grads), moved
    )
    proj_cut = attn_grads[:, 1280:].reshape(width, 4, wide)
    proj_share = total_of(z_received([pick(proj_cut, lax.rem(t + j, 4), 1) for j in range(4)]))
    text_other_grads = swap(text_grads)
    grad_proj_out = mm(after_ff_here, cot, 0, 0).reshape(2, 4, width, wide)
    grad_proj_own = pick(grad_proj_out, item) + swap(pick(grad_proj_out, 1 - item))
    grad_conv_second = conv_weight(marks, image_back, image_two, -1)
    received, cross_shares, proj_share, text_other_grads, grad_proj_own, grad_conv_second = together(
        received, cross_shares, proj_share, text_other_grads, grad_proj_own, grad_conv_second
    )
    grad_conv_second = grad_conv_second.reshape(3, 3, width, wide).transpose(0, 1, 3, 2)
    text_grads, text_other_grads = unfolded(text_grads), unfolded(text_other_grads)
    (grad_hidden,) = small(unpack_kernel, marks, (received,), [(64, channels)])
    hidden_pieces = z_pieces(grad_hidden)
    after_ff_all, grad_proj_own = after((after_ff_all, grad_proj_own), grad_hidden)
    grad_proj_out = h_collect([pick(grad_proj_own, h ^ j) for j in range(4)])
    output = residual_all + mm(after_ff_all, proj_out_full, 1, 0)
    output = output * own_valid
    grad_text_weight = mm(text_own, text_grads, 0, 0) + mm(text_other, text_other_grads, 0, 0)
    grad_time_weight = mm(own_features, grad_tau, 0, 0)
    (grad_hidden,) = small(rows_kernel, marks, hidden_pieces, [(256, channels)])
    extra = jnp.concatenate([received[:, 80:84, :], received[:, 84:88, :32]], axis=2)
    grad_gain_attn = lax.dynamic_slice_in_dim(extra[:, 0].reshape(channels), t * wide, wide, 0)
    gain_sums = jnp.sum(extra[:, 1:], axis=0)

    return (
        output[None],
        grad_hidden[None],
        grad_gain_in[0],
        grad_conv_first,
        grad_time_weight,
        grad_gain_mid[0],
        grad_conv_second,
        grad_gain_attn,
        proj_share.T,
        gain_sums[0],
        attn_grads[:, :320],
        attn_grads[:, 320:640],
        attn_grads[:, 640:960],
        attn_grads[:, 960:1280].T,
        gain_sums[1],
        cross_shares[:, :320],
        grad_text_weight[:, :wide],
        grad_text_weight[:, wide:],
        cross_shares[:, 320:].T,
        gain_sums[2],
        ff_grads[:, :2560].reshape(width, 2, channels),
        ff_grads[:, 2560:].T,
        grad_proj_out,
    )


def solution(mesh):
    placed = (
        P(I, H, None),
        P(I, None, None),
        P(I),
        P(I),
        P(IH),
        P(None, None, IH, T),
        P(IH, T),
        P(T),
        P(None, None, T, IH),
        P(T),
        P(T, IH),
        P(IH),
        P(IH, T),
        P(IH, T),
        P(IH, T),
        P(T, IH),
        P(IH),
        P(IH, T),
        P(IH, T),
        P(IH, T),
        P(T, IH),
        P(IH),
        P(IH, None, T),
        P(T, IH),
        P(IH, T),
        P(I, H, T),
    )
    sizes = (mesh.shape[I], mesh.shape[H], mesh.shape[T])
    body = fast_shards if sizes == (2, 4, 4) else shards
    return jax.shard_map(
        body,
        mesh=mesh,
        in_specs=placed,
        out_specs=(
            P(I, H, T),
            P(I, H, None),
            P(IH),
            P(None, None, IH, T),
            P(IH, T),
            P(T),
            P(None, None, T, IH),
            P(T),
            P(T, IH),
            P(IH),
            P(IH, T),
            P(IH, T),
            P(IH, T),
            P(T, IH),
            P(IH),
            P(IH, T),
            P(IH, T),
            P(IH, T),
            P(T, IH),
            P(IH),
            P(IH, None, T),
            P(T, IH),
            P(IH, T),
        ),
        check_vma=False,
    )
```

```python
import functools
import math

import jax
import jax.numpy as jnp
from jax import lax
from jax.experimental import pallas as pl
from jax.experimental.pallas import tpu as pltpu
from jax.sharding import PartitionSpec as P

HEAD_DIM = 64
GROUPS = 32
EDGE = 48


highest = lax.Precision.HIGHEST
norm_eps = 1e-05
masked_score = -1e30
edge_margin = 56
high = lax.Precision.HIGH
margin = 64
I, H, T = "items", "height", "tensor"
IH = (I, H)
E0 = "bc,bn->cn"
E1 = "bhqk,bkhd->bqhd"
E2 = "bhqk,bqhd->bkhd"
E3 = "bqhd,bkhd->bhqk"
E4 = "bqhd,bqhd->bhq"
E5 = "bsc,bsjf->cjf"
E6 = "bsc,cjf->bsjf"
E7 = "bsjf,cjf->bsc"
E8 = "bsk,bsn->kn"
E9 = "bsk,kn->bsn"
E10 = "bsn,kn->bsk"
QK, PV, PQ = "qhd,khd->hqk", "hqk,khd->qhd", "hqk,qhd->khd"


def padded_2(block, sides, width):
    for axis, dim in sides:
        count = lax.axis_size(axis)
        forward = [(i, i + 1) for i in range(count - 1)]
        backward = [(target, source) for source, target in forward]
        low = lax.ppermute(
            lax.slice_in_dim(block, block.shape[dim] - width, None, axis=dim), axis, forward
        )
        high = lax.ppermute(lax.slice_in_dim(block, 0, width, axis=dim), axis, backward)
        block = jnp.concatenate([low, block, high], axis=dim)
    return block


def grid_shape(bucket):
    strip_rows = jnp.where(bucket == 0, 8, jnp.where(bucket == 1, 6, 5)).astype(jnp.int32)
    strip_width = jnp.where(bucket == 0, 32, jnp.where(bucket == 1, 40, 48)).astype(jnp.int32)
    return (strip_rows, strip_width)


def tokens_dot(values, weight):
    return jnp.einsum(E9, values, weight, precision=highest)


def tokens_back(grad_values, weight):
    return jnp.einsum(E10, grad_values, weight, precision=highest)


def tokens_grad(values, grad_values):
    return jnp.einsum(E8, values, grad_values, precision=highest)


def tensor_sum(values):
    return lax.psum(values, T)


def expand_groups(stat, size_group):
    return jnp.repeat(stat, size_group, axis=1)[:, None, :]


def group_stats(values, valid_col, group_count, counts):
    item_count, slot_count, channels = values.shape
    size_group = channels // group_count
    grouped = (values * valid_col).reshape(item_count, slot_count, group_count, size_group)
    sum_values = jnp.sum(grouped, axis=(1, 3))
    sum_squares = jnp.sum(grouped * grouped, axis=(1, 3))
    sum_values, sum_squares = lax.psum((sum_values, sum_squares), H)
    mean_val = sum_values / counts[:, None]
    var_val = sum_squares / counts[:, None] - mean_val * mean_val
    return (
        expand_groups(mean_val, size_group),
        expand_groups(lax.rsqrt(var_val + norm_eps), size_group),
    )


def group_back(grad_out, centred, inv_std, gain_vector, valid_col, group_count, counts):
    item_count, slot_count, channels = grad_out.shape
    size_group = channels // group_count
    scaled = grad_out * gain_vector * valid_col
    sum_first = jnp.sum(
        scaled.reshape(item_count, slot_count, group_count, size_group), axis=(1, 3)
    )
    sum_second = jnp.sum(
        (scaled * centred).reshape(item_count, slot_count, group_count, size_group), axis=(1, 3)
    )
    sum_first, sum_second = lax.psum((sum_first, sum_second), H)
    mean_first = expand_groups(sum_first / counts[:, None], size_group)
    mean_second = expand_groups(sum_second / counts[:, None], size_group)
    grad_in = inv_std * (scaled - mean_first - centred * mean_second) * valid_col
    return (grad_in, jnp.sum(grad_out * centred, axis=(0, 1)))


def layer_norm(values, gain_vector):
    mean_val = jnp.mean(values, axis=-1, keepdims=True)
    var_val = jnp.mean(values * values, axis=-1, keepdims=True) - mean_val * mean_val
    inv_std = lax.rsqrt(var_val + norm_eps)
    centred = (values - mean_val) * inv_std
    return (centred * gain_vector, centred, inv_std)


def layer_back(grad_out, centred, inv_std, gain_vector):
    scaled = grad_out * gain_vector
    grad_in = inv_std * (
        scaled
        - jnp.mean(scaled, axis=-1, keepdims=True)
        - centred * jnp.mean(scaled * centred, axis=-1, keepdims=True)
    )
    return (grad_in, jnp.sum(grad_out * centred, axis=(0, 1)))


def edge_rows(values, strip_rows, strip_width):
    item_count, slot_count, channels = values.shape
    position = jnp.arange(EDGE, dtype=jnp.int32)

    def edge_one_item(item_vals, rows_here, width_here):
        keep_mask = (position < width_here)[:, None].astype(jnp.float32)
        padded = jnp.concatenate([item_vals, jnp.zeros((EDGE, channels), jnp.float32)], axis=0)
        top_row = item_vals[:EDGE] * keep_mask
        bottom_row = (
            lax.dynamic_slice_in_dim(padded, (rows_here - 1) * width_here, EDGE, 0) * keep_mask
        )
        return jnp.stack([top_row, bottom_row])

    return jax.vmap(edge_one_item)(values, strip_rows, strip_width)


def neighbour_stack(values, strip_rows, strip_width):
    edge_pair = edge_rows(values, strip_rows, strip_width)
    beside_all = padded_2(edge_pair, ((H, 1),), 1)
    item_count, slot_count, channels = values.shape
    position = jnp.arange(slot_count, dtype=jnp.int32)

    def neighbour_one_item(item_vals, item_around, rows_here, width_here):
        cell_span = rows_here * width_here
        extended = jnp.zeros((2 * edge_margin + slot_count, channels), jnp.float32)
        extended = lax.dynamic_update_slice_in_dim(
            extended, item_around[0], edge_margin - width_here, 0
        )
        extended = lax.dynamic_update_slice_in_dim(extended, item_vals, edge_margin, 0)
        extended = lax.dynamic_update_slice_in_dim(
            extended, item_around[3], edge_margin + cell_span, 0
        )
        column = position % width_here
        shifted_list = []
        for row_step in (-1, 0, 1):
            for col_step in (-1, 0, 1):
                shifted = lax.dynamic_slice_in_dim(
                    extended, edge_margin + row_step * width_here + col_step, slot_count, 0
                )
                keep_mask = (
                    (column + col_step >= 0)
                    & (column + col_step < width_here)
                    & (position < cell_span)
                )
                shifted_list.append(shifted * keep_mask[:, None].astype(jnp.float32))
        return jnp.stack(shifted_list, axis=1)

    return jax.vmap(neighbour_one_item)(values, beside_all, strip_rows, strip_width)


def conv_apply(neighbours, weight):
    item_count, slot_count = (neighbours.shape[0], neighbours.shape[1])
    flattened = neighbours.reshape(item_count, slot_count, -1)
    return tokens_dot(flattened, weight.reshape(-1, weight.shape[3]))


def conv_input_grad(neighbours_grad, weight):
    flipped = jnp.transpose(weight[::-1, ::-1], (0, 1, 3, 2))
    return conv_apply(neighbours_grad, flipped)


def conv_weight_grad(neighbours, grad_out, weight_shape):
    flattened = neighbours.reshape(neighbours.shape[0], neighbours.shape[1], -1)
    return tokens_grad(flattened, grad_out).reshape(weight_shape)


def time_features(timestep, channels):
    half_width = channels // 2
    frequency = jnp.exp(-math.log(10000.0) * jnp.arange(half_width, dtype=jnp.float32) / half_width)
    angles = timestep.astype(jnp.float32)[:, None] * frequency[None, :]
    return jnp.concatenate([jnp.cos(angles), jnp.sin(angles)], axis=1)


def exact_gelu(values):
    return jax.nn.gelu(values, approximate=False)


def head_split(values, heads_here):
    return values.reshape(
        values.shape[0], values.shape[1], heads_here, values.shape[2] // heads_here
    )


def score_block(queries, keys_all, key_valid, heads_here):
    head_size = queries.shape[2] // heads_here
    scores = jnp.einsum(
        E3,
        head_split(queries, heads_here),
        head_split(keys_all, heads_here),
        precision=highest,
    ) * (1.0 / math.sqrt(head_size))
    return jnp.where(key_valid[:, None, None, :], scores, masked_score)


def attend(queries, keys_all, values_all, key_valid, heads_here):
    scores = score_block(queries, keys_all, key_valid, heads_here)
    row_peak = jnp.max(scores, axis=-1, keepdims=True)
    exponent = jnp.exp(scores - row_peak)
    row_total = jnp.sum(exponent, axis=-1, keepdims=True)
    soft_weights = exponent / row_total
    attended = jnp.einsum(
        E1, soft_weights, head_split(values_all, heads_here), precision=highest
    )
    return (attended.reshape(queries.shape), row_peak + jnp.log(row_total))


def attend_back(
    queries, keys_all, values_all, key_valid, heads_here, attended, log_total, grad_attended
):
    head_size = queries.shape[2] // heads_here
    scaling = 1.0 / math.sqrt(head_size)
    soft_weights = jnp.exp(score_block(queries, keys_all, key_valid, heads_here) - log_total)
    grad_heads = head_split(grad_attended, heads_here)
    grad_soft = jnp.einsum(
        E3, grad_heads, head_split(values_all, heads_here), precision=highest
    )
    row_delta = jnp.einsum(
        E4, grad_heads, head_split(attended, heads_here), precision=highest
    )
    grad_scores = soft_weights * (grad_soft - row_delta[..., None])
    grad_query = (
        jnp.einsum(
            E1, grad_scores, head_split(keys_all, heads_here), precision=highest
        )
        * scaling
    )
    grad_key = (
        jnp.einsum(
            E2, grad_scores, head_split(queries, heads_here), precision=highest
        )
        * scaling
    )
    grad_value = jnp.einsum(E2, soft_weights, grad_heads, precision=highest)
    return (
        grad_query.reshape(queries.shape),
        grad_key.reshape(keys_all.shape),
        grad_value.reshape(values_all.shape),
    )


def shards(
    hidden,
    text_states,
    bucket,
    timestep,
    gain_in,
    conv_first,
    time_weight,
    gain_mid,
    conv_second,
    gain_attn_norm,
    proj_in,
    gain_self,
    query_self,
    key_self,
    value_self,
    out_self,
    gain_cross,
    query_cross,
    key_cross,
    value_cross,
    out_cross,
    gain_ff,
    ff_in,
    ff_out,
    proj_out,
    cotangent,
):
    item_count, slot_count, channels = hidden.shape
    local_width = gain_mid.shape[0]
    local_groups = GROUPS * local_width // channels
    heads_here = local_width // HEAD_DIM
    height_count = lax.axis_size(H)
    width_ih = lax.axis_size(I) * lax.axis_size(H)
    offset = lax.axis_index(T) * local_width
    strip_rows, strip_width = grid_shape(bucket)
    cell_span = strip_rows * strip_width
    position = jnp.arange(slot_count, dtype=jnp.int32)
    valid_mask = position[None, :] < cell_span[:, None]
    valid_col = valid_mask[:, :, None].astype(jnp.float32)
    full_counts = (height_count * cell_span * (channels // GROUPS)).astype(jnp.float32)
    key_valid = jnp.tile(valid_mask, (1, height_count))
    text_valid = jnp.ones((item_count, text_states.shape[1]), dtype=bool)
    resnet_full = (
        lax.all_gather(gain_in, IH, axis=0, tiled=True),
        lax.all_gather(conv_first, IH, axis=2, tiled=True),
        lax.all_gather(time_weight, IH, axis=0, tiled=True),
        lax.all_gather(conv_second, IH, axis=3, tiled=True),
    )
    block_full = (
        lax.all_gather(proj_in, IH, axis=1, tiled=True),
        lax.all_gather(gain_self, IH, axis=0, tiled=True),
        lax.all_gather(query_self, IH, axis=0, tiled=True),
        lax.all_gather(key_self, IH, axis=0, tiled=True),
        lax.all_gather(value_self, IH, axis=0, tiled=True),
        lax.all_gather(out_self, IH, axis=1, tiled=True),
        lax.all_gather(gain_cross, IH, axis=0, tiled=True),
        lax.all_gather(query_cross, IH, axis=0, tiled=True),
        lax.all_gather(key_cross, IH, axis=0, tiled=True),
        lax.all_gather(value_cross, IH, axis=0, tiled=True),
        lax.all_gather(out_cross, IH, axis=1, tiled=True),
        lax.all_gather(gain_ff, IH, axis=0, tiled=True),
        lax.all_gather(ff_in, IH, axis=0, tiled=True),
        lax.all_gather(ff_out, IH, axis=1, tiled=True),
        lax.all_gather(proj_out, IH, axis=0, tiled=True),
    )
    gain_in_full, conv_first_full, time_full, conv_second_full = resnet_full
    (
        proj_in_full,
        gain_self_full,
        query_self_full,
        key_self_full,
        value_self_full,
        out_self_full,
        gain_cross_full,
        query_cross_full,
        key_cross_full,
        value_cross_full,
        out_cross_full,
        gain_ff_full,
        ff_in_full,
        ff_out_full,
        proj_out_full,
    ) = block_full
    source = hidden * valid_col
    mean_one, inv_one = group_stats(source, valid_col, GROUPS, full_counts)
    centred_one = (source - mean_one) * inv_one * valid_col
    norm_one = centred_one * gain_in_full
    act_one, silu_pull_one = jax.vjp(jax.nn.silu, norm_one)
    stack_one = neighbour_stack(act_one, strip_rows, strip_width)
    silu_features = jax.nn.silu(time_features(timestep, channels))
    time_term = jnp.dot(
        silu_features, time_full, precision=highest, preferred_element_type=jnp.float32
    )
    conv_one = (conv_apply(stack_one, conv_first_full) + time_term[:, None, :]) * valid_col
    mean_two, inv_two = group_stats(conv_one, valid_col, local_groups, full_counts)
    centred_two = (conv_one - mean_two) * inv_two * valid_col
    norm_two = centred_two * gain_mid
    act_two, silu_pull_two = jax.vjp(jax.nn.silu, norm_two)
    stack_two = neighbour_stack(act_two, strip_rows, strip_width)
    conv_two = tensor_sum(conv_apply(stack_two, conv_second_full)) * valid_col
    residual = source + conv_two
    residual_local = lax.dynamic_slice_in_dim(residual, offset, local_width, 2)
    mean_three, inv_three = group_stats(residual_local, valid_col, local_groups, full_counts)
    centred_three = (residual_local - mean_three) * inv_three * valid_col
    norm_three = centred_three * gain_attn_norm
    projected = tensor_sum(tokens_dot(norm_three, proj_in_full))
    normed_self, centred_self, inv_self = layer_norm(projected, gain_self_full)
    queries = tokens_dot(normed_self, query_self_full)
    keys_here = tokens_dot(normed_self, key_self_full)
    values_here = tokens_dot(normed_self, value_self_full)
    keys_all, values_all = (
        lax.all_gather(keys_here, H, axis=1, tiled=True),
        lax.all_gather(values_here, H, axis=1, tiled=True),
    )
    attn_self, total_self = attend(queries, keys_all, values_all, key_valid, heads_here)
    after_self = projected + tensor_sum(tokens_dot(attn_self, out_self_full))
    normed_cross, centred_cross, inv_cross = layer_norm(after_self, gain_cross_full)
    queries_cross = tokens_dot(normed_cross, query_cross_full)
    keys_text = tokens_dot(text_states, key_cross_full)
    values_text = tokens_dot(text_states, value_cross_full)
    attn_cross, total_cross = attend(queries_cross, keys_text, values_text, text_valid, heads_here)
    after_cross = after_self + tensor_sum(tokens_dot(attn_cross, out_cross_full))
    normed_ff, centred_ff, inv_ff = layer_norm(after_cross, gain_ff_full)
    hidden_ff = jnp.einsum(E6, normed_ff, ff_in_full, precision=highest)
    value_half = hidden_ff[:, :, 0]
    gate_act, gelu_pull = jax.vjp(exact_gelu, hidden_ff[:, :, 1])
    ff_act = value_half * gate_act
    after_ff = after_cross + tensor_sum(tokens_dot(ff_act, ff_out_full))
    output = (residual_local + tokens_dot(after_ff, proj_out_full)) * valid_col
    (
        proj_in_back,
        gain_self_back,
        query_self_back,
        key_self_back,
        value_self_back,
        out_self_back,
        gain_cross_back,
        query_cross_back,
        key_cross_back,
        value_cross_back,
        out_cross_back,
        gain_ff_back,
        ff_in_back,
        ff_out_back,
        proj_out_back,
    ) = block_full
    grad_local = cotangent * valid_col
    grad_proj_out = tokens_grad(after_ff, grad_local)
    grad_after_ff = tensor_sum(tokens_back(grad_local, proj_out_back))
    grad_ff_out = tokens_grad(ff_act, grad_after_ff)
    grad_ff_act = tokens_back(grad_after_ff, ff_out_back)
    grad_value_half = grad_ff_act * gate_act
    grad_gate_half = gelu_pull(grad_ff_act * value_half)[0]
    grad_hidden_ff = jnp.stack([grad_value_half, grad_gate_half], axis=2)
    grad_ff_in = jnp.einsum(E5, normed_ff, grad_hidden_ff, precision=highest)
    grad_normed_ff = tensor_sum(
        jnp.einsum(E7, grad_hidden_ff, ff_in_back, precision=highest)
    )
    back_ff, grad_gain_ff = layer_back(grad_normed_ff, centred_ff, inv_ff, gain_ff_back)
    grad_after_cross = grad_after_ff + back_ff
    grad_out_cross = tokens_grad(attn_cross, grad_after_cross)
    grad_attn_cross = tokens_back(grad_after_cross, out_cross_back)
    grad_queries_cross, grad_keys_text, grad_values_text = attend_back(
        queries_cross,
        keys_text,
        values_text,
        text_valid,
        heads_here,
        attn_cross,
        total_cross,
        grad_attn_cross,
    )
    grad_query_cross = tokens_grad(normed_cross, grad_queries_cross)
    grad_key_cross = tokens_grad(text_states, grad_keys_text)
    grad_value_cross = tokens_grad(text_states, grad_values_text)
    grad_normed_cross = tensor_sum(tokens_back(grad_queries_cross, query_cross_back))
    back_cross, grad_gain_cross = layer_back(
        grad_normed_cross, centred_cross, inv_cross, gain_cross_back
    )
    grad_after_self = grad_after_cross + back_cross
    grad_out_self = tokens_grad(attn_self, grad_after_self)
    grad_attn_self = tokens_back(grad_after_self, out_self_back)
    grad_queries, grad_keys_all, grad_values_all = attend_back(
        queries, keys_all, values_all, key_valid, heads_here, attn_self, total_self, grad_attn_self
    )
    grad_keys_here, grad_values_here = (
        lax.psum_scatter(grad_keys_all, H, scatter_dimension=1, tiled=True),
        lax.psum_scatter(grad_values_all, H, scatter_dimension=1, tiled=True),
    )
    grad_query_self = tokens_grad(normed_self, grad_queries)
    grad_key_self = tokens_grad(normed_self, grad_keys_here)
    grad_value_self = tokens_grad(normed_self, grad_values_here)
    grad_normed_self = tensor_sum(
        tokens_back(grad_queries, query_self_back)
        + tokens_back(grad_keys_here, key_self_back)
        + tokens_back(grad_values_here, value_self_back)
    )
    back_self, grad_gain_self = layer_back(grad_normed_self, centred_self, inv_self, gain_self_back)
    grad_projected = grad_after_self + back_self
    grad_proj_in = tokens_grad(norm_three, grad_projected)
    grad_norm_three = tokens_back(grad_projected, proj_in_back)
    back_three, grad_gain_attn = group_back(
        grad_norm_three,
        centred_three,
        inv_three,
        gain_attn_norm,
        valid_col,
        local_groups,
        full_counts,
    )
    grad_residual_local = grad_local + back_three
    block_grads = (
        lax.psum_scatter(grad_proj_in, IH, scatter_dimension=1, tiled=True),
        lax.psum_scatter(
            jnp.tile(grad_gain_attn, width_ih), IH, scatter_dimension=0, tiled=True
        ),
        lax.psum_scatter(grad_gain_self, IH, scatter_dimension=0, tiled=True),
        lax.psum_scatter(grad_query_self, IH, scatter_dimension=0, tiled=True),
        lax.psum_scatter(grad_key_self, IH, scatter_dimension=0, tiled=True),
        lax.psum_scatter(grad_value_self, IH, scatter_dimension=0, tiled=True),
        lax.psum_scatter(grad_out_self, IH, scatter_dimension=1, tiled=True),
        lax.psum_scatter(grad_gain_cross, IH, scatter_dimension=0, tiled=True),
        lax.psum_scatter(grad_query_cross, IH, scatter_dimension=0, tiled=True),
        lax.psum_scatter(grad_key_cross, IH, scatter_dimension=0, tiled=True),
        lax.psum_scatter(grad_value_cross, IH, scatter_dimension=0, tiled=True),
        lax.psum_scatter(grad_out_cross, IH, scatter_dimension=1, tiled=True),
        lax.psum_scatter(grad_gain_ff, IH, scatter_dimension=0, tiled=True),
        lax.psum_scatter(grad_ff_in, IH, scatter_dimension=0, tiled=True),
        lax.psum_scatter(grad_ff_out, IH, scatter_dimension=1, tiled=True),
        lax.psum_scatter(grad_proj_out, IH, scatter_dimension=0, tiled=True),
    )
    gain_in_back, conv_first_back, time_back, conv_second_back = resnet_full
    grad_residual = lax.all_gather(grad_residual_local, T, axis=2, tiled=True)
    grad_conv_second = conv_weight_grad(stack_two, grad_residual, conv_second_back.shape)
    stack_grad_two = neighbour_stack(grad_residual, strip_rows, strip_width)
    grad_act_two = conv_input_grad(stack_grad_two, conv_second_back)
    grad_norm_two = silu_pull_two(grad_act_two)[0]
    grad_conv_one, grad_gain_mid = group_back(
        grad_norm_two, centred_two, inv_two, gain_mid, valid_col, local_groups, full_counts
    )
    grad_time_term = jnp.sum(grad_conv_one, axis=1)
    grad_time_weight = jnp.einsum(E0, silu_features, grad_time_term, precision=highest)
    grad_conv_first = conv_weight_grad(stack_one, grad_conv_one, conv_first_back.shape)
    stack_grad_one = neighbour_stack(grad_conv_one, strip_rows, strip_width)
    grad_act_one = tensor_sum(conv_input_grad(stack_grad_one, conv_first_back))
    grad_norm_one = silu_pull_one(grad_act_one)[0]
    back_one, grad_gain_in = group_back(
        grad_norm_one, centred_one, inv_one, gain_in_back, valid_col, GROUPS, full_counts
    )
    grad_hidden = (grad_residual + back_one) * valid_col
    resnet_grads = (
        lax.psum_scatter(grad_gain_in, IH, scatter_dimension=0, tiled=True),
        lax.psum_scatter(grad_conv_first, IH, scatter_dimension=2, tiled=True),
        lax.psum_scatter(grad_time_weight, IH, scatter_dimension=0, tiled=True),
        lax.psum_scatter(
            jnp.tile(grad_gain_mid, width_ih), IH, scatter_dimension=0, tiled=True
        ),
        lax.psum_scatter(grad_conv_second, IH, scatter_dimension=3, tiled=True),
    )
    return (
        output,
        grad_hidden,
        resnet_grads[0],
        resnet_grads[1],
        resnet_grads[2],
        resnet_grads[3],
        resnet_grads[4],
        block_grads[1],
        block_grads[0],
        block_grads[2],
        block_grads[3],
        block_grads[4],
        block_grads[5],
        block_grads[6],
        block_grads[7],
        block_grads[8],
        block_grads[9],
        block_grads[10],
        block_grads[11],
        block_grads[12],
        block_grads[13],
        block_grads[14],
        block_grads[15],
    )


def mm(left, right, left_dim, right_dim):
    return lax.dot_general(
        left,
        right,
        (((left_dim,), (right_dim,)), ((), ())),
        precision=high,
        preferred_element_type=jnp.float32,
    )


def swap(values):
    return lax.ppermute(values, I, [(0, 1), (1, 0)])


def flip(values, step):
    return lax.ppermute(values, H, [(s, s ^ step) for s in range(4)])


def turn(values, step):
    return lax.ppermute(values, T, [(s, (s + step) % 4) for s in range(4)])


def z_pieces(values):
    return [values] + [turn(values, 4 - j) for j in (1, 2, 3)]


def total_of(pieces):
    return (pieces[0] + pieces[1]) + (pieces[2] + pieces[3])


def z_received(pieces):
    return [pieces[0]] + [turn(pieces[j], j) for j in (1, 2, 3)]


def z_all(values):
    return lax.all_to_all(values, T, 0, 0)


def z_spread(values):
    return z_all(jnp.broadcast_to(values[None], (4,) + values.shape))


def folded(values):
    values = jnp.pad(values, ((0, 3), (0, 0)))
    return jnp.concatenate([values[:40], values[40:]], axis=1)


def unfolded(values):
    return jnp.concatenate([values[:, :640], values[:37, 640:]], axis=0)


def h_collect(pieces):
    total = pieces[0]
    for j in (1, 2, 3):
        total = total + flip(pieces[j], j)
    return total


def h_sum(values):
    pair = values + flip(values, 1)
    return pair + flip(pair, 2)


def pick(values, index, axis=0):
    return lax.dynamic_index_in_dim(values, index, axis, keepdims=False)


def plane_sum(own):
    part = h_collect([own[j] for j in range(4)])
    pieces = [part] + [flip(part, j) for j in (1, 2, 3)]
    return pieces + [swap(piece) for piece in pieces], part


def plane_exchange(packed):
    return lax.all_to_all(packed, IH, 0, 0)


IMAGE_ROWS = 1152
TAP_ROWS = range(16, 1136, 160)


def halves(values):
    top = values.astype(jnp.bfloat16)
    return top, (values - top.astype(jnp.float32)).astype(jnp.bfloat16)


def dot_halves(left, right, left_dim, right_dim):
    def one(a, b):
        return lax.dot_general(
            a, b, (((left_dim,), (right_dim,)), ((), ())), preferred_element_type=jnp.float32
        )

    return one(left[0], right[0]) + (one(left[0], right[1]) + one(left[1], right[0]))


def marks_of(marks, b):
    return marks[2 * b], marks[2 * b + 1]


def row_mask(span, rows, columns):
    return (lax.broadcasted_iota(jnp.int32, (rows, columns), 0) < span).astype(jnp.float32)


def unpack_quarter(packed):
    rest = jnp.concatenate([packed[64:80, 32 * g : 32 * g + 32] for g in range(4)], axis=0)
    return jnp.concatenate([packed[:64], rest], axis=1)


def put_quarter(out, place, values, row=0):
    out[place, row : row + 64, :] = values[:, :128]
    for g in range(4):
        out[place, row + 64 : row + 80, 32 * g : 32 * g + 32] = values[
            16 * g : 16 * g + 16, 128:160
        ]


def unpack_strip(packed):
    rest = jnp.concatenate([packed[256:320, 64 * g : 64 * g + 64] for g in range(4)], axis=0)
    return jnp.concatenate([packed[:256], rest], axis=1)


def put_packed_strip(out, place, values):
    out[place, 0:256, :] = values[:, :256]
    for g in range(4):
        out[place, 256:320, 64 * g : 64 * g + 64] = values[64 * g : 64 * g + 64, 256:320]


def put_strip(image, b, strip, span, values):
    at = pl.multiple_of(margin + strip * span, 8)
    image[b, pl.ds(at, 240)] = values[:240]

    @pl.when(span == 256)
    def _():
        image[b, pl.ds(pl.multiple_of(at + 240, 8), 16)] = values[240:]


def put_cells(image, b, strip, span, q, values):
    at = pl.multiple_of(margin + strip * span + q * 64, 8)
    image[b, pl.ds(at, 48)] = values[:48]

    @pl.when((q < 3) | (span == 256))
    def _():
        image[b, pl.ds(pl.multiple_of(at + 48, 8), 16)] = values[48:]


def quarter_mask(span, q):
    row = lax.broadcasted_iota(jnp.int32, (64, 160), 0) + q * 64
    return (row < span).astype(jnp.float32)


def widen(wide, image, b, width, sign):
    channels = image.shape[2]
    width_f = width.astype(jnp.float32)
    for base in TAP_ROWS:
        row = lax.broadcasted_iota(jnp.int32, (160, channels), 0).astype(jnp.float32)
        cell = row + float(base - margin)
        column = cell - width_f * jnp.floor((cell + 0.5) / width_f)
        for j in range(3):
            step = sign * (j - 1)
            values = image[b, base + step : base + step + 160, :]
            if step < 0:
                values = jnp.where(column > 0.5, values, 0.0)
            if step > 0:
                values = jnp.where(column < width_f - 1.5, values, 0.0)
            wide[base : base + 160, j * channels : (j + 1) * channels] = values


def split_weight(weight, top, low):
    for k in range(3):
        rows = weight.shape[0] // 3
        first, second = halves(weight[k * rows : (k + 1) * rows, :])
        top[k * rows : (k + 1) * rows, :] = first
        low[k * rows : (k + 1) * rows, :] = second


def split_weight_turned(weight, top, low):
    for tap in range(9):
        first, second = halves(weight[160 * tap : 160 * tap + 160, :].T)
        top[320 * tap : 320 * tap + 320, :] = first
        low[320 * tap : 320 * tap + 320, :] = second


def conv_strip(wide, top, low, strip, span, width, sign):
    rows = top.shape[0] // 3
    total = None
    for i in range(3):
        at = pl.multiple_of(margin + strip * span + sign * (i - 1) * width, 8)
        taps = halves(wide[pl.ds(at, 256), :])
        part = dot_halves(
            taps, (top[i * rows : (i + 1) * rows, :], low[i * rows : (i + 1) * rows, :]), 1, 0
        )
        total = part if total is None else total + part
    return total * row_mask(span, 256, total.shape[1])


def group_rows(sums):
    channels = sums.shape[1]
    lane = lax.broadcasted_iota(jnp.int32, (1, channels), 1)
    result = jnp.zeros((1, channels), jnp.float32)
    for g in range(channels // 40):
        inside = (lane >= 40 * g) & (lane < 40 * g + 40)
        result = jnp.where(inside, jnp.sum(jnp.where(inside, sums, 0.0)), result)
    return result


def group_row_stats(total, squares, span):
    count = (span * 160).astype(jnp.float32)
    mean = group_rows(total) / count
    var = group_rows(squares) / count - mean * mean
    return mean, lax.rsqrt(var + norm_eps)


def column_sum(values):
    return jnp.sum(values, axis=0, keepdims=True)


def first_kernel(
    marks, source, gain, tau, weight, own, other, image, stats, wide, top, low, cells
):
    item, h = marks[4], marks[5]
    split_weight(weight, top, low)
    image[...] = jnp.zeros_like(image)
    for b, out in ((0, own), (1, other)):
        span, width = marks_of(marks, b)
        base = (item ^ b) * 4
        total = jnp.zeros((1, 160), jnp.float32)
        squares = jnp.zeros((1, 160), jnp.float32)
        for k in range(4):
            for q in range(4):
                values = unpack_quarter(source[base + k, 80 * q : 80 * q + 80, :])
                cells[k, 64 * q : 64 * q + 64, :] = values
                total = total + column_sum(values)
                squares = squares + column_sum(values * values)
        mean, inv = group_row_stats(total, squares, span)
        stats[b, 0:1, :] = mean
        stats[b, 1:2, :] = inv
        for k in range(4):
            norm = (cells[k] - mean) * inv * row_mask(span, 256, 160) * gain[...]
            put_strip(image, b, k, span, norm * jax.nn.sigmoid(norm))
        widen(wide, image, b, width, 1)
        added = tau[b : b + 1, :]

        def step(k, _):
            conv = conv_strip(wide, top, low, k, span, width, 1)
            put_packed_strip(out, k ^ h, conv + added * row_mask(span, 256, 320))
            return 0

        lax.fori_loop(0, 4, step, 0)


def put_quarters(outs, tile, place, t):
    for j in range(4):
        at = pl.multiple_of(lax.rem(t + j, 4) * 64, 8)
        put_quarter(outs[j], place, tile[pl.ds(at, 64), :])


def second_kernel(marks, *refs):
    strips, gain, weight = refs[:8], refs[8], refs[9]
    outs, image, stats = refs[10:14], refs[14], refs[15]
    wide, top, low, tile = refs[16:]
    item, h, t = marks[4], marks[5], marks[6]
    split_weight_turned(weight, top, low)
    image[...] = jnp.zeros_like(image)
    for b in range(2):
        span, width = marks_of(marks, b)
        total = jnp.zeros((1, 320), jnp.float32)
        squares = jnp.zeros((1, 320), jnp.float32)
        for j in range(4):
            values = unpack_strip(strips[4 * b + j][...])
            total = total + column_sum(values)
            squares = squares + column_sum(values * values)
        mean, inv = group_row_stats(total, squares, span)
        stats[b, 0:1, :] = mean
        stats[b, 1:2, :] = inv
        for j in range(4):
            values = unpack_strip(strips[4 * b + j][...])
            norm = (values - mean) * inv * row_mask(span, 256, 320) * gain[...]
            put_strip(image, b, h ^ j, span, norm * jax.nn.sigmoid(norm))
        widen(wide, image, b, width, 1)

        def step(k, _):
            tile[...] = conv_strip(wide, top, low, k, span, width, 1)
            put_quarters(outs, tile, (item ^ b) * 4 + k, t)
            return 0

        lax.fori_loop(0, 4, step, 0)


def second_back_kernel(marks, *refs):
    quarters, weight = refs[:4], refs[4]
    own, other, image = refs[5:8]
    wide, top, low = refs[8:]
    item, h, t = marks[4], marks[5], marks[6]
    split_weight(weight, top, low)
    image[...] = jnp.zeros_like(image)
    for b, out in ((0, own), (1, other)):
        span, width = marks_of(marks, b)

        def fill(k, _):
            for j in range(4):
                values = unpack_quarter(quarters[j][(item ^ b) * 4 + k])
                put_cells(image, b, k, span, lax.rem(t + j, 4), values)
            return 0

        lax.fori_loop(0, 4, fill, 0)
        widen(wide, image, b, width, -1)

        def step(k, _):
            put_packed_strip(out, k ^ h, conv_strip(wide, top, low, k, span, width, -1))
            return 0

        lax.fori_loop(0, 4, step, 0)


def first_back_kernel(marks, *refs):
    grads, strips, gain, stats, weight = refs[:8], refs[8:16], refs[16], refs[17], refs[18]
    outs, image, sums, grad_gain = refs[19:23], refs[23], refs[24], refs[25]
    wide, top, low, tile, scaled_at, centred_at = refs[26:]
    item, h, t = marks[4], marks[5], marks[6]
    split_weight_turned(weight, top, low)
    image[...] = jnp.zeros_like(image)
    gain_total = jnp.zeros((1, 320), jnp.float32)
    for b in range(2):
        span, width = marks_of(marks, b)
        mean, inv = stats[b, 0:1, :], stats[b, 1:2, :]
        first = jnp.zeros((1, 320), jnp.float32)
        second = jnp.zeros((1, 320), jnp.float32)
        for j in range(4):
            values = unpack_strip(strips[4 * b + j][...])
            centred = (values - mean) * inv * row_mask(span, 256, 320)
            norm = centred * gain[...]
            gate = jax.nn.sigmoid(norm)
            grad_norm = unpack_strip(grads[4 * b + j][...]) * gate * (1.0 + norm * (1.0 - gate))
            scaled = grad_norm * gain[...]
            first = first + column_sum(scaled)
            second = second + column_sum(scaled * centred)
            gain_total = gain_total + column_sum(grad_norm * centred)
            scaled_at[j] = scaled
            centred_at[j] = centred
        count = (span * 160).astype(jnp.float32)
        first = group_rows(first) / count
        second = group_rows(second) / count
        tau_total = jnp.zeros((1, 320), jnp.float32)
        for j in range(4):
            grad = inv * row_mask(span, 256, 320) * (
                scaled_at[j] - first - centred_at[j] * second
            )
            tau_total = tau_total + column_sum(grad)
            put_strip(image, b, h ^ j, span, grad)
        sums[b : b + 1, :] = tau_total
        widen(wide, image, b, width, -1)

        def step(k, _):
            tile[...] = conv_strip(wide, top, low, k, span, width, -1)
            put_quarters(outs, tile, (item ^ b) * 4 + k, t)
            return 0

        lax.fori_loop(0, 4, step, 0)
    grad_gain[...] = gain_total


def conv_weight_kernel(sign, marks, image, cells, out, wide):
    out[...] = jnp.zeros_like(out)
    for b in range(2):
        _, width = marks_of(marks, b)
        widen(wide, image, b, width, sign)
        for i in range(3):

            def step(c, _):
                at = pl.multiple_of(margin + c * 256 + sign * (i - 1) * width, 8)
                taps = halves(wide[pl.ds(at, 256), :].T)
                values = halves(cells[b, pl.ds(pl.multiple_of(margin + c * 256, 8), 256), :])
                part = dot_halves(taps, values, 1, 0)
                for j in range(3):
                    out[3 * i + j] += part[160 * j : 160 * j + 160]
                return 0

            lax.fori_loop(0, 4, step, 0)


def wide_halves(values):
    top, low = halves(values)
    return jnp.concatenate([top, top, low], axis=1)


def other_halves(values):
    top, low = halves(values)
    return jnp.concatenate([top, low, top], axis=1)


def dot_last(left, right):
    return lax.dot_general(
        left, right, (((1,), (1,)), ((), ())), preferred_element_type=jnp.float32
    )


def dot_pair(left, values):
    top, low = halves(values)
    both = jnp.dot(left[0], jnp.concatenate([top, low], axis=1), preferred_element_type=jnp.float32)
    return (both[:, :64] + both[:, 64:]) + jnp.dot(
        left[1], top, preferred_element_type=jnp.float32
    )


def scores_turned(marks, queries, pieces, head, j):
    at = 64 * head
    keys = pieces[j][:, at : at + 64]
    scores = dot_last(wide_halves(keys), other_halves(queries[:, at : at + 64])) * 0.125
    slot = lax.broadcasted_iota(jnp.int32, (256, 256), 0) + marks[6] * 64
    slot = jnp.where(slot >= 256, slot - 256, slot)
    return jnp.where(slot < marks[0], scores, masked_score)


def attend_kernel(marks, qkv, *refs):
    pieces, out, totals, held = refs[:4], refs[4], refs[5], refs[6]
    totals[...] = jnp.zeros_like(totals)
    for head in range(5):
        peak = None
        for j in range(4):
            scores = scores_turned(marks, qkv, pieces, head, j)
            held[256 * j : 256 * j + 256, :] = scores
            here = jnp.max(scores, axis=0, keepdims=True)
            peak = here if peak is None else jnp.maximum(peak, here)
        total = jnp.zeros((1, 256), jnp.float32)
        attended = jnp.zeros((64, 256), jnp.float32)
        for j in range(4):
            exponent = jnp.exp(held[256 * j : 256 * j + 256, :] - peak)
            total = total + column_sum(exponent)
            values = halves(pieces[j][:, 320 + 64 * head : 384 + 64 * head].T)
            first, second = halves(exponent)
            both = jnp.dot(
                jnp.concatenate(values, axis=0), first, preferred_element_type=jnp.float32
            )
            attended = attended + (
                (both[:64] + both[64:])
                + jnp.dot(values[0], second, preferred_element_type=jnp.float32)
            )
        out[:, 64 * head : 64 * head + 64] = (attended / total).T
        totals[head : head + 1, :] = peak + jnp.log(total)


def attend_back_kernel(marks, qkv, *refs):
    pieces, totals, attended, grad = refs[:4], refs[4], refs[5], refs[6]
    grad_query, outs = refs[7], refs[8:12]
    for head in range(5):
        at = 64 * head
        grad_out = grad[:, at : at + 64]
        queries = qkv[:, at : at + 64]
        delta = column_sum((grad_out * attended[:, at : at + 64]).T)
        total = totals[head : head + 1, :]
        grad_other = other_halves(grad_out)
        query_grad = jnp.zeros((64, 256), jnp.float32)
        for j in range(4):
            weights = jnp.exp(scores_turned(marks, qkv, pieces, head, j) - total)
            values = pieces[j][:, 320 + at : 384 + at]
            grad_scores = weights * (dot_last(wide_halves(values), grad_other) - delta)
            outs[j][:, 320 + at : 384 + at] = dot_pair(halves(weights), grad_out)
            first, second = halves(grad_scores)
            outs[j][:, at : at + 64] = dot_pair((first, second), queries) * 0.125
            keys = halves(pieces[j][:, at : at + 64].T)
            both = jnp.dot(
                jnp.concatenate(keys, axis=0), first, preferred_element_type=jnp.float32
            )
            query_grad = query_grad + (
                (both[:64] + both[64:])
                + jnp.dot(keys[0], second, preferred_element_type=jnp.float32)
            )
        grad_query[:, at : at + 64] = query_grad.T * 0.125


def pack_kernel(marks, values, out):
    for q in range(values.shape[0] // 64):
        for k in range(8):
            part = values[64 * q : 64 * q + 64, 160 * k : 160 * k + 160]
            put_quarter(out, k, part, 80 * q)


def unpack_kernel(marks, packed, plain):
    for k in range(8):
        plain[:, 160 * k : 160 * k + 160] = unpack_quarter(packed[k, 0:80, :])


def unpack_norm_kernel(marks, packed, gain, scaled, plain):
    for k in range(8):
        centred = unpack_quarter(packed[k, 0:80, :])
        mean = jnp.concatenate([packed[k, 80:81, :], packed[k, 81:82, 0:32]], axis=1)
        inv = jnp.concatenate([packed[k, 82:83, :], packed[k, 83:84, 0:32]], axis=1)
        at = slice(160 * k, 160 * k + 160)
        scaled[:, at] = centred * gain[:, at]
        plain[:, at] = centred * (1.0 / inv) + mean


def cotangent_kernel(marks, pieces, total, out, whole):
    total[...] = (pieces[0, :, :1280] + pieces[1, :, :1280]) + (
        pieces[2, :, :1280] + pieces[3, :, :1280]
    )
    for part in range(4):
        whole[:, 320 * part : 320 * part + 320] = pieces[part, :, 1280:1600]
    for k in range(8):
        put_quarter(out, k, whole[:, 160 * k : 160 * k + 160])


def third_kernel(marks, *refs):
    pieces, out, gain = refs[:4], refs[4], refs[5]
    for first in range(4):

        @pl.when(marks[6] == first)
        def _():
            for j in range(4):
                at = (first + j) % 4 * 320
                gain[:, at : at + 320] = pieces[j][160:161, 0:320]
                for m in range(3):
                    out[:, 1280 * m + at : 1280 * m + at + 320] = pieces[j][
                        0:160, 320 * m : 320 * m + 320
                    ]


def text_kernel(marks, pieces, rows, keys, values):
    for part in range(4):
        at = pl.multiple_of(lax.rem(part - marks[6] + 4, 4) * 64, 8)
        rows[pl.ds(at, 64), :] = pieces[part, 0:64, :]
        lanes = slice(320 * part, 320 * part + 320)
        keys[0:40, lanes] = pieces[part, 64:104, 0:320]
        values[0:40, lanes] = pieces[part, 64:104, 320:640]
        keys[40:77, lanes] = pieces[part, 64:101, 640:960]
        values[40:77, lanes] = pieces[part, 64:101, 960:1280]


def text_grad_kernel(marks, keys, values, *outs):
    for first in range(4):

        @pl.when(marks[6] == first)
        def _():
            for j in range(4):
                at = (first + j) % 4 * 320
                lanes = slice(at, at + 320)
                outs[j][:, 0:320] = keys[0:40, lanes]
                outs[j][:, 320:640] = values[0:40, lanes]
                outs[j][0:37, 640:960] = keys[40:77, lanes]
                outs[j][0:37, 960:1280] = values[40:77, lanes]
                outs[j][37:40, 640:1280] = jnp.zeros((3, 640), jnp.float32)


def rows_kernel(marks, *refs):
    pieces, out = refs[:4], refs[4]
    for j in range(4):
        at = pl.multiple_of(lax.rem(marks[6] + j, 4) * 64, 8)
        out[pl.ds(at, 64), :] = pieces[j][...]


def residual_kernel(marks, source, first, second, third, fourth, out, sums):
    t = marks[6]
    at = pl.multiple_of(t * 80, 8)
    sums[...] = jnp.zeros_like(sums)
    for b in range(2):
        for k in range(4):
            place = 4 * b + k
            packed = source[place, pl.ds(at, 80), :] + (
                (first[place] + second[place]) + (third[place] + fourth[place])
            )
            out[place] = packed
            values = unpack_quarter(packed)
            sums[2 * b : 2 * b + 1, :] += column_sum(values)
            sums[2 * b + 1 : 2 * b + 2, :] += column_sum(values * values)


def span_of_item(marks, b):
    return jnp.where(marks[4] == b, marks[0], marks[2])


def norm_kernel(marks, residual, first, second, third, fourth, out, stats):
    total = (first[...] + second[...]) + (third[...] + fourth[...])
    for b in range(2):
        span = span_of_item(marks, b)
        mean, inv = group_row_stats(
            total[2 * b : 2 * b + 1, :], total[2 * b + 1 : 2 * b + 2, :], span
        )
        stats[2 * b : 2 * b + 1, :] = mean
        stats[2 * b + 1 : 2 * b + 2, :] = inv
        for k in range(4):
            values = unpack_quarter(residual[4 * b + k])
            centred = (values - mean) * inv * quarter_mask(span, marks[6])
            put_quarter(out, 4 * b + k, centred)
            out[4 * b + k, 80:88, :] = jnp.zeros((8, 128), jnp.float32)
            for row, value in ((80, mean), (82, inv)):
                out[4 * b + k, row : row + 1, :] = value[:, :128]
                out[4 * b + k, row + 1 : row + 2, 0:32] = value[:, 128:]


def centred_of(marks, residual, stats, b, k):
    values = unpack_quarter(residual[4 * b + k])
    mean, inv = stats[2 * b : 2 * b + 1, :], stats[2 * b + 1 : 2 * b + 2, :]
    return (values - mean) * inv * quarter_mask(span_of_item(marks, b), marks[6])


def norm_sums_kernel(marks, grad, residual, stats, gain, sums):
    sums[...] = jnp.zeros_like(sums)
    for b in range(2):
        for k in range(4):
            centred = centred_of(marks, residual, stats, b, k)
            values = unpack_quarter(grad[4 * b + k])
            scaled = values * gain[...]
            sums[3 * b : 3 * b + 1, :] += column_sum(scaled)
            sums[3 * b + 1 : 3 * b + 2, :] += column_sum(scaled * centred)
            sums[3 * b + 2 : 3 * b + 3, :] += column_sum(values * centred)


def sum_in_order(pieces, t):
    total = None
    for part in range(4):
        j = lax.rem(part - t + 4, 4)
        value = jnp.where(
            j < 2,
            jnp.where(j == 0, pieces[0][...], pieces[1][...]),
            jnp.where(j == 2, pieces[2][...], pieces[3][...]),
        )
        total = value if total is None else total + value
    return total


def norm_back_kernel(marks, *refs):
    grad, residual, stats, gain, base = refs[:5]
    pieces, out, grad_gain = refs[5:9], refs[9], refs[10]
    total = sum_in_order(pieces, marks[6])
    grad_gain[...] = jnp.zeros_like(grad_gain)
    grad_gain[0:1, :] = total[2:3, :] + total[5:6, :]
    for b in range(2):
        span = span_of_item(marks, b)
        count = (span * 160).astype(jnp.float32)
        first = group_rows(total[3 * b : 3 * b + 1, :]) / count
        second = group_rows(total[3 * b + 1 : 3 * b + 2, :]) / count
        inv = stats[2 * b + 1 : 2 * b + 2, :]
        for k in range(4):
            centred = centred_of(marks, residual, stats, b, k)
            scaled = unpack_quarter(grad[4 * b + k]) * gain[...]
            values = inv * quarter_mask(span, marks[6]) * (scaled - first - centred * second)
            put_quarter(out, 4 * b + k, values + unpack_quarter(base[4 * b + k]))


def input_sums_kernel(marks, source, gain, stats, *refs):
    pieces, out, sums = refs[:4], refs[4], refs[5]
    at = pl.multiple_of(marks[6] * 80, 8)
    sums[...] = jnp.zeros_like(sums)
    for b in range(2):
        span = span_of_item(marks, b)
        mine = marks[4] ^ b
        mean, inv = stats[mine, 0:1, :], stats[mine, 1:2, :]
        for k in range(4):
            place = 4 * b + k
            values = unpack_quarter(source[place, pl.ds(at, 80), :])
            centred = (values - mean) * inv * quarter_mask(span, marks[6])
            norm = centred * gain[...]
            gate = jax.nn.sigmoid(norm)
            packed = (pieces[0][place] + pieces[1][place]) + (pieces[2][place] + pieces[3][place])
            grad = unpack_quarter(packed) * gate * (1.0 + norm * (1.0 - gate))
            put_quarter(out, place, grad)
            scaled = grad * gain[...]
            sums[3 * b : 3 * b + 1, :] += column_sum(scaled)
            sums[3 * b + 1 : 3 * b + 2, :] += column_sum(scaled * centred)
            sums[3 * b + 2 : 3 * b + 3, :] += column_sum(grad * centred)


def input_back_kernel(marks, grad, source, gain, stats, base, extra, *refs):
    pieces, out, grad_gain = refs[:4], refs[4], refs[5]
    at = pl.multiple_of(marks[6] * 80, 8)
    total = sum_in_order(pieces, marks[6])
    grad_gain[...] = jnp.zeros_like(grad_gain)
    grad_gain[0:1, :] = total[2:3, :] + total[5:6, :]
    for b in range(2):
        span = span_of_item(marks, b)
        count = (span * 160).astype(jnp.float32)
        first = group_rows(total[3 * b : 3 * b + 1, :]) / count
        second = group_rows(total[3 * b + 1 : 3 * b + 2, :]) / count
        mine = marks[4] ^ b
        mean, inv = stats[mine, 0:1, :], stats[mine, 1:2, :]
        for k in range(4):
            place = 4 * b + k
            keep = quarter_mask(span, marks[6])
            centred = (unpack_quarter(source[place, pl.ds(at, 80), :]) - mean) * inv * keep
            scaled = unpack_quarter(grad[place]) * gain[...]
            values = inv * keep * (scaled - first - centred * second)
            put_quarter(out, place, values + unpack_quarter(base[place]))
            out[place, 80:88, :] = extra[place]


def run_kernel(body, marks, inputs, outs, scratch, flops):
    in_smem = pl.BlockSpec(memory_space=pltpu.SMEM)
    in_vmem = pl.BlockSpec(memory_space=pltpu.VMEM)
    return pl.pallas_call(
        body,
        out_shape=[jax.ShapeDtypeStruct(shape, jnp.float32) for shape in outs],
        in_specs=[in_smem] + [in_vmem] * len(inputs),
        out_specs=[in_vmem] * len(outs),
        scratch_shapes=[pltpu.VMEM(shape, kind) for shape, kind in scratch],
        compiler_params=pltpu.CompilerParams(vmem_limit_bytes=56 * 1024 * 1024),
        cost_estimate=pl.CostEstimate(
            flops=flops, bytes_accessed=10 * 1024 * 1024, transcendentals=0
        ),
    )(marks, *inputs)


def weight_kernel(plan, *refs):
    count = 1 + max(which for block in plan for _, _, which in block)
    lefts, right, out = refs[:count], refs[count], refs[-1]
    tokens = right.shape[0]
    for number, block in enumerate(plan):

        @pl.when(pl.program_id(0) == number)
        def _():
            for begin, columns, which in block:
                top, low = halves(right[:, begin : begin + columns])
                if tokens <= 64:
                    stacked = jnp.concatenate([top, low, top], axis=0)
                for m in range(0, 1280, 256):
                    cells = lefts[which][:, m : m + 256].T
                    if tokens <= 64:
                        first, second = halves(cells)
                        first = jnp.concatenate([first, first, second], axis=1)
                        part = jnp.dot(first, stacked, preferred_element_type=jnp.float32)
                    else:
                        part = dot_halves(halves(cells), (top, low), 1, 0)
                    out[m : m + 256, begin : begin + columns] = part


def weight_grads(plan, lefts, right, first=0, blocks=None, into=None):
    tokens = right.shape[0]
    blocks = blocks or len(plan)
    in_specs = [pl.BlockSpec((tokens, 1280), lambda i: (0, 0))] * len(lefts)
    in_specs.append(pl.BlockSpec((tokens, 1280), lambda i: (0, i)))
    inputs, alias = (*lefts, right), {}
    if into is not None:
        in_specs.append(pl.BlockSpec(memory_space=pl.ANY))
        alias = {len(inputs): 0}
        inputs = (*inputs, into)
    return pl.pallas_call(
        functools.partial(weight_kernel, plan),
        out_shape=jax.ShapeDtypeStruct((1280, 1280 * blocks), jnp.float32),
        grid=(len(plan),),
        in_specs=in_specs,
        out_specs=pl.BlockSpec((1280, 1280), lambda i: (0, i + first)),
        input_output_aliases=alias,
        compiler_params=pltpu.CompilerParams(vmem_limit_bytes=48 * 1024 * 1024),
        cost_estimate=pl.CostEstimate(
            flops=6 * tokens * 1280 * 1280 * len(plan),
            bytes_accessed=7 * 1024 * 1024 * len(plan),
            transcendentals=0,
        ),
    )(*inputs)


def after(values, *events):
    return lax.optimization_barrier((values,) + events)[0]


def together(*values):
    return lax.optimization_barrier(values)


def small(body, marks, inputs, outs, scratch=()):
    return run_kernel(body, marks, inputs, outs, scratch, 4 * 1024 * 1024)


CONV_FLOPS = 6 * 2048 * 1440 * 320


def first_conv(marks, source, gain, tau, weight):
    f32, b16 = jnp.float32, jnp.bfloat16
    return run_kernel(
        first_kernel,
        marks,
        (source, gain, tau, weight),
        [(4, 320, 256), (4, 320, 256), (2, IMAGE_ROWS, 160), (2, 8, 160)],
        [
            ((IMAGE_ROWS, 480), f32),
            ((1440, 320), b16),
            ((1440, 320), b16),
            ((4, 256, 160), f32),
        ],
        CONV_FLOPS,
    )


def second_conv(marks, strips, gain, weight):
    f32, b16 = jnp.float32, jnp.bfloat16
    return run_kernel(
        second_kernel,
        marks,
        (*strips, gain, weight),
        [(8, 80, 128)] * 4 + [(2, IMAGE_ROWS, 320), (2, 8, 320)],
        [
            ((IMAGE_ROWS, 960), f32),
            ((2880, 160), b16),
            ((2880, 160), b16),
            ((256, 160), f32),
        ],
        CONV_FLOPS,
    )


def second_conv_back(marks, quarters, weight):
    f32, b16 = jnp.float32, jnp.bfloat16
    return run_kernel(
        second_back_kernel,
        marks,
        (*quarters, weight),
        [(4, 320, 256), (4, 320, 256), (2, IMAGE_ROWS, 160)],
        [((IMAGE_ROWS, 480), f32), ((1440, 320), b16), ((1440, 320), b16)],
        CONV_FLOPS,
    )


def first_conv_back(marks, grads, strips, gain, stats, weight):
    f32, b16 = jnp.float32, jnp.bfloat16
    return run_kernel(
        first_back_kernel,
        marks,
        (*grads, *strips, gain, stats, weight),
        [(8, 80, 128)] * 4 + [(2, IMAGE_ROWS, 320), (2, 320), (1, 320)],
        [
            ((IMAGE_ROWS, 960), f32),
            ((2880, 160), b16),
            ((2880, 160), b16),
            ((256, 160), f32),
            ((4, 256, 320), f32),
            ((4, 256, 320), f32),
        ],
        CONV_FLOPS,
    )


def conv_weight(marks, image, cells, sign):
    return run_kernel(
        functools.partial(conv_weight_kernel, sign),
        marks,
        (image, cells),
        [(9, 160, 320)],
        [((IMAGE_ROWS, 480), jnp.float32)],
        CONV_FLOPS,
    )[0]


def heads_of(values, count):
    return values.reshape(values.shape[0], count, HEAD_DIM)


def ein(form, left, right):
    return jnp.einsum(form, left, right, precision=high, preferred_element_type=jnp.float32)


def soft_attend(queries, keys, values, key_valid, count):
    scores = ein(QK, heads_of(queries, count), heads_of(keys, count)) * (1.0 / math.sqrt(HEAD_DIM))
    if key_valid is not None:
        scores = jnp.where(key_valid[None, None, :], scores, masked_score)
    exponent = jnp.exp(scores - jnp.max(scores, axis=-1, keepdims=True))
    weights = exponent / jnp.sum(exponent, axis=-1, keepdims=True)
    attended = ein(PV, weights, heads_of(values, count))
    return attended.reshape(queries.shape), weights


def soft_back(queries, keys, values, count, weights, attended, grad_out):
    scaling = 1.0 / math.sqrt(HEAD_DIM)
    grad_heads = heads_of(grad_out, count)
    grad_soft = ein(QK, grad_heads, heads_of(values, count))
    delta = jnp.sum(grad_heads * heads_of(attended, count), axis=-1).T
    grad_scores = weights * (grad_soft - delta[..., None])
    grad_query = ein(PV, grad_scores, heads_of(keys, count)) * scaling
    grad_key = ein(PQ, grad_scores, heads_of(queries, count)) * scaling
    grad_value = ein(PQ, weights, grad_heads)
    return (
        grad_query.reshape(queries.shape),
        grad_key.reshape(keys.shape),
        grad_value.reshape(values.shape),
    )


def layer_grad(grad_out, centred, inv_std, gain_vector):
    scaled = grad_out * gain_vector
    grad_in = inv_std * (
        scaled
        - jnp.mean(scaled, axis=-1, keepdims=True)
        - centred * jnp.mean(scaled * centred, axis=-1, keepdims=True)
    )
    return grad_in, jnp.sum(grad_out * centred, axis=0)


def layer_forward(values, gain_vector):
    mean_val = jnp.mean(values, axis=-1, keepdims=True)
    var_val = jnp.mean(values * values, axis=-1, keepdims=True) - mean_val * mean_val
    inv_std = lax.rsqrt(var_val + norm_eps)
    centred = (values - mean_val) * inv_std
    return centred * gain_vector, centred, inv_std


def gather_plane(block):
    return lax.all_gather(block, IH, axis=0, tiled=True)


def scatter_plane(block):
    return lax.psum_scatter(block, IH, scatter_dimension=0, tiled=True)


def grid_cells(bucket):
    strip_rows, strip_width = grid_shape(bucket)
    return strip_rows * strip_width


def fast_shards(
    hidden,
    text_states,
    bucket,
    timestep,
    gain_in,
    conv_first,
    time_weight,
    gain_mid,
    conv_second,
    gain_attn_norm,
    proj_in,
    gain_self,
    query_self,
    key_self,
    value_self,
    out_self,
    gain_cross,
    query_cross,
    key_cross,
    value_cross,
    out_cross,
    gain_ff,
    ff_in,
    ff_out,
    proj_out,
    cotangent,
):
    item, h, t = lax.axis_index(I), lax.axis_index(H), lax.axis_index(T)
    block = item * 4 + h
    width, wide = 160, 320
    channels = 1280

    def rows_of(values):
        return [values[64 * j : 64 * j + 64] for j in range(4)]

    own_span = grid_cells(bucket[0])
    slot = jnp.arange(256, dtype=jnp.int32)
    own_valid = (slot < own_span).astype(jnp.float32)[:, None]
    both = jnp.stack([bucket[0], timestep[0]]).astype(jnp.float32)
    both_other = swap(both)
    times = jnp.stack([both[1], both_other[1]])
    other_rows, other_width = grid_shape(both_other[0].astype(jnp.int32))
    own_rows, own_width = grid_shape(bucket[0])
    marks = jnp.stack(
        [own_span, own_width, other_rows * other_width, other_width, item, h, t]
    ).astype(jnp.int32)

    (source,) = small(pack_kernel, marks, (hidden[0] * own_valid,), [(8, 320, 128)])
    source = plane_exchange(source)
    gains = jnp.stack([gain_self, gain_cross, gain_ff], axis=1)
    attn_full = gather_plane(
        jnp.concatenate(
            [
                query_self,
                key_self,
                value_self,
                proj_out,
                out_self.T,
                jnp.pad(gains, ((0, 0), (0, 125))),
            ],
            axis=1,
        )
    )
    qkv_full = attn_full[:, :960]
    proj_out_full = attn_full[:, 960:1280]
    out_self_full = attn_full[:, 1280:1600]
    gain_rows = attn_full[:, 1600:1603].T
    gain_self_full, gain_cross_full, gain_ff_full = (gain_rows[k : k + 1] for k in range(3))

    own_third = jnp.concatenate([proj_in.T, query_cross, out_cross.T], axis=1)
    own_third = jnp.concatenate(
        [own_third, jnp.pad(gain_attn_norm[None, :], ((0, 7), (0, 640)))], axis=0
    )
    third_pieces = [own_third, turn(own_third, 3), turn(own_third[:, :512], 2), turn(own_third, 1)]

    features = jax.nn.silu(time_features(times, channels))
    own_features = lax.dynamic_slice_in_dim(features, block * width, width, 1)
    tau = mm(own_features, time_weight, 1, 0)
    second_weight = conv_second.transpose(0, 1, 3, 2).reshape(9 * width, wide)
    own_one, other_one, image_one, stats_one = first_conv(
        marks, source, gain_in[None, :], tau, conv_first.reshape(9 * width, wide)
    )
    own_one, other_one, *third_pieces = together(own_one, other_one, *third_pieces)
    own_one = own_one + swap(other_one)
    strips_one, part = plane_sum(own_one)
    third_rest = turn(own_third[:, 512:], 2)
    third_pieces[2] = jnp.concatenate([third_pieces[2], third_rest], axis=1)
    third, gain_attn_full = small(
        third_kernel, marks, after(third_pieces, part), [(160, 3840), (1, channels)]
    )
    third_full = gather_plane(third)
    proj_in_full = third_full[:, :1280]
    query_cross_full = third_full[:, 1280:2560]
    out_cross_full = third_full[:, 2560:]
    ff_out_full = gather_plane(after(ff_out.T, third))
    cot = after(cotangent[0] * own_valid, own_one)
    grad_ff_part = mm(cot, proj_out_full, 1, 1)
    cot_pieces = z_all(jnp.concatenate([grad_ff_part, cot], axis=1).reshape(4, 64, channels + wide))
    *strips_one, cot_pieces = together(*strips_one, cot_pieces)

    *conv_two, image_two, stats_two = second_conv(
        marks, strips_one, gain_mid[None, :], second_weight
    )
    conv_two_pieces = z_received(conv_two)

    event = conv_two[0]
    grad_after_ff, cot_packed = small(
        cotangent_kernel,
        marks,
        (after(cot_pieces, event),),
        [(64, channels), (8, 80, 128)],
        [((64, channels), jnp.float32)],
    )
    cot_q = plane_exchange(cot_packed)
    text_here = after(text_states[0], event)
    text_own = lax.dynamic_slice_in_dim(text_here, block * 256, 256, 1)
    text_other = swap(lax.dynamic_slice_in_dim(text_here, ((1 - item) * 4 + h) * 256, 256, 1))
    text_weight = jnp.concatenate([key_cross, value_cross], axis=1)
    text_part = mm(text_own, text_weight, 1, 0) + swap(mm(text_other, text_weight, 1, 0))

    residual_q, sums = small(
        residual_kernel, marks, (source, *conv_two_pieces), [(8, 80, 128), (8, width)]
    )
    centred_three, stats_three = small(
        norm_kernel, marks, (residual_q, *z_pieces(sums)), [(8, 88, 128), (8, width)]
    )
    norm_three, residual_s = small(
        unpack_norm_kernel,
        marks,
        (plane_exchange(centred_three), gain_attn_full),
        [(64, channels), (64, channels)],
    )
    projected = mm(norm_three, proj_in_full, 1, 1)

    normed_self, centred_self, inv_self = layer_forward(projected, gain_self_full)
    normed_pieces = z_pieces(normed_self)
    text_sum = h_sum(after(text_part, normed_self))
    *normed_pieces, text_sum, cot_q = together(*normed_pieces, text_sum, cot_q)
    normed_self_all = jnp.concatenate(normed_pieces, axis=0)
    qkv = mm(normed_self_all, qkv_full, 1, 0)
    own_kv = qkv[:, wide:]
    kv_pieces = [own_kv] + [flip(own_kv, j) for j in (1, 2, 3)]
    text_sum, grad_here = after((text_sum, grad_after_ff), own_kv)
    side_pieces = z_spread(jnp.concatenate([grad_here, folded(text_sum)], axis=0))
    *kv_pieces, side_pieces = together(*kv_pieces, side_pieces)
    attn_self, totals_self = small(
        attend_kernel,
        marks,
        (qkv, *kv_pieces),
        [(256, wide), (8, 256)],
        [((1024, 256), jnp.float32)],
    )
    ff_in_full = gather_plane(after(ff_in.reshape(160, 2560), attn_self))
    self_part = mm(attn_self, out_self_full, 1, 1)
    self_pieces = z_received(rows_of(self_part))
    self_sum = total_of(self_pieces)
    event = self_pieces[1]
    grad_after_ff_all, keys_text, values_text = small(
        text_kernel,
        marks,
        (after(side_pieces, event),),
        [(256, channels), (77, channels), (77, channels)],
    )
    grad_ff_act = mm(grad_after_ff_all, ff_out_full, 1, 0)
    self_sum, grad_ff_act, keys_text, values_text = together(
        self_sum, grad_ff_act, keys_text, values_text
    )
    after_self = projected + self_sum

    normed_cross, centred_cross, inv_cross = layer_forward(after_self, gain_cross_full)
    queries_cross = mm(normed_cross, query_cross_full, 1, 0)
    attn_cross, weights_cross = soft_attend(queries_cross, keys_text, values_text, None, 20)
    after_cross = after_self + mm(attn_cross, out_cross_full, 1, 1)

    normed_ff, centred_ff, inv_ff = layer_forward(after_cross, gain_ff_full)
    normed_ff_all = jnp.concatenate(z_pieces(normed_ff), axis=0)
    hidden_ff = mm(normed_ff_all, ff_in_full, 1, 0)
    value_half, gate_half = hidden_ff[:, :channels], hidden_ff[:, channels:]
    phi = 0.5 * (1.0 + lax.erf(gate_half * math.sqrt(0.5)))
    slope = phi + gate_half * jnp.exp(-0.5 * gate_half * gate_half) * (1.0 / math.sqrt(2 * math.pi))
    gate_act = gate_half * phi
    ff_act = value_half * gate_act
    grad_value = grad_ff_act * gate_act
    grad_gate = grad_ff_act * value_half * slope
    grad_hidden_ff = jnp.concatenate([grad_value, grad_gate], axis=1)
    grad_normed_part = mm(grad_hidden_ff, ff_in_full, 1, 1)
    normed_pieces = z_received(rows_of(grad_normed_part))
    grad_normed_ff = total_of(normed_pieces)
    ff_right = jnp.concatenate(after([grad_hidden_ff, ff_act], normed_pieces[1]), axis=1)
    ff_grads = weight_grads(
        (((0, 1280, 0),), ((0, 1280, 0),), ((0, 1280, 1),)),
        (normed_ff_all, grad_after_ff_all),
        ff_right,
        0,
        5,
    )
    out_part = mm(after(ff_act, normed_pieces[1]), ff_out_full, 1, 1)
    grad_normed_ff, ff_grads, out_part = together(grad_normed_ff, ff_grads, out_part)

    back_ff, grad_gain_ff = layer_grad(grad_normed_ff, centred_ff, inv_ff, gain_ff_full)
    grad_after_cross = grad_after_ff + back_ff
    grad_attn_cross = mm(grad_after_cross, out_cross_full, 1, 0)
    grad_queries_cross, grad_keys_text, grad_values_text = soft_back(
        queries_cross, keys_text, values_text, 20, weights_cross, attn_cross, grad_attn_cross
    )
    grad_normed_cross = mm(grad_queries_cross, query_cross_full, 1, 1)
    back_cross, grad_gain_cross = layer_grad(
        grad_normed_cross, centred_cross, inv_cross, gain_cross_full
    )
    grad_after_self = grad_after_cross + back_cross
    grad_pieces = z_pieces(grad_after_self)
    cross_right = after((grad_queries_cross, attn_cross), grad_pieces[1])
    cross_right = jnp.concatenate(
        [side[:, wide * k : wide * k + wide] for k in range(4) for side in cross_right], axis=1
    )
    cross_grads = weight_grads(
        (((0, 320, 0), (320, 320, 1), (640, 320, 0), (960, 320, 1)),) * 2,
        (normed_cross, grad_after_cross),
        cross_right,
        3,
        5,
        ff_grads,
    )
    *grad_pieces, cross_grads = together(*grad_pieces, cross_grads)
    out_turned = jnp.concatenate([out_part, out_part], axis=0)
    out_turned = lax.dynamic_slice_in_dim(out_turned, lax.rem(4 - t, 4) * 64, 256, 0)
    out_sum = z_all(after(out_turned, grad_after_self).reshape(4, 64, channels))
    ff_grads = scatter_plane(cross_grads)
    ff_grads, cross_grads = ff_grads[:, :3840], ff_grads[:, 3840:]

    grad_after_self_all = jnp.concatenate(grad_pieces, axis=0)
    grad_attn_self = mm(grad_after_self_all, out_self_full, 1, 0)
    grad_queries, *kv_pieces = small(
        attend_back_kernel,
        marks,
        (qkv, *kv_pieces, totals_self, attn_self, grad_attn_self),
        [(256, wide)] + [(256, 2 * wide)] * 4,
    )
    kv_pieces = kv_pieces[:1] + [flip(kv_pieces[j], j) for j in (1, 2, 3)]
    grad_kv = total_of(kv_pieces)
    grad_qkv = jnp.concatenate([grad_queries, grad_kv], axis=1)
    grad_normed_part = mm(grad_qkv, qkv_full, 1, 1)
    normed_pieces = z_received(rows_of(grad_normed_part))
    grad_normed_self = total_of(normed_pieces)
    text_grads = small(
        text_grad_kernel,
        marks,
        after((grad_keys_text, grad_values_text), normed_pieces[1]),
        [(40, channels)] * 4,
    )
    grad_normed_self, out_sum, *text_grads = together(grad_normed_self, out_sum, *text_grads)
    back_self, grad_gain_self = layer_grad(grad_normed_self, centred_self, inv_self, gain_self_full)
    grad_projected = grad_after_self + back_self
    grad_norm_three = mm(grad_projected, proj_in_full, 1, 0)

    (grad_three,) = small(pack_kernel, marks, (grad_norm_three,), [(8, 80, 128)])
    grad_three_q = plane_exchange(grad_three)
    out_sum = jnp.sum(after(out_sum, grad_three), axis=0)
    text_grads = total_of(z_received(after(text_grads, grad_three)))
    grad_three_q, text_grads = together(grad_three_q, text_grads)
    gain_block = lax.dynamic_slice_in_dim(gain_attn_full, block * width, width, 1)
    (sums,) = small(
        norm_sums_kernel, marks, (grad_three_q, residual_q, stats_three, gain_block), [(8, width)]
    )
    grad_residual_q, grad_gain_three = small(
        norm_back_kernel,
        marks,
        (grad_three_q, residual_q, stats_three, gain_block, cot_q, *z_pieces(sums)),
        [(8, 80, 128), (8, width)],
    )

    residual_pieces = z_pieces(grad_residual_q)
    text_grads = after(text_grads, grad_residual_q)
    text_grads = text_grads + flip(text_grads, 1)
    attn_right = jnp.concatenate(
        [
            jnp.concatenate([grad_qkv, attn_self], axis=1),
            jnp.pad(norm_three, ((0, 192), (0, 0))),
        ],
        axis=1,
    )
    attn_grads = weight_grads(
        (((0, 960, 0), (960, 320, 1)), ((0, 1280, 2),)),
        (
            normed_self_all,
            grad_after_self_all,
            jnp.pad(grad_projected, ((0, 192), (0, 0))),
        ),
        after(attn_right, residual_pieces[1]),
    )
    *residual_pieces, text_grads, attn_grads = together(*residual_pieces, text_grads, attn_grads)
    attn_grads = scatter_plane(attn_grads)
    own_two, other_two, image_back = second_conv_back(marks, residual_pieces, second_weight)
    own_two = own_two + swap(other_two)
    grad_act_two, part = plane_sum(own_two)
    side = jnp.concatenate(
        [
            jnp.broadcast_to((after_cross + out_sum)[None], (4, 64, channels)),
            jnp.moveaxis(residual_s.reshape(64, 4, wide), 1, 0),
        ],
        axis=2,
    )
    gain_rows = jnp.stack([grad_gain_self, grad_gain_cross, grad_gain_ff])
    gain_rows = jnp.broadcast_to(jnp.pad(gain_rows, ((0, 5), (0, wide)))[None], (4, 8, 1600))
    side = z_all(after(jnp.concatenate([side, gain_rows], axis=1), own_two))
    side_here = after(side, part)
    after_ff_all = side_here[:, :64, :channels].reshape(256, channels)
    residual_all = side_here[:, :64, channels:].reshape(256, wide)
    gain_sums = jnp.sum(side_here[:, 64:67, :channels], axis=0)
    *grad_act_two, after_ff_all, gain_sums, residual_all = together(
        *grad_act_two, after_ff_all, gain_sums, residual_all
    )

    *grad_act_one, image_grad, grad_tau, grad_gain_mid = first_conv_back(
        marks,
        grad_act_two,
        strips_one,
        gain_mid[None, :],
        stats_two,
        conv_first.reshape(9 * width, wide),
    )
    grad_act_pieces = z_received(grad_act_one)
    image_grad, text_grads = after((image_grad, text_grads), grad_act_pieces[1])
    text_grads = text_grads + flip(text_grads, 2)
    grad_conv_first = conv_weight(marks, image_one, image_grad, 1)
    cross_cut = after(cross_grads, grad_act_pieces[1])
    cross_cut = [
        lax.dynamic_slice_in_dim(cross_cut, lax.rem(t + j, 4) * 640, 640, 1) for j in range(4)
    ]
    *grad_act_pieces, grad_conv_first, text_grads, cross_cut = together(
        *grad_act_pieces, grad_conv_first, text_grads, cross_cut
    )
    grad_conv_first = grad_conv_first.reshape(3, 3, width, wide)
    extra = jnp.concatenate(
        [
            jnp.broadcast_to(grad_gain_three[0], (8, 1, width)),
            jnp.moveaxis(gain_sums.reshape(3, 8, width), 1, 0),
        ],
        axis=1,
    )
    extra = jnp.concatenate(
        [extra[:, :, :128], jnp.pad(extra[:, :, 128:], ((0, 0), (0, 0), (0, 96)))], axis=1
    )
    grad_input_q, sums = small(
        input_sums_kernel,
        marks,
        (source, gain_in[None, :], stats_one, *grad_act_pieces),
        [(8, 80, 128), (8, width)],
    )
    cross_received = z_received(after(cross_cut, grad_input_q))
    moved, grad_gain_in = small(
        input_back_kernel,
        marks,
        (
            grad_input_q,
            source,
            gain_in[None, :],
            stats_one,
            grad_residual_q,
            extra,
            *z_pieces(sums),
        ),
        [(8, 88, 128), (8, width)],
    )
    received = plane_exchange(moved)
    text_grads, image_back, after_ff_here, attn_grads = after(
        (text_grads, image_back, after_ff_all, attn_grads), moved
    )
    proj_cut = attn_grads[:, 1280:].reshape(width, 4, wide)
    proj_share = total_of(z_received([pick(proj_cut, lax.rem(t + j, 4), 1) for j in range(4)]))
    text_other_grads = swap(text_grads)
    grad_proj_out = mm(after_ff_here, cot, 0, 0).reshape(2, 4, width, wide)
    grad_proj_own = pick(grad_proj_out, item) + swap(pick(grad_proj_out, 1 - item))
    grad_conv_second = conv_weight(marks, image_back, image_two, -1)
    received, text_other_grads, grad_proj_own, grad_conv_second = together(
        received, text_other_grads, grad_proj_own, grad_conv_second
    )
    grad_conv_second = grad_conv_second.reshape(3, 3, width, wide).transpose(0, 1, 3, 2)
    text_grads, text_other_grads = unfolded(text_grads), unfolded(text_other_grads)
    (grad_hidden,) = small(unpack_kernel, marks, (received,), [(64, channels)])
    hidden_pieces = z_pieces(grad_hidden)
    cross_shares = total_of(after(cross_received, hidden_pieces[1]))
    after_ff_all, grad_proj_own = after((after_ff_all, grad_proj_own), grad_hidden)
    grad_proj_out = h_collect([pick(grad_proj_own, h ^ j) for j in range(4)])
    output = residual_all + mm(after_ff_all, proj_out_full, 1, 0)
    output = output * own_valid
    grad_text_weight = mm(text_own, text_grads, 0, 0) + mm(text_other, text_other_grads, 0, 0)
    grad_time_weight = mm(own_features, grad_tau, 0, 0)
    (grad_hidden,) = small(rows_kernel, marks, hidden_pieces, [(256, channels)])
    extra = jnp.concatenate([received[:, 80:84, :], received[:, 84:88, :32]], axis=2)
    grad_gain_attn = lax.dynamic_slice_in_dim(extra[:, 0].reshape(channels), t * wide, wide, 0)
    gain_sums = jnp.sum(extra[:, 1:], axis=0)

    return (
        output[None],
        grad_hidden[None],
        grad_gain_in[0],
        grad_conv_first,
        grad_time_weight,
        grad_gain_mid[0],
        grad_conv_second,
        grad_gain_attn,
        proj_share.T,
        gain_sums[0],
        attn_grads[:, :320],
        attn_grads[:, 320:640],
        attn_grads[:, 640:960],
        attn_grads[:, 960:1280].T,
        gain_sums[1],
        cross_shares[:, :320],
        grad_text_weight[:, :wide],
        grad_text_weight[:, wide:],
        cross_shares[:, 320:].T,
        gain_sums[2],
        ff_grads[:, :2560].reshape(width, 2, channels),
        ff_grads[:, 2560:].T,
        grad_proj_out,
    )


def solution(mesh):
    placed = (
        P(I, H, None),
        P(I, None, None),
        P(I),
        P(I),
        P(IH),
        P(None, None, IH, T),
        P(IH, T),
        P(T),
        P(None, None, T, IH),
        P(T),
        P(T, IH),
        P(IH),
        P(IH, T),
        P(IH, T),
        P(IH, T),
        P(T, IH),
        P(IH),
        P(IH, T),
        P(IH, T),
        P(IH, T),
        P(T, IH),
        P(IH),
        P(IH, None, T),
        P(T, IH),
        P(IH, T),
        P(I, H, T),
    )
    sizes = (mesh.shape[I], mesh.shape[H], mesh.shape[T])
    body = fast_shards if sizes == (2, 4, 4) else shards
    return jax.shard_map(
        body,
        mesh=mesh,
        in_specs=placed,
        out_specs=(
            P(I, H, T),
            P(I, H, None),
            P(IH),
            P(None, None, IH, T),
            P(IH, T),
            P(T),
            P(None, None, T, IH),
            P(T),
            P(T, IH),
            P(IH),
            P(IH, T),
            P(IH, T),
            P(IH, T),
            P(T, IH),
            P(IH),
            P(IH, T),
            P(IH, T),
            P(IH, T),
            P(T, IH),
            P(IH),
            P(IH, None, T),
            P(T, IH),
            P(IH, T),
        ),
        check_vma=False,
    )
```
